32 devices in a mesh: grp: 4 (over y, x), tok: 8 (over z, core).
Axes of the slice: x: 2, y: 2, z: 4, core: 2. Of those that a mesh axis runs over, the one named last changes fastest.
Arguments:
- hidden_in: bfloat16 [4096, 960], P(('grp', 'tok')), may hold values from -6 to 6
- cotangent: bfloat16 [4096, 960], P(('grp', 'tok')), may hold values from -6 to 6
- lengths: int32 [4, 3], P('grp'), may hold values from 1 to 512, 1024 in all within a row
- active: int32 [3, 4096], P(None, ('grp', 'tok')), may hold values from 0 to 1, as said below
- norm_attn: bfloat16 [960], P('tok'), may hold values from 0.5 to 1.5
- w_query: bfloat16 [960, 960], P('tok'), may hold values from -0.1875 to 0.1875
- w_key: bfloat16 [960, 320], P('tok'), may hold values from -0.1875 to 0.1875
- w_value: bfloat16 [960, 320], P('tok'), may hold values from -0.1875 to 0.1875
- w_out: bfloat16 [960, 960], P('tok'), may hold values from -0.75 to 0.75
- norm_mlp: bfloat16 [960], P('tok'), may hold values from 0.5 to 1.5
- w_gate: bfloat16 [960, 2560], P('tok'), may hold values from -0.1875 to 0.1875
- w_up: bfloat16 [960, 2560], P('tok'), may hold values from -0.1875 to 0.1875
- w_down: bfloat16 [2560, 960], P('tok'), may hold values from -0.125 to 0.125
- w_router: bfloat16 [960], P('tok'), may hold values from -0.1875 to 0.1875
Outputs:
- output: bfloat16 [4096, 960], P(('grp', 'tok'))
- grad_hidden: float32 [4096, 960], P(('grp', 'tok'))
- grad_norm_attn: float32 [960], replicated
- grad_w_query: float32 [960, 960], replicated
- grad_w_key: float32 [960, 320], replicated
- grad_w_value: float32 [960, 320], replicated
- grad_w_out: float32 [960, 960], replicated
- grad_norm_mlp: float32 [960], replicated
- grad_w_gate: float32 [960, 2560], replicated
- grad_w_up: float32 [960, 2560], replicated
- grad_w_down: float32 [2560, 960], replicated
- grad_w_router: float32 [960], replicated
The draws below stay inside these ranges and needn't reach their ends.
Inputs may be any that keep to these rules, and one draw needn't show every extreme that they name: `active`: at recursion r exactly (3 - r) * 256 tokens of each group are 1, and a token that is 1 at recursion r is 1 at every earlier recursion. `lengths`: each row sums to 1024 and its largest entry is exactly 512.
All inputs are finite; a program needn't handle non-finite values.
Results may differ from the reference program's by a relative error of at most 0.024.
Values may be sent and summed in bfloat16 or wider, within the bound.
A program may use at most 320 MiB of HBM per device.

```python
import math
import jax
import jax.numpy as jnp
import numpy as np
from jax import lax

D = 960
H = 15
KVH = 5
HD = 64
FF = 2560
TOK_DEV = 128
RECUR = 3
GROUPS = 4
TOK_GRP = 1024
TOKENS = 4096
NSEQ = 3
LONGEST = 512


def draw_active(key, part):
    blocks = TOK_GRP // TOK_DEV
    device_load = jax.random.randint(jax.random.fold_in(key, 7), (GROUPS, blocks), 0, 4)
    leaning = jnp.repeat(device_load, TOK_DEV, axis=1)
    token_order = jnp.arange(TOK_GRP, dtype=jnp.int32)[None, :]
    group_rows = jnp.arange(GROUPS, dtype=jnp.int32)[:, None]
    selected = jnp.ones((GROUPS, TOK_GRP), jnp.int32)
    stacked = []
    for each_step in range(RECUR):
        noise_draw = jax.random.randint(jax.random.fold_in(key, 100 + each_step), (GROUPS, TOK_GRP), 0, 1024)
        scores = (noise_draw + leaning * 512) * TOK_GRP + token_order
        scores = jnp.where(selected > 0, scores, -1)
        chosen = lax.top_k(scores, (RECUR - each_step) * TOK_GRP // (RECUR + 1))[1]
        selected = jnp.zeros((GROUPS, TOK_GRP), jnp.int32).at[group_rows, chosen].set(1)
        stacked.append(selected.reshape(-1))
    return jnp.stack(stacked)


def level_of(rng, shape, cuts, least, largest):
    def one(position, parts):
        steps = jax.random.uniform(jax.random.fold_in(jax.random.fold_in(rng, 6), position), (parts,), jnp.float32, least / len(cuts), largest / len(cuts))
        return jnp.repeat(jnp.exp(steps), shape[position] // parts).reshape((-1,) + (1,) * (len(shape) - position - 1))

    level = one(*cuts[0])
    for cut in cuts[1:]:
        level = level * one(*cut)
    return level


def length_profile(number_of, total, most, skew):
    loads = [(1 << 20) // math.isqrt(standing ** skew) + 1 for standing in range(2, number_of + 1)]
    surplus, counts = total - most - (number_of - 1), [1] * (number_of - 1)
    while surplus > 0:
        free = [i for i in range(number_of - 1) if counts[i] < most]
        mass, left = sum([loads[i] for i in free]), surplus
        for i in free:
            extra = min(most - counts[i], max(1, left * loads[i] // mass), surplus)
            counts[i] = counts[i] + extra
            surplus = surplus - extra
    return np.array([most] + counts)


def ragged_sizes(own_key, number_of, total, bound, skew):
    if number_of == 2:
        one = jax.random.randint(own_key, (), max(1, total - bound), min(bound, total - 1) + 1)
        return jnp.stack([one, total - one])
    sizes = jnp.asarray(length_profile(number_of, total, bound, skew), jnp.int32)
    couples = (number_of - 1) // 2
    giver, taker = sizes[1:1 + 2 * couples:2], sizes[2:2 + 2 * couples:2]
    margin = jnp.minimum(giver - 1, bound - taker)
    shifted = jax.random.randint(jax.random.fold_in(own_key, 1), (couples,), 0, 1 << 20) % (margin + 1)
    sizes = sizes.at[1:1 + 2 * couples:2].set(giver - shifted).at[2:2 + 2 * couples:2].set(taker + shifted)
    return sizes[jax.random.permutation(jax.random.fold_in(own_key, 2), number_of)]


def centred(rng, dims, scale, most, pieces=(), kind=jnp.bfloat16):
    entries = jax.random.normal(rng, dims, jnp.float32) * scale
    if len(pieces) > 0:
        entries = level_of(rng, dims, pieces, -0.22, 0.18) * entries
    return jnp.clip(entries, min=-most, max=most).astype(kind)


def setup_inputs(seed: int = 0) -> dict:
    key_of = jax.random.split(jax.random.key(seed), 15)
    return {
        "hidden_in": centred(key_of[0], (TOKENS, D), 1.0, 6.0, ((0, 32),)),
        "cotangent": centred(key_of[1], (TOKENS, D), 1.0, 6.0, ((0, 32),)),
        "lengths": jax.vmap(lambda own: ragged_sizes(own, NSEQ, TOK_GRP, LONGEST, 2))(jax.random.split(key_of[2], GROUPS)).reshape((GROUPS, NSEQ)).astype(jnp.int32),
        "active": draw_active(jax.random.fold_in(key_of[14], 71), 0),
        "norm_attn": jnp.clip(1.0 + 0.1 * jax.random.normal(key_of[4], (D,), jnp.float32), 0.5, 1.5).astype(jnp.bfloat16),
        "w_query": centred(key_of[5], (D, H * HD), D ** -0.5, 0.1875, ((0, 8),)),
        "w_key": centred(key_of[6], (D, KVH * HD), D ** -0.5, 0.1875, ((0, 8),)),
        "w_value": centred(key_of[7], (D, KVH * HD), D ** -0.5, 0.1875, ((0, 8),)),
        "w_out": centred(key_of[8], (H * HD, D), (H * HD // 16) ** -0.5, 0.75, ((0, 8),)),
        "norm_mlp": jnp.clip(1.0 + 0.1 * jax.random.normal(key_of[9], (D,), jnp.float32), 0.5, 1.5).astype(jnp.bfloat16),
        "w_gate": centred(key_of[10], (D, FF), D ** -0.5, 0.1875, ((0, 8),)),
        "w_up": centred(key_of[11], (D, FF), D ** -0.5, 0.1875, ((0, 8),)),
        "w_down": centred(key_of[12], (FF, D), FF ** -0.5, 0.125, ((0, 8),)),
        "w_router": centred(key_of[13], (D,), D ** -0.5, 0.1875, ((0, 8),)),
    }


@jax.custom_vjp
def low(v):
    return lax.optimization_barrier(v.astype(jnp.bfloat16)).astype(jnp.float32)

@jax.custom_vjp
def low_back(v):
    return v

def low_keep(v):
    return (low(v), None)

def low_pass(kept, grad):
    return (grad,)

def back_keep(v):
    return (v, None)

def back_low(kept, grad):
    return (low(grad),)
low.defvjp(low_keep, low_pass)
low_back.defvjp(back_keep, back_low)
epsilon = 1e-05
theta = 10000.0
masked = -1000000000.0
highest = lax.Precision.HIGHEST

def matmul(left, right):
    return jnp.dot(left, right, precision=highest, preferred_element_type=jnp.float32)

def norm_apply(values_in, gain_vec):
    inverse_rms = lax.rsqrt(lax.optimization_barrier(jnp.mean(values_in * values_in, axis=-1, keepdims=True)) + epsilon)
    return values_in * inverse_rms * gain_vec

def segment_of(lengths_row, global_rows):
    ends_at = jnp.cumsum(lengths_row)
    return lax.optimization_barrier(jnp.sum((global_rows[:, None] >= ends_at[None, :]).astype(jnp.int32), axis=1))

def position_of(lengths_row, global_rows, segments):
    ends_at = jnp.cumsum(lengths_row)
    starts_at = ends_at - lengths_row
    picked = segments[:, None] == jnp.arange(lengths_row.shape[0], dtype=jnp.int32)[None, :]
    return global_rows - lax.optimization_barrier(jnp.sum(jnp.where(picked, starts_at[None, :], 0), axis=1))

def rotary_tables(positions):
    half_dim = HD // 2
    inverse = jnp.power(theta, -jnp.arange(half_dim, dtype=jnp.float32) * (2.0 / HD))
    angle = positions.astype(jnp.float32)[..., None] * inverse
    return (jnp.cos(angle), jnp.sin(angle))

def rotate(tensor, cosine_table, sine_table):
    half_dim = tensor.shape[-1] // 2
    first_half = tensor[..., :half_dim]
    second_half = tensor[..., half_dim:]
    cos_b = cosine_table[..., None, :]
    sin_b = sine_table[..., None, :]
    return jnp.concatenate([first_half * cos_b - second_half * sin_b, second_half * cos_b + first_half * sin_b], axis=-1)

def group_attention(queries, keys_all, values_all, segments, live_row):
    block_rows = min(512, TOK_GRP)
    reach = -(-(LONGEST - 1) // block_rows) * block_rows
    per_group = H // KVH
    score_scale = HD ** (-0.5)
    key_pad = jnp.concatenate([jnp.zeros((reach, KVH, HD), jnp.float32), keys_all], axis=0)
    value_pad = jnp.concatenate([jnp.zeros((reach, KVH, HD), jnp.float32), values_all], axis=0)
    segment_pad = jnp.concatenate([jnp.full((reach,), -1, jnp.int32), segments])
    live_pad = jnp.concatenate([jnp.zeros((reach,), jnp.float32), live_row])
    global_pad = jnp.arange(reach + TOK_GRP, dtype=jnp.int32) - reach

    def one_block(block_index):
        start_row = (block_index * block_rows).astype(jnp.int32)
        query_block = lax.dynamic_slice_in_dim(queries, start_row, block_rows, 0).reshape(block_rows, KVH, per_group, HD)
        key_block = lax.dynamic_slice_in_dim(key_pad, start_row, reach + block_rows, 0)
        value_block = lax.dynamic_slice_in_dim(value_pad, start_row, reach + block_rows, 0)
        segment_keys = lax.dynamic_slice_in_dim(segment_pad, start_row, reach + block_rows, 0)
        live_keys = lax.dynamic_slice_in_dim(live_pad, start_row, reach + block_rows, 0)
        global_keys = lax.dynamic_slice_in_dim(global_pad, start_row, reach + block_rows, 0)
        segment_query = lax.dynamic_slice_in_dim(segments, start_row, block_rows, 0)
        global_query = start_row + jnp.arange(block_rows, dtype=jnp.int32)
        allowed = (segment_query[:, None] == segment_keys[None, :]) & (global_keys[None, :] <= global_query[:, None]) & (live_keys[None, :] > 0)
        scores = jnp.einsum('rhgd,khd->hgrk', query_block, key_block, precision=highest) * score_scale
        scores = low_back(jnp.where(allowed[None, None], scores, masked))
        probs = jax.nn.softmax(scores, axis=-1)
        mixed_block = jnp.einsum('hgrk,khd->rhgd', low(probs), value_block, precision=highest)
        return mixed_block.reshape(block_rows, H * HD)
    blocks_out = lax.map(jax.checkpoint(one_block), jnp.arange(TOK_GRP // block_rows, dtype=jnp.int32))
    return blocks_out.reshape(TOK_GRP, H * HD)

def recursion(hidden_state, live_f, params, segments, cosine_table, sine_table):
    norm_attn, w_query, w_key, w_value, w_out, norm_mlp, w_gate, w_up, w_down, w_router = params
    flat_rows = hidden_state.reshape(-1, D)
    router_gate = jax.nn.sigmoid(jnp.dot(flat_rows, w_router, precision=highest))
    normed = low(norm_apply(flat_rows, norm_attn))
    queries = low_back(matmul(normed, w_query)).reshape(GROUPS, TOK_GRP, H, HD)
    keys_all = low_back(matmul(normed, w_key)).reshape(GROUPS, TOK_GRP, KVH, HD)
    values_all = low_back(low(matmul(normed, w_value))).reshape(GROUPS, TOK_GRP, KVH, HD)
    queries = low(rotate(queries, cosine_table, sine_table))
    keys_all = low(rotate(keys_all, cosine_table, sine_table))
    mixed_rows = jnp.stack([group_attention(queries[group_index], keys_all[group_index], values_all[group_index], segments[group_index], live_f[group_index]) for group_index in range(GROUPS)])
    mixed_rows = low_back(low(mixed_rows.reshape(-1, H * HD)))
    attn_out = low_back(matmul(mixed_rows, w_out))
    middle = flat_rows + attn_out
    normed_two = low_back(low(norm_apply(middle, norm_mlp)))
    gate_pre = low_back(matmul(normed_two, w_gate))
    up_pre = low_back(matmul(normed_two, w_up))
    hidden_low = low(jax.nn.silu(gate_pre) * up_pre)
    mlp_out = low_back(low(matmul(hidden_low, w_down)))
    factor = live_f.reshape(-1) * router_gate
    return (flat_rows + factor[:, None] * (attn_out + mlp_out)).reshape(GROUPS, TOK_GRP, D)

def reference(hidden_in, cotangent, lengths, active, norm_attn, w_query, w_key, w_value, w_out, norm_mlp, w_gate, w_up, w_down, w_router):
    global_rows = jnp.arange(TOK_GRP, dtype=jnp.int32)
    segments = jnp.stack([segment_of(lengths[group_index], global_rows) for group_index in range(GROUPS)])
    positions = jnp.stack([position_of(lengths[group_index], global_rows, segments[group_index]) for group_index in range(GROUPS)])
    cosine_table, sine_table = rotary_tables(positions)
    live_f = active.astype(jnp.float32).reshape(RECUR, GROUPS, TOK_GRP)
    params = tuple((matrix.astype(jnp.float32) for matrix in (norm_attn, w_query, w_key, w_value, w_out, norm_mlp, w_gate, w_up, w_down, w_router)))

    def forward(start_state, weights):
        current = start_state
        for each_step in range(RECUR):
            current = jax.checkpoint(recursion)(current, live_f[each_step], weights, segments, cosine_table, sine_table)
        return current
    start_state = hidden_in.astype(jnp.float32).reshape(GROUPS, TOK_GRP, D)
    final_state, pullback = jax.vjp(forward, start_state, params)
    grad_start, grad_params = pullback(cotangent.astype(jnp.float32).reshape(GROUPS, TOK_GRP, D))
    return (final_state.reshape(TOKENS, D).astype(jnp.bfloat16), grad_start.reshape(TOKENS, D), grad_params[0], grad_params[1], grad_params[2], grad_params[3], grad_params[4], grad_params[5], grad_params[6], grad_params[7], grad_params[8], grad_params[9])
```

```python
import jax
import jax.numpy as jnp
from jax import lax
from jax.experimental import pallas as pl
from jax.experimental.pallas import tpu as pltpu
from jax.sharding import PartitionSpec as P

MESH = pl.DeviceIdType.MESH

H = 15
KVH = 5
HD = 64
RECUR = 3
SPAN = 16


epsilon = 1e-05
theta = 10000.0
masked = -1000000000.0
highest = lax.Precision.HIGHEST


PARTS = 16
HALF = 480
COLS = 640
STREAMS = (("x", True, 0, 160), ("y", True, 160, 160), ("x", False, 320, 80), ("y", False, 400, 80))


def place():
    g, t = lax.axis_index("grp"), lax.axis_index("tok")
    return g // 2, lax.rem(g, 2), t // 2, lax.rem(t, 2)


def dev(y, x, z, c):
    return (y * 2 + x, z * 2 + c)


def pick(z, values):
    out = jnp.int32(values[3])
    for i in (2, 1, 0):
        out = jnp.where(z == i, jnp.int32(values[i]), out)
    return out


def copy_to(src, dst, send, recv, device):
    return pltpu.make_async_remote_copy(src_ref=src, dst_ref=dst, send_sem=send, recv_sem=recv, device_id=device, device_id_type=MESH)


def add_rows(dst, src, rows, step):
    def body(i, _):
        at = pl.ds(pl.multiple_of(i * step, step), step)
        dst[at, :] = dst[at, :] + src[at, :]
        return 0
    lax.fori_loop(0, rows // step, body, 0)


def reduce_kernel(g_ref, v_ref, o_ref, vo_ref, mine, other, ra0, ra1, ra2, ra3, rz0, rz1, rz2, rz3, rb0, rb1, rb2, rb3,
                  vrecv, load_sem, core_s, core_r, as_, ar, zs, zr, bs, br, ob, obr, oz, ozr, oa, oar, oc, ocr, vs, vr, own_sem):
    y, x, z, c = place()
    ra, rz, rb = (ra0, ra1, ra2, ra3), (rz0, rz1, rz2, rz3), (rb0, rb1, rb2, rb3)
    partner = dev(y, x, z, 1 - c)
    across = {"x": dev(y, 1 - x, z, c), "y": dev(1 - y, x, z, c)}
    left, right = dev(y, x, z - 1, c), dev(y, x, z + 1, c)
    at_axis = {"x": x, "y": y}
    order = (pick(z, (3, 3, 0, 0)), pick(z, (2, 0, 3, 1)), pick(z, (1, 2, 1, 2)), z)

    bar = pltpu.get_barrier_semaphore()
    for d in (partner, across["x"], across["y"]):
        pl.semaphore_signal(bar, inc=1, device_id=d, device_id_type=MESH)

    @pl.when(z > 0)
    def _():
        pl.semaphore_signal(bar, inc=1, device_id=left, device_id_type=MESH)

    @pl.when(z < 3)
    def _():
        pl.semaphore_signal(bar, inc=1, device_id=right, device_id_type=MESH)
    far = dev(y, x, jnp.where(z < 2, z + 2, z - 2), c)
    pl.semaphore_signal(bar, inc=1, device_id=far, device_id_type=MESH)
    pl.semaphore_wait(bar, 4 + (z > 0).astype(jnp.int32) + (z < 3).astype(jnp.int32))

    def part_xy(px, py, pz):
        return (px * 2 + py) * 4 + pz

    def part_of(s, pa, pb, pz):
        return part_xy(pa, pb, pz) if STREAMS[s][0] == "x" else part_xy(pb, pa, pz)

    def ab(s):
        a = STREAMS[s][0]
        b = "y" if a == "x" else "x"
        return at_axis[a], at_axis[b], across[a], across[b]

    def core_copy(p):
        return copy_to(g_ref.at[p, pl.ds(pl.multiple_of((1 - c) * HALF, HALF), HALF)], other.at[p], core_s.at[p], core_r.at[p], partner)

    def load(p):
        return pltpu.make_async_copy(g_ref.at[p, pl.ds(pl.multiple_of(c * HALF, HALF), HALF)], mine.at[p], load_sem.at[p])

    waits = []
    seq = [(k, px, py) for k in range(4) for px, py in ((1 - x, 1 - y), (1 - x, y), (x, 1 - y), (x, y))]
    for k, px, py in seq:
        p = part_xy(px, py, order[k])
        core_copy(p).start()
        load(p).start()

    def a_copy(s, pb, pz):
        a, b, to_a, _ = ab(s)
        _, _, r0, n = STREAMS[s]
        return copy_to(mine.at[part_of(s, 1 - a, pb, pz), pl.ds(r0, n)], ra[s].at[pb * 4 + pz], as_.at[s, pb * 4 + pz], ar.at[s, pb * 4 + pz], to_a)

    def core_step(k):
        for i, (px, py) in enumerate(((1 - x, 1 - y), (1 - x, y), (x, 1 - y), (x, y))):
            p = part_xy(px, py, order[k])
            load(p).wait()
            core_copy(p).wait_recv()
            add_rows(mine.at[p], other.at[p], HALF, 16)
            for s in range(4):
                a_axis = STREAMS[s][0]
                if i == 0 or (i == 1 and a_axis == "x") or (i == 2 and a_axis == "y"):
                    pb = py if a_axis == "x" else px
                    cp = a_copy(s, pb, order[k])
                    cp.start()
                    waits.append(cp)

    def z_copy(s, pb, pz, to_right):
        a, b, _, _ = ab(s)
        _, _, r0, n = STREAMS[s]
        src = mine.at[part_of(s, a, pb, pz), pl.ds(r0, n)]
        slot = pz if to_right else jnp.where(pz == z - 1, 4, pz)
        i = pb * 5 + slot
        return copy_to(src, rz[s].at[i], zs.at[s, i], zr.at[s, i], right if to_right else left)

    def z_wait(s, pb, slot):
        _, _, r0, n = STREAMS[s]
        i = pb * 5 + slot
        copy_to(mine.at[0, pl.ds(r0, n)], rz[s].at[i], zs.at[s, i], zr.at[s, i], left).wait_recv()

    def z_step(s, pb, k):
        a, b, _, _ = ab(s)
        _, _, r0, n = STREAMS[s]
        pz = order[k]
        acc = mine.at[part_of(s, a, pb, pz), pl.ds(r0, n)]
        if k < 3:
            up = jnp.where(pz > z, (z > 0).astype(jnp.int32), (z < 3).astype(jnp.int32))

            @pl.when(up == 1)
            def _():
                z_wait(s, pb, pz)
                add_rows(acc, rz[s].at[pb * 5 + pz], n, 16)

            @pl.when(pz > z)
            def _():
                z_copy(s, pb, pz, True).start()

            @pl.when(pz < z)
            def _():
                z_copy(s, pb, pz, False).start()
        else:
            @pl.when(z > 0)
            def _():
                z_wait(s, pb, z)
                add_rows(acc, rz[s].at[pb * 5 + z], n, 16)

            @pl.when(z < 3)
            def _():
                z_wait(s, pb, 4)
                add_rows(acc, rz[s].at[pb * 5 + 4], n, 16)

    def z_drain(s, pb, k):
        pz = order[k]

        @pl.when(pz > z)
        def _():
            z_copy(s, pb, pz, True).wait_send()

        @pl.when(pz < z)
        def _():
            z_copy(s, pb, pz, False).wait_send()

    def a_step(s, pb, k):
        a, b, to_a, _ = ab(s)
        _, _, r0, n = STREAMS[s]
        pz = order[k]
        a_copy(s, pb, pz).wait_recv()
        add_rows(mine.at[part_of(s, a, pb, pz), pl.ds(r0, n)], ra[s].at[pb * 4 + pz], n, 16)

    def b_copy(s, pz):
        a, b, _, to_b = ab(s)
        _, second_z, r0, n = STREAMS[s]
        i = 0 if second_z else pz
        return copy_to(mine.at[part_of(s, a, 1 - b, pz), pl.ds(r0, n)], rb[s].at[i], bs.at[s, i], br.at[s, i], to_b)

    def b_step(s, pz):
        a, b, _, _ = ab(s)
        _, second_z, r0, n = STREAMS[s]
        i = 0 if second_z else pz
        b_copy(s, pz).wait_recv()
        add_rows(mine.at[part_of(s, a, b, pz), pl.ds(r0, n)], rb[s].at[i], n, 16)

    def stream_step(k):
        for s in range(4):
            _, b, _, _ = ab(s)
            if STREAMS[s][1]:
                a_step(s, 1 - b, k)
                z_step(s, 1 - b, k)
                a_step(s, b, k)
                z_step(s, b, k)
                if k == 3:
                    cp = b_copy(s, z)
                    cp.start()
                    waits.append(cp)
            else:
                a_step(s, 1 - b, k)
                cp = b_copy(s, order[k])
                cp.start()
                waits.append(cp)
                a_step(s, b, k)

    def stream_step2(k):
        for s in range(4):
            _, b, _, _ = ab(s)
            if not STREAMS[s][1]:
                b_step(s, order[k])
                z_step(s, b, k)
            elif k == 3:
                b_step(s, z)

    def vec_to(i):
        return (partner, across["x"], across["y"], dev(y, x, jnp.where(lax.rem(z, 2) == 0, z + 1, z - 1), c), far)[i]

    def vec_copy(i):
        return copy_to(vo_ref, vrecv.at[i], vs.at[i], vr.at[i], vec_to(i))

    def vec_start(i):
        vec_copy(i).start()

    def vec_end(i):
        vec_copy(i).wait()
        vo_ref[...] = vo_ref[...] + vrecv[i]

    vo_ref[...] = v_ref[...]
    vec_start(0)
    core_step(0)
    vec_end(0)
    vec_start(1)
    core_step(1)
    vec_end(1)
    vec_start(2)
    stream_step(0)
    vec_end(2)
    vec_start(3)
    core_step(2)
    stream_step2(0)
    vec_end(3)
    vec_start(4)
    stream_step(1)
    core_step(3)
    stream_step2(1)
    vec_end(4)
    stream_step(2)
    stream_step2(2)
    stream_step(3)

    half0 = c * HALF

    def out_at(s, p):
        _, _, r0, n = STREAMS[s]
        return o_ref.at[p, pl.ds(pl.multiple_of(half0 + r0, 16), n)]

    def mine_at(s, p):
        _, _, r0, n = STREAMS[s]
        return mine.at[p, pl.ds(r0, n)]

    def go(cp):
        cp.start()
        waits.append(cp)

    def to_core(s, p, src):
        return copy_to(src, out_at(s, p), oc.at[s, p], ocr.at[s, p], partner)

    def to_a(s, pb, pz, src):
        a, b, na, _ = ab(s)
        return copy_to(src, out_at(s, part_of(s, a, pb, pz)), oa.at[s, pb * 4 + pz], oar.at[s, pb * 4 + pz], na)

    def to_b(s, pz, src):
        a, b, _, nb = ab(s)
        return copy_to(src, out_at(s, part_of(s, a, b, pz)), ob.at[s, pz], obr.at[s, pz], nb)

    def to_z(s, pb, pz, src, to_right):
        a, b, _, _ = ab(s)
        i = pb * 8 + pz * 2 + (0 if to_right else 1)
        return copy_to(src, out_at(s, part_of(s, a, pb, pz)), oz.at[s, i], ozr.at[s, pb * 4 + pz], right if to_right else left)

    def spread_z(s, pb, pz, src, from_left=None):
        if from_left is None:
            @pl.when(z < 3)
            def _():
                to_z(s, pb, pz, src, True).start()

            @pl.when(z > 0)
            def _():
                to_z(s, pb, pz, src, False).start()
        elif from_left:
            @pl.when(z < 3)
            def _():
                to_z(s, pb, pz, src, True).start()
        else:
            @pl.when(z > 0)
            def _():
                to_z(s, pb, pz, src, False).start()

    for s in range(4):
        a, b, _, _ = ab(s)
        p = part_of(s, a, b, z)
        if STREAMS[s][1]:
            b_step(s, z)
            src = mine_at(s, p)
            go(to_b(s, z, src))
            spread_z(s, b, z, src)
            go(to_a(s, b, z, src))
        else:
            b_step(s, z)
            z_step(s, b, 3)
            src = mine_at(s, p)
            spread_z(s, b, z, src)
            go(to_b(s, z, src))
            go(to_a(s, b, z, src))
        go(to_core(s, p, src))
        pltpu.make_async_copy(src, out_at(s, p), own_sem.at[s]).start()

    def got_b(s, pz):
        a, b, _, _ = ab(s)
        p = part_of(s, a, 1 - b, pz)
        src = out_at(s, p)
        copy_to(src, src, ob.at[s, pz], obr.at[s, pz], partner).wait_recv()
        if STREAMS[s][1]:
            spread_z(s, 1 - b, pz, src)
        to_a(s, 1 - b, pz, src).start()
        to_core(s, p, src).start()

    def got_z(s, pb, pz, from_left):
        a, b, _, _ = ab(s)
        p = part_of(s, a, pb, pz)
        src = out_at(s, p)
        copy_to(src, src, oz.at[s, 0], ozr.at[s, pb * 4 + pz], partner).wait_recv()
        spread_z(s, pb, pz, src, from_left)
        to_a(s, pb, pz, src).start()
        to_core(s, p, src).start()
        if not STREAMS[s][1]:
            to_b(s, pz, src).start()

    def got_a(s, pb, pz):
        a, b, _, _ = ab(s)
        p = part_of(s, 1 - a, pb, pz)
        src = out_at(s, p)
        copy_to(src, src, oa.at[s, pb * 4 + pz], oar.at[s, pb * 4 + pz], partner).wait_recv()
        to_core(s, p, src).start()

    for s in range(4):
        got_b(s, z)
    for s in range(4):
        a, b, _, _ = ab(s)
        got_a(s, b, z)
        got_a(s, 1 - b, z)
    for t in range(1, 4):
        for lft in (True, False):
            pz = z - t if lft else z + t
            ok = (z >= t) if lft else (z + t <= 3)

            @pl.when(ok)
            def _():
                for s in range(4):
                    a, b, _, _ = ab(s)
                    got_z(s, b, pz, lft)
                    if STREAMS[s][1]:
                        got_z(s, 1 - b, pz, lft)
                for s in range(4):
                    if not STREAMS[s][1]:
                        got_b(s, pz)
                for s in range(4):
                    a, b, _, _ = ab(s)
                    got_a(s, b, pz)
                    got_a(s, 1 - b, pz)

    for cp in waits:
        cp.wait_send()
    for k, px, py in seq:
        core_copy(part_xy(px, py, order[k])).wait_send()
    for s in range(4):
        a, b, _, _ = ab(s)
        pltpu.make_async_copy(mine_at(s, part_of(s, a, b, z)), out_at(s, part_of(s, a, b, z)), own_sem.at[s]).wait()
        pbs = (b, 1 - b) if STREAMS[s][1] else (b,)
        for pb in pbs:
            for k in range(3):
                z_drain(s, pb, k)
        for pz in range(4):
            for pb in pbs:
                src = out_at(s, part_of(s, a, pb, pz))

                @pl.when((z >= pz) & (z < 3))
                def _():
                    to_z(s, pb, pz, src, True).wait_send()

                @pl.when((z <= pz) & (z > 0))
                def _():
                    to_z(s, pb, pz, src, False).wait_send()
            for pb in (0, 1):
                src = out_at(s, part_of(s, a, pb, pz))

                @pl.when(((pb == b) & (pz == z)) == False)
                def _():
                    to_a(s, pb, pz, src).wait_send()
            if not STREAMS[s][1]:
                @pl.when(z != pz)
                def _():
                    to_b(s, pz, out_at(s, 0)).wait_send()
        for p in range(16):
            src = out_at(s, p)

            @pl.when(p != part_of(s, a, b, z))
            def _():
                to_core(s, p, src).wait_send()
            _, _, r0, n = STREAMS[s]
            dst = o_ref.at[p, pl.ds(pl.multiple_of((1 - c) * HALF + r0, 16), n)]
            copy_to(dst, dst, oc.at[s, p], ocr.at[s, p], partner).wait_recv()


def all_sum(grads, vectors):
    dma = pltpu.SemaphoreType.DMA
    bf = jnp.bfloat16
    rows = [s[3] for s in STREAMS]
    return pl.pallas_call(
        reduce_kernel,
        name="all_sum",
        out_shape=(jax.ShapeDtypeStruct(grads.shape, bf), jax.ShapeDtypeStruct(vectors.shape, jnp.float32)),
        in_specs=[pl.BlockSpec(memory_space=pl.ANY), pl.BlockSpec(memory_space=pltpu.VMEM)],
        out_specs=(pl.BlockSpec(memory_space=pl.ANY), pl.BlockSpec(memory_space=pltpu.VMEM)),
        scratch_shapes=[
            pltpu.VMEM((PARTS, HALF, COLS), bf), pltpu.VMEM((PARTS, HALF, COLS), bf),
            *[pltpu.VMEM((8, n, COLS), bf) for n in rows],
            *[pltpu.VMEM((10, n, COLS), bf) for n in rows],
            *[pltpu.VMEM((1 if s[1] else 4, s[3], COLS), bf) for s in STREAMS],
            pltpu.VMEM((5, *vectors.shape), jnp.float32),
            dma((16,)), dma((16,)), dma((16,)),
            dma((4, 8)), dma((4, 8)), dma((4, 10)), dma((4, 10)), dma((4, 4)), dma((4, 4)),
            dma((4, 4)), dma((4, 4)), dma((4, 16)), dma((4, 8)), dma((4, 8)), dma((4, 8)), dma((4, 16)), dma((4, 16)),
            dma((5,)), dma((5,)), dma((4,)),
        ],
        compiler_params=pltpu.CompilerParams(collective_id=1, has_side_effects=True, vmem_limit_bytes=56 * 2**20),
    )(grads, vectors)


def from_behind(block, axis, distance):
    devices = range(lax.axis_size(axis))
    route = [(i - distance, i) for i in devices if i - distance in devices]
    return lax.ppermute(block, axis, route)


def matmul(left, right):
    return jnp.dot(left, right, preferred_element_type=jnp.float32)


def matmul_tn(left, right):
    return lax.dot_general(
        left, right, (((0,), (0,)), ((), ())), preferred_element_type=jnp.float32
    )


def matmul_nt(left, right):
    return lax.dot_general(
        left, right, (((1,), (1,)), ((), ())), preferred_element_type=jnp.float32
    )


def norm_forward(values_in, gain_vec):
    inverse_rms = lax.rsqrt(jnp.mean(values_in * values_in, axis=-1, keepdims=True) + epsilon)
    scaled = values_in * inverse_rms
    return (scaled * gain_vec, scaled, inverse_rms)


def norm_backward(grad_in, scaled, inverse_rms, gain_vec):
    grad_scaled = grad_in * gain_vec
    inner = jnp.mean(grad_scaled * scaled, axis=-1, keepdims=True)
    return (inverse_rms * (grad_scaled - scaled * inner), jnp.sum(grad_in * scaled, axis=0))


def ends_of(lengths_row):
    count = lengths_row.shape[0]
    until = jnp.arange(count)[:, None] >= jnp.arange(count)[None, :]
    return jnp.sum(jnp.where(until, lengths_row[None, :], 0), axis=1)


def segment_of(lengths_row, global_rows):
    ends_at = ends_of(lengths_row)
    return jnp.sum((global_rows[:, None] >= ends_at[None, :]).astype(jnp.int32), axis=1)


def position_of(lengths_row, global_rows, segments):
    ends_at = ends_of(lengths_row)
    starts_at = ends_at - lengths_row
    picked = segments[:, None] == jnp.arange(lengths_row.shape[0], dtype=jnp.int32)[None, :]
    return global_rows - jnp.sum(jnp.where(picked, starts_at[None, :], 0), axis=1)


def rotary_tables(positions):
    half_dim = HD // 2
    inverse = jnp.power(theta, -jnp.arange(half_dim, dtype=jnp.float32) * (2.0 / HD))
    angle = positions.astype(jnp.float32)[..., None] * inverse
    return (jnp.cos(angle), jnp.sin(angle))


def rotate(tensor, cosine_table, sine_table):
    half_dim = tensor.shape[-1] // 2
    first_half = tensor[..., :half_dim]
    second_half = tensor[..., half_dim:]
    cos_b = cosine_table[..., None, :]
    sin_b = sine_table[..., None, :]
    return jnp.concatenate(
        [first_half * cos_b - second_half * sin_b, second_half * cos_b + first_half * sin_b],
        axis=-1,
    )


def rotate_back(gradient, cosine_table, sine_table):
    half_dim = gradient.shape[-1] // 2
    first_half = gradient[..., :half_dim]
    second_half = gradient[..., half_dim:]
    cos_b = cosine_table[..., None, :]
    sin_b = sine_table[..., None, :]
    return jnp.concatenate(
        [first_half * cos_b + second_half * sin_b, second_half * cos_b - first_half * sin_b],
        axis=-1,
    )


def head_layout(queries, keys_all, values_all):
    row_count = queries.shape[0]
    key_count = keys_all.shape[0]
    per_group = H // KVH
    query_heads = jnp.transpose(queries.reshape(row_count, KVH, per_group, HD), (1, 0, 2, 3))
    key_heads = jnp.transpose(keys_all.reshape(key_count, KVH, HD), (1, 0, 2))
    value_heads = jnp.transpose(values_all.reshape(key_count, KVH, HD), (1, 0, 2))
    return (query_heads, key_heads, value_heads)


def attend(queries, keys_all, values_all, allowed):
    row_count = queries.shape[0]
    score_scale = HD ** (-0.5)
    query_heads, key_heads, value_heads = head_layout(queries, keys_all, values_all)

    def one_head(operands):
        query_h, key_h, value_h = operands
        scores = (
            jnp.einsum("rgd,kd->grk", query_h, key_h, preferred_element_type=jnp.float32)
            * score_scale
        )
        scores = jnp.where(allowed[None], scores, masked)
        largest = jnp.max(scores, axis=-1, keepdims=True)
        exponent = jnp.exp(scores - largest)
        totals = jnp.sum(exponent, axis=-1, keepdims=True)
        probs_low = (exponent / totals).astype(jnp.bfloat16)
        mixed_h = jnp.einsum("grk,kd->rgd", probs_low, value_h, preferred_element_type=jnp.float32)
        return (mixed_h.astype(jnp.bfloat16), (largest + jnp.log(totals))[..., 0])

    mixed_heads, log_totals = lax.map(one_head, (query_heads, key_heads, value_heads))
    mixed_rows = jnp.transpose(mixed_heads, (1, 0, 2, 3)).reshape(row_count, H * HD)
    return (mixed_rows, log_totals)


def attend_back(queries, keys_all, values_all, allowed, log_totals, grad_mixed):
    row_count = queries.shape[0]
    key_count = keys_all.shape[0]
    per_group = H // KVH
    score_scale = HD ** (-0.5)
    query_heads, key_heads, value_heads = head_layout(queries, keys_all, values_all)
    grad_heads = jnp.transpose(grad_mixed.reshape(row_count, KVH, per_group, HD), (1, 0, 2, 3))

    def one_head(operands):
        query_h, key_h, value_h, grad_h, log_h = operands
        scores = (
            jnp.einsum("rgd,kd->grk", query_h, key_h, preferred_element_type=jnp.float32)
            * score_scale
        )
        scores = jnp.where(allowed[None], scores, masked)
        probs = jnp.exp(scores - log_h[..., None])
        grad_value_h = jnp.einsum(
            "grk,rgd->kd", probs.astype(jnp.bfloat16), grad_h, preferred_element_type=jnp.float32
        )
        grad_probs = jnp.einsum("rgd,kd->grk", grad_h, value_h, preferred_element_type=jnp.float32)
        grad_scores = (
            probs * (grad_probs - jnp.sum(probs * grad_probs, axis=-1, keepdims=True))
        ).astype(jnp.bfloat16)
        grad_query_h = (
            jnp.einsum("grk,kd->rgd", grad_scores, key_h, preferred_element_type=jnp.float32)
            * score_scale
        )
        grad_key_h = (
            jnp.einsum("grk,rgd->kd", grad_scores, query_h, preferred_element_type=jnp.float32)
            * score_scale
        )
        return (grad_query_h, grad_key_h, grad_value_h)

    grad_q_heads, grad_k_heads, grad_v_heads = lax.map(
        one_head, (query_heads, key_heads, value_heads, grad_heads, log_totals)
    )
    grad_queries = jnp.transpose(grad_q_heads, (1, 0, 2, 3)).reshape(row_count, H * HD)
    grad_keys = jnp.transpose(grad_k_heads, (1, 0, 2)).reshape(key_count, KVH * HD)
    grad_values = jnp.transpose(grad_v_heads, (1, 0, 2)).reshape(key_count, KVH * HD)
    return (grad_queries, grad_keys, grad_values)


def attention_front(hidden_state, live_int, weights, context, pieces):
    lengths_row, global_rows, cosine_table, sine_table, segment_rows, tok_dev, nback = context
    normed, scaled_one, inverse_one = norm_forward(hidden_state, weights[0].astype(jnp.float32))
    normed_low = normed.astype(jnp.bfloat16)
    row_count = hidden_state.shape[0]
    queries = rotate(
        matmul(normed_low, weights[1]).reshape(row_count, H, HD), cosine_table, sine_table
    )
    queries = queries.astype(jnp.bfloat16).reshape(row_count, H * HD)
    keys_own = rotate(
        matmul(normed_low, weights[2]).reshape(row_count, KVH, HD), cosine_table, sine_table
    )
    keys_own = keys_own.astype(jnp.bfloat16).reshape(row_count, KVH * HD)
    values_own = matmul(normed_low, weights[3]).astype(jnp.bfloat16)
    live_low = live_int.astype(jnp.bfloat16)
    pieces = [
        from_behind((keys_own, values_own, live_low), "tok", distance)
        for distance in range(1, nback + 1)
    ]
    keys_all = jnp.concatenate([keys_own] + [one_piece[0] for one_piece in pieces], axis=0)
    values_all = jnp.concatenate([values_own] + [one_piece[1] for one_piece in pieces], axis=0)
    live_all = jnp.concatenate([live_low] + [one_piece[2] for one_piece in pieces], axis=0)
    global_keys = jnp.concatenate(
        [global_rows - distance * tok_dev for distance in range(nback + 1)]
    )
    segment_keys = segment_of(lengths_row, global_keys)
    allowed = (
        (segment_rows[:, None] == segment_keys[None, :])
        & (global_keys[None, :] <= global_rows[:, None])
        & (live_all[None, :] > 0)
    )
    mixed_rows, log_totals = attend(queries, keys_all, values_all, allowed)
    attn_out = matmul(mixed_rows, weights[4])
    middle = hidden_state + attn_out
    normed_two, scaled_two, inverse_two = norm_forward(middle, weights[5].astype(jnp.float32))
    return (
        normed_low,
        scaled_one,
        inverse_one,
        queries,
        keys_all,
        values_all,
        allowed,
        mixed_rows,
        log_totals,
        attn_out,
        normed_two.astype(jnp.bfloat16),
        scaled_two,
        inverse_two,
        pieces,
    )


def ffn_forward(rows_in, w_gate, w_up, w_down):
    gate_pre = matmul(rows_in, w_gate)
    up_pre = matmul(rows_in, w_up)
    hidden_low = (jax.nn.silu(gate_pre) * up_pre).astype(jnp.bfloat16)
    return matmul(hidden_low, w_down).astype(jnp.bfloat16)


def ffn_backward(rows_in, grad_rows, w_gate, w_up, w_down):
    gate_pre = matmul(rows_in, w_gate)
    up_pre = matmul(rows_in, w_up)
    sigmoid_gate = jax.nn.sigmoid(gate_pre)
    silu_gate = jax.nn.silu(gate_pre)
    hidden_low = (silu_gate * up_pre).astype(jnp.bfloat16)
    grad_hidden = matmul_nt(grad_rows, w_down)
    grad_up_low = (grad_hidden * silu_gate).astype(jnp.bfloat16)
    grad_gate_low = (
        grad_hidden * up_pre * (sigmoid_gate * (1.0 + gate_pre * (1.0 - sigmoid_gate)))
    ).astype(jnp.bfloat16)
    grad_input = (matmul_nt(grad_gate_low, w_gate) + matmul_nt(grad_up_low, w_up)).astype(
        jnp.bfloat16
    )
    return (grad_input, hidden_low, grad_gate_low, grad_up_low)


def feed_forward(normed_two, weights):
    mlp_low = ffn_forward(normed_two, weights[6], weights[7], weights[8])
    return mlp_low


def recursion_forward(hidden_state, live_int, weights, context):
    front = attention_front(hidden_state, live_int, weights, context, None)
    mlp_low = feed_forward(front[10], weights)
    router_gate = jax.nn.sigmoid(
        jnp.dot(hidden_state, weights[9].astype(jnp.float32), precision=highest)
    )
    factor = live_int.astype(jnp.float32) * router_gate
    updated = hidden_state + factor[:, None] * (front[9] + mlp_low.astype(jnp.float32))
    return (updated, front, mlp_low)


def recursion_backward(hidden_state, live_int, weights, context, front, mlp_low, grad_after):
    (
        normed_low,
        scaled_one,
        inverse_one,
        queries,
        keys_all,
        values_all,
        allowed,
        mixed_rows,
        log_totals,
        attn_out,
        normed_two,
        scaled_two,
        inverse_two,
        pieces,
    ) = front
    lengths_row, global_rows, cosine_table, sine_table, segment_rows, tok_dev, nback = context
    live_f = live_int.astype(jnp.float32)
    router_vec = weights[9].astype(jnp.float32)
    router_gate = jax.nn.sigmoid(jnp.dot(hidden_state, router_vec, precision=highest))
    branch_sum = attn_out + mlp_low.astype(jnp.float32)
    grad_branch = (live_f * router_gate)[:, None] * grad_after
    grad_logit = (
        live_f * jnp.sum(branch_sum * grad_after, axis=1) * router_gate * (1.0 - router_gate)
    )
    grad_router = jnp.dot(grad_logit, hidden_state, precision=highest)
    grad_state = grad_after + grad_logit[:, None] * router_vec[None, :]
    grad_mlp_low = grad_branch.astype(jnp.bfloat16)
    grad_normed_two, hidden_low, grad_gate_low, grad_up_low = ffn_backward(
        normed_two, grad_mlp_low, weights[6], weights[7], weights[8]
    )
    grad_middle, grad_gain_two = norm_backward(
        grad_normed_two.astype(jnp.float32), scaled_two, inverse_two, weights[5].astype(jnp.float32)
    )
    grad_state = grad_state + grad_middle
    grad_attn = (grad_branch + grad_middle).astype(jnp.bfloat16)
    grad_mixed = matmul_nt(grad_attn, weights[4]).astype(jnp.bfloat16)
    grad_queries, grad_keys, grad_values = attend_back(
        queries, keys_all, values_all, allowed, log_totals, grad_mixed
    )
    row_count = hidden_state.shape[0]
    keys_home = grad_keys[:row_count]
    values_home = grad_values[:row_count]
    for distance in range(1, nback + 1):
        returned = (
            from_behind(
                grad_keys[distance * row_count : (distance + 1) * row_count].astype(jnp.bfloat16),
                "tok",
                -distance,
            ).astype(jnp.float32),
            from_behind(
                grad_values[distance * row_count : (distance + 1) * row_count].astype(jnp.bfloat16),
                "tok",
                -distance,
            ).astype(jnp.float32),
        )
        keys_home = keys_home + returned[0]
        values_home = values_home + returned[1]
    grad_q_low = (
        rotate_back(grad_queries.reshape(row_count, H, HD), cosine_table, sine_table)
        .reshape(row_count, H * HD)
        .astype(jnp.bfloat16)
    )
    grad_k_low = (
        rotate_back(keys_home.reshape(row_count, KVH, HD), cosine_table, sine_table)
        .reshape(row_count, KVH * HD)
        .astype(jnp.bfloat16)
    )
    grad_v_low = values_home.astype(jnp.bfloat16)
    grad_normed = (
        matmul_nt(grad_q_low, weights[1])
        + matmul_nt(grad_k_low, weights[2])
        + matmul_nt(grad_v_low, weights[3])
    )
    grad_input, grad_gain_one = norm_backward(
        grad_normed, scaled_one, inverse_one, weights[0].astype(jnp.float32)
    )
    grad_state = grad_state + grad_input
    rows = (
        normed_two,
        grad_mlp_low,
        normed_low,
        mixed_rows,
        grad_gate_low,
        grad_up_low,
        hidden_low,
        grad_q_low,
        grad_k_low,
        grad_v_low,
        grad_attn,
    )
    return (grad_state, rows, (grad_gain_one, grad_gain_two, grad_router))


def weight_grads(rows):
    (n_two, g_mlp, n_one, mixed, g_gate, g_up, hidden, g_q, g_k, g_v, g_attn) = rows
    low = jnp.bfloat16

    def product(left, right):
        return matmul_tn(left, right).astype(low)

    return (
        product(n_two, g_gate),
        product(n_two, g_up),
        product(g_mlp, hidden),
        product(n_one, g_q),
        product(n_one, g_k),
        product(n_one, g_v),
        product(mixed, g_attn),
    )


def to_parts(d_gate, d_up, d_down_t, d_q, d_k, d_v, d_o):
    blocks = []
    for wide in (d_gate, d_up, d_down_t, jnp.concatenate([d_q, d_k], axis=1), jnp.concatenate([d_o, d_v], axis=1)):
        blocks += [wide[:, i : i + COLS] for i in range(0, wide.shape[1], COLS)]
    return jnp.stack(blocks)


def from_parts(parts):
    wide = parts.astype(jnp.float32)

    def side(low, high):
        return jnp.concatenate([wide[i] for i in range(low, high)], axis=1)

    d_down = jnp.concatenate([wide[i].T for i in range(8, 12)], axis=0)
    width = wide.shape[1]
    queries_keys, out_values = side(12, 14), side(14, 16)
    return (
        side(0, 4),
        side(4, 8),
        d_down,
        queries_keys[:, :width],
        queries_keys[:, width:],
        out_values[:, width:],
        out_values[:, :width],
    )


def on_device(
    hidden_in,
    cotangent,
    lengths,
    active,
    norm_attn,
    w_query,
    w_key,
    w_value,
    w_out,
    norm_mlp,
    w_gate,
    w_up,
    w_down,
    w_router,
):
    n_tok = lax.axis_size("tok")
    n_grp = lax.axis_size("grp")
    me_index = lax.axis_index("tok")
    tok_dev = hidden_in.shape[0]
    nback = min(SPAN, n_tok // 2)
    shards = (norm_attn, w_query, w_key, w_value, w_out, norm_mlp, w_gate, w_up, w_down, w_router)
    weights = tuple(lax.all_gather(shard, "tok", axis=0, tiled=True) for shard in shards)
    lengths_row = lengths[0]
    global_rows = me_index * tok_dev + jnp.arange(tok_dev, dtype=jnp.int32)
    segment_rows = segment_of(lengths_row, global_rows)
    cosine_table, sine_table = rotary_tables(position_of(lengths_row, global_rows, segment_rows))
    context = (lengths_row, global_rows, cosine_table, sine_table, segment_rows, tok_dev, nback)
    hidden_state = hidden_in.astype(jnp.float32)
    inputs_kept = []
    fronts_kept = []
    mlp_kept = []
    for each_step in range(RECUR):
        inputs_kept.append(hidden_state)
        hidden_state, front, mlp_low = recursion_forward(
            hidden_state, active[each_step], weights, context
        )
        fronts_kept.append(front)
        mlp_kept.append(mlp_low)
    grad_state = cotangent.astype(jnp.float32)
    all_rows = []
    small = None
    for each_step in reversed(range(RECUR)):
        grad_state, rows, gains = recursion_backward(
            inputs_kept[each_step],
            active[each_step],
            weights,
            context,
            fronts_kept[each_step],
            mlp_kept[each_step],
            grad_state,
        )
        all_rows.append(rows)
        small = gains if small is None else tuple(a + b for a, b in zip(small, gains))
    matrices = weight_grads(tuple(jnp.concatenate(each, axis=0) for each in zip(*all_rows)))
    if (n_grp, n_tok) == (4, 8):
        width = small[0].shape[0]
        vectors = jnp.pad(jnp.stack(small), ((0, 8 - len(small)), (0, 1024 - width)))
        parts, vectors = all_sum(to_parts(*matrices), vectors)
        d_gate, d_up, d_down, d_q, d_k, d_v, d_o = from_parts(parts)
        small = tuple(vectors[i, :width] for i in range(3))
    else:
        d_gate, d_up, d_down, d_q, d_k, d_v, d_o = lax.psum(
            tuple(each.astype(jnp.float32) for each in matrices), ("grp", "tok")
        )
        d_down = d_down.T
        small = lax.psum(small, ("grp", "tok"))
    return (
        hidden_state.astype(jnp.bfloat16),
        grad_state,
        small[0],
        d_q,
        d_k,
        d_v,
        d_o,
        small[1],
        d_gate,
        d_up,
        d_down,
        small[2],
    )


def solution(mesh):
    placed = (
        P(("grp", "tok"), None),
        P(("grp", "tok"), None),
        P("grp", None),
        P(None, ("grp", "tok")),
        P("tok"),
        P("tok", None),
        P("tok", None),
        P("tok", None),
        P("tok", None),
        P("tok"),
        P("tok", None),
        P("tok", None),
        P("tok", None),
        P("tok"),
    )
    return jax.shard_map(
        on_device,
        mesh=mesh,
        in_specs=placed,
        out_specs=(
            P(("grp", "tok"), None),
            P(("grp", "tok"), None),
            P(),
            P(),
            P(),
            P(),
            P(),
            P(),
            P(),
            P(),
            P(),
            P(),
        ),
        check_vma=False,
    )
```

```python
import jax
import jax.numpy as jnp
from jax import lax
from jax.experimental import pallas as pl
from jax.experimental.pallas import tpu as pltpu
from jax.sharding import PartitionSpec as P

MESH = pl.DeviceIdType.MESH

H = 15
KVH = 5
HD = 64
RECUR = 3
SPAN = 16

epsilon = 1e-05
theta = 10000.0
masked = -1000000000.0

def ends_of(lengths_row):
    count = lengths_row.shape[0]
    until = jnp.arange(count)[:, None] >= jnp.arange(count)[None, :]
    return jnp.sum(jnp.where(until, lengths_row[None, :], 0), axis=1)


def segment_of(lengths_row, global_rows):
    ends_at = ends_of(lengths_row)
    return jnp.sum((global_rows[:, None] >= ends_at[None, :]).astype(jnp.int32), axis=1)


def position_of(lengths_row, global_rows, segments):
    ends_at = ends_of(lengths_row)
    starts_at = ends_at - lengths_row
    picked = segments[:, None] == jnp.arange(lengths_row.shape[0], dtype=jnp.int32)[None, :]
    return global_rows - jnp.sum(jnp.where(picked, starts_at[None, :], 0), axis=1)


def rotary_tables(positions):
    half_dim = HD // 2
    inverse = jnp.power(theta, -jnp.arange(half_dim, dtype=jnp.float32) * (2.0 / HD))
    angle = positions.astype(jnp.float32)[..., None] * inverse
    return (jnp.cos(angle), jnp.sin(angle))


PARTS = 16
HALF = 480
COLS = 640
STREAMS = (("x", True, 0, 160), ("y", True, 160, 160), ("x", False, 320, 80), ("y", False, 400, 80))


def place():
    g, t = lax.axis_index("grp"), lax.axis_index("tok")
    return g // 2, lax.rem(g, 2), t // 2, lax.rem(t, 2)


def dev(y, x, z, c):
    return (y * 2 + x, z * 2 + c)


def pick(z, values):
    out = jnp.int32(values[3])
    for i in (2, 1, 0):
        out = jnp.where(z == i, jnp.int32(values[i]), out)
    return out


def copy_to(src, dst, send, recv, device):
    return pltpu.make_async_remote_copy(src_ref=src, dst_ref=dst, send_sem=send, recv_sem=recv, device_id=device, device_id_type=MESH)


def add_rows(dst, src, rows, step):
    def body(i, _):
        at = pl.ds(pl.multiple_of(i * step, step), step)
        dst[at, :] = dst[at, :] + src[at, :]
        return 0
    lax.fori_loop(0, rows // step, body, 0)


def reduce_kernel(g_ref, v_ref, o_ref, vo_ref, mine, other, ra0, ra1, ra2, ra3, rz0, rz1, rz2, rz3, rb0, rb1, rb2, rb3,
                  vrecv, load_sem, core_s, core_r, as_, ar, zs, zr, bs, br, ob, obr, oz, ozr, oa, oar, oc, ocr, vs, vr, own_sem):
    y, x, z, c = place()
    ra, rz, rb = (ra0, ra1, ra2, ra3), (rz0, rz1, rz2, rz3), (rb0, rb1, rb2, rb3)
    partner = dev(y, x, z, 1 - c)
    across = {"x": dev(y, 1 - x, z, c), "y": dev(1 - y, x, z, c)}
    left, right = dev(y, x, z - 1, c), dev(y, x, z + 1, c)
    at_axis = {"x": x, "y": y}
    order = (pick(z, (3, 3, 0, 0)), pick(z, (2, 0, 3, 1)), pick(z, (1, 2, 1, 2)), z)

    bar = pltpu.get_barrier_semaphore()
    for d in (partner, across["x"], across["y"]):
        pl.semaphore_signal(bar, inc=1, device_id=d, device_id_type=MESH)

    @pl.when(z > 0)
    def _():
        pl.semaphore_signal(bar, inc=1, device_id=left, device_id_type=MESH)

    @pl.when(z < 3)
    def _():
        pl.semaphore_signal(bar, inc=1, device_id=right, device_id_type=MESH)
    far = dev(y, x, jnp.where(z < 2, z + 2, z - 2), c)
    pl.semaphore_signal(bar, inc=1, device_id=far, device_id_type=MESH)
    pl.semaphore_wait(bar, 4 + (z > 0).astype(jnp.int32) + (z < 3).astype(jnp.int32))

    def part_xy(px, py, pz):
        return (px * 2 + py) * 4 + pz

    def part_of(s, pa, pb, pz):
        return part_xy(pa, pb, pz) if STREAMS[s][0] == "x" else part_xy(pb, pa, pz)

    def ab(s):
        a = STREAMS[s][0]
        b = "y" if a == "x" else "x"
        return at_axis[a], at_axis[b], across[a], across[b]

    def core_copy(p):
        return copy_to(g_ref.at[p, pl.ds(pl.multiple_of((1 - c) * HALF, HALF), HALF)], other.at[p], core_s.at[p], core_r.at[p], partner)

    def load(p):
        return pltpu.make_async_copy(g_ref.at[p, pl.ds(pl.multiple_of(c * HALF, HALF), HALF)], mine.at[p], load_sem.at[p])

    waits = []
    seq = [(k, px, py) for k in range(4) for px, py in ((1 - x, 1 - y), (1 - x, y), (x, 1 - y), (x, y))]
    for k, px, py in seq:
        p = part_xy(px, py, order[k])
        core_copy(p).start()
        load(p).start()

    def a_copy(s, pb, pz):
        a, b, to_a, _ = ab(s)
        _, _, r0, n = STREAMS[s]
        return copy_to(mine.at[part_of(s, 1 - a, pb, pz), pl.ds(r0, n)], ra[s].at[pb * 4 + pz], as_.at[s, pb * 4 + pz], ar.at[s, pb * 4 + pz], to_a)

    def core_step(k):
        for i, (px, py) in enumerate(((1 - x, 1 - y), (1 - x, y), (x, 1 - y), (x, y))):
            p = part_xy(px, py, order[k])
            load(p).wait()
            core_copy(p).wait_recv()
            add_rows(mine.at[p], other.at[p], HALF, 16)
            for s in range(4):
                a_axis = STREAMS[s][0]
                if i == 0 or (i == 1 and a_axis == "x") or (i == 2 and a_axis == "y"):
                    pb = py if a_axis == "x" else px
                    cp = a_copy(s, pb, order[k])
                    cp.start()
                    waits.append(cp)

    def z_copy(s, pb, pz, to_right):
        a, b, _, _ = ab(s)
        _, _, r0, n = STREAMS[s]
        src = mine.at[part_of(s, a, pb, pz), pl.ds(r0, n)]
        slot = pz if to_right else jnp.where(pz == z - 1, 4, pz)
        i = pb * 5 + slot
        return copy_to(src, rz[s].at[i], zs.at[s, i], zr.at[s, i], right if to_right else left)

    def z_wait(s, pb, slot):
        _, _, r0, n = STREAMS[s]
        i = pb * 5 + slot
        copy_to(mine.at[0, pl.ds(r0, n)], rz[s].at[i], zs.at[s, i], zr.at[s, i], left).wait_recv()

    def z_step(s, pb, k):
        a, b, _, _ = ab(s)
        _, _, r0, n = STREAMS[s]
        pz = order[k]
        acc = mine.at[part_of(s, a, pb, pz), pl.ds(r0, n)]
        if k < 3:
            up = jnp.where(pz > z, (z > 0).astype(jnp.int32), (z < 3).astype(jnp.int32))

            @pl.when(up == 1)
            def _():
                z_wait(s, pb, pz)
                add_rows(acc, rz[s].at[pb * 5 + pz], n, 16)

            @pl.when(pz > z)
            def _():
                z_copy(s, pb, pz, True).start()

            @pl.when(pz < z)
            def _():
                z_copy(s, pb, pz, False).start()
        else:
            @pl.when(z > 0)
            def _():
                z_wait(s, pb, z)
                add_rows(acc, rz[s].at[pb * 5 + z], n, 16)

            @pl.when(z < 3)
            def _():
                z_wait(s, pb, 4)
                add_rows(acc, rz[s].at[pb * 5 + 4], n, 16)

    def z_drain(s, pb, k):
        pz = order[k]

        @pl.when(pz > z)
        def _():
            z_copy(s, pb, pz, True).wait_send()

        @pl.when(pz < z)
        def _():
            z_copy(s, pb, pz, False).wait_send()

    def a_step(s, pb, k):
        a, b, to_a, _ = ab(s)
        _, _, r0, n = STREAMS[s]
        pz = order[k]
        a_copy(s, pb, pz).wait_recv()
        add_rows(mine.at[part_of(s, a, pb, pz), pl.ds(r0, n)], ra[s].at[pb * 4 + pz], n, 16)

    def b_copy(s, pz):
        a, b, _, to_b = ab(s)
        _, second_z, r0, n = STREAMS[s]
        i = 0 if second_z else pz
        return copy_to(mine.at[part_of(s, a, 1 - b, pz), pl.ds(r0, n)], rb[s].at[i], bs.at[s, i], br.at[s, i], to_b)

    def b_step(s, pz):
        a, b, _, _ = ab(s)
        _, second_z, r0, n = STREAMS[s]
        i = 0 if second_z else pz
        b_copy(s, pz).wait_recv()
        add_rows(mine.at[part_of(s, a, b, pz), pl.ds(r0, n)], rb[s].at[i], n, 16)

    def stream_step(k):
        for s in range(4):
            _, b, _, _ = ab(s)
            if STREAMS[s][1]:
                a_step(s, 1 - b, k)
                z_step(s, 1 - b, k)
                a_step(s, b, k)
                z_step(s, b, k)
                if k == 3:
                    cp = b_copy(s, z)
                    cp.start()
                    waits.append(cp)
            else:
                a_step(s, 1 - b, k)
                cp = b_copy(s, order[k])
                cp.start()
                waits.append(cp)
                a_step(s, b, k)

    def stream_step2(k):
        for s in range(4):
            _, b, _, _ = ab(s)
            if not STREAMS[s][1]:
                b_step(s, order[k])
                z_step(s, b, k)
            elif k == 3:
                b_step(s, z)

    def vec_to(i):
        return (partner, across["x"], across["y"], dev(y, x, jnp.where(lax.rem(z, 2) == 0, z + 1, z - 1), c), far)[i]

    def vec_copy(i):
        return copy_to(vo_ref, vrecv.at[i], vs.at[i], vr.at[i], vec_to(i))

    def vec_start(i):
        vec_copy(i).start()

    def vec_end(i):
        vec_copy(i).wait()
        vo_ref[...] = vo_ref[...] + vrecv[i]

    vo_ref[...] = v_ref[...]
    vec_start(0)
    core_step(0)
    vec_end(0)
    vec_start(1)
    core_step(1)
    vec_end(1)
    vec_start(2)
    stream_step(0)
    vec_end(2)
    vec_start(3)
    core_step(2)
    stream_step2(0)
    vec_end(3)
    vec_start(4)
    stream_step(1)
    core_step(3)
    stream_step2(1)
    vec_end(4)
    stream_step(2)
    stream_step2(2)
    stream_step(3)

    half0 = c * HALF

    def out_at(s, p):
        _, _, r0, n = STREAMS[s]
        return o_ref.at[p, pl.ds(pl.multiple_of(half0 + r0, 16), n)]

    def mine_at(s, p):
        _, _, r0, n = STREAMS[s]
        return mine.at[p, pl.ds(r0, n)]

    def go(cp):
        cp.start()
        waits.append(cp)

    def to_core(s, p, src):
        return copy_to(src, out_at(s, p), oc.at[s, p], ocr.at[s, p], partner)

    def to_a(s, pb, pz, src):
        a, b, na, _ = ab(s)
        return copy_to(src, out_at(s, part_of(s, a, pb, pz)), oa.at[s, pb * 4 + pz], oar.at[s, pb * 4 + pz], na)

    def to_b(s, pz, src):
        a, b, _, nb = ab(s)
        return copy_to(src, out_at(s, part_of(s, a, b, pz)), ob.at[s, pz], obr.at[s, pz], nb)

    def to_z(s, pb, pz, src, to_right):
        a, b, _, _ = ab(s)
        i = pb * 8 + pz * 2 + (0 if to_right else 1)
        return copy_to(src, out_at(s, part_of(s, a, pb, pz)), oz.at[s, i], ozr.at[s, pb * 4 + pz], right if to_right else left)

    def spread_z(s, pb, pz, src, from_left=None):
        if from_left is None:
            @pl.when(z < 3)
            def _():
                to_z(s, pb, pz, src, True).start()

            @pl.when(z > 0)
            def _():
                to_z(s, pb, pz, src, False).start()
        elif from_left:
            @pl.when(z < 3)
            def _():
                to_z(s, pb, pz, src, True).start()
        else:
            @pl.when(z > 0)
            def _():
                to_z(s, pb, pz, src, False).start()

    for s in range(4):
        a, b, _, _ = ab(s)
        p = part_of(s, a, b, z)
        if STREAMS[s][1]:
            b_step(s, z)
            src = mine_at(s, p)
            go(to_b(s, z, src))
            spread_z(s, b, z, src)
            go(to_a(s, b, z, src))
        else:
            b_step(s, z)
            z_step(s, b, 3)
            src = mine_at(s, p)
            spread_z(s, b, z, src)
            go(to_b(s, z, src))
            go(to_a(s, b, z, src))
        go(to_core(s, p, src))
        pltpu.make_async_copy(src, out_at(s, p), own_sem.at[s]).start()

    def got_b(s, pz):
        a, b, _, _ = ab(s)
        p = part_of(s, a, 1 - b, pz)
        src = out_at(s, p)
        copy_to(src, src, ob.at[s, pz], obr.at[s, pz], partner).wait_recv()
        if STREAMS[s][1]:
            spread_z(s, 1 - b, pz, src)
        to_a(s, 1 - b, pz, src).start()
        to_core(s, p, src).start()

    def got_z(s, pb, pz, from_left):
        a, b, _, _ = ab(s)
        p = part_of(s, a, pb, pz)
        src = out_at(s, p)
        copy_to(src, src, oz.at[s, 0], ozr.at[s, pb * 4 + pz], partner).wait_recv()
        spread_z(s, pb, pz, src, from_left)
        to_a(s, pb, pz, src).start()
        to_core(s, p, src).start()
        if not STREAMS[s][1]:
            to_b(s, pz, src).start()

    def got_a(s, pb, pz):
        a, b, _, _ = ab(s)
        p = part_of(s, 1 - a, pb, pz)
        src = out_at(s, p)
        copy_to(src, src, oa.at[s, pb * 4 + pz], oar.at[s, pb * 4 + pz], partner).wait_recv()
        to_core(s, p, src).start()

    for s in range(4):
        got_b(s, z)
    for s in range(4):
        a, b, _, _ = ab(s)
        got_a(s, b, z)
        got_a(s, 1 - b, z)
    for t in range(1, 4):
        for lft in (True, False):
            pz = z - t if lft else z + t
            ok = (z >= t) if lft else (z + t <= 3)

            @pl.when(ok)
            def _():
                for s in range(4):
                    a, b, _, _ = ab(s)
                    got_z(s, b, pz, lft)
                    if STREAMS[s][1]:
                        got_z(s, 1 - b, pz, lft)
                for s in range(4):
                    if not STREAMS[s][1]:
                        got_b(s, pz)
                for s in range(4):
                    a, b, _, _ = ab(s)
                    got_a(s, b, pz)
                    got_a(s, 1 - b, pz)

    for cp in waits:
        cp.wait_send()
    for k, px, py in seq:
        core_copy(part_xy(px, py, order[k])).wait_send()
    for s in range(4):
        a, b, _, _ = ab(s)
        pltpu.make_async_copy(mine_at(s, part_of(s, a, b, z)), out_at(s, part_of(s, a, b, z)), own_sem.at[s]).wait()
        pbs = (b, 1 - b) if STREAMS[s][1] else (b,)
        for pb in pbs:
            for k in range(3):
                z_drain(s, pb, k)
        for pz in range(4):
            for pb in pbs:
                src = out_at(s, part_of(s, a, pb, pz))

                @pl.when((z >= pz) & (z < 3))
                def _():
                    to_z(s, pb, pz, src, True).wait_send()

                @pl.when((z <= pz) & (z > 0))
                def _():
                    to_z(s, pb, pz, src, False).wait_send()
            for pb in (0, 1):
                src = out_at(s, part_of(s, a, pb, pz))

                @pl.when(((pb == b) & (pz == z)) == False)
                def _():
                    to_a(s, pb, pz, src).wait_send()
            if not STREAMS[s][1]:
                @pl.when(z != pz)
                def _():
                    to_b(s, pz, out_at(s, 0)).wait_send()
        for p in range(16):
            src = out_at(s, p)

            @pl.when(p != part_of(s, a, b, z))
            def _():
                to_core(s, p, src).wait_send()
            _, _, r0, n = STREAMS[s]
            dst = o_ref.at[p, pl.ds(pl.multiple_of((1 - c) * HALF + r0, 16), n)]
            copy_to(dst, dst, oc.at[s, p], ocr.at[s, p], partner).wait_recv()


def all_sum(grads, vectors):
    dma = pltpu.SemaphoreType.DMA
    bf = jnp.bfloat16
    rows = [s[3] for s in STREAMS]
    return pl.pallas_call(
        reduce_kernel,
        name="all_sum",
        out_shape=(jax.ShapeDtypeStruct(grads.shape, bf), jax.ShapeDtypeStruct(vectors.shape, jnp.float32)),
        in_specs=[pl.BlockSpec(memory_space=pl.ANY), pl.BlockSpec(memory_space=pltpu.VMEM)],
        out_specs=(pl.BlockSpec(memory_space=pl.ANY), pl.BlockSpec(memory_space=pltpu.VMEM)),
        scratch_shapes=[
            pltpu.VMEM((PARTS, HALF, COLS), bf), pltpu.VMEM((PARTS, HALF, COLS), bf),
            *[pltpu.VMEM((8, n, COLS), bf) for n in rows],
            *[pltpu.VMEM((10, n, COLS), bf) for n in rows],
            *[pltpu.VMEM((1 if s[1] else 4, s[3], COLS), bf) for s in STREAMS],
            pltpu.VMEM((5, *vectors.shape), jnp.float32),
            dma((16,)), dma((16,)), dma((16,)),
            dma((4, 8)), dma((4, 8)), dma((4, 10)), dma((4, 10)), dma((4, 4)), dma((4, 4)),
            dma((4, 4)), dma((4, 4)), dma((4, 16)), dma((4, 8)), dma((4, 8)), dma((4, 8)), dma((4, 16)), dma((4, 16)),
            dma((5,)), dma((5,)), dma((4,)),
        ],
        compiler_params=pltpu.CompilerParams(collective_id=1, has_side_effects=True, vmem_limit_bytes=56 * 2**20),
    )(grads, vectors)


F32 = jnp.float32
BF = jnp.bfloat16
CHUNK = 512
WEIGHTS = ("wq", "wk", "wv", "wo", "wg", "wu", "wd")


def dot_nn(left, right):
    return lax.dot_general(left, right, (((1,), (0,)), ((), ())), preferred_element_type=F32)


def dot_nt(left, right):
    return lax.dot_general(left, right, (((1,), (1,)), ((), ())), preferred_element_type=F32)


def rope_lanes(tensor, cosine, sine, sign):
    rows, width = tensor.shape
    lane = lax.broadcasted_iota(jnp.int32, (rows, 2 * HD), 1)
    first = lax.rem(lane, HD) < HD // 2
    out = []
    for i in range(0, width, 2 * HD):
        piece = tensor[:, i : i + 2 * HD]
        other = jnp.where(first, pltpu.roll(piece, 2 * HD - HD // 2, 1), pltpu.roll(piece, HD // 2, 1))
        out.append(piece * cosine + (other * sine) * sign)
    return jnp.concatenate(out, axis=1)


def inverse_of(rows):
    return lax.rsqrt(jnp.mean(rows * rows, axis=1, keepdims=True) + epsilon)


def front_part(r, wait, state):
    gain = r["gains"][0:1, :]
    normed = (state * inverse_of(state) * gain).astype(BF)
    r["normed"][...] = normed
    wait("wk")
    keys = dot_nn(normed, r["wk_v"][...])
    wait("wv")
    values = dot_nn(normed, r["wv_v"][...])
    wait("wq")
    queries = dot_nn(normed, r["wq_v"][...])
    turned = rope_lanes(jnp.concatenate([queries, keys], axis=1), r["cos"][...], r["sin"][...], 1.0).astype(BF)
    qw = queries.shape[1]
    r["q"][...] = turned[:, :qw]
    r["kv"][...] = jnp.concatenate([turned[:, qw:], values.astype(BF)], axis=1)


def head_rows(tensor, g):
    per = H // KVH
    return jnp.concatenate([tensor[:, (g * per + i) * HD : (g * per + i + 1) * HD] for i in range(per)], axis=0)


def window(r):
    rows = r["mask"].shape[0]
    start = lax.rem(lax.axis_index("tok"), 2) * r["q_in"].shape[0]
    return r["kvw"][pl.ds(pl.multiple_of(start, 128), rows), :]


def attention_part(r):
    per = H // KVH
    kv = window(r)
    q = r["q_in"][...]
    rows = q.shape[0]
    allowed = jnp.concatenate([r["mask"][...]] * per, axis=1) > 0
    mixed_t, logs = [], []
    for g in range(KVH):
        k_g = kv[:, g * HD : (g + 1) * HD]
        v_g = kv[:, (KVH + g) * HD : (KVH + g + 1) * HD]
        scores = jnp.where(allowed, dot_nt(k_g, head_rows(q, g)) * HD**-0.5, masked)
        largest = jnp.max(scores, axis=0, keepdims=True)
        exponent = jnp.exp(scores - largest)
        total = jnp.sum(exponent, axis=0, keepdims=True)
        probs = (exponent * (1.0 / total)).astype(BF)
        mix = dot_nn(v_g.T, probs)
        mixed_t += [mix[:, i * rows : (i + 1) * rows] for i in range(per)]
        logs.append(largest + jnp.log(total))
    r["lse"][...] = jnp.concatenate(logs + [logs[0]] * (r["lse"].shape[0] - KVH), axis=0)
    return jnp.concatenate(mixed_t, axis=0).T.astype(BF)


def rest_part(r, wait):
    state = r["state"][...]
    mixed = attention_part(r)
    r["mixed"][...] = mixed
    wait("wo")
    attn_out = dot_nn(mixed, r["wo_v"][...])
    middle = state + attn_out
    r["middle"][...] = middle
    normed_two = (middle * inverse_of(middle) * r["gains"][1:2, :]).astype(BF)
    r["normed_two"][...] = normed_two
    wait("wg")
    wait("wu")
    wait("wd")
    ff = r["wg_v"].shape[1]
    mlp = jnp.zeros(state.shape, F32)
    for i in range(0, ff, CHUNK):
        at = slice(i, i + CHUNK)
        gate = dot_nn(normed_two, r["wg_v"][:, at])
        up = dot_nn(normed_two, r["wu_v"][:, at])
        r["gate"][:, at] = gate
        r["up"][:, at] = up
        hidden = (gate * jax.nn.sigmoid(gate) * up).astype(BF)
        r["hidden"][:, at] = hidden
        mlp = mlp + dot_nn(hidden, r["wd_v"][at, :])
    branch = attn_out + mlp.astype(BF).astype(F32)
    r["branch"][...] = branch
    router = jax.nn.sigmoid(jnp.sum(state * r["gains"][2:3, :], axis=1, keepdims=True))
    return state + (r["live"][:, 0:1] * router) * branch


def norm_back(grad, rows, gain):
    inverse = inverse_of(rows)
    scaled = rows * inverse
    weighted = grad * gain
    inner = jnp.mean(weighted * scaled, axis=1, keepdims=True)
    return inverse * (weighted - scaled * inner), jnp.sum(grad * scaled, axis=0, keepdims=True)


def back_part(r, wait, grad_after):
    state, live = r["b_state"][...], r["b_live"][:, 0:1]
    width = state.shape[1]
    router_vec = r["gains"][2:3, :]
    router = jax.nn.sigmoid(jnp.sum(state * router_vec, axis=1, keepdims=True))
    d_branch = (live * router) * grad_after
    d_logit = live * (router * (1.0 - router)) * jnp.sum(r["b_branch"][...] * grad_after, axis=1, keepdims=True)
    d_router = jnp.sum(d_logit * state, axis=0, keepdims=True)
    d_mlp = d_branch.astype(BF)
    r["d_mlp"][...] = d_mlp
    wait("wd")
    wait("wg")
    wait("wu")
    ff = r["wg_v"].shape[1]
    d_two = jnp.zeros(state.shape, F32)
    for i in range(0, ff, CHUNK):
        at = slice(i, i + CHUNK)
        gate, up = r["b_gate"][:, at], r["b_up"][:, at]
        sig = jax.nn.sigmoid(gate)
        d_hidden = dot_nt(d_mlp, r["wd_v"][at, :])
        d_up = (d_hidden * (gate * sig)).astype(BF)
        d_gate = (d_hidden * up * (sig * (1.0 + gate * (1.0 - sig)))).astype(BF)
        r["d_up"][:, at] = d_up
        r["d_gate"][:, at] = d_gate
        d_two = d_two + dot_nt(d_gate, r["wg_v"][:, at]) + dot_nt(d_up, r["wu_v"][:, at])
    d_two = d_two.astype(BF).astype(F32)
    d_middle, d_gain_two = norm_back(d_two, r["b_middle"][...], r["gains"][1:2, :])
    r["acc_out"][1:2, :width] = r["acc"][1:2, :width] + d_gain_two
    r["acc_out"][2:3, :width] = r["acc"][2:3, :width] + d_router
    d_attn = (d_branch + d_middle).astype(BF)
    r["d_attn"][...] = d_attn
    r["d_state"][...] = grad_after + d_logit * router_vec + d_middle
    wait("wo")
    d_mixed = dot_nt(d_attn, r["wo_v"][...]).astype(BF)

    per = H // KVH
    kv = window(r)
    q = r["q_in"][...]
    rows = q.shape[0]
    allowed = jnp.concatenate([r["mask"][...]] * per, axis=1) > 0
    d_keys, d_values, dq_t = [], [], []
    for g in range(KVH):
        k_g = kv[:, g * HD : (g + 1) * HD]
        v_g = kv[:, (KVH + g) * HD : (KVH + g + 1) * HD]
        q_g, do_g = head_rows(q, g), head_rows(d_mixed, g)
        scores = jnp.where(allowed, dot_nt(k_g, q_g) * HD**-0.5, masked)
        probs = jnp.exp(scores - r["b_lse"][g : g + 1, :])
        d_values.append(dot_nn(probs.astype(BF), do_g))
        d_probs = dot_nt(v_g, do_g)
        d_scores = (probs * (d_probs - jnp.sum(probs * d_probs, axis=0, keepdims=True))).astype(BF)
        d_keys.append(dot_nn(d_scores, q_g) * HD**-0.5)
        dq = dot_nn(k_g.T, d_scores) * HD**-0.5
        dq_t += [dq[:, i * rows : (i + 1) * rows] for i in range(per)]
    d_queries = jnp.concatenate(dq_t + [jnp.zeros((HD, rows), F32)], axis=0).T
    d_queries = rope_lanes(d_queries, r["cos"][...], r["sin"][...], -1.0)
    r["d_q"][...] = d_queries[:, : H * HD].astype(BF)
    start = lax.rem(lax.axis_index("tok"), 2) * rows
    partial = r["dkv"]
    keep = partial.shape[0] - kv.shape[0]
    partial[pl.ds(pl.multiple_of((1 - lax.rem(lax.axis_index("tok"), 2)) * kv.shape[0], 128), keep), :] = jnp.zeros((keep, kv.shape[1]), BF)
    partial[pl.ds(pl.multiple_of(start, 128), kv.shape[0]), :] = jnp.concatenate(d_keys + d_values, axis=1).astype(BF)


def home_part(r, wait):
    half = KVH * HD
    total = r["home"][0].astype(F32)
    for i in range(1, r["home"].shape[0]):
        total = total + r["home"][i].astype(F32)
    rows = total.shape[0]
    padded = jnp.concatenate([total[:, :half], jnp.zeros((rows, half % (2 * HD)), F32)], axis=1)
    d_keys = rope_lanes(padded, r["cos"][...], r["sin"][...], -1.0)[:, :half].astype(BF)
    d_values = total[:, half:].astype(BF)
    r["d_k"][...] = d_keys
    r["d_v"][...] = d_values
    wait("wq")
    wait("wk")
    wait("wv")
    d_normed = dot_nt(r["h_dq"][...], r["wq_v"][...]) + dot_nt(d_keys, r["wk_v"][...]) + dot_nt(d_values, r["wv_v"][...])
    state = r["h_state"][...]
    width = state.shape[1]
    d_in, d_gain = norm_back(d_normed, state, r["gains"][0:1, :])
    r["acc_out"][0:1, :width] = r["acc"][0:1, :width] + d_gain
    return r["h_d_state"][...] + d_in


def stage(name, parts, needed, inputs, outputs, weights, rename=None):
    in_names, out_names = list(inputs), list(outputs)
    w_names = [w for w in needed]

    def body(*refs):
        it = iter(refs)
        r = {n: next(it) for n in in_names}
        src = {n: next(it) for n in w_names}
        for n in out_names:
            r[n] = next(it)
        for n in w_names:
            r[n + "_v"] = next(it)
        sems = next(it)
        copies = {n: pltpu.make_async_copy(src[n], r[n + "_v"], sems.at[i]) for i, n in enumerate(w_names)}
        for n in w_names:
            copies[n].start()
        done = set()

        def wait(n):
            if n not in done:
                copies[n].wait()
                done.add(n)

        parts(r, wait)
        for n in w_names:
            wait(n)

    vm = pl.BlockSpec(memory_space=pltpu.VMEM)
    out = pl.pallas_call(
        body,
        name=name,
        out_shape=tuple(outputs.values()),
        in_specs=[vm] * len(in_names) + [pl.BlockSpec(memory_space=pl.ANY)] * len(w_names),
        out_specs=tuple([vm] * len(out_names)),
        scratch_shapes=[pltpu.VMEM(weights[n].shape, BF) for n in w_names] + [pltpu.SemaphoreType.DMA((len(w_names),))],
        compiler_params=pltpu.CompilerParams(vmem_limit_bytes=60 * 2**20),
    )(*inputs.values(), *[weights[n] for n in w_names])
    return dict(zip(out_names, out))


def shaped(shape, kind):
    return jax.ShapeDtypeStruct(shape, kind)


def front_outs(rows, width):
    return {"normed": shaped((rows, width), BF), "q": shaped((rows, H * HD), BF), "kv": shaped((rows, 2 * KVH * HD), BF)}


def forward_stage(state, q, kvw, mask, live, tables, gains, weights, last):
    rows, width = state.shape
    ff = weights["wg"].shape[1]
    outs = {
        "mixed": shaped((rows, H * HD), BF), "lse": shaped((8, (H // KVH) * rows), F32), "middle": shaped((rows, width), F32),
        "normed_two": shaped((rows, width), BF), "gate": shaped((rows, ff), F32), "up": shaped((rows, ff), F32),
        "hidden": shaped((rows, ff), BF), "branch": shaped((rows, width), F32), "next": shaped((rows, width), F32),
    }
    if not last:
        outs |= front_outs(rows, width)

    def parts(r, wait):
        state_next = rest_part(r, wait)
        r["next"][...] = state_next
        if not last:
            front_part(r, wait, state_next)

    needed = ("wo", "wg", "wu", "wd") + (() if last else ("wk", "wv", "wq"))
    ins = {"state": state, "q_in": q, "kvw": kvw, "mask": mask, "live": live, "cos": tables[0], "sin": tables[1], "gains": gains}
    return stage("forward", parts, needed, ins, outs, weights)


def first_stage(hidden_in, tables, gains, weights):
    rows, width = hidden_in.shape

    def parts(r, wait):
        state = r["hidden"][...].astype(F32)
        r["state"][...] = state
        front_part(r, wait, state)

    outs = front_outs(rows, width) | {"state": shaped((rows, width), F32)}
    return stage("first", parts, ("wk", "wv", "wq"), {"hidden": hidden_in, "cos": tables[0], "sin": tables[1], "gains": gains}, outs, weights)


def backward_stage(kept, before, mask, live, tables, gains, acc, weights, cotangent):
    ins = {"cos": tables[0], "sin": tables[1], "gains": gains, "acc": acc}
    outs = {"acc_out": shaped(acc.shape, F32)}
    needed = ()
    rows, width = (kept or before)["state"].shape
    ff = weights["wg"].shape[1]
    kvr = 2 * KVH * HD
    if before is not None:
        ins |= {"home": before["home"], "h_dq": before["d_q"], "h_state": before["state"], "h_d_state": before["d_state"]}
        outs |= {"d_k": shaped((rows, kvr // 2), BF), "d_v": shaped((rows, kvr // 2), BF)}
        needed += ("wq", "wk", "wv")
    else:
        ins |= {"cot": cotangent}
    if kept is not None:
        ins |= {"b_state": kept["state"], "b_live": live, "b_branch": kept["branch"], "b_gate": kept["gate"], "b_up": kept["up"],
                "b_middle": kept["middle"], "b_lse": kept["lse"], "kvw": kept["kvw"], "q_in": kept["q"], "mask": mask}
        outs |= {"d_mlp": shaped((rows, width), BF), "d_up": shaped((rows, ff), BF), "d_gate": shaped((rows, ff), BF),
                 "d_attn": shaped((rows, width), BF), "d_state": shaped((rows, width), F32), "d_q": shaped((rows, H * HD), BF),
                 "dkv": shaped(kept["kvw"].shape, BF)}
        needed += ("wd", "wg", "wu", "wo")
    else:
        outs |= {"grad": shaped((rows, width), F32)}

    def parts(r, wait):
        r["acc_out"][...] = r["acc"][...]
        grad = home_part(r, wait) if before is not None else r["cot"][...].astype(F32)
        if kept is not None:
            back_part(r, wait, grad)
        else:
            r["grad"][...] = grad

    return stage("backward", parts, needed, ins, outs, weights)


def keys_kernel(chips, back, kv_ref, w_ref, s_right, r_left, s_core, r_core):
    g, t = lax.axis_index("grp"), lax.axis_index("tok")
    z, c = t // 2, lax.rem(t, 2)
    rows = kv_ref.shape[0]
    partner, right = (g, z * 2 + 1 - c), (g, t + 2)

    def slot(d, core):
        return w_ref.at[pl.ds(pl.multiple_of(((back - d) * 2 + core) * rows, 128), rows)]

    bar = pltpu.get_barrier_semaphore()
    pl.semaphore_signal(bar, inc=1, device_id=partner, device_id_type=MESH)

    @pl.when(z > 0)
    def _():
        pl.semaphore_signal(bar, inc=1, device_id=(g, t - 2), device_id_type=MESH)

    def along(d, src):
        return copy_to(src, slot(d, c), s_right.at[d - 1], r_left.at[d - 1], right)

    def beside(d, src):
        return copy_to(src, slot(d, c), s_core.at[d], r_core.at[d], partner)

    own = w_ref.at[pl.ds(pl.multiple_of((back * 2 + c) * rows, 128), rows)]
    own[...] = kv_ref[...]
    for d in range(1, back + 1):
        @pl.when(z < d)
        def _():
            for core in (0, 1):
                slot(d, core)[...] = jnp.zeros(kv_ref.shape, kv_ref.dtype)

    pl.semaphore_wait(bar, 1 + (z < chips - 1).astype(jnp.int32))

    @pl.when(z < chips - 1)
    def _():
        along(1, kv_ref).start()

    beside(0, kv_ref).start()
    for d in range(1, back + 1):
        @pl.when(z >= d)
        def _():
            along(d, slot(d, c)).wait_recv()
            if d < back:
                @pl.when(z < chips - 1)
                def _():
                    along(d + 1, slot(d, c)).start()
            beside(d, slot(d, c)).start()

    def mine_to(d):
        return copy_to(slot(d, 1 - c), slot(d, 1 - c), s_core.at[d], r_core.at[d], partner)

    mine_to(0).wait_recv()
    beside(0, kv_ref).wait_send()

    @pl.when(z < chips - 1)
    def _():
        along(1, kv_ref).wait_send()

    for d in range(1, back + 1):
        @pl.when(z >= d)
        def _():
            mine_to(d).wait_recv()
            beside(d, slot(d, c)).wait_send()
            if d < back:
                @pl.when(z < chips - 1)
                def _():
                    along(d + 1, slot(d, c)).wait_send()


def exchange_keys(kv, n_tok, nback):
    back = nback // 2
    rows = kv.shape[0]
    dma = pltpu.SemaphoreType.DMA
    return pl.pallas_call(
        lambda *refs: keys_kernel(n_tok // 2, back, *refs),
        name="exchange_keys",
        out_shape=jax.ShapeDtypeStruct(((2 * back + 2) * rows, kv.shape[1]), kv.dtype),
        in_specs=[pl.BlockSpec(memory_space=pltpu.VMEM)],
        out_specs=pl.BlockSpec(memory_space=pltpu.VMEM),
        scratch_shapes=[dma((back,)), dma((back,)), dma((back + 1,)), dma((back + 1,))],
        compiler_params=pltpu.CompilerParams(collective_id=2, has_side_effects=True, vmem_limit_bytes=32 * 2**20),
    )(kv)


def home_kernel(chips, back, p_ref, h_ref, beside_in, sums, after_in, s_left, r_right, s_core, r_core):
    g, t = lax.axis_index("grp"), lax.axis_index("tok")
    z, c = t // 2, lax.rem(t, 2)
    rows = h_ref.shape[1]
    partner, left = (g, z * 2 + 1 - c), (g, t - 2)

    def block(d, core):
        return p_ref.at[pl.ds(pl.multiple_of(((back - d) * 2 + core) * rows, 128), rows)]

    bar = pltpu.get_barrier_semaphore()
    pl.semaphore_signal(bar, inc=1, device_id=partner, device_id_type=MESH)

    @pl.when(z < chips - 1)
    def _():
        pl.semaphore_signal(bar, inc=1, device_id=(g, t + 2), device_id_type=MESH)

    pl.semaphore_wait(bar, 1 + (z > 0).astype(jnp.int32))

    def beside(d):
        return copy_to(block(d, 1 - c), beside_in.at[d], s_core.at[d], r_core.at[d], partner)

    def along(d):
        return copy_to(sums.at[d - 1], after_in.at[d - 1], s_left.at[d - 1], r_right.at[d - 1], left)

    for d in range(back, 0, -1):
        @pl.when(z >= d)
        def _():
            beside(d).start()
    beside(0).start()
    for d in range(back, 0, -1):
        @pl.when(z >= d)
        def _():
            beside(d).wait_recv()
            sums[d - 1] = (block(d, c)[...].astype(F32) + beside_in[d].astype(F32)).astype(BF)
            if d < back:
                @pl.when(z < chips - 1)
                def _():
                    along(d + 1).wait_recv()
                    sums[d - 1] = (sums[d - 1].astype(F32) + after_in[d].astype(F32)).astype(BF)
            along(d).start()
    beside(0).wait_recv()
    h_ref[0] = block(0, c)[...].astype(F32) + beside_in[0].astype(F32)

    @pl.when(z < chips - 1)
    def _():
        along(1).wait_recv()
        h_ref[0] = h_ref[0] + after_in[0].astype(F32)

    beside(0).wait_send()
    for d in range(1, back + 1):
        @pl.when(z >= d)
        def _():
            beside(d).wait_send()
            along(d).wait_send()


def exchange_home(partial, n_tok, nback):
    back = nback // 2
    rows = partial.shape[0] // (2 * back + 2)
    width = partial.shape[1]
    dma = pltpu.SemaphoreType.DMA
    return pl.pallas_call(
        lambda *refs: home_kernel(n_tok // 2, back, *refs),
        name="exchange_home",
        out_shape=jax.ShapeDtypeStruct((1, rows, width), F32),
        in_specs=[pl.BlockSpec(memory_space=pltpu.VMEM)],
        out_specs=pl.BlockSpec(memory_space=pltpu.VMEM),
        scratch_shapes=[
            pltpu.VMEM((back + 1, rows, width), BF), pltpu.VMEM((back, rows, width), BF), pltpu.VMEM((back, rows, width), BF),
            dma((back,)), dma((back,)), dma((back + 1,)), dma((back + 1,)),
        ],
        compiler_params=pltpu.CompilerParams(collective_id=3, has_side_effects=True, vmem_limit_bytes=32 * 2**20),
    )(partial)


ROW_NAMES = ("normed_two", "d_mlp", "normed", "mixed", "d_gate", "d_up", "hidden", "d_q", "d_k", "d_v", "d_attn")


def grads_kernel(count, *refs):
    n = len(ROW_NAMES)
    r = {name: refs[i * count : (i + 1) * count] for i, name in enumerate(ROW_NAMES)}
    g_ref, left_t, slots, sems = refs[n * count :]
    for i, name in enumerate(ROW_NAMES[:4]):
        left_t[i] = jnp.concatenate([each[...].astype(F32).T.astype(BF) for each in r[name]], axis=1)

    def rows_of(name, low, high):
        return jnp.concatenate([each[:, low:high] for each in r[name]], axis=0)

    def out_copy(p):
        return pltpu.make_async_copy(slots.at[p % 2], g_ref.at[p], sems.at[p % 2])

    width = left_t.shape[1]
    for p in range(PARTS):
        if p >= 2:
            out_copy(p - 2).wait()
        slot = slots.at[p % 2]
        if p < 12:
            name, left = (("d_gate", 0), ("d_up", 0), ("hidden", 1))[p // 4]
            low = (p % 4) * COLS
            slot[...] = dot_nn(left_t[left], rows_of(name, low, low + COLS)).astype(BF)
        elif p == 12:
            slot[...] = dot_nn(left_t[2], rows_of("d_q", 0, COLS)).astype(BF)
        elif p == 13:
            right = jnp.concatenate([rows_of("d_q", COLS, width), rows_of("d_k", 0, 2 * COLS - width)], axis=1)
            slot[...] = dot_nn(left_t[2], right).astype(BF)
        elif p == 14:
            slot[...] = dot_nn(left_t[3], rows_of("d_attn", 0, COLS)).astype(BF)
        else:
            one = dot_nn(left_t[3], rows_of("d_attn", COLS, width))
            two = dot_nn(left_t[2], rows_of("d_v", 0, 2 * COLS - width))
            slot[...] = jnp.concatenate([one, two], axis=1).astype(BF)
        out_copy(p).start()
    out_copy(PARTS - 2).wait()
    out_copy(PARTS - 1).wait()


def weight_gradients(rows):
    count = len(rows["d_q"])
    flat = [each for name in ROW_NAMES for each in rows[name]]
    tokens, width = rows["normed"][0].shape
    return pl.pallas_call(
        lambda *refs: grads_kernel(count, *refs),
        name="weight_gradients",
        out_shape=jax.ShapeDtypeStruct((PARTS, width, COLS), BF),
        in_specs=[pl.BlockSpec(memory_space=pltpu.VMEM)] * len(flat),
        out_specs=pl.BlockSpec(memory_space=pl.ANY),
        scratch_shapes=[pltpu.VMEM((4, width, count * tokens), BF), pltpu.VMEM((2, width, COLS), BF), pltpu.SemaphoreType.DMA((2,))],
        compiler_params=pltpu.CompilerParams(vmem_limit_bytes=60 * 2**20),
    )(*flat)


def spread_kernel(p_ref, gate, up, down, d_q, d_k, d_v, d_o, came, wide, turned, q_full, k_full, o_full, v_full, sem_in, sem_out, sem_full):
    width = q_full.shape[0]
    cut = 2 * COLS - width
    order = [12, 13, 14, 15] + list(range(12))

    def fetch(i):
        return pltpu.make_async_copy(p_ref.at[order[i]], came.at[i % 3], sem_in.at[i % 3])

    def put(i):
        p = order[i]
        if p >= 8:
            return pltpu.make_async_copy(turned.at[i % 2], down.at[pl.ds((p - 8) * COLS, COLS)], sem_out.at[i % 2])
        return pltpu.make_async_copy(wide.at[i % 2], (gate, up)[p // 4].at[:, pl.ds((p % 4) * COLS, COLS)], sem_out.at[i % 2])

    fulls = [(q_full, d_q), (k_full, d_k), (o_full, d_o), (v_full, d_v)]

    def put_full(j):
        return pltpu.make_async_copy(fulls[j][0], fulls[j][1], sem_full.at[j])

    fetch(0).start()
    fetch(1).start()
    for i, p in enumerate(order):
        if i + 2 < len(order):
            fetch(i + 2).start()
        fetch(i).wait()
        part = came.at[i % 3]
        if i >= 6:
            put(i - 2).wait()
        if p >= 12:
            full, other = (q_full, k_full) if p < 14 else (o_full, v_full)
            if p % 2 == 0:
                full[:, :COLS] = part[...].astype(F32)
            else:
                got = part[...].astype(F32)
                full[:, COLS:] = got[:, : width - COLS]
                other[...] = got[:, width - COLS :]
                put_full(0 if p < 14 else 2).start()
                put_full(1 if p < 14 else 3).start()
        elif p >= 8:
            turned[i % 2] = part[...].astype(F32).T
            put(i).start()
        else:
            wide[i % 2] = part[...].astype(F32)
            put(i).start()
    put(len(order) - 2).wait()
    put(len(order) - 1).wait()
    for j in range(4):
        put_full(j).wait()


def spread_out(parts):
    n, width, cols = parts.shape
    kv = 2 * cols - width
    ff = 4 * cols
    shapes = [(width, ff), (width, ff), (ff, width), (width, width), (width, kv), (width, kv), (width, width)]
    vm = pltpu.VMEM
    return pl.pallas_call(
        spread_kernel,
        name="spread_out",
        out_shape=tuple(jax.ShapeDtypeStruct(s, F32) for s in shapes),
        in_specs=[pl.BlockSpec(memory_space=pl.ANY)],
        out_specs=tuple([pl.BlockSpec(memory_space=pl.ANY)] * 7),
        scratch_shapes=[
            vm((3, width, cols), BF), vm((2, width, cols), F32), vm((2, cols, width), F32),
            vm((width, width), F32), vm((width, kv), F32), vm((width, width), F32), vm((width, kv), F32),
            pltpu.SemaphoreType.DMA((3,)), pltpu.SemaphoreType.DMA((2,)), pltpu.SemaphoreType.DMA((4,)),
        ],
        compiler_params=pltpu.CompilerParams(vmem_limit_bytes=60 * 2**20),
    )(parts)


def on_device(
    hidden_in,
    cotangent,
    lengths,
    active,
    norm_attn,
    w_query,
    w_key,
    w_value,
    w_out,
    norm_mlp,
    w_gate,
    w_up,
    w_down,
    w_router,
):
    n_tok = lax.axis_size("tok")
    n_grp = lax.axis_size("grp")
    me_index = lax.axis_index("tok")
    rows, width = hidden_in.shape
    nback = min(SPAN, n_tok // 2)

    def gathered(shard):
        return lax.all_gather(shard, "tok", axis=0, tiled=True)

    matrices = (w_query, w_key, w_value, w_out, w_gate, w_up, w_down)
    weights = {name: gathered(shard) for name, shard in zip(WEIGHTS, matrices)}
    gains = jnp.stack([gathered(norm_attn), gathered(norm_mlp), gathered(w_router)]).astype(F32)
    gains = jnp.pad(gains, ((0, 5), (0, 0)))

    lengths_row = lengths[0]
    token = jnp.arange(rows, dtype=jnp.int32)
    global_rows = me_index * rows + token
    segment_rows = segment_of(lengths_row, global_rows)
    cosine, sine = rotary_tables(position_of(lengths_row, global_rows, segment_rows))
    tables = (jnp.concatenate([cosine] * 4, axis=1), jnp.concatenate([-sine, sine] * 2, axis=1))
    reach = (nback + 1) * rows
    global_keys = (me_index - nback) * rows + jnp.arange(reach, dtype=jnp.int32)
    live_all = lax.all_gather(active.astype(BF), "tok", axis=1, tiled=True)
    live_all = jnp.pad(live_all, ((0, 0), (nback * rows, 0)))
    live_keys = lax.dynamic_slice_in_dim(live_all, me_index * rows, reach, 1)
    reachable = (segment_rows[None, :] == segment_of(lengths_row, global_keys)[:, None]) & (
        global_keys[:, None] <= global_rows[None, :]
    )
    masks = jnp.where(reachable[None] & (live_keys[:, :, None] > 0), 1.0, 0.0).astype(F32)
    lives = [active[i].astype(F32)[:, None] for i in range(RECUR)]

    kept = []
    made = first_stage(hidden_in, tables, gains, weights)
    state = made["state"]
    for step in range(RECUR):
        kvw = exchange_keys(made["kv"], n_tok, nback)
        last = step == RECUR - 1
        done = forward_stage(state, made["q"], kvw, masks[step], lives[step], tables, gains, weights, last)
        kept.append({**done, "state": state, "q": made["q"], "kvw": kvw, "normed_r": made["normed"]})
        made, state = done, done["next"]

    acc = jnp.zeros((8, 1024), F32)
    before = None
    rows_of = {name: [] for name in ROW_NAMES}
    for step in reversed(range(RECUR)):
        back = backward_stage(kept[step], before, masks[step], lives[step], tables, gains, acc, weights, cotangent)
        acc = back["acc_out"]
        for name in ("d_k", "d_v"):
            if before is not None:
                rows_of[name].append(back[name])
        for name in ("d_mlp", "d_gate", "d_up", "d_q", "d_attn"):
            rows_of[name].append(back[name])
        for name in ("normed_two", "mixed", "hidden"):
            rows_of[name].append(kept[step][name])
        rows_of["normed"].append(kept[step]["normed_r"])
        before = {"home": exchange_home(back["dkv"], n_tok, nback), "d_q": back["d_q"], "state": kept[step]["state"], "d_state": back["d_state"]}
    back = backward_stage(None, before, None, None, tables, gains, acc, weights, None)
    for name in ("d_k", "d_v"):
        rows_of[name].append(back[name])
    acc = back["acc_out"]
    parts = weight_gradients(rows_of)
    if (n_grp, n_tok) == (4, 8):
        parts, acc = all_sum(parts, acc)
    else:
        parts = lax.psum(parts.astype(F32), ("grp", "tok")).astype(BF)
        acc = lax.psum(acc, ("grp", "tok"))
    d_gate, d_up, d_down, d_q, d_k, d_v, d_o = spread_out(parts)
    return (
        state.astype(BF),
        back["grad"],
        acc[0, :width],
        d_q,
        d_k,
        d_v,
        d_o,
        acc[1, :width],
        d_gate,
        d_up,
        d_down,
        acc[2, :width],
    )


def solution(mesh):
    placed = (
        P(("grp", "tok"), None),
        P(("grp", "tok"), None),
        P("grp", None),
        P(None, ("grp", "tok")),
        P("tok"),
        P("tok", None),
        P("tok", None),
        P("tok", None),
        P("tok", None),
        P("tok"),
        P("tok", None),
        P("tok", None),
        P("tok", None),
        P("tok"),
    )
    return jax.shard_map(
        on_device,
        mesh=mesh,
        in_specs=placed,
        out_specs=(
            P(("grp", "tok"), None),
            P(("grp", "tok"), None),
            P(),
            P(),
            P(),
            P(),
            P(),
            P(),
            P(),
            P(),
            P(),
            P(),
        ),
        check_vma=False,
    )
```

```python
import jax
import jax.numpy as jnp
from jax import lax
from jax.experimental import pallas as pl
from jax.experimental.pallas import tpu as pltpu
from jax.sharding import PartitionSpec as P

MESH = pl.DeviceIdType.MESH

H = 15
KVH = 5
HD = 64
RECUR = 3
SPAN = 16

epsilon = 1e-05
theta = 10000.0
masked = -1000000000.0

def ends_of(lengths_row):
    count = lengths_row.shape[0]
    until = jnp.arange(count)[:, None] >= jnp.arange(count)[None, :]
    return jnp.sum(jnp.where(until, lengths_row[None, :], 0), axis=1)


def segment_of(lengths_row, global_rows):
    ends_at = ends_of(lengths_row)
    return jnp.sum((global_rows[:, None] >= ends_at[None, :]).astype(jnp.int32), axis=1)


def position_of(lengths_row, global_rows, segments):
    ends_at = ends_of(lengths_row)
    starts_at = ends_at - lengths_row
    picked = segments[:, None] == jnp.arange(lengths_row.shape[0], dtype=jnp.int32)[None, :]
    return global_rows - jnp.sum(jnp.where(picked, starts_at[None, :], 0), axis=1)


def rotary_tables(positions):
    half_dim = HD // 2
    inverse = jnp.power(theta, -jnp.arange(half_dim, dtype=jnp.float32) * (2.0 / HD))
    angle = positions.astype(jnp.float32)[..., None] * inverse
    return (jnp.cos(angle), jnp.sin(angle))


PARTS = 16
HALF = 480
COLS = 640
STREAMS = (("x", True, 0, 160), ("y", True, 160, 160), ("x", False, 320, 80), ("y", False, 400, 80))


def place():
    g, t = lax.axis_index("grp"), lax.axis_index("tok")
    return g // 2, lax.rem(g, 2), t // 2, lax.rem(t, 2)


def dev(y, x, z, c):
    return (y * 2 + x, z * 2 + c)


def pick(z, values):
    out = jnp.int32(values[3])
    for i in (2, 1, 0):
        out = jnp.where(z == i, jnp.int32(values[i]), out)
    return out


def copy_to(src, dst, send, recv, device):
    return pltpu.make_async_remote_copy(src_ref=src, dst_ref=dst, send_sem=send, recv_sem=recv, device_id=device, device_id_type=MESH)


def add_rows(dst, src, rows, step):
    def body(i, _):
        at = pl.ds(pl.multiple_of(i * step, step), step)
        dst[at, :] = dst[at, :] + src[at, :]
        return 0
    lax.fori_loop(0, rows // step, body, 0)


def reduce_kernel(g_ref, v_ref, o_ref, vo_ref, mine, other, ra0, ra1, ra2, ra3, rz0, rz1, rz2, rz3, rb0, rb1, rb2, rb3,
                  vrecv, load_sem, core_s, core_r, as_, ar, zs, zr, bs, br, ob, obr, oz, ozr, oa, oar, oc, ocr, vs, vr, own_sem):
    y, x, z, c = place()
    ra, rz, rb = (ra0, ra1, ra2, ra3), (rz0, rz1, rz2, rz3), (rb0, rb1, rb2, rb3)
    partner = dev(y, x, z, 1 - c)
    across = {"x": dev(y, 1 - x, z, c), "y": dev(1 - y, x, z, c)}
    left, right = dev(y, x, z - 1, c), dev(y, x, z + 1, c)
    at_axis = {"x": x, "y": y}
    order = (pick(z, (3, 3, 0, 0)), pick(z, (2, 0, 3, 1)), pick(z, (1, 2, 1, 2)), z)

    bar = pltpu.get_barrier_semaphore()
    for d in (partner, across["x"], across["y"]):
        pl.semaphore_signal(bar, inc=1, device_id=d, device_id_type=MESH)

    @pl.when(z > 0)
    def _():
        pl.semaphore_signal(bar, inc=1, device_id=left, device_id_type=MESH)

    @pl.when(z < 3)
    def _():
        pl.semaphore_signal(bar, inc=1, device_id=right, device_id_type=MESH)
    far = dev(y, x, jnp.where(z < 2, z + 2, z - 2), c)
    pl.semaphore_signal(bar, inc=1, device_id=far, device_id_type=MESH)
    pl.semaphore_wait(bar, 4 + (z > 0).astype(jnp.int32) + (z < 3).astype(jnp.int32))

    def part_xy(px, py, pz):
        return (px * 2 + py) * 4 + pz

    def part_of(s, pa, pb, pz):
        return part_xy(pa, pb, pz) if STREAMS[s][0] == "x" else part_xy(pb, pa, pz)

    def ab(s):
        a = STREAMS[s][0]
        b = "y" if a == "x" else "x"
        return at_axis[a], at_axis[b], across[a], across[b]

    def core_copy(p):
        return copy_to(g_ref.at[p, pl.ds(pl.multiple_of((1 - c) * HALF, HALF), HALF)], other.at[p], core_s.at[p], core_r.at[p], partner)

    def load(p):
        return pltpu.make_async_copy(g_ref.at[p, pl.ds(pl.multiple_of(c * HALF, HALF), HALF)], mine.at[p], load_sem.at[p])

    waits = []
    seq = [(k, px, py) for k in range(4) for px, py in ((1 - x, 1 - y), (1 - x, y), (x, 1 - y), (x, y))]
    for k, px, py in seq:
        p = part_xy(px, py, order[k])
        core_copy(p).start()
        load(p).start()

    def a_copy(s, pb, pz):
        a, b, to_a, _ = ab(s)
        _, _, r0, n = STREAMS[s]
        return copy_to(mine.at[part_of(s, 1 - a, pb, pz), pl.ds(r0, n)], ra[s].at[pb * 4 + pz], as_.at[s, pb * 4 + pz], ar.at[s, pb * 4 + pz], to_a)

    def core_step(k):
        for i, (px, py) in enumerate(((1 - x, 1 - y), (1 - x, y), (x, 1 - y), (x, y))):
            p = part_xy(px, py, order[k])
            load(p).wait()
            core_copy(p).wait_recv()
            add_rows(mine.at[p], other.at[p], HALF, 16)
            for s in range(4):
                a_axis = STREAMS[s][0]
                if i == 0 or (i == 1 and a_axis == "x") or (i == 2 and a_axis == "y"):
                    pb = py if a_axis == "x" else px
                    cp = a_copy(s, pb, order[k])
                    cp.start()
                    waits.append(cp)

    def z_copy(s, pb, pz, to_right):
        a, b, _, _ = ab(s)
        _, _, r0, n = STREAMS[s]
        src = mine.at[part_of(s, a, pb, pz), pl.ds(r0, n)]
        slot = pz if to_right else jnp.where(pz == z - 1, 4, pz)
        i = pb * 5 + slot
        return copy_to(src, rz[s].at[i], zs.at[s, i], zr.at[s, i], right if to_right else left)

    def z_wait(s, pb, slot):
        _, _, r0, n = STREAMS[s]
        i = pb * 5 + slot
        copy_to(mine.at[0, pl.ds(r0, n)], rz[s].at[i], zs.at[s, i], zr.at[s, i], left).wait_recv()

    def z_step(s, pb, k):
        a, b, _, _ = ab(s)
        _, _, r0, n = STREAMS[s]
        pz = order[k]
        acc = mine.at[part_of(s, a, pb, pz), pl.ds(r0, n)]
        if k < 3:
            up = jnp.where(pz > z, (z > 0).astype(jnp.int32), (z < 3).astype(jnp.int32))

            @pl.when(up == 1)
            def _():
                z_wait(s, pb, pz)
                add_rows(acc, rz[s].at[pb * 5 + pz], n, 16)

            @pl.when(pz > z)
            def _():
                z_copy(s, pb, pz, True).start()

            @pl.when(pz < z)
            def _():
                z_copy(s, pb, pz, False).start()
        else:
            @pl.when(z > 0)
            def _():
                z_wait(s, pb, z)
                add_rows(acc, rz[s].at[pb * 5 + z], n, 16)

            @pl.when(z < 3)
            def _():
                z_wait(s, pb, 4)
                add_rows(acc, rz[s].at[pb * 5 + 4], n, 16)

    def z_drain(s, pb, k):
        pz = order[k]

        @pl.when(pz > z)
        def _():
            z_copy(s, pb, pz, True).wait_send()

        @pl.when(pz < z)
        def _():
            z_copy(s, pb, pz, False).wait_send()

    def a_step(s, pb, k):
        a, b, to_a, _ = ab(s)
        _, _, r0, n = STREAMS[s]
        pz = order[k]
        a_copy(s, pb, pz).wait_recv()
        add_rows(mine.at[part_of(s, a, pb, pz), pl.ds(r0, n)], ra[s].at[pb * 4 + pz], n, 16)

    def b_copy(s, pz):
        a, b, _, to_b = ab(s)
        _, second_z, r0, n = STREAMS[s]
        i = 0 if second_z else pz
        return copy_to(mine.at[part_of(s, a, 1 - b, pz), pl.ds(r0, n)], rb[s].at[i], bs.at[s, i], br.at[s, i], to_b)

    def b_step(s, pz):
        a, b, _, _ = ab(s)
        _, second_z, r0, n = STREAMS[s]
        i = 0 if second_z else pz
        b_copy(s, pz).wait_recv()
        add_rows(mine.at[part_of(s, a, b, pz), pl.ds(r0, n)], rb[s].at[i], n, 16)

    def stream_step(k):
        for s in range(4):
            _, b, _, _ = ab(s)
            if STREAMS[s][1]:
                a_step(s, 1 - b, k)
                z_step(s, 1 - b, k)
                a_step(s, b, k)
                z_step(s, b, k)
                if k == 3:
                    cp = b_copy(s, z)
                    cp.start()
                    waits.append(cp)
            else:
                a_step(s, 1 - b, k)
                cp = b_copy(s, order[k])
                cp.start()
                waits.append(cp)
                a_step(s, b, k)

    def stream_step2(k):
        for s in range(4):
            _, b, _, _ = ab(s)
            if not STREAMS[s][1]:
                b_step(s, order[k])
                z_step(s, b, k)
            elif k == 3:
                b_step(s, z)

    def vec_to(i):
        return (partner, across["x"], across["y"], dev(y, x, jnp.where(lax.rem(z, 2) == 0, z + 1, z - 1), c), far)[i]

    def vec_copy(i):
        return copy_to(vo_ref, vrecv.at[i], vs.at[i], vr.at[i], vec_to(i))

    def vec_start(i):
        vec_copy(i).start()

    def vec_end(i):
        vec_copy(i).wait()
        vo_ref[...] = vo_ref[...] + vrecv[i]

    vo_ref[...] = v_ref[...]
    vec_start(0)
    core_step(0)
    vec_end(0)
    vec_start(1)
    core_step(1)
    vec_end(1)
    vec_start(2)
    stream_step(0)
    vec_end(2)
    vec_start(3)
    core_step(2)
    stream_step2(0)
    vec_end(3)
    vec_start(4)
    stream_step(1)
    core_step(3)
    stream_step2(1)
    vec_end(4)
    stream_step(2)
    stream_step2(2)
    stream_step(3)

    half0 = c * HALF

    def out_at(s, p):
        _, _, r0, n = STREAMS[s]
        return o_ref.at[p, pl.ds(pl.multiple_of(half0 + r0, 16), n)]

    def mine_at(s, p):
        _, _, r0, n = STREAMS[s]
        return mine.at[p, pl.ds(r0, n)]

    def go(cp):
        cp.start()
        waits.append(cp)

    def to_core(s, p, src):
        return copy_to(src, out_at(s, p), oc.at[s, p], ocr.at[s, p], partner)

    def to_a(s, pb, pz, src):
        a, b, na, _ = ab(s)
        return copy_to(src, out_at(s, part_of(s, a, pb, pz)), oa.at[s, pb * 4 + pz], oar.at[s, pb * 4 + pz], na)

    def to_b(s, pz, src):
        a, b, _, nb = ab(s)
        return copy_to(src, out_at(s, part_of(s, a, b, pz)), ob.at[s, pz], obr.at[s, pz], nb)

    def to_z(s, pb, pz, src, to_right):
        a, b, _, _ = ab(s)
        i = pb * 8 + pz * 2 + (0 if to_right else 1)
        return copy_to(src, out_at(s, part_of(s, a, pb, pz)), oz.at[s, i], ozr.at[s, pb * 4 + pz], right if to_right else left)

    def spread_z(s, pb, pz, src, from_left=None):
        if from_left is None:
            @pl.when(z < 3)
            def _():
                to_z(s, pb, pz, src, True).start()

            @pl.when(z > 0)
            def _():
                to_z(s, pb, pz, src, False).start()
        elif from_left:
            @pl.when(z < 3)
            def _():
                to_z(s, pb, pz, src, True).start()
        else:
            @pl.when(z > 0)
            def _():
                to_z(s, pb, pz, src, False).start()

    for s in range(4):
        a, b, _, _ = ab(s)
        p = part_of(s, a, b, z)
        if STREAMS[s][1]:
            b_step(s, z)
            src = mine_at(s, p)
            go(to_b(s, z, src))
            spread_z(s, b, z, src)
            go(to_a(s, b, z, src))
        else:
            b_step(s, z)
            z_step(s, b, 3)
            src = mine_at(s, p)
            spread_z(s, b, z, src)
            go(to_b(s, z, src))
            go(to_a(s, b, z, src))
        go(to_core(s, p, src))
        pltpu.make_async_copy(src, out_at(s, p), own_sem.at[s]).start()

    def got_b(s, pz):
        a, b, _, _ = ab(s)
        p = part_of(s, a, 1 - b, pz)
        src = out_at(s, p)
        copy_to(src, src, ob.at[s, pz], obr.at[s, pz], partner).wait_recv()
        if STREAMS[s][1]:
            spread_z(s, 1 - b, pz, src)
        to_a(s, 1 - b, pz, src).start()
        to_core(s, p, src).start()

    def got_z(s, pb, pz, from_left):
        a, b, _, _ = ab(s)
        p = part_of(s, a, pb, pz)
        src = out_at(s, p)
        copy_to(src, src, oz.at[s, 0], ozr.at[s, pb * 4 + pz], partner).wait_recv()
        spread_z(s, pb, pz, src, from_left)
        to_a(s, pb, pz, src).start()
        to_core(s, p, src).start()
        if not STREAMS[s][1]:
            to_b(s, pz, src).start()

    def got_a(s, pb, pz):
        a, b, _, _ = ab(s)
        p = part_of(s, 1 - a, pb, pz)
        src = out_at(s, p)
        copy_to(src, src, oa.at[s, pb * 4 + pz], oar.at[s, pb * 4 + pz], partner).wait_recv()
        to_core(s, p, src).start()

    for s in range(4):
        got_b(s, z)
    for s in range(4):
        a, b, _, _ = ab(s)
        got_a(s, b, z)
        got_a(s, 1 - b, z)
    for t in range(1, 4):
        for lft in (True, False):
            pz = z - t if lft else z + t
            ok = (z >= t) if lft else (z + t <= 3)

            @pl.when(ok)
            def _():
                for s in range(4):
                    a, b, _, _ = ab(s)
                    got_z(s, b, pz, lft)
                    if STREAMS[s][1]:
                        got_z(s, 1 - b, pz, lft)
                for s in range(4):
                    if not STREAMS[s][1]:
                        got_b(s, pz)
                for s in range(4):
                    a, b, _, _ = ab(s)
                    got_a(s, b, pz)
                    got_a(s, 1 - b, pz)

    for cp in waits:
        cp.wait_send()
    for k, px, py in seq:
        core_copy(part_xy(px, py, order[k])).wait_send()
    for s in range(4):
        a, b, _, _ = ab(s)
        pltpu.make_async_copy(mine_at(s, part_of(s, a, b, z)), out_at(s, part_of(s, a, b, z)), own_sem.at[s]).wait()
        pbs = (b, 1 - b) if STREAMS[s][1] else (b,)
        for pb in pbs:
            for k in range(3):
                z_drain(s, pb, k)
        for pz in range(4):
            for pb in pbs:
                src = out_at(s, part_of(s, a, pb, pz))

                @pl.when((z >= pz) & (z < 3))
                def _():
                    to_z(s, pb, pz, src, True).wait_send()

                @pl.when((z <= pz) & (z > 0))
                def _():
                    to_z(s, pb, pz, src, False).wait_send()
            for pb in (0, 1):
                src = out_at(s, part_of(s, a, pb, pz))

                @pl.when(((pb == b) & (pz == z)) == False)
                def _():
                    to_a(s, pb, pz, src).wait_send()
            if not STREAMS[s][1]:
                @pl.when(z != pz)
                def _():
                    to_b(s, pz, out_at(s, 0)).wait_send()
        for p in range(16):
            src = out_at(s, p)

            @pl.when(p != part_of(s, a, b, z))
            def _():
                to_core(s, p, src).wait_send()
            _, _, r0, n = STREAMS[s]
            dst = o_ref.at[p, pl.ds(pl.multiple_of((1 - c) * HALF + r0, 16), n)]
            copy_to(dst, dst, oc.at[s, p], ocr.at[s, p], partner).wait_recv()


def all_sum(grads, vectors):
    dma = pltpu.SemaphoreType.DMA
    bf = jnp.bfloat16
    rows = [s[3] for s in STREAMS]
    return pl.pallas_call(
        reduce_kernel,
        name="all_sum",
        out_shape=(jax.ShapeDtypeStruct(grads.shape, bf), jax.ShapeDtypeStruct(vectors.shape, jnp.float32)),
        in_specs=[pl.BlockSpec(memory_space=pl.ANY), pl.BlockSpec(memory_space=pltpu.VMEM)],
        out_specs=(pl.BlockSpec(memory_space=pl.ANY), pl.BlockSpec(memory_space=pltpu.VMEM)),
        scratch_shapes=[
            pltpu.VMEM((PARTS, HALF, COLS), bf), pltpu.VMEM((PARTS, HALF, COLS), bf),
            *[pltpu.VMEM((8, n, COLS), bf) for n in rows],
            *[pltpu.VMEM((10, n, COLS), bf) for n in rows],
            *[pltpu.VMEM((1 if s[1] else 4, s[3], COLS), bf) for s in STREAMS],
            pltpu.VMEM((5, *vectors.shape), jnp.float32),
            dma((16,)), dma((16,)), dma((16,)),
            dma((4, 8)), dma((4, 8)), dma((4, 10)), dma((4, 10)), dma((4, 4)), dma((4, 4)),
            dma((4, 4)), dma((4, 4)), dma((4, 16)), dma((4, 8)), dma((4, 8)), dma((4, 8)), dma((4, 16)), dma((4, 16)),
            dma((5,)), dma((5,)), dma((4,)),
        ],
        compiler_params=pltpu.CompilerParams(collective_id=1, has_side_effects=True, vmem_limit_bytes=56 * 2**20),
    )(grads, vectors)


F32 = jnp.float32
BF = jnp.bfloat16
CHUNK = 512
WEIGHTS = ("wa", "wg", "wu", "wd")
QK = (H + KVH) * HD
QKO = QK + H * HD


def dot_nn(left, right):
    return lax.dot_general(left, right, (((1,), (0,)), ((), ())), preferred_element_type=F32)


def dot_nt(left, right):
    return lax.dot_general(left, right, (((1,), (1,)), ((), ())), preferred_element_type=F32)


def rope_lanes(tensor, cosine, sine, sign):
    rows, width = tensor.shape
    lane = lax.broadcasted_iota(jnp.int32, (rows, 2 * HD), 1)
    first = lax.rem(lane, HD) < HD // 2
    out = []
    for i in range(0, width, 2 * HD):
        piece = tensor[:, i : i + 2 * HD]
        other = jnp.where(first, pltpu.roll(piece, 2 * HD - HD // 2, 1), pltpu.roll(piece, HD // 2, 1))
        out.append(piece * cosine + (other * sine) * sign)
    return jnp.concatenate(out, axis=1)


def inverse_of(rows):
    return lax.rsqrt(jnp.mean(rows * rows, axis=1, keepdims=True) + epsilon)


def front_part(r, wait, state):
    gain = r["gains"][0:1, :]
    normed = (state * inverse_of(state) * gain).astype(BF)
    r["normed"][...] = normed
    wait("wa")
    values = dot_nn(normed, r["wa_v"][:, QKO:])
    turned = rope_lanes(dot_nn(normed, r["wa_v"][:, :QK]), r["cos"][...], r["sin"][...], 1.0).astype(BF)
    qw = H * HD
    r["q"][...] = turned[:, :qw]
    r["kv"][...] = jnp.concatenate([turned[:, qw:], values.astype(BF)], axis=1)


def head_rows(tensor, g):
    per = H // KVH
    return jnp.concatenate([tensor[:, (g * per + i) * HD : (g * per + i + 1) * HD] for i in range(per)], axis=0)


def window(r):
    rows = r["mask"].shape[0]
    start = lax.rem(lax.axis_index("tok"), 2) * r["q_in"].shape[0]
    return r["kvw"][pl.ds(pl.multiple_of(start, 128), rows), :]


def attention_part(r):
    per = H // KVH
    kv = window(r)
    q = r["q_in"][...]
    rows = q.shape[0]
    allowed = jnp.concatenate([r["mask"][...]] * per, axis=1) > 0
    mixed_t, logs = [], []
    for g in range(KVH):
        k_g = kv[:, g * HD : (g + 1) * HD]
        v_g = kv[:, (KVH + g) * HD : (KVH + g + 1) * HD]
        scores = jnp.where(allowed, dot_nt(k_g, head_rows(q, g)) * HD**-0.5, masked)
        largest = jnp.max(scores, axis=0, keepdims=True)
        exponent = jnp.exp(scores - largest)
        total = jnp.sum(exponent, axis=0, keepdims=True)
        probs = (exponent * (1.0 / total)).astype(BF)
        mix = dot_nn(v_g.T, probs)
        mixed_t += [mix[:, i * rows : (i + 1) * rows] for i in range(per)]
        logs.append(largest + jnp.log(total))
    r["lse"][...] = jnp.concatenate(logs + [logs[0]] * (r["lse"].shape[0] - KVH), axis=0)
    return jnp.concatenate(mixed_t, axis=0).T.astype(BF)


def rest_part(r, wait):
    state = r["state"][...]
    mixed = attention_part(r)
    r["mixed"][...] = mixed
    wait("wa")
    attn_out = dot_nn(mixed, r["wa_v"][:, QK:QKO])
    middle = state + attn_out
    r["middle"][...] = middle
    normed_two = (middle * inverse_of(middle) * r["gains"][1:2, :]).astype(BF)
    r["normed_two"][...] = normed_two
    wait("wg")
    wait("wu")
    wait("wd")
    ff = r["wg_v"].shape[1]
    mlp = jnp.zeros(state.shape, F32)
    for i in range(0, ff, CHUNK):
        at = slice(i, i + CHUNK)
        gate = dot_nn(normed_two, r["wg_v"][:, at])
        up = dot_nn(normed_two, r["wu_v"][:, at])
        r["gate"][:, at] = gate
        r["up"][:, at] = up
        hidden = (gate * jax.nn.sigmoid(gate) * up).astype(BF)
        r["hidden"][:, at] = hidden
        mlp = mlp + dot_nn(hidden, r["wd_v"][at, :])
    branch = attn_out + mlp.astype(BF).astype(F32)
    r["branch"][...] = branch
    router = jax.nn.sigmoid(jnp.sum(state * r["gains"][2:3, :], axis=1, keepdims=True))
    return state + (r["live"][:, 0:1] * router) * branch


def norm_back(grad, rows, gain):
    inverse = inverse_of(rows)
    scaled = rows * inverse
    weighted = grad * gain
    inner = jnp.mean(weighted * scaled, axis=1, keepdims=True)
    return inverse * (weighted - scaled * inner), jnp.sum(grad * scaled, axis=0, keepdims=True)


def back_part(r, wait, grad_after):
    state, live = r["b_state"][...], r["b_live"][:, 0:1]
    width = state.shape[1]
    router_vec = r["gains"][2:3, :]
    router = jax.nn.sigmoid(jnp.sum(state * router_vec, axis=1, keepdims=True))
    d_branch = (live * router) * grad_after
    d_logit = live * (router * (1.0 - router)) * jnp.sum(r["b_branch"][...] * grad_after, axis=1, keepdims=True)
    d_router = jnp.sum(d_logit * state, axis=0, keepdims=True)
    d_mlp = d_branch.astype(BF)
    r["d_mlp"][...] = d_mlp
    wait("wd")
    wait("wg")
    wait("wu")
    ff = r["wg_v"].shape[1]
    d_two = jnp.zeros(state.shape, F32)
    for i in range(0, ff, CHUNK):
        at = slice(i, i + CHUNK)
        gate, up = r["b_gate"][:, at], r["b_up"][:, at]
        sig = jax.nn.sigmoid(gate)
        d_hidden = dot_nt(d_mlp, r["wd_v"][at, :])
        d_up = (d_hidden * (gate * sig)).astype(BF)
        d_gate = (d_hidden * up * (sig * (1.0 + gate * (1.0 - sig)))).astype(BF)
        r["d_up"][:, at] = d_up
        r["d_gate"][:, at] = d_gate
        d_two = d_two + dot_nt(d_gate, r["wg_v"][:, at]) + dot_nt(d_up, r["wu_v"][:, at])
    d_two = d_two.astype(BF).astype(F32)
    d_middle, d_gain_two = norm_back(d_two, r["b_middle"][...], r["gains"][1:2, :])
    r["acc_out"][1:2, :width] = r["acc"][1:2, :width] + d_gain_two
    r["acc_out"][2:3, :width] = r["acc"][2:3, :width] + d_router
    d_attn = (d_branch + d_middle).astype(BF)
    r["d_attn"][...] = d_attn
    r["d_state"][...] = grad_after + d_logit * router_vec + d_middle
    wait("wa")
    d_mixed = dot_nt(d_attn, r["wa_v"][:, QK:QKO]).astype(BF)

    per = H // KVH
    kv = window(r)
    q = r["q_in"][...]
    rows = q.shape[0]
    allowed = jnp.concatenate([r["mask"][...]] * per, axis=1) > 0
    d_keys, d_values, dq_t = [], [], []
    for g in range(KVH):
        k_g = kv[:, g * HD : (g + 1) * HD]
        v_g = kv[:, (KVH + g) * HD : (KVH + g + 1) * HD]
        q_g, do_g = head_rows(q, g), head_rows(d_mixed, g)
        scores = jnp.where(allowed, dot_nt(k_g, q_g) * HD**-0.5, masked)
        probs = jnp.exp(scores - r["b_lse"][g : g + 1, :])
        d_values.append(dot_nn(probs.astype(BF), do_g))
        d_probs = dot_nt(v_g, do_g)
        d_scores = (probs * (d_probs - jnp.sum(probs * d_probs, axis=0, keepdims=True))).astype(BF)
        d_keys.append(dot_nn(d_scores, q_g) * HD**-0.5)
        dq = dot_nn(k_g.T, d_scores) * HD**-0.5
        dq_t += [dq[:, i * rows : (i + 1) * rows] for i in range(per)]
    d_queries = jnp.concatenate(dq_t + [jnp.zeros((HD, rows), F32)], axis=0).T
    d_queries = rope_lanes(d_queries, r["cos"][...], r["sin"][...], -1.0)
    r["d_q"][...] = d_queries[:, : H * HD].astype(BF)
    start = lax.rem(lax.axis_index("tok"), 2) * rows
    partial = r["dkv"]
    keep = partial.shape[0] - kv.shape[0]
    partial[pl.ds(pl.multiple_of((1 - lax.rem(lax.axis_index("tok"), 2)) * kv.shape[0], 128), keep), :] = jnp.zeros((keep, kv.shape[1]), BF)
    partial[pl.ds(pl.multiple_of(start, 128), kv.shape[0]), :] = jnp.concatenate(d_keys + d_values, axis=1).astype(BF)


def home_part(r, wait):
    half = KVH * HD
    total = r["home"][0].astype(F32)
    for i in range(1, r["home"].shape[0]):
        total = total + r["home"][i].astype(F32)
    rows = total.shape[0]
    padded = jnp.concatenate([total[:, :half], jnp.zeros((rows, half % (2 * HD)), F32)], axis=1)
    d_keys = rope_lanes(padded, r["cos"][...], r["sin"][...], -1.0)[:, :half].astype(BF)
    d_values = total[:, half:].astype(BF)
    r["d_k"][...] = d_keys
    r["d_v"][...] = d_values
    wait("wa")
    both = jnp.concatenate([r["h_dq"][...], d_keys], axis=1)
    d_normed = dot_nt(both, r["wa_v"][:, :QK]) + dot_nt(d_values, r["wa_v"][:, QKO:])
    state = r["h_state"][...]
    width = state.shape[1]
    d_in, d_gain = norm_back(d_normed, state, r["gains"][0:1, :])
    r["acc_out"][0:1, :width] = r["acc"][0:1, :width] + d_gain
    return r["h_d_state"][...] + d_in


def stage(name, parts, needed, inputs, outputs, weights, rename=None):
    in_names, out_names = list(inputs), list(outputs)
    w_names = [w for w in needed]

    def body(*refs):
        it = iter(refs)
        r = {n: next(it) for n in in_names}
        src = {n: next(it) for n in w_names}
        for n in out_names:
            r[n] = next(it)
        for n in w_names:
            r[n + "_v"] = next(it)
        sems = next(it)
        copies = {n: pltpu.make_async_copy(src[n], r[n + "_v"], sems.at[i]) for i, n in enumerate(w_names)}
        for n in w_names:
            copies[n].start()
        done = set()

        def wait(n):
            if n not in done:
                copies[n].wait()
                done.add(n)

        parts(r, wait)
        for n in w_names:
            wait(n)

    vm = pl.BlockSpec(memory_space=pltpu.VMEM)
    out = pl.pallas_call(
        body,
        name=name,
        out_shape=tuple(outputs.values()),
        in_specs=[vm] * len(in_names) + [pl.BlockSpec(memory_space=pl.ANY)] * len(w_names),
        out_specs=tuple([vm] * len(out_names)),
        scratch_shapes=[pltpu.VMEM(weights[n].shape, BF) for n in w_names] + [pltpu.SemaphoreType.DMA((len(w_names),))],
        compiler_params=pltpu.CompilerParams(vmem_limit_bytes=60 * 2**20),
    )(*inputs.values(), *[weights[n] for n in w_names])
    return dict(zip(out_names, out))


def shaped(shape, kind):
    return jax.ShapeDtypeStruct(shape, kind)


def front_outs(rows, width):
    return {"normed": shaped((rows, width), BF), "q": shaped((rows, H * HD), BF), "kv": shaped((rows, 2 * KVH * HD), BF)}


def forward_stage(state, q, kvw, mask, live, tables, gains, weights, last):
    rows, width = state.shape
    ff = weights["wg"].shape[1]
    outs = {
        "mixed": shaped((rows, H * HD), BF), "lse": shaped((8, (H // KVH) * rows), F32), "middle": shaped((rows, width), F32),
        "normed_two": shaped((rows, width), BF), "gate": shaped((rows, ff), F32), "up": shaped((rows, ff), F32),
        "hidden": shaped((rows, ff), BF), "branch": shaped((rows, width), F32),
    }
    if last:
        outs["output"] = shaped((width, rows), BF)
    else:
        outs |= front_outs(rows, width) | {"next": shaped((rows, width), F32)}

    def parts(r, wait):
        state_next = rest_part(r, wait)
        if last:
            r["output"][...] = state_next.T.astype(BF)
        else:
            r["next"][...] = state_next
            front_part(r, wait, state_next)

    needed = ("wa", "wg", "wu", "wd")
    ins = {"state": state, "q_in": q, "kvw": kvw, "mask": mask, "live": live, "cos": tables[0], "sin": tables[1], "gains": gains}
    return stage("forward", parts, needed, ins, outs, weights)


def first_stage(hidden_in, tables, gains, weights):
    width, rows = hidden_in.shape

    def parts(r, wait):
        state = r["hidden"][...].astype(F32).T
        r["state"][...] = state
        front_part(r, wait, state)

    outs = front_outs(rows, width) | {"state": shaped((rows, width), F32)}
    return stage("first", parts, ("wa",), {"hidden": hidden_in, "cos": tables[0], "sin": tables[1], "gains": gains}, outs, weights)


def backward_stage(kept, before, mask, live, tables, gains, acc, weights, cotangent):
    ins = {"cos": tables[0], "sin": tables[1], "gains": gains, "acc": acc}
    outs = {"acc_out": shaped(acc.shape, F32)}
    needed = ()
    rows, width = (kept or before)["state"].shape
    ff = weights["wg"].shape[1]
    kvr = 2 * KVH * HD
    if before is not None:
        ins |= {"home": before["home"], "h_dq": before["d_q"], "h_state": before["state"], "h_d_state": before["d_state"]}
        outs |= {"d_k": shaped((rows, kvr // 2), BF), "d_v": shaped((rows, kvr // 2), BF)}
        needed += ("wa",)
    else:
        ins |= {"cot": cotangent}
    if kept is not None:
        ins |= {"b_state": kept["state"], "b_live": live, "b_branch": kept["branch"], "b_gate": kept["gate"], "b_up": kept["up"],
                "b_middle": kept["middle"], "b_lse": kept["lse"], "kvw": kept["kvw"], "q_in": kept["q"], "mask": mask}
        outs |= {"d_mlp": shaped((rows, width), BF), "d_up": shaped((rows, ff), BF), "d_gate": shaped((rows, ff), BF),
                 "d_attn": shaped((rows, width), BF), "d_state": shaped((rows, width), F32), "d_q": shaped((rows, H * HD), BF),
                 "dkv": shaped(kept["kvw"].shape, BF)}
        needed += ("wd", "wg", "wu") + (("wa",) if before is None else ())
    else:
        outs |= {"grad": shaped((width, rows), F32)}

    def parts(r, wait):
        r["acc_out"][...] = r["acc"][...]
        grad = home_part(r, wait) if before is not None else r["cot"][...].astype(F32).T
        if kept is not None:
            back_part(r, wait, grad)
        else:
            r["grad"][...] = grad.T

    return stage("backward", parts, needed, ins, outs, weights)


QUARTERS = 4


def gather_kernel(*refs):
    ins, outs = refs[:5], refs[5:10]
    zs, xs, ys, cs, got, cgot, own_s, own_c, own_r, ss, sr, sc, scr = refs[10:]
    y, x, z, c = place()
    partner, to_x, to_y = dev(y, x, z, 1 - c), dev(y, 1 - x, z, c), dev(1 - y, x, z, c)
    left, right = dev(y, x, z - 1, c), dev(y, x, z + 1, c)
    quarter = (x * 2 + y, (1 - x) * 2 + y, x * 2 + (1 - y), (1 - x) * 2 + (1 - y))
    lasting = []

    def go(cp, when=None):
        if when is None:
            cp.start()
        else:
            @pl.when(when)
            def _():
                cp.start()
        lasting.append((cp, when))

    def cut(ref, m, q):
        if m < 3:
            n = ref.shape[1] // QUARTERS
            return ref.at[:, pl.ds(pl.multiple_of(q * n, 128), n)]
        n = ref.shape[0] // QUARTERS
        return ref.at[pl.ds(pl.multiple_of(q * n, 16), n), :]

    def out_piece(m, kind, zz, core):
        return cut(outs[m].at[zz * 2 + core], m, quarter[kind])

    bar = pltpu.get_barrier_semaphore()
    for d in (partner, to_x, to_y):
        pl.semaphore_signal(bar, inc=1, device_id=d, device_id_type=MESH)

    @pl.when(z > 0)
    def _():
        pl.semaphore_signal(bar, inc=1, device_id=left, device_id_type=MESH)

    @pl.when(z < 3)
    def _():
        pl.semaphore_signal(bar, inc=1, device_id=right, device_id_type=MESH)

    pl.semaphore_wait(bar, 3 + (z > 0).astype(jnp.int32) + (z < 3).astype(jnp.int32))

    def small_copy(zz, core, src, device, sems):
        return copy_to(src, outs[4].at[zz * 2 + core], sems[0], sems[1], device)

    go(small_copy(z, c, ins[4], right, (ss.at[z, 0], sr.at[z])), z < 3)
    go(small_copy(z, c, ins[4], left, (ss.at[z, 1], sr.at[z])), z > 0)
    go(small_copy(z, c, ins[4], partner, (sc.at[z], scr.at[z])))
    for m in range(4):
        src, dst = cut(ins[m], m, quarter[0]), out_piece(m, 0, z, c)
        go(copy_to(src, dst, zs.at[m, z, 0], got.at[0, m, z], right), z < 3)
        go(copy_to(src, dst, zs.at[m, z, 1], got.at[0, m, z], left), z > 0)
    for m in range(4):
        go(copy_to(ins[m], outs[m].at[z * 2 + c], own_c.at[m], own_r.at[m], partner))
    local = [pltpu.make_async_copy(ins[m], outs[m].at[z * 2 + c], own_s.at[m]) for m in range(5)]
    for cp in local:
        cp.start()

    steps = [(t, side) for t in (1, 2, 3) for side in (0, 1)]

    def source(t, side):
        return (z - t, z >= t) if side == 0 else (z + t, z + t <= 3)

    def wait_for(kind, m, zz):
        piece = out_piece(m, kind, zz, c)
        copy_to(piece, piece, cs.at[kind, m, zz], got.at[kind, m, zz], partner).wait_recv()
        return piece

    def each(kind, m, t, side):
        zz, there = source(t, side)
        onward = (z < 3) if side == 0 else (z > 0)

        @pl.when(there)
        def _():
            piece = wait_for(kind, m, zz)
            first_x = m % 2 == 0
            sends = []
            if kind == 0:
                on = copy_to(piece, piece, zs.at[m, zz, side], got.at[0, m, zz], right if side == 0 else left)

                @pl.when(onward)
                def _():
                    on.start()

                sends.append(copy_to(piece, piece, xs.at[0, m, zz], got.at[1, m, zz], to_x))
                sends.append(copy_to(piece, piece, ys.at[0, m, zz], got.at[2, m, zz], to_y))
            elif kind == 1 and first_x:
                sends.append(copy_to(piece, piece, ys.at[1, m, zz], got.at[3, m, zz], to_y))
            elif kind == 2 and not first_x:
                sends.append(copy_to(piece, piece, xs.at[1, m, zz], got.at[3, m, zz], to_x))
            sends.append(copy_to(piece, piece, cs.at[kind, m, zz], cgot.at[kind, m, zz], partner))
            for cp in sends:
                cp.start()

        lasting.append((("s", kind, m, t, side), there))
        if kind == 0:
            lasting.append((("z", m, t, side), there & onward))

    def small_step(t, side):
        zz, there = source(t, side)

        @pl.when(there)
        def _():
            piece = outs[4].at[zz * 2 + c]
            copy_to(piece, piece, sc.at[zz], sr.at[zz], partner).wait_recv()

            @pl.when((z < 3) if side == 0 else (z > 0))
            def _():
                small_copy(zz, c, piece, right if side == 0 else left, (ss.at[zz, side], sr.at[zz])).start()

            small_copy(zz, c, piece, partner, (sc.at[zz], scr.at[zz])).start()

        lasting.append((("m", t, side), there))

    for t, side in steps:
        small_step(t, side)
    for turn in range(4 + 2):
        for t, side in steps:
            if turn < 4:
                each(0, turn, t, side)
            if 1 <= turn < 5:
                m = turn - 1
                relay, leaf = (1, 2) if m % 2 == 0 else (2, 1)
                each(relay, m, t, side)
                each(leaf, m, t, side)
            if turn >= 2:
                each(3, turn - 2, t, side)

    for cp, when in lasting:
        if not isinstance(cp, tuple):
            if when is None:
                cp.wait_send()
            else:
                @pl.when(when)
                def _():
                    cp.wait_send()
        elif cp[0] == "z":
            _, m, t, side = cp
            zz, _ = source(t, side)
            piece = out_piece(m, 0, zz, c)

            @pl.when(when)
            def _():
                copy_to(piece, piece, zs.at[m, zz, side], got.at[0, m, zz], partner).wait_send()
        elif cp[0] == "m":
            _, t, side = cp
            zz, _ = source(t, side)
            piece = outs[4].at[zz * 2 + c]

            @pl.when(when)
            def _():
                @pl.when((z < 3) if side == 0 else (z > 0))
                def _():
                    small_copy(zz, c, piece, partner, (ss.at[zz, side], sr.at[zz])).wait_send()

                small_copy(zz, c, piece, partner, (sc.at[zz], scr.at[zz])).wait_send()
                other = outs[4].at[zz * 2 + 1 - c]
                copy_to(other, other, sc.at[zz], scr.at[zz], partner).wait_recv()
        else:
            _, kind, m, t, side = cp
            zz, _ = source(t, side)
            piece = out_piece(m, kind, zz, c)
            other = out_piece(m, kind, zz, 1 - c)
            first_x = m % 2 == 0

            @pl.when(when)
            def _():
                if kind == 0 or (kind == 2 and not first_x):
                    copy_to(piece, piece, xs.at[min(kind, 1), m, zz], got.at[1, m, zz], partner).wait_send()
                if kind == 0 or (kind == 1 and first_x):
                    copy_to(piece, piece, ys.at[min(kind, 1), m, zz], got.at[1, m, zz], partner).wait_send()
                copy_to(piece, piece, cs.at[kind, m, zz], cgot.at[kind, m, zz], partner).wait_send()
                copy_to(other, other, cs.at[kind, m, zz], cgot.at[kind, m, zz], partner).wait_recv()

    for m in range(4):
        other = outs[m].at[z * 2 + 1 - c]
        copy_to(other, other, own_c.at[m], own_r.at[m], partner).wait_recv()
    other = outs[4].at[z * 2 + 1 - c]
    copy_to(other, other, sc.at[z], scr.at[z], partner).wait_recv()
    for cp in local:
        cp.wait()


def gather_rows(shards):
    dma = pltpu.SemaphoreType.DMA
    return pl.pallas_call(
        gather_kernel,
        name="gather_rows",
        out_shape=tuple(jax.ShapeDtypeStruct((8, *s.shape), s.dtype) for s in shards),
        in_specs=[pl.BlockSpec(memory_space=pl.ANY)] * 5,
        out_specs=tuple([pl.BlockSpec(memory_space=pl.ANY)] * 5),
        scratch_shapes=[
            dma((4, 4, 2)), dma((2, 4, 4)), dma((2, 4, 4)), dma((4, 4, 4)), dma((4, 4, 4)), dma((4, 4, 4)),
            dma((5,)), dma((4,)), dma((4,)), dma((4, 2)), dma((4,)), dma((4,)), dma((4,)),
        ],
        compiler_params=pltpu.CompilerParams(collective_id=4, has_side_effects=True),
    )(*shards)


def keys_kernel(chips, back, kv_ref, w_ref, s_right, r_left, s_core, r_core):
    g, t = lax.axis_index("grp"), lax.axis_index("tok")
    z, c = t // 2, lax.rem(t, 2)
    rows = kv_ref.shape[0]
    partner, right = (g, z * 2 + 1 - c), (g, t + 2)

    def slot(d, core):
        return w_ref.at[pl.ds(pl.multiple_of(((back - d) * 2 + core) * rows, 128), rows)]

    bar = pltpu.get_barrier_semaphore()
    pl.semaphore_signal(bar, inc=1, device_id=partner, device_id_type=MESH)

    @pl.when(z > 0)
    def _():
        pl.semaphore_signal(bar, inc=1, device_id=(g, t - 2), device_id_type=MESH)

    def along(d, src):
        return copy_to(src, slot(d, c), s_right.at[d - 1], r_left.at[d - 1], right)

    def beside(d, src):
        return copy_to(src, slot(d, c), s_core.at[d], r_core.at[d], partner)

    own = w_ref.at[pl.ds(pl.multiple_of((back * 2 + c) * rows, 128), rows)]
    own[...] = kv_ref[...]
    for d in range(1, back + 1):
        @pl.when(z < d)
        def _():
            for core in (0, 1):
                slot(d, core)[...] = jnp.zeros(kv_ref.shape, kv_ref.dtype)

    pl.semaphore_wait(bar, 1 + (z < chips - 1).astype(jnp.int32))

    @pl.when(z < chips - 1)
    def _():
        along(1, kv_ref).start()

    beside(0, kv_ref).start()
    for d in range(1, back + 1):
        @pl.when(z >= d)
        def _():
            along(d, slot(d, c)).wait_recv()
            if d < back:
                @pl.when(z < chips - 1)
                def _():
                    along(d + 1, slot(d, c)).start()
            beside(d, slot(d, c)).start()

    def mine_to(d):
        return copy_to(slot(d, 1 - c), slot(d, 1 - c), s_core.at[d], r_core.at[d], partner)

    mine_to(0).wait_recv()
    beside(0, kv_ref).wait_send()

    @pl.when(z < chips - 1)
    def _():
        along(1, kv_ref).wait_send()

    for d in range(1, back + 1):
        @pl.when(z >= d)
        def _():
            mine_to(d).wait_recv()
            beside(d, slot(d, c)).wait_send()
            if d < back:
                @pl.when(z < chips - 1)
                def _():
                    along(d + 1, slot(d, c)).wait_send()


def exchange_keys(kv, n_tok, nback):
    back = nback // 2
    rows = kv.shape[0]
    dma = pltpu.SemaphoreType.DMA
    return pl.pallas_call(
        lambda *refs: keys_kernel(n_tok // 2, back, *refs),
        name="exchange_keys",
        out_shape=jax.ShapeDtypeStruct(((2 * back + 2) * rows, kv.shape[1]), kv.dtype),
        in_specs=[pl.BlockSpec(memory_space=pltpu.VMEM)],
        out_specs=pl.BlockSpec(memory_space=pltpu.VMEM),
        scratch_shapes=[dma((back,)), dma((back,)), dma((back + 1,)), dma((back + 1,))],
        compiler_params=pltpu.CompilerParams(collective_id=2, has_side_effects=True, vmem_limit_bytes=32 * 2**20),
    )(kv)


def home_kernel(chips, back, p_ref, h_ref, beside_in, sums, after_in, s_left, r_right, s_core, r_core):
    g, t = lax.axis_index("grp"), lax.axis_index("tok")
    z, c = t // 2, lax.rem(t, 2)
    rows = h_ref.shape[1]
    partner, left = (g, z * 2 + 1 - c), (g, t - 2)

    def block(d, core):
        return p_ref.at[pl.ds(pl.multiple_of(((back - d) * 2 + core) * rows, 128), rows)]

    bar = pltpu.get_barrier_semaphore()
    pl.semaphore_signal(bar, inc=1, device_id=partner, device_id_type=MESH)

    @pl.when(z < chips - 1)
    def _():
        pl.semaphore_signal(bar, inc=1, device_id=(g, t + 2), device_id_type=MESH)

    pl.semaphore_wait(bar, 1 + (z > 0).astype(jnp.int32))

    def beside(d):
        return copy_to(block(d, 1 - c), beside_in.at[d], s_core.at[d], r_core.at[d], partner)

    def along(d):
        return copy_to(sums.at[d - 1], after_in.at[d - 1], s_left.at[d - 1], r_right.at[d - 1], left)

    for d in range(back, 0, -1):
        @pl.when(z >= d)
        def _():
            beside(d).start()
    beside(0).start()
    for d in range(back, 0, -1):
        @pl.when(z >= d)
        def _():
            beside(d).wait_recv()
            sums[d - 1] = (block(d, c)[...].astype(F32) + beside_in[d].astype(F32)).astype(BF)
            if d < back:
                @pl.when(z < chips - 1)
                def _():
                    along(d + 1).wait_recv()
                    sums[d - 1] = (sums[d - 1].astype(F32) + after_in[d].astype(F32)).astype(BF)
            along(d).start()
    beside(0).wait_recv()
    h_ref[0] = block(0, c)[...].astype(F32) + beside_in[0].astype(F32)

    @pl.when(z < chips - 1)
    def _():
        along(1).wait_recv()
        h_ref[0] = h_ref[0] + after_in[0].astype(F32)

    beside(0).wait_send()
    for d in range(1, back + 1):
        @pl.when(z >= d)
        def _():
            beside(d).wait_send()
            along(d).wait_send()


def exchange_home(partial, n_tok, nback):
    back = nback // 2
    rows = partial.shape[0] // (2 * back + 2)
    width = partial.shape[1]
    dma = pltpu.SemaphoreType.DMA
    return pl.pallas_call(
        lambda *refs: home_kernel(n_tok // 2, back, *refs),
        name="exchange_home",
        out_shape=jax.ShapeDtypeStruct((1, rows, width), F32),
        in_specs=[pl.BlockSpec(memory_space=pltpu.VMEM)],
        out_specs=pl.BlockSpec(memory_space=pltpu.VMEM),
        scratch_shapes=[
            pltpu.VMEM((back + 1, rows, width), BF), pltpu.VMEM((back, rows, width), BF), pltpu.VMEM((back, rows, width), BF),
            dma((back,)), dma((back,)), dma((back + 1,)), dma((back + 1,)),
        ],
        compiler_params=pltpu.CompilerParams(collective_id=3, has_side_effects=True, vmem_limit_bytes=32 * 2**20),
    )(partial)


ROW_NAMES = ("normed_two", "d_mlp", "normed", "mixed", "d_gate", "d_up", "hidden", "d_q", "d_k", "d_v", "d_attn")


def grads_kernel(count, *refs):
    n = len(ROW_NAMES)
    r = {name: refs[i * count : (i + 1) * count] for i, name in enumerate(ROW_NAMES)}
    g_ref, left_t, slots, sems = refs[n * count :]
    for i, name in enumerate(ROW_NAMES[:4]):
        left_t[i] = jnp.concatenate([each[...].astype(F32).T.astype(BF) for each in r[name]], axis=1)

    def rows_of(name, low, high):
        return jnp.concatenate([each[:, low:high] for each in r[name]], axis=0)

    def out_copy(p):
        return pltpu.make_async_copy(slots.at[p % 2], g_ref.at[p], sems.at[p % 2])

    width = left_t.shape[1]
    for p in range(PARTS):
        if p >= 2:
            out_copy(p - 2).wait()
        slot = slots.at[p % 2]
        if p < 12:
            name, left = (("d_gate", 0), ("d_up", 0), ("hidden", 1))[p // 4]
            low = (p % 4) * COLS
            slot[...] = dot_nn(left_t[left], rows_of(name, low, low + COLS)).astype(BF)
        elif p == 12:
            slot[...] = dot_nn(left_t[2], rows_of("d_q", 0, COLS)).astype(BF)
        elif p == 13:
            right = jnp.concatenate([rows_of("d_q", COLS, width), rows_of("d_k", 0, 2 * COLS - width)], axis=1)
            slot[...] = dot_nn(left_t[2], right).astype(BF)
        elif p == 14:
            slot[...] = dot_nn(left_t[3], rows_of("d_attn", 0, COLS)).astype(BF)
        else:
            one = dot_nn(left_t[3], rows_of("d_attn", COLS, width))
            two = dot_nn(left_t[2], rows_of("d_v", 0, 2 * COLS - width))
            slot[...] = jnp.concatenate([one, two], axis=1).astype(BF)
        out_copy(p).start()
    out_copy(PARTS - 2).wait()
    out_copy(PARTS - 1).wait()


def weight_gradients(rows):
    count = len(rows["d_q"])
    flat = [each for name in ROW_NAMES for each in rows[name]]
    tokens, width = rows["normed"][0].shape
    return pl.pallas_call(
        lambda *refs: grads_kernel(count, *refs),
        name="weight_gradients",
        out_shape=jax.ShapeDtypeStruct((PARTS, width, COLS), BF),
        in_specs=[pl.BlockSpec(memory_space=pltpu.VMEM)] * len(flat),
        out_specs=pl.BlockSpec(memory_space=pl.ANY),
        scratch_shapes=[pltpu.VMEM((4, width, count * tokens), BF), pltpu.VMEM((2, width, COLS), BF), pltpu.SemaphoreType.DMA((2,))],
        compiler_params=pltpu.CompilerParams(vmem_limit_bytes=60 * 2**20),
    )(*flat)


def spread_kernel(p_ref, gate, up, down, d_q, d_k, d_v, d_o, came, wide, q_full, k_full, o_full, v_full, sem_in, sem_out, sem_full):
    width = q_full.shape[0]
    order = [12, 13, 14, 15] + list(range(12))

    def fetch(i):
        return pltpu.make_async_copy(p_ref.at[order[i]], came.at[i % 3], sem_in.at[i % 3])

    def put(i):
        p = order[i]
        return pltpu.make_async_copy(wide.at[i % 2], (gate, up, down)[p // 4].at[:, pl.ds((p % 4) * COLS, COLS)], sem_out.at[i % 2])

    fulls = [(q_full, d_q), (k_full, d_k), (o_full, d_o), (v_full, d_v)]

    def put_full(j):
        return pltpu.make_async_copy(fulls[j][0], fulls[j][1], sem_full.at[j])

    fetch(0).start()
    fetch(1).start()
    for i, p in enumerate(order):
        if i + 2 < len(order):
            fetch(i + 2).start()
        fetch(i).wait()
        part = came.at[i % 3]
        if i >= 6:
            put(i - 2).wait()
        if p >= 12:
            full, other = (q_full, k_full) if p < 14 else (o_full, v_full)
            if p % 2 == 0:
                full[:, :COLS] = part[...].astype(F32)
            else:
                got = part[...].astype(F32)
                full[:, COLS:] = got[:, : width - COLS]
                other[...] = got[:, width - COLS :].T
                put_full(0 if p < 14 else 2).start()
                put_full(1 if p < 14 else 3).start()
        else:
            wide[i % 2] = part[...].astype(F32)
            put(i).start()
    put(len(order) - 2).wait()
    put(len(order) - 1).wait()
    for j in range(4):
        put_full(j).wait()


def spread_out(parts):
    n, width, cols = parts.shape
    kv = 2 * cols - width
    ff = 4 * cols
    shapes = [(width, ff), (width, ff), (width, ff), (width, width), (kv, width), (kv, width), (width, width)]
    vm = pltpu.VMEM
    return pl.pallas_call(
        spread_kernel,
        name="spread_out",
        out_shape=tuple(jax.ShapeDtypeStruct(s, F32) for s in shapes),
        in_specs=[pl.BlockSpec(memory_space=pl.ANY)],
        out_specs=tuple([pl.BlockSpec(memory_space=pl.ANY)] * 7),
        scratch_shapes=[
            vm((3, width, cols), BF), vm((2, width, cols), F32),
            vm((width, width), F32), vm((kv, width), F32), vm((width, width), F32), vm((kv, width), F32),
            pltpu.SemaphoreType.DMA((3,)), pltpu.SemaphoreType.DMA((2,)), pltpu.SemaphoreType.DMA((4,)),
        ],
        compiler_params=pltpu.CompilerParams(vmem_limit_bytes=60 * 2**20),
    )(parts)


def on_device(
    hidden_in,
    cotangent,
    lengths,
    active,
    norm_attn,
    w_query,
    w_key,
    w_value,
    w_out,
    norm_mlp,
    w_gate,
    w_up,
    w_down,
    w_router,
):
    n_tok = lax.axis_size("tok")
    n_grp = lax.axis_size("grp")
    me_index = lax.axis_index("tok")
    rows, width = hidden_in.shape
    nback = min(SPAN, n_tok // 2)

    share = norm_attn.shape[0]
    vectors = jnp.pad(jnp.stack([norm_attn, norm_mlp, w_router]), ((0, 0), (0, 128 - share)))
    small = jnp.concatenate([vectors, active.astype(BF), jnp.zeros((10, 128), BF)], axis=0)
    shards = (jnp.concatenate([w_query, w_key, w_out, w_value], axis=1), w_gate, w_up, w_down, small)
    whole = gather_rows(shards) if (n_grp, n_tok) == (4, 8) else [lax.all_gather(each, "tok", axis=0) for each in shards]
    weights = {name: each.reshape(-1, each.shape[-1]) for name, each in zip(WEIGHTS, whole)}
    gains = jnp.transpose(whole[4][:, :3, :share], (1, 0, 2)).reshape(3, width).astype(F32)
    gains = jnp.pad(gains, ((0, 5), (0, 0)))

    lengths_row = lengths[0]
    token = jnp.arange(rows, dtype=jnp.int32)
    global_rows = me_index * rows + token
    segment_rows = segment_of(lengths_row, global_rows)
    cosine, sine = rotary_tables(position_of(lengths_row, global_rows, segment_rows))
    tables = (jnp.concatenate([cosine] * 4, axis=1), jnp.concatenate([-sine, sine] * 2, axis=1))
    reach = (nback + 1) * rows
    global_keys = (me_index - nback) * rows + jnp.arange(reach, dtype=jnp.int32)
    live_all = jnp.transpose(whole[4][:, 3:6], (1, 0, 2)).reshape(3, -1)
    live_all = jnp.pad(live_all, ((0, 0), (nback * rows, 0)))
    live_keys = lax.dynamic_slice_in_dim(live_all, me_index * rows, reach, 1)
    reachable = (segment_rows[None, :] == segment_of(lengths_row, global_keys)[:, None]) & (
        global_keys[:, None] <= global_rows[None, :]
    )
    masks = jnp.where(reachable[None] & (live_keys[:, :, None] > 0), 1.0, 0.0).astype(F32)
    lives = [active[i].astype(F32)[:, None] for i in range(RECUR)]

    kept = []
    made = first_stage(hidden_in.T, tables, gains, weights)
    state = made["state"]
    for step in range(RECUR):
        kvw = exchange_keys(made["kv"], n_tok, nback)
        last = step == RECUR - 1
        done = forward_stage(state, made["q"], kvw, masks[step], lives[step], tables, gains, weights, last)
        kept.append({**done, "state": state, "q": made["q"], "kvw": kvw, "normed_r": made["normed"]})
        made, state = done, done.get("next")

    acc = jnp.zeros((8, 1024), F32)
    before = None
    rows_of = {name: [] for name in ROW_NAMES}
    for step in reversed(range(RECUR)):
        back = backward_stage(kept[step], before, masks[step], lives[step], tables, gains, acc, weights, cotangent.T)
        acc = back["acc_out"]
        for name in ("d_k", "d_v"):
            if before is not None:
                rows_of[name].append(back[name])
        for name in ("d_mlp", "d_gate", "d_up", "d_q", "d_attn"):
            rows_of[name].append(back[name])
        for name in ("normed_two", "mixed", "hidden"):
            rows_of[name].append(kept[step][name])
        rows_of["normed"].append(kept[step]["normed_r"])
        before = {"home": exchange_home(back["dkv"], n_tok, nback), "d_q": back["d_q"], "state": kept[step]["state"], "d_state": back["d_state"]}
    back = backward_stage(None, before, None, None, tables, gains, acc, weights, None)
    for name in ("d_k", "d_v"):
        rows_of[name].append(back[name])
    acc = back["acc_out"]
    parts = weight_gradients(rows_of)
    if (n_grp, n_tok) == (4, 8):
        parts, acc = all_sum(parts, acc)
    else:
        parts = lax.psum(parts.astype(F32), ("grp", "tok")).astype(BF)
        acc = lax.psum(acc, ("grp", "tok"))
    d_gate, d_up, d_down, d_q, d_k, d_v, d_o = spread_out(parts)
    return (
        kept[-1]["output"].T,
        back["grad"].T,
        acc[0, :width],
        d_q,
        d_k.T,
        d_v.T,
        d_o,
        acc[1, :width],
        d_gate,
        d_up,
        d_down.T,
        acc[2, :width],
    )


def solution(mesh):
    placed = (
        P(("grp", "tok"), None),
        P(("grp", "tok"), None),
        P("grp", None),
        P(None, ("grp", "tok")),
        P("tok"),
        P("tok", None),
        P("tok", None),
        P("tok", None),
        P("tok", None),
        P("tok"),
        P("tok", None),
        P("tok", None),
        P("tok", None),
        P("tok"),
    )
    return jax.shard_map(
        on_device,
        mesh=mesh,
        in_specs=placed,
        out_specs=(
            P(("grp", "tok"), None),
            P(("grp", "tok"), None),
            P(),
            P(),
            P(),
            P(),
            P(),
            P(),
            P(),
            P(),
            P(),
            P(),
        ),
        check_vma=False,
    )
```

```python
import jax
import jax.numpy as jnp
from jax import lax
from jax.experimental import pallas as pl
from jax.experimental.pallas import tpu as pltpu
from jax.sharding import PartitionSpec as P

MESH = pl.DeviceIdType.MESH

H = 15
KVH = 5
HD = 64
RECUR = 3
SPAN = 16

epsilon = 1e-05
theta = 10000.0
masked = -1000000000.0

def ends_of(lengths_row):
    count = lengths_row.shape[0]
    until = jnp.arange(count)[:, None] >= jnp.arange(count)[None, :]
    return jnp.sum(jnp.where(until, lengths_row[None, :], 0), axis=1)


def segment_of(lengths_row, global_rows):
    ends_at = ends_of(lengths_row)
    return jnp.sum((global_rows[:, None] >= ends_at[None, :]).astype(jnp.int32), axis=1)


def position_of(lengths_row, global_rows, segments):
    ends_at = ends_of(lengths_row)
    starts_at = ends_at - lengths_row
    picked = segments[:, None] == jnp.arange(lengths_row.shape[0], dtype=jnp.int32)[None, :]
    return global_rows - jnp.sum(jnp.where(picked, starts_at[None, :], 0), axis=1)


def rotary_tables(positions):
    half_dim = HD // 2
    inverse = jnp.power(theta, -jnp.arange(half_dim, dtype=jnp.float32) * (2.0 / HD))
    angle = positions.astype(jnp.float32)[..., None] * inverse
    return (jnp.cos(angle), jnp.sin(angle))


F32 = jnp.float32
BF = jnp.bfloat16
CHUNK = 512
WEIGHTS = ("wa", "wg", "wu", "wd")
QK = (H + KVH) * HD
QKO = QK + H * HD


def dot_nn(left, right):
    return lax.dot_general(left, right, (((1,), (0,)), ((), ())), preferred_element_type=F32)


def dot_nt(left, right):
    return lax.dot_general(left, right, (((1,), (1,)), ((), ())), preferred_element_type=F32)


def rope_lanes(tensor, cosine, sine, sign):
    rows, width = tensor.shape
    lane = lax.broadcasted_iota(jnp.int32, (rows, 2 * HD), 1)
    first = lax.rem(lane, HD) < HD // 2
    out = []
    for i in range(0, width, 2 * HD):
        piece = tensor[:, i : i + 2 * HD]
        other = jnp.where(first, pltpu.roll(piece, 2 * HD - HD // 2, 1), pltpu.roll(piece, HD // 2, 1))
        out.append(piece * cosine + (other * sine) * sign)
    return jnp.concatenate(out, axis=1)


def inverse_of(rows):
    return lax.rsqrt(jnp.mean(rows * rows, axis=1, keepdims=True) + epsilon)


def front_part(r, wait, state):
    gain = r["gains"][0:1, :]
    normed = (state * inverse_of(state) * gain).astype(BF)
    r["normed"][...] = normed
    wait("wa")
    values = dot_nn(normed, r["wa_v"][:, QKO:])
    turned = rope_lanes(dot_nn(normed, r["wa_v"][:, :QK]), r["cos"][...], r["sin"][...], 1.0).astype(BF)
    qw = H * HD
    r["q"][...] = turned[:, :qw]
    r["kv"][...] = jnp.concatenate([turned[:, qw:], values.astype(BF)], axis=1)


def head_rows(tensor, g):
    per = H // KVH
    return jnp.concatenate([tensor[:, (g * per + i) * HD : (g * per + i + 1) * HD] for i in range(per)], axis=0)


def window(r):
    rows = r["mask"].shape[0]
    start = lax.rem(lax.axis_index("tok"), 2) * r["q_in"].shape[0]
    return r["kvw"][pl.ds(pl.multiple_of(start, 128), rows), :]


def attention_part(r):
    per = H // KVH
    kv = window(r)
    q = r["q_in"][...]
    rows = q.shape[0]
    allowed = jnp.concatenate([r["mask"][...]] * per, axis=1) > 0
    mixed_t, logs = [], []
    for g in range(KVH):
        k_g = kv[:, g * HD : (g + 1) * HD]
        v_g = kv[:, (KVH + g) * HD : (KVH + g + 1) * HD]
        scores = jnp.where(allowed, dot_nt(k_g, head_rows(q, g)) * HD**-0.5, masked)
        largest = jnp.max(scores, axis=0, keepdims=True)
        exponent = jnp.exp(scores - largest)
        total = jnp.sum(exponent, axis=0, keepdims=True)
        probs = (exponent * (1.0 / total)).astype(BF)
        mix = dot_nn(v_g.T, probs)
        mixed_t += [mix[:, i * rows : (i + 1) * rows] for i in range(per)]
        logs.append(largest + jnp.log(total))
    r["lse"][...] = jnp.concatenate(logs + [logs[0]] * (r["lse"].shape[0] - KVH), axis=0)
    return jnp.concatenate(mixed_t, axis=0).T.astype(BF)


def rest_part(r, wait):
    state = r["state"][...]
    mixed = attention_part(r)
    r["mixed"][...] = mixed
    wait("wa")
    attn_out = dot_nn(mixed, r["wa_v"][:, QK:QKO])
    middle = state + attn_out
    r["middle"][...] = middle
    normed_two = (middle * inverse_of(middle) * r["gains"][1:2, :]).astype(BF)
    r["normed_two"][...] = normed_two
    wait("wg")
    wait("wu")
    wait("wd")
    ff = r["wg_v"].shape[1]
    mlp = jnp.zeros(state.shape, F32)
    for i in range(0, ff, CHUNK):
        at = slice(i, i + CHUNK)
        gate = dot_nn(normed_two, r["wg_v"][:, at])
        up = dot_nn(normed_two, r["wu_v"][:, at])
        r["gate"][:, at] = gate
        r["up"][:, at] = up
        hidden = (gate * jax.nn.sigmoid(gate) * up).astype(BF)
        r["hidden"][:, at] = hidden
        mlp = mlp + dot_nn(hidden, r["wd_v"][at, :])
    branch = attn_out + mlp.astype(BF).astype(F32)
    r["branch"][...] = branch
    router = jax.nn.sigmoid(jnp.sum(state * r["gains"][2:3, :], axis=1, keepdims=True))
    return state + (r["live"][:, 0:1] * router) * branch


def norm_back(grad, rows, gain):
    inverse = inverse_of(rows)
    scaled = rows * inverse
    weighted = grad * gain
    inner = jnp.mean(weighted * scaled, axis=1, keepdims=True)
    return inverse * (weighted - scaled * inner), jnp.sum(grad * scaled, axis=0, keepdims=True)


def back_part(r, wait, grad_after):
    state, live = r["b_state"][...], r["b_live"][:, 0:1]
    width = state.shape[1]
    router_vec = r["gains"][2:3, :]
    router = jax.nn.sigmoid(jnp.sum(state * router_vec, axis=1, keepdims=True))
    d_branch = (live * router) * grad_after
    d_logit = live * (router * (1.0 - router)) * jnp.sum(r["b_branch"][...] * grad_after, axis=1, keepdims=True)
    d_router = jnp.sum(d_logit * state, axis=0, keepdims=True)
    d_mlp = d_branch.astype(BF)
    r["d_mlp"][...] = d_mlp
    wait("wd")
    wait("wg")
    wait("wu")
    ff = r["wg_v"].shape[1]
    d_two = jnp.zeros(state.shape, F32)
    for i in range(0, ff, CHUNK):
        at = slice(i, i + CHUNK)
        gate, up = r["b_gate"][:, at], r["b_up"][:, at]
        sig = jax.nn.sigmoid(gate)
        d_hidden = dot_nt(d_mlp, r["wd_v"][at, :])
        d_up = (d_hidden * (gate * sig)).astype(BF)
        d_gate = (d_hidden * up * (sig * (1.0 + gate * (1.0 - sig)))).astype(BF)
        r["d_up"][:, at] = d_up
        r["d_gate"][:, at] = d_gate
        d_two = d_two + dot_nt(d_gate, r["wg_v"][:, at]) + dot_nt(d_up, r["wu_v"][:, at])
    d_two = d_two.astype(BF).astype(F32)
    d_middle, d_gain_two = norm_back(d_two, r["b_middle"][...], r["gains"][1:2, :])
    r["acc_out"][1:2, :width] = r["acc"][1:2, :width] + d_gain_two
    r["acc_out"][2:3, :width] = r["acc"][2:3, :width] + d_router
    d_attn = (d_branch + d_middle).astype(BF)
    r["d_attn"][...] = d_attn
    r["d_state"][...] = grad_after + d_logit * router_vec + d_middle
    wait("wa")
    d_mixed = dot_nt(d_attn, r["wa_v"][:, QK:QKO]).astype(BF)

    per = H // KVH
    kv = window(r)
    q = r["q_in"][...]
    rows = q.shape[0]
    allowed = jnp.concatenate([r["mask"][...]] * per, axis=1) > 0
    d_keys, d_values, dq_t = [], [], []
    for g in range(KVH):
        k_g = kv[:, g * HD : (g + 1) * HD]
        v_g = kv[:, (KVH + g) * HD : (KVH + g + 1) * HD]
        q_g, do_g = head_rows(q, g), head_rows(d_mixed, g)
        scores = jnp.where(allowed, dot_nt(k_g, q_g) * HD**-0.5, masked)
        probs = jnp.exp(scores - r["b_lse"][g : g + 1, :])
        d_values.append(dot_nn(probs.astype(BF), do_g))
        d_probs = dot_nt(v_g, do_g)
        d_scores = (probs * (d_probs - jnp.sum(probs * d_probs, axis=0, keepdims=True))).astype(BF)
        d_keys.append(dot_nn(d_scores, q_g) * HD**-0.5)
        dq = dot_nn(k_g.T, d_scores) * HD**-0.5
        dq_t += [dq[:, i * rows : (i + 1) * rows] for i in range(per)]
    d_queries = jnp.concatenate(dq_t + [jnp.zeros((HD, rows), F32)], axis=0).T
    d_queries = rope_lanes(d_queries, r["cos"][...], r["sin"][...], -1.0)
    r["d_q"][...] = d_queries[:, : H * HD].astype(BF)
    start = lax.rem(lax.axis_index("tok"), 2) * rows
    partial = r["dkv"]
    keep = partial.shape[0] - kv.shape[0]
    partial[pl.ds(pl.multiple_of((1 - lax.rem(lax.axis_index("tok"), 2)) * kv.shape[0], 128), keep), :] = jnp.zeros((keep, kv.shape[1]), BF)
    partial[pl.ds(pl.multiple_of(start, 128), kv.shape[0]), :] = jnp.concatenate(d_keys + d_values, axis=1).astype(BF)


def home_part(r, wait):
    half = KVH * HD
    total = r["home"][0].astype(F32)
    for i in range(1, r["home"].shape[0]):
        total = total + r["home"][i].astype(F32)
    rows = total.shape[0]
    padded = jnp.concatenate([total[:, :half], jnp.zeros((rows, half % (2 * HD)), F32)], axis=1)
    d_keys = rope_lanes(padded, r["cos"][...], r["sin"][...], -1.0)[:, :half].astype(BF)
    d_values = total[:, half:].astype(BF)
    wait("wa")
    packed = jnp.concatenate([r["h_dq"][...], d_keys, r["h_d_attn"][...], d_values], axis=1)
    r["d_packed"][...] = packed
    d_normed = dot_nt(packed[:, :QK], r["wa_v"][:, :QK]) + dot_nt(d_values, r["wa_v"][:, QKO:])
    state = r["h_state"][...]
    width = state.shape[1]
    d_in, d_gain = norm_back(d_normed, state, r["gains"][0:1, :])
    r["acc_out"][0:1, :width] = r["acc"][0:1, :width] + d_gain
    return r["h_d_state"][...] + d_in


def stage(name, parts, needed, inputs, outputs, weights, rename=None):
    in_names, out_names = list(inputs), list(outputs)
    w_names = [w for w in needed]

    def body(*refs):
        it = iter(refs)
        r = {n: next(it) for n in in_names}
        src = {n: next(it) for n in w_names}
        for n in out_names:
            r[n] = next(it)
        for n in w_names:
            r[n + "_v"] = next(it)
        sems = next(it)
        copies = {n: pltpu.make_async_copy(src[n], r[n + "_v"], sems.at[i]) for i, n in enumerate(w_names)}
        for n in w_names:
            copies[n].start()
        done = set()

        def wait(n):
            if n not in done:
                copies[n].wait()
                done.add(n)

        parts(r, wait)
        for n in w_names:
            wait(n)

    vm = pl.BlockSpec(memory_space=pltpu.VMEM)
    out = pl.pallas_call(
        body,
        name=name,
        out_shape=tuple(outputs.values()),
        in_specs=[vm] * len(in_names) + [pl.BlockSpec(memory_space=pl.ANY)] * len(w_names),
        out_specs=tuple([vm] * len(out_names)),
        scratch_shapes=[pltpu.VMEM(weights[n].shape, BF) for n in w_names] + [pltpu.SemaphoreType.DMA((len(w_names),))],
        compiler_params=pltpu.CompilerParams(vmem_limit_bytes=60 * 2**20),
    )(*inputs.values(), *[weights[n] for n in w_names])
    return dict(zip(out_names, out))


def shaped(shape, kind):
    return jax.ShapeDtypeStruct(shape, kind)


def front_outs(rows, width):
    return {"normed": shaped((rows, width), BF), "q": shaped((rows, H * HD), BF), "kv": shaped((rows, 2 * KVH * HD), BF)}


def forward_stage(state, q, kvw, mask, live, tables, gains, weights, last):
    rows, width = state.shape
    ff = weights["wg"].shape[1]
    outs = {
        "mixed": shaped((rows, H * HD), BF), "lse": shaped((8, (H // KVH) * rows), F32), "middle": shaped((rows, width), F32),
        "normed_two": shaped((rows, width), BF), "gate": shaped((rows, ff), F32), "up": shaped((rows, ff), F32),
        "hidden": shaped((rows, ff), BF), "branch": shaped((rows, width), F32),
    }
    if last:
        outs["output"] = shaped((width, rows), BF)
    else:
        outs |= front_outs(rows, width) | {"next": shaped((rows, width), F32)}

    def parts(r, wait):
        state_next = rest_part(r, wait)
        if last:
            r["output"][...] = state_next.T.astype(BF)
        else:
            r["next"][...] = state_next
            front_part(r, wait, state_next)

    needed = ("wa", "wg", "wu", "wd")
    ins = {"state": state, "q_in": q, "kvw": kvw, "mask": mask, "live": live, "cos": tables[0], "sin": tables[1], "gains": gains}
    return stage("forward", parts, needed, ins, outs, weights)


def first_stage(hidden_in, tables, gains, weights):
    width, rows = hidden_in.shape

    def parts(r, wait):
        state = r["hidden"][...].astype(F32).T
        r["state"][...] = state
        front_part(r, wait, state)

    outs = front_outs(rows, width) | {"state": shaped((rows, width), F32)}
    return stage("first", parts, ("wa",), {"hidden": hidden_in, "cos": tables[0], "sin": tables[1], "gains": gains}, outs, weights)


def backward_stage(kept, before, mask, live, tables, gains, acc, weights, cotangent):
    ins = {"cos": tables[0], "sin": tables[1], "gains": gains, "acc": acc}
    outs = {"acc_out": shaped(acc.shape, F32)}
    needed = ()
    rows, width = (kept or before)["state"].shape
    ff = weights["wg"].shape[1]
    kvr = 2 * KVH * HD
    if before is not None:
        ins |= {"home": before["home"], "h_dq": before["d_q"], "h_state": before["state"], "h_d_state": before["d_state"], "h_d_attn": before["d_attn"]}
        outs |= {"d_packed": shaped((rows, QKO + kvr // 2), BF)}
        needed += ("wa",)
    else:
        ins |= {"cot": cotangent}
    if kept is not None:
        ins |= {"b_state": kept["state"], "b_live": live, "b_branch": kept["branch"], "b_gate": kept["gate"], "b_up": kept["up"],
                "b_middle": kept["middle"], "b_lse": kept["lse"], "kvw": kept["kvw"], "q_in": kept["q"], "mask": mask}
        outs |= {"d_mlp": shaped((rows, width), BF), "d_up": shaped((rows, ff), BF), "d_gate": shaped((rows, ff), BF),
                 "d_attn": shaped((rows, width), BF), "d_state": shaped((rows, width), F32), "d_q": shaped((rows, H * HD), BF),
                 "dkv": shaped(kept["kvw"].shape, BF)}
        needed += ("wd", "wg", "wu") + (("wa",) if before is None else ())
    else:
        outs |= {"grad": shaped((width, rows), F32)}

    def parts(r, wait):
        r["acc_out"][...] = r["acc"][...]
        grad = home_part(r, wait) if before is not None else r["cot"][...].astype(F32).T
        if kept is not None:
            back_part(r, wait, grad)
        else:
            r["grad"][...] = grad.T

    return stage("backward", parts, needed, ins, outs, weights)


PARTS = 16
HALF = 480
COLS = 640
STREAMS = (
    ("x", True, 0, 80, 0), ("y", True, 80, 80, 0), ("x", False, 160, 48, 0), ("y", False, 208, 32, 0),
    ("x", True, 240, 80, 1), ("y", True, 320, 80, 1), ("x", False, 400, 32, 1), ("y", False, 432, 48, 1),
)
SLOTS = 4


def place():
    g, t = lax.axis_index("grp"), lax.axis_index("tok")
    return g // 2, lax.rem(g, 2), t // 2, lax.rem(t, 2)


def dev(y, x, z, c):
    return (y * 2 + x, z * 2 + c)


def pick(z, values):
    out = jnp.int32(values[3])
    for i in (2, 1, 0):
        out = jnp.where(z == i, jnp.int32(values[i]), out)
    return out


def copy_to(src, dst, send, recv, device):
    return pltpu.make_async_remote_copy(src_ref=src, dst_ref=dst, send_sem=send, recv_sem=recv, device_id=device, device_id_type=MESH)


def add_rows(dst, src, rows, step):
    def body(i, _):
        at = pl.ds(pl.multiple_of(i * step, step), step)
        dst[at, :] = dst[at, :] + src[at, :]
        return 0

    lax.fori_loop(0, rows // step, body, 0)


def tail_kernel(count, *refs):
    left_refs, refs = refs[: 4 * count], refs[4 * count :]
    right_refs, refs = refs[: 4 * count], refs[4 * count :]
    n_s = len(STREAMS)
    v_ref, o_ref, vo_ref, left_t, right, theirs, mine, other = refs[:8]
    ra, rz, rb = refs[8 : 8 + n_s], refs[8 + n_s : 8 + 2 * n_s], refs[8 + 2 * n_s : 8 + 3 * n_s]
    vrecv, load_sem, core_s, core_r, as_, ar, zs, zr, bs, br, ob, obr, oz, ozr, oa, oar, oc, ocr, vs, vr, own_sem = refs[8 + 3 * n_s :]
    y, x, z, c = place()
    partner = dev(y, x, z, 1 - c)
    across = {"x": dev(y, 1 - x, z, c), "y": dev(1 - y, x, z, c)}
    left_dev, right_dev = dev(y, x, z - 1, c), dev(y, x, z + 1, c)
    at_axis = {"x": x, "y": y}
    order = (pick(z, (3, 3, 0, 0)), pick(z, (2, 0, 3, 1)), pick(z, (1, 2, 1, 2)), z)
    far = dev(y, x, jnp.where(z < 2, z + 2, z - 2), c)
    tokens = left_refs[0].shape[0]

    loads = []
    for p in range(PARTS):
        for i in range(count):
            src = right_refs[(p // 4) * count + i].at[:, pl.ds((p % 4) * COLS, COLS)]
            loads.append(pltpu.make_async_copy(src, right.at[p, pl.ds(i * tokens, tokens)], load_sem.at[p * count + i]))
    for cp in loads:
        cp.start()

    bar = pltpu.get_barrier_semaphore()
    for d in (partner, across["x"], across["y"], far):
        pl.semaphore_signal(bar, inc=1, device_id=d, device_id_type=MESH)

    @pl.when(z > 0)
    def _():
        pl.semaphore_signal(bar, inc=1, device_id=left_dev, device_id_type=MESH)

    @pl.when(z < 3)
    def _():
        pl.semaphore_signal(bar, inc=1, device_id=right_dev, device_id_type=MESH)

    for j in range(4):
        left_t[j] = jnp.concatenate([each[...].astype(F32).T.astype(BF) for each in left_refs[j * count : (j + 1) * count]], axis=1)
    for cp in loads:
        cp.wait()
    pl.semaphore_wait(bar, 4 + (z > 0).astype(jnp.int32) + (z < 3).astype(jnp.int32))

    def part_xy(px, py, pz):
        return (px * 2 + py) * 4 + pz

    def part_of(s, pa, pb, pz):
        return part_xy(pa, pb, pz) if STREAMS[s][0] == "x" else part_xy(pb, pa, pz)

    def ab(s):
        a = STREAMS[s][0]
        b = "y" if a == "x" else "x"
        return at_axis[a], at_axis[b], across[a], across[b]

    waits = []
    seq = [(k, i, px, py) for k in range(4) for i, (px, py) in enumerate(((1 - x, 1 - y), (1 - x, y), (x, 1 - y), (x, y)))]

    def core_copy(j):
        k, _, px, py = seq[j]
        p = part_xy(px, py, order[k])
        return copy_to(theirs.at[j % SLOTS, pl.ds(pl.multiple_of((1 - c) * HALF, 16), HALF)], other.at[p], core_s.at[j], core_r.at[p], partner)

    def core_make(j):
        k, _, px, py = seq[j]
        p = part_xy(px, py, order[k])
        if j >= SLOTS:
            core_copy(j - SLOTS).wait_send()
        which = jnp.where(p < 8, 0, jnp.where(p < 12, 1, jnp.where(p < 14, 2, 3)))
        split = 2 * COLS - 2 * HALF
        theirs[j % SLOTS] = dot_nn(left_t[which], right[p]).astype(BF)

        @pl.when(p == PARTS - 1)
        def _():
            theirs[j % SLOTS, :, COLS - split :] = dot_nn(left_t[2], right[p, :, COLS - split :]).astype(BF)

        core_copy(j).start()

    def core_add(j):
        k, i, px, py = seq[j]
        p = part_xy(px, py, order[k])
        core_copy(j).wait_recv()
        mine[p] = theirs[j % SLOTS, pl.ds(pl.multiple_of(c * HALF, 16), HALF), :] + other[p]

    def a_copy(s, pb, pz):
        a, b, to_a, _ = ab(s)
        _, _, r0, n, _ = STREAMS[s]
        return copy_to(mine.at[part_of(s, 1 - a, pb, pz), pl.ds(r0, n)], ra[s].at[pb * 4 + pz], as_.at[s, pb * 4 + pz], ar.at[s, pb * 4 + pz], to_a)

    def a_send(j, batch):
        k, i, px, py = seq[j]
        for s in range(n_s):
            a_axis = STREAMS[s][0]
            if STREAMS[s][4] == batch and (i == 0 or (i == 1 and a_axis == "x") or (i == 2 and a_axis == "y")):
                cp = a_copy(s, py if a_axis == "x" else px, order[k])
                cp.start()
                waits.append(cp)

    def z_index(s, pb, slot):
        return pb * 5 + slot if STREAMS[s][1] else slot

    def z_copy(s, pb, pz, to_right):
        a, b, _, _ = ab(s)
        _, _, r0, n, _ = STREAMS[s]
        src = mine.at[part_of(s, a, pb, pz), pl.ds(r0, n)]
        i = z_index(s, pb, pz if to_right else jnp.where(pz == z - 1, 4, pz))
        return copy_to(src, rz[s].at[i], zs.at[s, i], zr.at[s, i], right_dev if to_right else left_dev)

    def z_take(s, pb, slot):
        a, _, _, _ = ab(s)
        _, _, r0, n, _ = STREAMS[s]
        i = z_index(s, pb, slot)
        copy_to(mine.at[0, pl.ds(r0, n)], rz[s].at[i], zs.at[s, i], zr.at[s, i], left_dev).wait_recv()
        pz = z if slot is z or isinstance(slot, int) else slot
        add_rows(mine.at[part_of(s, a, pb, pz), pl.ds(r0, n)], rz[s].at[i], n, 16)

    def z_step(s, pb, k):
        pz = order[k]
        if k < 3:
            up = jnp.where(pz > z, (z > 0).astype(jnp.int32), (z < 3).astype(jnp.int32))

            @pl.when(up == 1)
            def _():
                z_take(s, pb, pz)

            @pl.when(pz > z)
            def _():
                z_copy(s, pb, pz, True).start()

            @pl.when(pz < z)
            def _():
                z_copy(s, pb, pz, False).start()
        else:
            @pl.when(z > 0)
            def _():
                z_take(s, pb, z)

            @pl.when(z < 3)
            def _():
                z_take(s, pb, 4)

    def z_drain(s, pb, k):
        pz = order[k]

        @pl.when(pz > z)
        def _():
            z_copy(s, pb, pz, True).wait_send()

        @pl.when(pz < z)
        def _():
            z_copy(s, pb, pz, False).wait_send()

    def a_step(s, pb, k):
        a, b, to_a, _ = ab(s)
        _, _, r0, n, _ = STREAMS[s]
        pz = order[k]
        a_copy(s, pb, pz).wait_recv()
        add_rows(mine.at[part_of(s, a, pb, pz), pl.ds(r0, n)], ra[s].at[pb * 4 + pz], n, 16)

    def b_copy(s, pz):
        a, b, _, to_b = ab(s)
        _, second_z, r0, n, _ = STREAMS[s]
        i = 0 if second_z else pz
        return copy_to(mine.at[part_of(s, a, 1 - b, pz), pl.ds(r0, n)], rb[s].at[i], bs.at[s, i], br.at[s, i], to_b)

    def b_step(s, pz):
        a, b, _, _ = ab(s)
        _, second_z, r0, n, _ = STREAMS[s]
        i = 0 if second_z else pz
        b_copy(s, pz).wait_recv()
        add_rows(mine.at[part_of(s, a, b, pz), pl.ds(r0, n)], rb[s].at[i], n, 16)

    def of_batch(batch):
        return [s for s in range(n_s) if STREAMS[s][4] == batch]

    def first_step(batch, k):
        for s in of_batch(batch):
            _, b, _, _ = ab(s)
            a_step(s, 1 - b, k)
            if STREAMS[s][1]:
                z_step(s, 1 - b, k)
                a_step(s, b, k)
                z_step(s, b, k)
                if k == 3:
                    cp = b_copy(s, z)
                    cp.start()
                    waits.append(cp)
            else:
                cp = b_copy(s, order[k])
                cp.start()
                waits.append(cp)
                a_step(s, b, k)

    def second_step(batch, k):
        for s in of_batch(batch):
            _, b, _, _ = ab(s)
            if not STREAMS[s][1]:
                b_step(s, order[k])
                z_step(s, b, k)

    def vec_copy(i):
        to = (partner, across["x"], across["y"], dev(y, x, jnp.where(lax.rem(z, 2) == 0, z + 1, z - 1), c), far)[i]
        return copy_to(vo_ref, vrecv.at[i], vs.at[i], vr.at[i], to)

    def vec_end(i):
        vec_copy(i).wait()
        vo_ref[...] = vo_ref[...] + vrecv[i]

    half0 = c * HALF

    def out_at(s, p):
        _, _, r0, n, _ = STREAMS[s]
        return o_ref.at[p, pl.ds(pl.multiple_of(half0 + r0, 16), n)]

    def mine_at(s, p):
        _, _, r0, n, _ = STREAMS[s]
        return mine.at[p, pl.ds(r0, n)]

    def go(cp):
        cp.start()
        waits.append(cp)

    def to_core(s, p, src):
        return copy_to(src, out_at(s, p), oc.at[s, p], ocr.at[s, p], partner)

    def to_a(s, pb, pz, src):
        a, b, na, _ = ab(s)
        return copy_to(src, out_at(s, part_of(s, a, pb, pz)), oa.at[s, pb * 4 + pz], oar.at[s, pb * 4 + pz], na)

    def to_b(s, pz, src):
        a, b, _, nb = ab(s)
        return copy_to(src, out_at(s, part_of(s, a, b, pz)), ob.at[s, pz], obr.at[s, pz], nb)

    def to_z(s, pb, pz, src, to_right):
        a, b, _, _ = ab(s)
        i = pb * 8 + pz * 2 + (0 if to_right else 1)
        return copy_to(src, out_at(s, part_of(s, a, pb, pz)), oz.at[s, i], ozr.at[s, pb * 4 + pz], right_dev if to_right else left_dev)

    def spread_z(s, pb, pz, src, sides):
        if 0 in sides:
            @pl.when(z < 3)
            def _():
                to_z(s, pb, pz, src, True).start()
        if 1 in sides:
            @pl.when(z > 0)
            def _():
                to_z(s, pb, pz, src, False).start()

    def finish(batch):
        for s in of_batch(batch):
            a, b, _, _ = ab(s)
            p = part_of(s, a, b, z)
            b_step(s, z)
            if not STREAMS[s][1]:
                z_step(s, b, 3)
            src = mine_at(s, p)
            if STREAMS[s][1]:
                go(to_b(s, z, src))
                spread_z(s, b, z, src, (0, 1))
            else:
                spread_z(s, b, z, src, (0, 1))
                go(to_b(s, z, src))
            go(to_a(s, b, z, src))
            go(to_core(s, p, src))
            pltpu.make_async_copy(src, out_at(s, p), own_sem.at[s]).start()

    def got_b(s, pz):
        a, b, _, _ = ab(s)
        p = part_of(s, a, 1 - b, pz)
        src = out_at(s, p)
        copy_to(src, src, ob.at[s, pz], obr.at[s, pz], partner).wait_recv()
        if STREAMS[s][1]:
            spread_z(s, 1 - b, pz, src, (0, 1))
        to_a(s, 1 - b, pz, src).start()
        to_core(s, p, src).start()

    def got_z(s, pb, pz, from_left):
        a, b, _, _ = ab(s)
        p = part_of(s, a, pb, pz)
        src = out_at(s, p)
        copy_to(src, src, oz.at[s, 0], ozr.at[s, pb * 4 + pz], partner).wait_recv()
        spread_z(s, pb, pz, src, (0,) if from_left else (1,))
        to_a(s, pb, pz, src).start()
        if not STREAMS[s][1]:
            to_b(s, pz, src).start()
        to_core(s, p, src).start()

    def got_a(s, pb, pz):
        a, b, _, _ = ab(s)
        p = part_of(s, 1 - a, pb, pz)
        src = out_at(s, p)
        copy_to(src, src, oa.at[s, pb * 4 + pz], oar.at[s, pb * 4 + pz], partner).wait_recv()
        to_core(s, p, src).start()

    def gather_b(batch):
        for s in of_batch(batch):
            got_b(s, z)

    def gather_a(batch):
        for s in of_batch(batch):
            _, b, _, _ = ab(s)
            got_a(s, b, z)
            got_a(s, 1 - b, z)

    def from_side(t, side):
        return (z - t, z >= t) if side == 0 else (z + t, z + t <= 3)

    def gather_z(batch, t):
        for side in (0, 1):
            pz, there = from_side(t, side)

            @pl.when(there)
            def _():
                for s in of_batch(batch):
                    _, b, _, _ = ab(s)
                    got_z(s, b, pz, side == 0)
                    if STREAMS[s][1]:
                        got_z(s, 1 - b, pz, side == 0)

    def gather_rest(batch, t):
        for side in (0, 1):
            pz, there = from_side(t, side)

            @pl.when(there)
            def _():
                for s in of_batch(batch):
                    if not STREAMS[s][1]:
                        got_b(s, pz)
                for s in of_batch(batch):
                    _, b, _, _ = ab(s)
                    got_a(s, b, pz)
                    got_a(s, 1 - b, pz)

    vo_ref[...] = v_ref[...]
    vec_copy(0).start()

    def group(k, batches=(0,)):
        for i in range(4):
            j = k * 4 + i
            core_make(j)
            if j > 0:
                core_add(j - 1)
                a_send(j - 1, 0)
        if k == 3:
            core_add(15)
            a_send(15, 0)

    group(0)
    vec_end(0)
    vec_copy(1).start()
    group(1)
    vec_end(1)
    vec_copy(2).start()
    first_step(0, 0)
    group(2)
    vec_end(2)
    vec_copy(3).start()
    second_step(0, 0)
    first_step(0, 1)
    group(3)
    vec_end(3)
    vec_copy(4).start()
    second_step(0, 1)
    for j in range(0, 4):
        a_send(j, 1)
    first_step(0, 2)
    vec_end(4)
    second_step(0, 2)
    for j in range(4, 8):
        a_send(j, 1)
    first_step(0, 3)
    first_step(1, 0)
    finish(0)
    for j in range(8, 12):
        a_send(j, 1)
    second_step(1, 0)
    gather_b(0)
    first_step(1, 1)
    second_step(1, 1)
    gather_z(0, 1)
    for j in range(12, 16):
        a_send(j, 1)
    gather_a(0)
    first_step(1, 2)
    second_step(1, 2)
    gather_z(0, 2)
    gather_rest(0, 1)
    first_step(1, 3)
    finish(1)
    gather_z(0, 3)
    gather_rest(0, 2)
    gather_b(1)
    gather_z(1, 1)
    gather_rest(0, 3)
    gather_a(1)
    gather_z(1, 2)
    gather_rest(1, 1)
    gather_z(1, 3)
    gather_rest(1, 2)
    gather_rest(1, 3)

    for cp in waits:
        cp.wait_send()
    for j in range(PARTS - SLOTS, PARTS):
        core_copy(j).wait_send()
    for s in range(n_s):
        a, b, _, _ = ab(s)
        pltpu.make_async_copy(mine_at(s, part_of(s, a, b, z)), out_at(s, part_of(s, a, b, z)), own_sem.at[s]).wait()
        pbs = (b, 1 - b) if STREAMS[s][1] else (b,)
        for pb in pbs:
            for k in range(3):
                z_drain(s, pb, k)
        for pz in range(4):
            for pb in pbs:
                src = out_at(s, part_of(s, a, pb, pz))

                @pl.when((z >= pz) & (z < 3))
                def _():
                    to_z(s, pb, pz, src, True).wait_send()

                @pl.when((z <= pz) & (z > 0))
                def _():
                    to_z(s, pb, pz, src, False).wait_send()
            for pb in (0, 1):
                src = out_at(s, part_of(s, a, pb, pz))

                @pl.when(jnp.logical_not((pb == b) & (pz == z)))
                def _():
                    to_a(s, pb, pz, src).wait_send()
            if not STREAMS[s][1]:
                @pl.when(z != pz)
                def _():
                    to_b(s, pz, out_at(s, 0)).wait_send()
        for p in range(16):
            src = out_at(s, p)

            @pl.when(p != part_of(s, a, b, z))
            def _():
                to_core(s, p, src).wait_send()
            _, _, r0, n, _ = STREAMS[s]
            dst = o_ref.at[p, pl.ds(pl.multiple_of((1 - c) * HALF + r0, 16), n)]
            copy_to(dst, dst, oc.at[s, p], ocr.at[s, p], partner).wait_recv()


def summed_gradients(lefts, rights, vectors):
    dma = pltpu.SemaphoreType.DMA
    count = len(lefts[0])
    tokens, width = lefts[0][0].shape
    rows = count * tokens
    n_s = len(STREAMS)
    vm = pl.BlockSpec(memory_space=pltpu.VMEM)
    return pl.pallas_call(
        lambda *refs: tail_kernel(count, *refs),
        name="summed_gradients",
        out_shape=(jax.ShapeDtypeStruct((PARTS, width, COLS), BF), jax.ShapeDtypeStruct(vectors.shape, F32)),
        in_specs=[vm] * (4 * count) + [pl.BlockSpec(memory_space=pl.ANY)] * (4 * count) + [vm],
        out_specs=(pl.BlockSpec(memory_space=pl.ANY), vm),
        scratch_shapes=[
            pltpu.VMEM((4, width, rows), BF), pltpu.VMEM((PARTS, rows, COLS), BF), pltpu.VMEM((SLOTS, 2 * HALF, COLS), BF),
            pltpu.VMEM((PARTS, HALF, COLS), BF), pltpu.VMEM((PARTS, HALF, COLS), BF),
            *[pltpu.VMEM((8, s[3], COLS), BF) for s in STREAMS],
            *[pltpu.VMEM((10 if s[1] else 5, s[3], COLS), BF) for s in STREAMS],
            *[pltpu.VMEM((1 if s[1] else 4, s[3], COLS), BF) for s in STREAMS],
            pltpu.VMEM((5, *vectors.shape), F32),
            dma((PARTS * count,)), dma((16,)), dma((16,)),
            dma((n_s, 8)), dma((n_s, 8)), dma((n_s, 10)), dma((n_s, 10)), dma((n_s, 4)), dma((n_s, 4)),
            dma((n_s, 4)), dma((n_s, 4)), dma((n_s, 16)), dma((n_s, 8)), dma((n_s, 8)), dma((n_s, 8)), dma((n_s, 16)), dma((n_s, 16)),
            dma((5,)), dma((5,)), dma((n_s,)),
        ],
        compiler_params=pltpu.CompilerParams(collective_id=1, has_side_effects=True, vmem_limit_bytes=60 * 2**20),
    )(*[a for l in lefts for a in l], *[a for l in rights for a in l], vectors)


QUARTERS = 4


def gather_kernel(*refs):
    ins, outs = refs[:5], refs[5:10]
    zs, xs, ys, cs, got, cgot, own_s, own_c, own_r, ss, sr, sc, scr = refs[10:]
    y, x, z, c = place()
    partner, to_x, to_y = dev(y, x, z, 1 - c), dev(y, 1 - x, z, c), dev(1 - y, x, z, c)
    left, right = dev(y, x, z - 1, c), dev(y, x, z + 1, c)
    quarter = (x * 2 + y, (1 - x) * 2 + y, x * 2 + (1 - y), (1 - x) * 2 + (1 - y))
    lasting = []

    def go(cp, when=None):
        if when is None:
            cp.start()
        else:
            @pl.when(when)
            def _():
                cp.start()
        lasting.append((cp, when))

    def cut(ref, m, q):
        if m < 3:
            n = ref.shape[1] // QUARTERS
            return ref.at[:, pl.ds(pl.multiple_of(q * n, 128), n)]
        n = ref.shape[0] // QUARTERS
        return ref.at[pl.ds(pl.multiple_of(q * n, 16), n), :]

    def out_piece(m, kind, zz, core):
        return cut(outs[m].at[zz * 2 + core], m, quarter[kind])

    bar = pltpu.get_barrier_semaphore()
    for d in (partner, to_x, to_y):
        pl.semaphore_signal(bar, inc=1, device_id=d, device_id_type=MESH)

    @pl.when(z > 0)
    def _():
        pl.semaphore_signal(bar, inc=1, device_id=left, device_id_type=MESH)

    @pl.when(z < 3)
    def _():
        pl.semaphore_signal(bar, inc=1, device_id=right, device_id_type=MESH)

    pl.semaphore_wait(bar, 3 + (z > 0).astype(jnp.int32) + (z < 3).astype(jnp.int32))

    def small_copy(zz, core, src, device, sems):
        return copy_to(src, outs[4].at[zz * 2 + core], sems[0], sems[1], device)

    go(small_copy(z, c, ins[4], right, (ss.at[z, 0], sr.at[z])), z < 3)
    go(small_copy(z, c, ins[4], left, (ss.at[z, 1], sr.at[z])), z > 0)
    go(small_copy(z, c, ins[4], partner, (sc.at[z], scr.at[z])))
    for m in range(4):
        src, dst = cut(ins[m], m, quarter[0]), out_piece(m, 0, z, c)
        go(copy_to(src, dst, zs.at[m, z, 0], got.at[0, m, z], right), z < 3)
        go(copy_to(src, dst, zs.at[m, z, 1], got.at[0, m, z], left), z > 0)
    for m in range(4):
        go(copy_to(ins[m], outs[m].at[z * 2 + c], own_c.at[m], own_r.at[m], partner))
    local = [pltpu.make_async_copy(ins[m], outs[m].at[z * 2 + c], own_s.at[m]) for m in range(5)]
    for cp in local:
        cp.start()

    steps = [(t, side) for t in (1, 2, 3) for side in (0, 1)]

    def source(t, side):
        return (z - t, z >= t) if side == 0 else (z + t, z + t <= 3)

    def wait_for(kind, m, zz):
        piece = out_piece(m, kind, zz, c)
        copy_to(piece, piece, cs.at[kind, m, zz], got.at[kind, m, zz], partner).wait_recv()
        return piece

    def each(kind, m, t, side):
        zz, there = source(t, side)
        onward = (z < 3) if side == 0 else (z > 0)

        @pl.when(there)
        def _():
            piece = wait_for(kind, m, zz)
            first_x = m % 2 == 0
            sends = []
            if kind == 0:
                on = copy_to(piece, piece, zs.at[m, zz, side], got.at[0, m, zz], right if side == 0 else left)

                @pl.when(onward)
                def _():
                    on.start()

                sends.append(copy_to(piece, piece, xs.at[0, m, zz], got.at[1, m, zz], to_x))
                sends.append(copy_to(piece, piece, ys.at[0, m, zz], got.at[2, m, zz], to_y))
            elif kind == 1 and first_x:
                sends.append(copy_to(piece, piece, ys.at[1, m, zz], got.at[3, m, zz], to_y))
            elif kind == 2 and not first_x:
                sends.append(copy_to(piece, piece, xs.at[1, m, zz], got.at[3, m, zz], to_x))
            sends.append(copy_to(piece, piece, cs.at[kind, m, zz], cgot.at[kind, m, zz], partner))
            for cp in sends:
                cp.start()

        lasting.append((("s", kind, m, t, side), there))
        if kind == 0:
            lasting.append((("z", m, t, side), there & onward))

    def small_step(t, side):
        zz, there = source(t, side)

        @pl.when(there)
        def _():
            piece = outs[4].at[zz * 2 + c]
            copy_to(piece, piece, sc.at[zz], sr.at[zz], partner).wait_recv()

            @pl.when((z < 3) if side == 0 else (z > 0))
            def _():
                small_copy(zz, c, piece, right if side == 0 else left, (ss.at[zz, side], sr.at[zz])).start()

            small_copy(zz, c, piece, partner, (sc.at[zz], scr.at[zz])).start()

        lasting.append((("m", t, side), there))

    for t, side in steps:
        small_step(t, side)
    for turn in range(4 + 2):
        for t, side in steps:
            if turn < 4:
                each(0, turn, t, side)
            if 1 <= turn < 5:
                m = turn - 1
                relay, leaf = (1, 2) if m % 2 == 0 else (2, 1)
                each(relay, m, t, side)
                each(leaf, m, t, side)
            if turn >= 2:
                each(3, turn - 2, t, side)

    for cp, when in lasting:
        if not isinstance(cp, tuple):
            if when is None:
                cp.wait_send()
            else:
                @pl.when(when)
                def _():
                    cp.wait_send()
        elif cp[0] == "z":
            _, m, t, side = cp
            zz, _ = source(t, side)
            piece = out_piece(m, 0, zz, c)

            @pl.when(when)
            def _():
                copy_to(piece, piece, zs.at[m, zz, side], got.at[0, m, zz], partner).wait_send()
        elif cp[0] == "m":
            _, t, side = cp
            zz, _ = source(t, side)
            piece = outs[4].at[zz * 2 + c]

            @pl.when(when)
            def _():
                @pl.when((z < 3) if side == 0 else (z > 0))
                def _():
                    small_copy(zz, c, piece, partner, (ss.at[zz, side], sr.at[zz])).wait_send()

                small_copy(zz, c, piece, partner, (sc.at[zz], scr.at[zz])).wait_send()
                other = outs[4].at[zz * 2 + 1 - c]
                copy_to(other, other, sc.at[zz], scr.at[zz], partner).wait_recv()
        else:
            _, kind, m, t, side = cp
            zz, _ = source(t, side)
            piece = out_piece(m, kind, zz, c)
            other = out_piece(m, kind, zz, 1 - c)
            first_x = m % 2 == 0

            @pl.when(when)
            def _():
                if kind == 0 or (kind == 2 and not first_x):
                    copy_to(piece, piece, xs.at[min(kind, 1), m, zz], got.at[1, m, zz], partner).wait_send()
                if kind == 0 or (kind == 1 and first_x):
                    copy_to(piece, piece, ys.at[min(kind, 1), m, zz], got.at[1, m, zz], partner).wait_send()
                copy_to(piece, piece, cs.at[kind, m, zz], cgot.at[kind, m, zz], partner).wait_send()
                copy_to(other, other, cs.at[kind, m, zz], cgot.at[kind, m, zz], partner).wait_recv()

    for m in range(4):
        other = outs[m].at[z * 2 + 1 - c]
        copy_to(other, other, own_c.at[m], own_r.at[m], partner).wait_recv()
    other = outs[4].at[z * 2 + 1 - c]
    copy_to(other, other, sc.at[z], scr.at[z], partner).wait_recv()
    for cp in local:
        cp.wait()


def gather_rows(shards):
    dma = pltpu.SemaphoreType.DMA
    return pl.pallas_call(
        gather_kernel,
        name="gather_rows",
        out_shape=tuple(jax.ShapeDtypeStruct((8, *s.shape), s.dtype) for s in shards),
        in_specs=[pl.BlockSpec(memory_space=pl.ANY)] * 5,
        out_specs=tuple([pl.BlockSpec(memory_space=pl.ANY)] * 5),
        scratch_shapes=[
            dma((4, 4, 2)), dma((2, 4, 4)), dma((2, 4, 4)), dma((4, 4, 4)), dma((4, 4, 4)), dma((4, 4, 4)),
            dma((5,)), dma((4,)), dma((4,)), dma((4, 2)), dma((4,)), dma((4,)), dma((4,)),
        ],
        compiler_params=pltpu.CompilerParams(collective_id=4, has_side_effects=True),
    )(*shards)


def keys_kernel(chips, back, kv_ref, w_ref, s_right, r_left, s_core, r_core):
    g, t = lax.axis_index("grp"), lax.axis_index("tok")
    z, c = t // 2, lax.rem(t, 2)
    rows = kv_ref.shape[0]
    partner, right = (g, z * 2 + 1 - c), (g, t + 2)

    def slot(d, core):
        return w_ref.at[pl.ds(pl.multiple_of(((back - d) * 2 + core) * rows, 128), rows)]

    bar = pltpu.get_barrier_semaphore()
    pl.semaphore_signal(bar, inc=1, device_id=partner, device_id_type=MESH)

    @pl.when(z > 0)
    def _():
        pl.semaphore_signal(bar, inc=1, device_id=(g, t - 2), device_id_type=MESH)

    def along(d, src):
        return copy_to(src, slot(d, c), s_right.at[d - 1], r_left.at[d - 1], right)

    def beside(d, src):
        return copy_to(src, slot(d, c), s_core.at[d], r_core.at[d], partner)

    own = w_ref.at[pl.ds(pl.multiple_of((back * 2 + c) * rows, 128), rows)]
    own[...] = kv_ref[...]
    for d in range(1, back + 1):
        @pl.when(z < d)
        def _():
            for core in (0, 1):
                slot(d, core)[...] = jnp.zeros(kv_ref.shape, kv_ref.dtype)

    pl.semaphore_wait(bar, 1 + (z < chips - 1).astype(jnp.int32))

    @pl.when(z < chips - 1)
    def _():
        along(1, kv_ref).start()

    beside(0, kv_ref).start()
    for d in range(1, back + 1):
        @pl.when(z >= d)
        def _():
            along(d, slot(d, c)).wait_recv()
            if d < back:
                @pl.when(z < chips - 1)
                def _():
                    along(d + 1, slot(d, c)).start()
            beside(d, slot(d, c)).start()

    def mine_to(d):
        return copy_to(slot(d, 1 - c), slot(d, 1 - c), s_core.at[d], r_core.at[d], partner)

    mine_to(0).wait_recv()
    beside(0, kv_ref).wait_send()

    @pl.when(z < chips - 1)
    def _():
        along(1, kv_ref).wait_send()

    for d in range(1, back + 1):
        @pl.when(z >= d)
        def _():
            mine_to(d).wait_recv()
            beside(d, slot(d, c)).wait_send()
            if d < back:
                @pl.when(z < chips - 1)
                def _():
                    along(d + 1, slot(d, c)).wait_send()


def exchange_keys(kv, n_tok, nback):
    back = nback // 2
    rows = kv.shape[0]
    dma = pltpu.SemaphoreType.DMA
    return pl.pallas_call(
        lambda *refs: keys_kernel(n_tok // 2, back, *refs),
        name="exchange_keys",
        out_shape=jax.ShapeDtypeStruct(((2 * back + 2) * rows, kv.shape[1]), kv.dtype),
        in_specs=[pl.BlockSpec(memory_space=pltpu.VMEM)],
        out_specs=pl.BlockSpec(memory_space=pltpu.VMEM),
        scratch_shapes=[dma((back,)), dma((back,)), dma((back + 1,)), dma((back + 1,))],
        compiler_params=pltpu.CompilerParams(collective_id=2, has_side_effects=True, vmem_limit_bytes=32 * 2**20),
    )(kv)


def home_kernel(chips, back, p_ref, h_ref, beside_in, sums, after_in, s_left, r_right, s_core, r_core):
    g, t = lax.axis_index("grp"), lax.axis_index("tok")
    z, c = t // 2, lax.rem(t, 2)
    rows = h_ref.shape[1]
    partner, left = (g, z * 2 + 1 - c), (g, t - 2)

    def block(d, core):
        return p_ref.at[pl.ds(pl.multiple_of(((back - d) * 2 + core) * rows, 128), rows)]

    bar = pltpu.get_barrier_semaphore()
    pl.semaphore_signal(bar, inc=1, device_id=partner, device_id_type=MESH)

    @pl.when(z < chips - 1)
    def _():
        pl.semaphore_signal(bar, inc=1, device_id=(g, t + 2), device_id_type=MESH)

    pl.semaphore_wait(bar, 1 + (z > 0).astype(jnp.int32))

    def beside(d):
        return copy_to(block(d, 1 - c), beside_in.at[d], s_core.at[d], r_core.at[d], partner)

    def along(d):
        return copy_to(sums.at[d - 1], after_in.at[d - 1], s_left.at[d - 1], r_right.at[d - 1], left)

    for d in range(back, 0, -1):
        @pl.when(z >= d)
        def _():
            beside(d).start()
    beside(0).start()
    for d in range(back, 0, -1):
        @pl.when(z >= d)
        def _():
            beside(d).wait_recv()
            sums[d - 1] = (block(d, c)[...].astype(F32) + beside_in[d].astype(F32)).astype(BF)
            if d < back:
                @pl.when(z < chips - 1)
                def _():
                    along(d + 1).wait_recv()
                    sums[d - 1] = (sums[d - 1].astype(F32) + after_in[d].astype(F32)).astype(BF)
            along(d).start()
    beside(0).wait_recv()
    h_ref[0] = block(0, c)[...].astype(F32) + beside_in[0].astype(F32)

    @pl.when(z < chips - 1)
    def _():
        along(1).wait_recv()
        h_ref[0] = h_ref[0] + after_in[0].astype(F32)

    beside(0).wait_send()
    for d in range(1, back + 1):
        @pl.when(z >= d)
        def _():
            beside(d).wait_send()
            along(d).wait_send()


def exchange_home(partial, n_tok, nback):
    back = nback // 2
    rows = partial.shape[0] // (2 * back + 2)
    width = partial.shape[1]
    dma = pltpu.SemaphoreType.DMA
    return pl.pallas_call(
        lambda *refs: home_kernel(n_tok // 2, back, *refs),
        name="exchange_home",
        out_shape=jax.ShapeDtypeStruct((1, rows, width), F32),
        in_specs=[pl.BlockSpec(memory_space=pltpu.VMEM)],
        out_specs=pl.BlockSpec(memory_space=pltpu.VMEM),
        scratch_shapes=[
            pltpu.VMEM((back + 1, rows, width), BF), pltpu.VMEM((back, rows, width), BF), pltpu.VMEM((back, rows, width), BF),
            dma((back,)), dma((back,)), dma((back + 1,)), dma((back + 1,)),
        ],
        compiler_params=pltpu.CompilerParams(collective_id=3, has_side_effects=True, vmem_limit_bytes=32 * 2**20),
    )(partial)


ROW_NAMES = ("normed_two", "d_mlp", "normed", "mixed", "d_gate", "d_up", "hidden", "d_packed")


def grads_kernel(count, *refs):
    r = {name: refs[i * count : (i + 1) * count] for i, name in enumerate(ROW_NAMES)}
    g_ref, left_t, slots, sems = refs[len(ROW_NAMES) * count :]
    for i, name in enumerate(ROW_NAMES[:4]):
        left_t[i] = jnp.concatenate([each[...].astype(F32).T.astype(BF) for each in r[name]], axis=1)

    def out_copy(p):
        return pltpu.make_async_copy(slots.at[p % 2], g_ref.at[p], sems.at[p % 2])

    split = 2 * COLS - left_t.shape[1]
    for p in range(PARTS):
        if p >= 2:
            out_copy(p - 2).wait()
        low = (p % 4) * COLS
        right = jnp.concatenate([each[:, low : low + COLS] for each in r[ROW_NAMES[4 + p // 4]]], axis=0)
        result = dot_nn(left_t[((0,) * 8 + (1,) * 4 + (2, 2, 3, 3))[p]], right)
        if p == PARTS - 1:
            result = jnp.concatenate([result[:, : COLS - split], dot_nn(left_t[2], right[:, COLS - split :])], axis=1)
        slots[p % 2] = result.astype(BF)
        out_copy(p).start()
    out_copy(PARTS - 2).wait()
    out_copy(PARTS - 1).wait()


def weight_gradients(rows):
    count = len(rows["d_mlp"])
    flat = [each for name in ROW_NAMES for each in rows[name]]
    tokens, width = rows["normed"][0].shape
    return pl.pallas_call(
        lambda *refs: grads_kernel(count, *refs),
        name="weight_gradients",
        out_shape=jax.ShapeDtypeStruct((PARTS, width, COLS), BF),
        in_specs=[pl.BlockSpec(memory_space=pltpu.VMEM)] * len(flat),
        out_specs=pl.BlockSpec(memory_space=pl.ANY),
        scratch_shapes=[pltpu.VMEM((4, width, count * tokens), BF), pltpu.VMEM((2, width, COLS), BF), pltpu.SemaphoreType.DMA((2,))],
        compiler_params=pltpu.CompilerParams(vmem_limit_bytes=60 * 2**20),
    )(*flat)


def spread_kernel(p_ref, gate, up, down, d_q, d_k, d_v, d_o, came, wide, q_full, k_full, o_full, v_full, sem_in, sem_out, sem_full):
    width = q_full.shape[0]
    order = [12, 13, 14, 15] + list(range(12))

    def fetch(i):
        return pltpu.make_async_copy(p_ref.at[order[i]], came.at[i % 3], sem_in.at[i % 3])

    def put(i):
        p = order[i]
        return pltpu.make_async_copy(wide.at[i % 2], (gate, up, down)[p // 4].at[:, pl.ds((p % 4) * COLS, COLS)], sem_out.at[i % 2])

    fulls = [(q_full, d_q), (k_full, d_k), (o_full, d_o), (v_full, d_v)]

    def put_full(j):
        return pltpu.make_async_copy(fulls[j][0], fulls[j][1], sem_full.at[j])

    fetch(0).start()
    fetch(1).start()
    for i, p in enumerate(order):
        if i + 2 < len(order):
            fetch(i + 2).start()
        fetch(i).wait()
        part = came.at[i % 3]
        if i >= 6:
            put(i - 2).wait()
        if p >= 12:
            full, other = (q_full, k_full) if p < 14 else (o_full, v_full)
            if p % 2 == 0:
                full[:, :COLS] = part[...].astype(F32)
            else:
                got = part[...].astype(F32)
                full[:, COLS:] = got[:, : width - COLS]
                other[...] = got[:, width - COLS :].T
                put_full(0 if p < 14 else 2).start()
                put_full(1 if p < 14 else 3).start()
        else:
            wide[i % 2] = part[...].astype(F32)
            put(i).start()
    put(len(order) - 2).wait()
    put(len(order) - 1).wait()
    for j in range(4):
        put_full(j).wait()


def spread_out(parts):
    n, width, cols = parts.shape
    kv = 2 * cols - width
    ff = 4 * cols
    shapes = [(width, ff), (width, ff), (width, ff), (width, width), (kv, width), (kv, width), (width, width)]
    vm = pltpu.VMEM
    return pl.pallas_call(
        spread_kernel,
        name="spread_out",
        out_shape=tuple(jax.ShapeDtypeStruct(s, F32) for s in shapes),
        in_specs=[pl.BlockSpec(memory_space=pl.ANY)],
        out_specs=tuple([pl.BlockSpec(memory_space=pl.ANY)] * 7),
        scratch_shapes=[
            vm((3, width, cols), BF), vm((2, width, cols), F32),
            vm((width, width), F32), vm((kv, width), F32), vm((width, width), F32), vm((kv, width), F32),
            pltpu.SemaphoreType.DMA((3,)), pltpu.SemaphoreType.DMA((2,)), pltpu.SemaphoreType.DMA((4,)),
        ],
        compiler_params=pltpu.CompilerParams(vmem_limit_bytes=60 * 2**20),
    )(parts)


def on_device(
    hidden_in,
    cotangent,
    lengths,
    active,
    norm_attn,
    w_query,
    w_key,
    w_value,
    w_out,
    norm_mlp,
    w_gate,
    w_up,
    w_down,
    w_router,
):
    n_tok = lax.axis_size("tok")
    n_grp = lax.axis_size("grp")
    me_index = lax.axis_index("tok")
    rows, width = hidden_in.shape
    nback = min(SPAN, n_tok // 2)

    share = norm_attn.shape[0]
    vectors = jnp.pad(jnp.stack([norm_attn, norm_mlp, w_router]), ((0, 0), (0, 128 - share)))
    small = jnp.concatenate([vectors, active.astype(BF), jnp.zeros((10, 128), BF)], axis=0)
    shards = (jnp.concatenate([w_query, w_key, w_out, w_value], axis=1), w_gate, w_up, w_down, small)
    whole = gather_rows(shards) if (n_grp, n_tok) == (4, 8) else [lax.all_gather(each, "tok", axis=0) for each in shards]
    weights = {name: each.reshape(-1, each.shape[-1]) for name, each in zip(WEIGHTS, whole)}
    gains = jnp.transpose(whole[4][:, :3, :share], (1, 0, 2)).reshape(3, width).astype(F32)
    gains = jnp.pad(gains, ((0, 5), (0, 0)))

    lengths_row = lengths[0]
    token = jnp.arange(rows, dtype=jnp.int32)
    global_rows = me_index * rows + token
    segment_rows = segment_of(lengths_row, global_rows)
    cosine, sine = rotary_tables(position_of(lengths_row, global_rows, segment_rows))
    tables = (jnp.concatenate([cosine] * 4, axis=1), jnp.concatenate([-sine, sine] * 2, axis=1))
    reach = (nback + 1) * rows
    global_keys = (me_index - nback) * rows + jnp.arange(reach, dtype=jnp.int32)
    live_all = jnp.transpose(whole[4][:, 3:6], (1, 0, 2)).reshape(3, -1)
    live_all = jnp.pad(live_all, ((0, 0), (nback * rows, 0)))
    live_keys = lax.dynamic_slice_in_dim(live_all, me_index * rows, reach, 1)
    reachable = (segment_rows[None, :] == segment_of(lengths_row, global_keys)[:, None]) & (
        global_keys[:, None] <= global_rows[None, :]
    )
    masks = jnp.where(reachable[None] & (live_keys[:, :, None] > 0), 1.0, 0.0).astype(F32)
    lives = [active[i].astype(F32)[:, None] for i in range(RECUR)]

    kept = []
    made = first_stage(hidden_in.T, tables, gains, weights)
    state = made["state"]
    for step in range(RECUR):
        kvw = exchange_keys(made["kv"], n_tok, nback)
        last = step == RECUR - 1
        done = forward_stage(state, made["q"], kvw, masks[step], lives[step], tables, gains, weights, last)
        kept.append({**done, "state": state, "q": made["q"], "kvw": kvw, "normed_r": made["normed"]})
        made, state = done, done.get("next")

    acc = jnp.zeros((8, 1024), F32)
    before = None
    rows_of = {name: [] for name in ROW_NAMES}
    for step in reversed(range(RECUR)):
        back = backward_stage(kept[step], before, masks[step], lives[step], tables, gains, acc, weights, cotangent.T)
        acc = back["acc_out"]
        if before is not None:
            rows_of["d_packed"].append(back["d_packed"])
        for name in ("d_mlp", "d_gate", "d_up"):
            rows_of[name].append(back[name])
        for name in ("normed_two", "mixed", "hidden"):
            rows_of[name].append(kept[step][name])
        rows_of["normed"].append(kept[step]["normed_r"])
        before = {"home": exchange_home(back["dkv"], n_tok, nback), "d_q": back["d_q"], "state": kept[step]["state"], "d_state": back["d_state"], "d_attn": back["d_attn"]}
    back = backward_stage(None, before, None, None, tables, gains, acc, weights, None)
    rows_of["d_packed"].append(back["d_packed"])
    acc = back["acc_out"]
    if (n_grp, n_tok) == (4, 8):
        lefts, rights = ([rows_of[name] for name in names] for names in (ROW_NAMES[:4], ROW_NAMES[4:]))
        parts, acc = summed_gradients(lefts, rights, acc)
    else:
        parts = weight_gradients(rows_of)
        parts = lax.psum(parts.astype(F32), ("grp", "tok")).astype(BF)
        acc = lax.psum(acc, ("grp", "tok"))
    d_gate, d_up, d_down, d_q, d_k, d_v, d_o = spread_out(parts)
    return (
        kept[-1]["output"].T,
        back["grad"].T,
        acc[0, :width],
        d_q,
        d_k.T,
        d_v.T,
        d_o,
        acc[1, :width],
        d_gate,
        d_up,
        d_down.T,
        acc[2, :width],
    )


def solution(mesh):
    placed = (
        P(("grp", "tok"), None),
        P(("grp", "tok"), None),
        P("grp", None),
        P(None, ("grp", "tok")),
        P("tok"),
        P("tok", None),
        P("tok", None),
        P("tok", None),
        P("tok", None),
        P("tok"),
        P("tok", None),
        P("tok", None),
        P("tok", None),
        P("tok"),
    )
    return jax.shard_map(
        on_device,
        mesh=mesh,
        in_specs=placed,
        out_specs=(
            P(("grp", "tok"), None),
            P(("grp", "tok"), None),
            P(),
            P(),
            P(),
            P(),
            P(),
            P(),
            P(),
            P(),
            P(),
            P(),
        ),
        check_vma=False,
    )
```

```python
import jax
import jax.numpy as jnp
from jax import lax
from jax.experimental import pallas as pl
from jax.experimental.pallas import tpu as pltpu
from jax.sharding import PartitionSpec as P

MESH = pl.DeviceIdType.MESH

H = 15
KVH = 5
HD = 64
RECUR = 3
SPAN = 16

epsilon = 1e-05
theta = 10000.0
masked = -1000000000.0

def ends_of(lengths_row):
    count = lengths_row.shape[0]
    until = jnp.arange(count)[:, None] >= jnp.arange(count)[None, :]
    return jnp.sum(jnp.where(until, lengths_row[None, :], 0), axis=1)


def segment_of(lengths_row, global_rows):
    ends_at = ends_of(lengths_row)
    return jnp.sum((global_rows[:, None] >= ends_at[None, :]).astype(jnp.int32), axis=1)


def position_of(lengths_row, global_rows, segments):
    ends_at = ends_of(lengths_row)
    starts_at = ends_at - lengths_row
    picked = segments[:, None] == jnp.arange(lengths_row.shape[0], dtype=jnp.int32)[None, :]
    return global_rows - jnp.sum(jnp.where(picked, starts_at[None, :], 0), axis=1)


def rotary_tables(positions):
    half_dim = HD // 2
    inverse = jnp.power(theta, -jnp.arange(half_dim, dtype=jnp.float32) * (2.0 / HD))
    angle = positions.astype(jnp.float32)[..., None] * inverse
    return (jnp.cos(angle), jnp.sin(angle))


F32 = jnp.float32
BF = jnp.bfloat16
CHUNK = 512
WEIGHTS = ("wa", "wg", "wu", "wd")
QK = (H + KVH) * HD
QKO = QK + H * HD


def dot_nn(left, right):
    return lax.dot_general(left, right, (((1,), (0,)), ((), ())), preferred_element_type=F32)


def dot_nt(left, right):
    return lax.dot_general(left, right, (((1,), (1,)), ((), ())), preferred_element_type=F32)


def rope_lanes(tensor, cosine, sine, sign):
    rows, width = tensor.shape
    lane = lax.broadcasted_iota(jnp.int32, (rows, 2 * HD), 1)
    first = lax.rem(lane, HD) < HD // 2
    out = []
    for i in range(0, width, 2 * HD):
        piece = tensor[:, i : i + 2 * HD]
        other = jnp.where(first, pltpu.roll(piece, 2 * HD - HD // 2, 1), pltpu.roll(piece, HD // 2, 1))
        out.append(piece * cosine + (other * sine) * sign)
    return jnp.concatenate(out, axis=1)


def inverse_of(rows):
    return lax.rsqrt(jnp.mean(rows * rows, axis=1, keepdims=True) + epsilon)


def front_part(r, wait, state):
    gain = r["gains"][0:1, :]
    normed = (state * inverse_of(state) * gain).astype(BF)
    r["normed"][...] = normed
    wait("wa")
    values = dot_nn(normed, r["wa_v"][:, QKO:])
    turned = rope_lanes(dot_nn(normed, r["wa_v"][:, :QK]), r["cos"][...], r["sin"][...], 1.0).astype(BF)
    qw = H * HD
    r["q"][...] = turned[:, :qw]
    r["kv"][...] = jnp.concatenate([turned[:, qw:], values.astype(BF)], axis=1)


def head_rows(tensor, g):
    per = H // KVH
    return jnp.concatenate([tensor[:, (g * per + i) * HD : (g * per + i + 1) * HD] for i in range(per)], axis=0)


def window(r):
    rows = r["mask"].shape[0]
    start = lax.rem(lax.axis_index("tok"), 2) * r["q_in"].shape[0]
    return r["kvw"][pl.ds(pl.multiple_of(start, 128), rows), :]


def attention_part(r):
    per = H // KVH
    kv = window(r)
    q = r["q_in"][...]
    rows = q.shape[0]
    allowed = jnp.concatenate([r["mask"][...]] * per, axis=1) > 0
    mixed_t, logs = [], []
    for g in range(KVH):
        k_g = kv[:, g * HD : (g + 1) * HD]
        v_g = kv[:, (KVH + g) * HD : (KVH + g + 1) * HD]
        scores = jnp.where(allowed, dot_nt(k_g, head_rows(q, g)) * HD**-0.5, masked)
        largest = jnp.max(scores, axis=0, keepdims=True)
        exponent = jnp.exp(scores - largest)
        total = jnp.sum(exponent, axis=0, keepdims=True)
        probs = (exponent * (1.0 / total)).astype(BF)
        mix = dot_nn(v_g.T, probs)
        mixed_t += [mix[:, i * rows : (i + 1) * rows] for i in range(per)]
        logs.append(largest + jnp.log(total))
    r["lse"][...] = jnp.concatenate(logs + [logs[0]] * (r["lse"].shape[0] - KVH), axis=0)
    return jnp.concatenate(mixed_t, axis=0).T.astype(BF)


def rest_part(r, wait):
    state = r["state"][...]
    mixed = attention_part(r)
    r["mixed"][...] = mixed
    wait("wa")
    attn_out = dot_nn(mixed, r["wa_v"][:, QK:QKO])
    middle = state + attn_out
    r["middle"][...] = middle
    normed_two = (middle * inverse_of(middle) * r["gains"][1:2, :]).astype(BF)
    r["normed_two"][...] = normed_two
    wait("wg")
    wait("wu")
    wait("wd")
    ff = r["wg_v"].shape[1]
    mlp = jnp.zeros(state.shape, F32)
    for i in range(0, ff, CHUNK):
        at = slice(i, i + CHUNK)
        gate = dot_nn(normed_two, r["wg_v"][:, at])
        up = dot_nn(normed_two, r["wu_v"][:, at])
        r["gate"][:, at] = gate
        r["up"][:, at] = up
        hidden = (gate * jax.nn.sigmoid(gate) * up).astype(BF)
        r["hidden"][:, at] = hidden
        mlp = mlp + dot_nn(hidden, r["wd_v"][at, :])
    branch = attn_out + mlp.astype(BF).astype(F32)
    r["branch"][...] = branch
    router = jax.nn.sigmoid(jnp.sum(state * r["gains"][2:3, :], axis=1, keepdims=True))
    return state + (r["live"][:, 0:1] * router) * branch


def norm_back(grad, rows, gain):
    inverse = inverse_of(rows)
    scaled = rows * inverse
    weighted = grad * gain
    inner = jnp.mean(weighted * scaled, axis=1, keepdims=True)
    return inverse * (weighted - scaled * inner), jnp.sum(grad * scaled, axis=0, keepdims=True)


def back_part(r, wait, grad_after):
    state, live = r["b_state"][...], r["b_live"][:, 0:1]
    width = state.shape[1]
    router_vec = r["gains"][2:3, :]
    router = jax.nn.sigmoid(jnp.sum(state * router_vec, axis=1, keepdims=True))
    d_branch = (live * router) * grad_after
    d_logit = live * (router * (1.0 - router)) * jnp.sum(r["b_branch"][...] * grad_after, axis=1, keepdims=True)
    d_router = jnp.sum(d_logit * state, axis=0, keepdims=True)
    d_mlp = d_branch.astype(BF)
    r["d_mlp"][...] = d_mlp
    wait("wd")
    wait("wg")
    wait("wu")
    ff = r["wg_v"].shape[1]
    d_two = jnp.zeros(state.shape, F32)
    for i in range(0, ff, CHUNK):
        at = slice(i, i + CHUNK)
        gate, up = r["b_gate"][:, at], r["b_up"][:, at]
        sig = jax.nn.sigmoid(gate)
        d_hidden = dot_nt(d_mlp, r["wd_v"][at, :])
        d_up = (d_hidden * (gate * sig)).astype(BF)
        d_gate = (d_hidden * up * (sig * (1.0 + gate * (1.0 - sig)))).astype(BF)
        r["d_up"][:, at] = d_up
        r["d_gate"][:, at] = d_gate
        d_two = d_two + dot_nt(d_gate, r["wg_v"][:, at]) + dot_nt(d_up, r["wu_v"][:, at])
    d_two = d_two.astype(BF).astype(F32)
    d_middle, d_gain_two = norm_back(d_two, r["b_middle"][...], r["gains"][1:2, :])
    r["acc_out"][1:2, :width] = r["acc"][1:2, :width] + d_gain_two
    r["acc_out"][2:3, :width] = r["acc"][2:3, :width] + d_router
    d_attn = (d_branch + d_middle).astype(BF)
    r["d_attn"][...] = d_attn
    r["d_state"][...] = grad_after + d_logit * router_vec + d_middle
    wait("wa")
    d_mixed = dot_nt(d_attn, r["wa_v"][:, QK:QKO]).astype(BF)

    per = H // KVH
    kv = window(r)
    q = r["q_in"][...]
    rows = q.shape[0]
    allowed = jnp.concatenate([r["mask"][...]] * per, axis=1) > 0
    d_keys, d_values, dq_t = [], [], []
    for g in range(KVH):
        k_g = kv[:, g * HD : (g + 1) * HD]
        v_g = kv[:, (KVH + g) * HD : (KVH + g + 1) * HD]
        q_g, do_g = head_rows(q, g), head_rows(d_mixed, g)
        scores = jnp.where(allowed, dot_nt(k_g, q_g) * HD**-0.5, masked)
        probs = jnp.exp(scores - r["b_lse"][g : g + 1, :])
        d_values.append(dot_nn(probs.astype(BF), do_g))
        d_probs = dot_nt(v_g, do_g)
        d_scores = (probs * (d_probs - jnp.sum(probs * d_probs, axis=0, keepdims=True))).astype(BF)
        d_keys.append(dot_nn(d_scores, q_g) * HD**-0.5)
        dq = dot_nn(k_g.T, d_scores) * HD**-0.5
        dq_t += [dq[:, i * rows : (i + 1) * rows] for i in range(per)]
    d_queries = jnp.concatenate(dq_t + [jnp.zeros((HD, rows), F32)], axis=0).T
    d_queries = rope_lanes(d_queries, r["cos"][...], r["sin"][...], -1.0)
    r["d_q"][...] = d_queries[:, : H * HD].astype(BF)
    start = lax.rem(lax.axis_index("tok"), 2) * rows
    partial = r["dkv"]
    keep = partial.shape[0] - kv.shape[0]
    partial[pl.ds(pl.multiple_of((1 - lax.rem(lax.axis_index("tok"), 2)) * kv.shape[0], 128), keep), :] = jnp.zeros((keep, kv.shape[1]), BF)
    partial[pl.ds(pl.multiple_of(start, 128), kv.shape[0]), :] = jnp.concatenate(d_keys + d_values, axis=1).astype(BF)


def home_part(r, wait):
    half = KVH * HD
    total = r["home"][0].astype(F32)
    for i in range(1, r["home"].shape[0]):
        total = total + r["home"][i].astype(F32)
    rows = total.shape[0]
    padded = jnp.concatenate([total[:, :half], jnp.zeros((rows, half % (2 * HD)), F32)], axis=1)
    d_keys = rope_lanes(padded, r["cos"][...], r["sin"][...], -1.0)[:, :half].astype(BF)
    d_values = total[:, half:].astype(BF)
    wait("wa")
    packed = jnp.concatenate([r["h_dq"][...], d_keys, r["h_d_attn"][...], d_values], axis=1)
    r["d_packed"][...] = packed
    d_normed = dot_nt(packed[:, :QK], r["wa_v"][:, :QK]) + dot_nt(d_values, r["wa_v"][:, QKO:])
    state = r["h_state"][...]
    width = state.shape[1]
    d_in, d_gain = norm_back(d_normed, state, r["gains"][0:1, :])
    r["acc_out"][0:1, :width] = r["acc"][0:1, :width] + d_gain
    return r["h_d_state"][...] + d_in


def stage(name, parts, needed, inputs, outputs, weights, rename=None):
    in_names, out_names = list(inputs), list(outputs)
    w_names = [w for w in needed]

    def body(*refs):
        it = iter(refs)
        r = {n: next(it) for n in in_names}
        for n in w_names:
            r[n + "_v"] = next(it)
        for n in out_names:
            r[n] = next(it)
        parts(r, lambda n: None)

    vm = pl.BlockSpec(memory_space=pltpu.VMEM)
    out = pl.pallas_call(
        body,
        name=name,
        out_shape=tuple(outputs.values()),
        in_specs=[vm] * (len(in_names) + len(w_names)),
        out_specs=tuple([vm] * len(out_names)),
        compiler_params=pltpu.CompilerParams(vmem_limit_bytes=20 * 2**20),
    )(*inputs.values(), *[weights[n] for n in w_names])
    return dict(zip(out_names, out))


def shaped(shape, kind):
    return jax.ShapeDtypeStruct(shape, kind)


def front_outs(rows, width):
    return {"normed": shaped((rows, width), BF), "q": shaped((rows, H * HD), BF), "kv": shaped((rows, 2 * KVH * HD), BF)}


def forward_stage(state, q, kvw, mask, live, tables, gains, weights, last):
    rows, width = state.shape
    ff = weights["wg"].shape[1]
    outs = {
        "mixed": shaped((rows, H * HD), BF), "lse": shaped((8, (H // KVH) * rows), F32), "middle": shaped((rows, width), F32),
        "normed_two": shaped((rows, width), BF), "gate": shaped((rows, ff), F32), "up": shaped((rows, ff), F32),
        "hidden": shaped((rows, ff), BF), "branch": shaped((rows, width), F32),
    }
    if last:
        outs["output"] = shaped((width, rows), BF)
    else:
        outs |= front_outs(rows, width) | {"next": shaped((rows, width), F32)}

    def parts(r, wait):
        state_next = rest_part(r, wait)
        if last:
            r["output"][...] = state_next.T.astype(BF)
        else:
            r["next"][...] = state_next
            front_part(r, wait, state_next)

    needed = ("wa", "wg", "wu", "wd")
    ins = {"state": state, "q_in": q, "kvw": kvw, "mask": mask, "live": live, "cos": tables[0], "sin": tables[1], "gains": gains}
    return stage("forward", parts, needed, ins, outs, weights)


def first_stage(hidden_in, tables, gains, weights):
    width, rows = hidden_in.shape

    def parts(r, wait):
        state = r["hidden"][...].astype(F32).T
        r["state"][...] = state
        front_part(r, wait, state)

    outs = front_outs(rows, width) | {"state": shaped((rows, width), F32)}
    return stage("first", parts, ("wa",), {"hidden": hidden_in, "cos": tables[0], "sin": tables[1], "gains": gains}, outs, weights)


def backward_stage(kept, before, mask, live, tables, gains, acc, weights, cotangent):
    ins = {"cos": tables[0], "sin": tables[1], "gains": gains, "acc": acc}
    outs = {"acc_out": shaped(acc.shape, F32)}
    needed = ()
    rows, width = (kept or before)["state"].shape
    ff = weights["wg"].shape[1]
    kvr = 2 * KVH * HD
    if before is not None:
        ins |= {"home": before["home"], "h_dq": before["d_q"], "h_state": before["state"], "h_d_state": before["d_state"], "h_d_attn": before["d_attn"]}
        outs |= {"d_packed": shaped((rows, QKO + kvr // 2), BF)}
        needed += ("wa",)
    else:
        ins |= {"cot": cotangent}
    if kept is not None:
        ins |= {"b_state": kept["state"], "b_live": live, "b_branch": kept["branch"], "b_gate": kept["gate"], "b_up": kept["up"],
                "b_middle": kept["middle"], "b_lse": kept["lse"], "kvw": kept["kvw"], "q_in": kept["q"], "mask": mask}
        outs |= {"d_mlp": shaped((rows, width), BF), "d_up": shaped((rows, ff), BF), "d_gate": shaped((rows, ff), BF),
                 "d_attn": shaped((rows, width), BF), "d_state": shaped((rows, width), F32), "d_q": shaped((rows, H * HD), BF),
                 "dkv": shaped(kept["kvw"].shape, BF)}
        needed += ("wd", "wg", "wu") + (("wa",) if before is None else ())
    else:
        outs |= {"grad": shaped((width, rows), F32)}

    def parts(r, wait):
        r["acc_out"][...] = r["acc"][...]
        grad = home_part(r, wait) if before is not None else r["cot"][...].astype(F32).T
        if kept is not None:
            back_part(r, wait, grad)
        else:
            r["grad"][...] = grad.T

    return stage("backward", parts, needed, ins, outs, weights)


PARTS = 16
HALF = 480
COLS = 640
STREAMS = (
    ("x", True, 0, 80, 0), ("y", True, 80, 80, 0), ("x", False, 160, 48, 0), ("y", False, 208, 32, 0),
    ("x", True, 240, 80, 1), ("y", True, 320, 80, 1), ("x", False, 400, 32, 1), ("y", False, 432, 48, 1),
)
SLOTS = 4


def place():
    g, t = lax.axis_index("grp"), lax.axis_index("tok")
    return g // 2, lax.rem(g, 2), t // 2, lax.rem(t, 2)


def dev(y, x, z, c):
    return (y * 2 + x, z * 2 + c)


def pick(z, values):
    out = jnp.int32(values[3])
    for i in (2, 1, 0):
        out = jnp.where(z == i, jnp.int32(values[i]), out)
    return out


def copy_to(src, dst, send, recv, device):
    return pltpu.make_async_remote_copy(src_ref=src, dst_ref=dst, send_sem=send, recv_sem=recv, device_id=device, device_id_type=MESH)


def add_rows(dst, src, rows, step):
    def body(i, _):
        at = pl.ds(pl.multiple_of(i * step, step), step)
        dst[at, :] = dst[at, :] + src[at, :]
        return 0

    lax.fori_loop(0, rows // step, body, 0)


def tail_kernel(count, *refs):
    left_refs, refs = refs[: 4 * count], refs[4 * count :]
    right_refs, refs = refs[: 4 * count], refs[4 * count :]
    n_s = len(STREAMS)
    v_ref, o_ref, vo_ref, left_t, right, theirs, mine, other = refs[:8]
    ra, rz, rb = refs[8 : 8 + n_s], refs[8 + n_s : 8 + 2 * n_s], refs[8 + 2 * n_s : 8 + 3 * n_s]
    vrecv, load_sem, core_s, core_r, as_, ar, zs, zr, bs, br, ob, obr, oz, ozr, oa, oar, oc, ocr, vs, vr, own_sem = refs[8 + 3 * n_s :]
    y, x, z, c = place()
    partner = dev(y, x, z, 1 - c)
    across = {"x": dev(y, 1 - x, z, c), "y": dev(1 - y, x, z, c)}
    left_dev, right_dev = dev(y, x, z - 1, c), dev(y, x, z + 1, c)
    at_axis = {"x": x, "y": y}
    order = (pick(z, (3, 3, 0, 0)), pick(z, (2, 0, 3, 1)), pick(z, (1, 2, 1, 2)), z)
    far = dev(y, x, jnp.where(z < 2, z + 2, z - 2), c)
    tokens = left_refs[0].shape[0]

    loads = []
    for p in range(PARTS):
        for i in range(count):
            src = right_refs[(p // 4) * count + i].at[:, pl.ds((p % 4) * COLS, COLS)]
            loads.append(pltpu.make_async_copy(src, right.at[p, pl.ds(i * tokens, tokens)], load_sem.at[p * count + i]))
    for cp in loads:
        cp.start()

    bar = pltpu.get_barrier_semaphore()
    for d in (partner, across["x"], across["y"], far):
        pl.semaphore_signal(bar, inc=1, device_id=d, device_id_type=MESH)

    @pl.when(z > 0)
    def _():
        pl.semaphore_signal(bar, inc=1, device_id=left_dev, device_id_type=MESH)

    @pl.when(z < 3)
    def _():
        pl.semaphore_signal(bar, inc=1, device_id=right_dev, device_id_type=MESH)

    for j in range(4):
        left_t[j] = jnp.concatenate([each[...].astype(F32).T.astype(BF) for each in left_refs[j * count : (j + 1) * count]], axis=1)
    for cp in loads:
        cp.wait()
    pl.semaphore_wait(bar, 4 + (z > 0).astype(jnp.int32) + (z < 3).astype(jnp.int32))

    def part_xy(px, py, pz):
        return (px * 2 + py) * 4 + pz

    def part_of(s, pa, pb, pz):
        return part_xy(pa, pb, pz) if STREAMS[s][0] == "x" else part_xy(pb, pa, pz)

    def ab(s):
        a = STREAMS[s][0]
        b = "y" if a == "x" else "x"
        return at_axis[a], at_axis[b], across[a], across[b]

    waits = []
    seq = [(k, i, px, py) for k in range(4) for i, (px, py) in enumerate(((1 - x, 1 - y), (1 - x, y), (x, 1 - y), (x, y)))]

    def core_copy(j):
        k, _, px, py = seq[j]
        p = part_xy(px, py, order[k])
        return copy_to(theirs.at[j % SLOTS, pl.ds(pl.multiple_of((1 - c) * HALF, 16), HALF)], other.at[p], core_s.at[j], core_r.at[p], partner)

    def core_make(j):
        k, _, px, py = seq[j]
        p = part_xy(px, py, order[k])
        if j >= SLOTS:
            core_copy(j - SLOTS).wait_send()
        which = jnp.where(p < 8, 0, jnp.where(p < 12, 1, jnp.where(p < 14, 2, 3)))
        split = 2 * COLS - 2 * HALF
        theirs[j % SLOTS] = dot_nn(left_t[which], right[p]).astype(BF)

        @pl.when(p == PARTS - 1)
        def _():
            theirs[j % SLOTS, :, COLS - split :] = dot_nn(left_t[2], right[p, :, COLS - split :]).astype(BF)

        core_copy(j).start()

    def core_add(j):
        k, i, px, py = seq[j]
        p = part_xy(px, py, order[k])
        core_copy(j).wait_recv()
        mine[p] = theirs[j % SLOTS, pl.ds(pl.multiple_of(c * HALF, 16), HALF), :] + other[p]

    def a_copy(s, pb, pz):
        a, b, to_a, _ = ab(s)
        _, _, r0, n, _ = STREAMS[s]
        return copy_to(mine.at[part_of(s, 1 - a, pb, pz), pl.ds(r0, n)], ra[s].at[pb * 4 + pz], as_.at[s, pb * 4 + pz], ar.at[s, pb * 4 + pz], to_a)

    def a_send(j, batch):
        k, i, px, py = seq[j]
        for s in range(n_s):
            a_axis = STREAMS[s][0]
            if STREAMS[s][4] == batch and (i == 0 or (i == 1 and a_axis == "x") or (i == 2 and a_axis == "y")):
                cp = a_copy(s, py if a_axis == "x" else px, order[k])
                cp.start()
                waits.append(cp)

    def z_index(s, pb, slot):
        return pb * 5 + slot if STREAMS[s][1] else slot

    def z_copy(s, pb, pz, to_right):
        a, b, _, _ = ab(s)
        _, _, r0, n, _ = STREAMS[s]
        src = mine.at[part_of(s, a, pb, pz), pl.ds(r0, n)]
        i = z_index(s, pb, pz if to_right else jnp.where(pz == z - 1, 4, pz))
        return copy_to(src, rz[s].at[i], zs.at[s, i], zr.at[s, i], right_dev if to_right else left_dev)

    def z_take(s, pb, slot):
        a, _, _, _ = ab(s)
        _, _, r0, n, _ = STREAMS[s]
        i = z_index(s, pb, slot)
        copy_to(mine.at[0, pl.ds(r0, n)], rz[s].at[i], zs.at[s, i], zr.at[s, i], left_dev).wait_recv()
        pz = z if slot is z or isinstance(slot, int) else slot
        add_rows(mine.at[part_of(s, a, pb, pz), pl.ds(r0, n)], rz[s].at[i], n, 16)

    def z_step(s, pb, k):
        pz = order[k]
        if k < 3:
            up = jnp.where(pz > z, (z > 0).astype(jnp.int32), (z < 3).astype(jnp.int32))

            @pl.when(up == 1)
            def _():
                z_take(s, pb, pz)

            @pl.when(pz > z)
            def _():
                z_copy(s, pb, pz, True).start()

            @pl.when(pz < z)
            def _():
                z_copy(s, pb, pz, False).start()
        else:
            @pl.when(z > 0)
            def _():
                z_take(s, pb, z)

            @pl.when(z < 3)
            def _():
                z_take(s, pb, 4)

    def z_drain(s, pb, k):
        pz = order[k]

        @pl.when(pz > z)
        def _():
            z_copy(s, pb, pz, True).wait_send()

        @pl.when(pz < z)
        def _():
            z_copy(s, pb, pz, False).wait_send()

    def a_step(s, pb, k):
        a, b, to_a, _ = ab(s)
        _, _, r0, n, _ = STREAMS[s]
        pz = order[k]
        a_copy(s, pb, pz).wait_recv()
        add_rows(mine.at[part_of(s, a, pb, pz), pl.ds(r0, n)], ra[s].at[pb * 4 + pz], n, 16)

    def b_copy(s, pz):
        a, b, _, to_b = ab(s)
        _, second_z, r0, n, _ = STREAMS[s]
        i = 0 if second_z else pz
        return copy_to(mine.at[part_of(s, a, 1 - b, pz), pl.ds(r0, n)], rb[s].at[i], bs.at[s, i], br.at[s, i], to_b)

    def b_step(s, pz):
        a, b, _, _ = ab(s)
        _, second_z, r0, n, _ = STREAMS[s]
        i = 0 if second_z else pz
        b_copy(s, pz).wait_recv()
        add_rows(mine.at[part_of(s, a, b, pz), pl.ds(r0, n)], rb[s].at[i], n, 16)

    def of_batch(batch):
        return [s for s in range(n_s) if STREAMS[s][4] == batch]

    def first_step(batch, k):
        for s in of_batch(batch):
            _, b, _, _ = ab(s)
            a_step(s, 1 - b, k)
            if STREAMS[s][1]:
                z_step(s, 1 - b, k)
                a_step(s, b, k)
                z_step(s, b, k)
                if k == 3:
                    cp = b_copy(s, z)
                    cp.start()
                    waits.append(cp)
            else:
                cp = b_copy(s, order[k])
                cp.start()
                waits.append(cp)
                a_step(s, b, k)

    def second_step(batch, k):
        for s in of_batch(batch):
            _, b, _, _ = ab(s)
            if not STREAMS[s][1]:
                b_step(s, order[k])
                z_step(s, b, k)

    def vec_copy(i):
        to = (partner, across["x"], across["y"], dev(y, x, jnp.where(lax.rem(z, 2) == 0, z + 1, z - 1), c), far)[i]
        return copy_to(vo_ref, vrecv.at[i], vs.at[i], vr.at[i], to)

    def vec_end(i):
        vec_copy(i).wait()
        vo_ref[...] = vo_ref[...] + vrecv[i]

    half0 = c * HALF

    def out_at(s, p):
        _, _, r0, n, _ = STREAMS[s]
        return o_ref.at[p, pl.ds(pl.multiple_of(half0 + r0, 16), n)]

    def mine_at(s, p):
        _, _, r0, n, _ = STREAMS[s]
        return mine.at[p, pl.ds(r0, n)]

    def go(cp):
        cp.start()
        waits.append(cp)

    def to_core(s, p, src):
        return copy_to(src, out_at(s, p), oc.at[s, p], ocr.at[s, p], partner)

    def to_a(s, pb, pz, src):
        a, b, na, _ = ab(s)
        return copy_to(src, out_at(s, part_of(s, a, pb, pz)), oa.at[s, pb * 4 + pz], oar.at[s, pb * 4 + pz], na)

    def to_b(s, pz, src):
        a, b, _, nb = ab(s)
        return copy_to(src, out_at(s, part_of(s, a, b, pz)), ob.at[s, pz], obr.at[s, pz], nb)

    def to_z(s, pb, pz, src, to_right):
        a, b, _, _ = ab(s)
        i = pb * 8 + pz * 2 + (0 if to_right else 1)
        return copy_to(src, out_at(s, part_of(s, a, pb, pz)), oz.at[s, i], ozr.at[s, pb * 4 + pz], right_dev if to_right else left_dev)

    def spread_z(s, pb, pz, src, sides):
        if 0 in sides:
            @pl.when(z < 3)
            def _():
                to_z(s, pb, pz, src, True).start()
        if 1 in sides:
            @pl.when(z > 0)
            def _():
                to_z(s, pb, pz, src, False).start()

    def finish(batch):
        for s in of_batch(batch):
            a, b, _, _ = ab(s)
            p = part_of(s, a, b, z)
            b_step(s, z)
            if not STREAMS[s][1]:
                z_step(s, b, 3)
            src = mine_at(s, p)
            if STREAMS[s][1]:
                go(to_b(s, z, src))
                spread_z(s, b, z, src, (0, 1))
            else:
                spread_z(s, b, z, src, (0, 1))
                go(to_b(s, z, src))
            go(to_a(s, b, z, src))
            go(to_core(s, p, src))
            pltpu.make_async_copy(src, out_at(s, p), own_sem.at[s]).start()

    def got_b(s, pz):
        a, b, _, _ = ab(s)
        p = part_of(s, a, 1 - b, pz)
        src = out_at(s, p)
        copy_to(src, src, ob.at[s, pz], obr.at[s, pz], partner).wait_recv()
        if STREAMS[s][1]:
            spread_z(s, 1 - b, pz, src, (0, 1))
        to_a(s, 1 - b, pz, src).start()
        to_core(s, p, src).start()

    def got_z(s, pb, pz, from_left):
        a, b, _, _ = ab(s)
        p = part_of(s, a, pb, pz)
        src = out_at(s, p)
        copy_to(src, src, oz.at[s, 0], ozr.at[s, pb * 4 + pz], partner).wait_recv()
        spread_z(s, pb, pz, src, (0,) if from_left else (1,))
        to_a(s, pb, pz, src).start()
        if not STREAMS[s][1]:
            to_b(s, pz, src).start()
        to_core(s, p, src).start()

    def got_a(s, pb, pz):
        a, b, _, _ = ab(s)
        p = part_of(s, 1 - a, pb, pz)
        src = out_at(s, p)
        copy_to(src, src, oa.at[s, pb * 4 + pz], oar.at[s, pb * 4 + pz], partner).wait_recv()
        to_core(s, p, src).start()

    def gather_b(batch):
        for s in of_batch(batch):
            got_b(s, z)

    def gather_a(batch):
        for s in of_batch(batch):
            _, b, _, _ = ab(s)
            got_a(s, b, z)
            got_a(s, 1 - b, z)

    def from_side(t, side):
        return (z - t, z >= t) if side == 0 else (z + t, z + t <= 3)

    def gather_z(batch, t):
        for side in (0, 1):
            pz, there = from_side(t, side)

            @pl.when(there)
            def _():
                for s in of_batch(batch):
                    _, b, _, _ = ab(s)
                    got_z(s, b, pz, side == 0)
                    if STREAMS[s][1]:
                        got_z(s, 1 - b, pz, side == 0)

    def gather_rest(batch, t):
        for side in (0, 1):
            pz, there = from_side(t, side)

            @pl.when(there)
            def _():
                for s in of_batch(batch):
                    if not STREAMS[s][1]:
                        got_b(s, pz)
                for s in of_batch(batch):
                    _, b, _, _ = ab(s)
                    got_a(s, b, pz)
                    got_a(s, 1 - b, pz)

    vo_ref[...] = v_ref[...]
    vec_copy(0).start()

    def group(k, batches=(0,)):
        for i in range(4):
            j = k * 4 + i
            core_make(j)
            if j > 0:
                core_add(j - 1)
                a_send(j - 1, 0)
        if k == 3:
            core_add(15)
            a_send(15, 0)

    group(0)
    vec_end(0)
    vec_copy(1).start()
    group(1)
    vec_end(1)
    vec_copy(2).start()
    first_step(0, 0)
    group(2)
    vec_end(2)
    vec_copy(3).start()
    second_step(0, 0)
    first_step(0, 1)
    group(3)
    vec_end(3)
    vec_copy(4).start()
    second_step(0, 1)
    for j in range(0, 4):
        a_send(j, 1)
    first_step(0, 2)
    vec_end(4)
    second_step(0, 2)
    for j in range(4, 8):
        a_send(j, 1)
    first_step(0, 3)
    first_step(1, 0)
    finish(0)
    for j in range(8, 12):
        a_send(j, 1)
    second_step(1, 0)
    gather_b(0)
    first_step(1, 1)
    second_step(1, 1)
    gather_z(0, 1)
    for j in range(12, 16):
        a_send(j, 1)
    gather_a(0)
    first_step(1, 2)
    second_step(1, 2)
    gather_z(0, 2)
    gather_rest(0, 1)
    first_step(1, 3)
    finish(1)
    gather_z(0, 3)
    gather_rest(0, 2)
    gather_b(1)
    gather_z(1, 1)
    gather_rest(0, 3)
    gather_a(1)
    gather_z(1, 2)
    gather_rest(1, 1)
    gather_z(1, 3)
    gather_rest(1, 2)
    gather_rest(1, 3)

    for cp in waits:
        cp.wait_send()
    for j in range(PARTS - SLOTS, PARTS):
        core_copy(j).wait_send()
    for s in range(n_s):
        a, b, _, _ = ab(s)
        pltpu.make_async_copy(mine_at(s, part_of(s, a, b, z)), out_at(s, part_of(s, a, b, z)), own_sem.at[s]).wait()
        pbs = (b, 1 - b) if STREAMS[s][1] else (b,)
        for pb in pbs:
            for k in range(3):
                z_drain(s, pb, k)
        for pz in range(4):
            for pb in pbs:
                src = out_at(s, part_of(s, a, pb, pz))

                @pl.when((z >= pz) & (z < 3))
                def _():
                    to_z(s, pb, pz, src, True).wait_send()

                @pl.when((z <= pz) & (z > 0))
                def _():
                    to_z(s, pb, pz, src, False).wait_send()
            for pb in (0, 1):
                src = out_at(s, part_of(s, a, pb, pz))

                @pl.when(jnp.logical_not((pb == b) & (pz == z)))
                def _():
                    to_a(s, pb, pz, src).wait_send()
            if not STREAMS[s][1]:
                @pl.when(z != pz)
                def _():
                    to_b(s, pz, out_at(s, 0)).wait_send()
        for p in range(16):
            src = out_at(s, p)

            @pl.when(p != part_of(s, a, b, z))
            def _():
                to_core(s, p, src).wait_send()
            _, _, r0, n, _ = STREAMS[s]
            dst = o_ref.at[p, pl.ds(pl.multiple_of((1 - c) * HALF + r0, 16), n)]
            copy_to(dst, dst, oc.at[s, p], ocr.at[s, p], partner).wait_recv()


def summed_gradients(lefts, rights, vectors):
    dma = pltpu.SemaphoreType.DMA
    count = len(lefts[0])
    tokens, width = lefts[0][0].shape
    rows = count * tokens
    n_s = len(STREAMS)
    vm = pl.BlockSpec(memory_space=pltpu.VMEM)
    return pl.pallas_call(
        lambda *refs: tail_kernel(count, *refs),
        name="summed_gradients",
        out_shape=(jax.ShapeDtypeStruct((PARTS, width, COLS), BF), jax.ShapeDtypeStruct(vectors.shape, F32)),
        in_specs=[vm] * (4 * count) + [pl.BlockSpec(memory_space=pl.ANY)] * (4 * count) + [vm],
        out_specs=(pl.BlockSpec(memory_space=pl.ANY), vm),
        scratch_shapes=[
            pltpu.VMEM((4, width, rows), BF), pltpu.VMEM((PARTS, rows, COLS), BF), pltpu.VMEM((SLOTS, 2 * HALF, COLS), BF),
            pltpu.VMEM((PARTS, HALF, COLS), BF), pltpu.VMEM((PARTS, HALF, COLS), BF),
            *[pltpu.VMEM((8, s[3], COLS), BF) for s in STREAMS],
            *[pltpu.VMEM((10 if s[1] else 5, s[3], COLS), BF) for s in STREAMS],
            *[pltpu.VMEM((1 if s[1] else 4, s[3], COLS), BF) for s in STREAMS],
            pltpu.VMEM((5, *vectors.shape), F32),
            dma((PARTS * count,)), dma((16,)), dma((16,)),
            dma((n_s, 8)), dma((n_s, 8)), dma((n_s, 10)), dma((n_s, 10)), dma((n_s, 4)), dma((n_s, 4)),
            dma((n_s, 4)), dma((n_s, 4)), dma((n_s, 16)), dma((n_s, 8)), dma((n_s, 8)), dma((n_s, 8)), dma((n_s, 16)), dma((n_s, 16)),
            dma((5,)), dma((5,)), dma((n_s,)),
        ],
        compiler_params=pltpu.CompilerParams(collective_id=1, has_side_effects=True, vmem_limit_bytes=60 * 2**20),
    )(*[a for l in lefts for a in l], *[a for l in rights for a in l], vectors)


QUARTERS = 4


def gather_kernel(*refs):
    ins, outs = refs[:5], refs[5:10]
    zs, xs, ys, cs, got, cgot, own_s, own_c, own_r, ss, sr, sc, scr = refs[10:]
    y, x, z, c = place()
    partner, to_x, to_y = dev(y, x, z, 1 - c), dev(y, 1 - x, z, c), dev(1 - y, x, z, c)
    left, right = dev(y, x, z - 1, c), dev(y, x, z + 1, c)
    quarter = (x * 2 + y, (1 - x) * 2 + y, x * 2 + (1 - y), (1 - x) * 2 + (1 - y))
    lasting = []

    def go(cp, when=None):
        if when is None:
            cp.start()
        else:
            @pl.when(when)
            def _():
                cp.start()
        lasting.append((cp, when))

    def cut(ref, m, q):
        if m < 3:
            n = ref.shape[1] // QUARTERS
            return ref.at[:, pl.ds(pl.multiple_of(q * n, 128), n)]
        n = ref.shape[0] // QUARTERS
        return ref.at[pl.ds(pl.multiple_of(q * n, 16), n), :]

    def out_piece(m, kind, zz, core):
        return cut(outs[m].at[zz * 2 + core], m, quarter[kind])

    bar = pltpu.get_barrier_semaphore()
    for d in (partner, to_x, to_y):
        pl.semaphore_signal(bar, inc=1, device_id=d, device_id_type=MESH)

    @pl.when(z > 0)
    def _():
        pl.semaphore_signal(bar, inc=1, device_id=left, device_id_type=MESH)

    @pl.when(z < 3)
    def _():
        pl.semaphore_signal(bar, inc=1, device_id=right, device_id_type=MESH)

    pl.semaphore_wait(bar, 3 + (z > 0).astype(jnp.int32) + (z < 3).astype(jnp.int32))

    def small_copy(zz, core, src, device, sems):
        return copy_to(src, outs[4].at[zz * 2 + core], sems[0], sems[1], device)

    go(small_copy(z, c, ins[4], right, (ss.at[z, 0], sr.at[z])), z < 3)
    go(small_copy(z, c, ins[4], left, (ss.at[z, 1], sr.at[z])), z > 0)
    go(small_copy(z, c, ins[4], partner, (sc.at[z], scr.at[z])))
    for m in range(4):
        src, dst = cut(ins[m], m, quarter[0]), out_piece(m, 0, z, c)
        go(copy_to(src, dst, zs.at[m, z, 0], got.at[0, m, z], right), z < 3)
        go(copy_to(src, dst, zs.at[m, z, 1], got.at[0, m, z], left), z > 0)
    for m in range(4):
        go(copy_to(ins[m], outs[m].at[z * 2 + c], own_c.at[m], own_r.at[m], partner))
    local = [pltpu.make_async_copy(ins[m], outs[m].at[z * 2 + c], own_s.at[m]) for m in range(5)]
    for cp in local:
        cp.start()

    steps = [(t, side) for t in (1, 2, 3) for side in (0, 1)]

    def source(t, side):
        return (z - t, z >= t) if side == 0 else (z + t, z + t <= 3)

    def wait_for(kind, m, zz):
        piece = out_piece(m, kind, zz, c)
        copy_to(piece, piece, cs.at[kind, m, zz], got.at[kind, m, zz], partner).wait_recv()
        return piece

    def each(kind, m, t, side):
        zz, there = source(t, side)
        onward = (z < 3) if side == 0 else (z > 0)

        @pl.when(there)
        def _():
            piece = wait_for(kind, m, zz)
            first_x = m % 2 == 0
            sends = []
            if kind == 0:
                on = copy_to(piece, piece, zs.at[m, zz, side], got.at[0, m, zz], right if side == 0 else left)

                @pl.when(onward)
                def _():
                    on.start()

                sends.append(copy_to(piece, piece, xs.at[0, m, zz], got.at[1, m, zz], to_x))
                sends.append(copy_to(piece, piece, ys.at[0, m, zz], got.at[2, m, zz], to_y))
            elif kind == 1 and first_x:
                sends.append(copy_to(piece, piece, ys.at[1, m, zz], got.at[3, m, zz], to_y))
            elif kind == 2 and not first_x:
                sends.append(copy_to(piece, piece, xs.at[1, m, zz], got.at[3, m, zz], to_x))
            sends.append(copy_to(piece, piece, cs.at[kind, m, zz], cgot.at[kind, m, zz], partner))
            for cp in sends:
                cp.start()

        lasting.append((("s", kind, m, t, side), there))
        if kind == 0:
            lasting.append((("z", m, t, side), there & onward))

    def small_step(t, side):
        zz, there = source(t, side)

        @pl.when(there)
        def _():
            piece = outs[4].at[zz * 2 + c]
            copy_to(piece, piece, sc.at[zz], sr.at[zz], partner).wait_recv()

            @pl.when((z < 3) if side == 0 else (z > 0))
            def _():
                small_copy(zz, c, piece, right if side == 0 else left, (ss.at[zz, side], sr.at[zz])).start()

            small_copy(zz, c, piece, partner, (sc.at[zz], scr.at[zz])).start()

        lasting.append((("m", t, side), there))

    for t, side in steps:
        small_step(t, side)
    for turn in range(4 + 2):
        for t, side in steps:
            if turn < 4:
                each(0, turn, t, side)
            if 1 <= turn < 5:
                m = turn - 1
                relay, leaf = (1, 2) if m % 2 == 0 else (2, 1)
                each(relay, m, t, side)
                each(leaf, m, t, side)
            if turn >= 2:
                each(3, turn - 2, t, side)

    for cp, when in lasting:
        if not isinstance(cp, tuple):
            if when is None:
                cp.wait_send()
            else:
                @pl.when(when)
                def _():
                    cp.wait_send()
        elif cp[0] == "z":
            _, m, t, side = cp
            zz, _ = source(t, side)
            piece = out_piece(m, 0, zz, c)

            @pl.when(when)
            def _():
                copy_to(piece, piece, zs.at[m, zz, side], got.at[0, m, zz], partner).wait_send()
        elif cp[0] == "m":
            _, t, side = cp
            zz, _ = source(t, side)
            piece = outs[4].at[zz * 2 + c]

            @pl.when(when)
            def _():
                @pl.when((z < 3) if side == 0 else (z > 0))
                def _():
                    small_copy(zz, c, piece, partner, (ss.at[zz, side], sr.at[zz])).wait_send()

                small_copy(zz, c, piece, partner, (sc.at[zz], scr.at[zz])).wait_send()
                other = outs[4].at[zz * 2 + 1 - c]
                copy_to(other, other, sc.at[zz], scr.at[zz], partner).wait_recv()
        else:
            _, kind, m, t, side = cp
            zz, _ = source(t, side)
            piece = out_piece(m, kind, zz, c)
            other = out_piece(m, kind, zz, 1 - c)
            first_x = m % 2 == 0

            @pl.when(when)
            def _():
                if kind == 0 or (kind == 2 and not first_x):
                    copy_to(piece, piece, xs.at[min(kind, 1), m, zz], got.at[1, m, zz], partner).wait_send()
                if kind == 0 or (kind == 1 and first_x):
                    copy_to(piece, piece, ys.at[min(kind, 1), m, zz], got.at[1, m, zz], partner).wait_send()
                copy_to(piece, piece, cs.at[kind, m, zz], cgot.at[kind, m, zz], partner).wait_send()
                copy_to(other, other, cs.at[kind, m, zz], cgot.at[kind, m, zz], partner).wait_recv()

    for m in range(4):
        other = outs[m].at[z * 2 + 1 - c]
        copy_to(other, other, own_c.at[m], own_r.at[m], partner).wait_recv()
    other = outs[4].at[z * 2 + 1 - c]
    copy_to(other, other, sc.at[z], scr.at[z], partner).wait_recv()
    for cp in local:
        cp.wait()


def gather_rows(shards):
    dma = pltpu.SemaphoreType.DMA
    return pl.pallas_call(
        gather_kernel,
        name="gather_rows",
        out_shape=tuple(jax.ShapeDtypeStruct((8, *s.shape), s.dtype) for s in shards),
        in_specs=[pl.BlockSpec(memory_space=pl.ANY)] * 5,
        out_specs=tuple([pl.BlockSpec(memory_space=pl.ANY)] * 5),
        scratch_shapes=[
            dma((4, 4, 2)), dma((2, 4, 4)), dma((2, 4, 4)), dma((4, 4, 4)), dma((4, 4, 4)), dma((4, 4, 4)),
            dma((5,)), dma((4,)), dma((4,)), dma((4, 2)), dma((4,)), dma((4,)), dma((4,)),
        ],
        compiler_params=pltpu.CompilerParams(collective_id=4, has_side_effects=True),
    )(*shards)


def keys_kernel(chips, back, kv_ref, w_ref, s_right, r_left, s_core, r_core):
    g, t = lax.axis_index("grp"), lax.axis_index("tok")
    z, c = t // 2, lax.rem(t, 2)
    rows = kv_ref.shape[0]
    partner, right = (g, z * 2 + 1 - c), (g, t + 2)

    def slot(d, core):
        return w_ref.at[pl.ds(pl.multiple_of(((back - d) * 2 + core) * rows, 128), rows)]

    bar = pltpu.get_barrier_semaphore()
    pl.semaphore_signal(bar, inc=1, device_id=partner, device_id_type=MESH)

    @pl.when(z > 0)
    def _():
        pl.semaphore_signal(bar, inc=1, device_id=(g, t - 2), device_id_type=MESH)

    def along(d, src):
        return copy_to(src, slot(d, c), s_right.at[d - 1], r_left.at[d - 1], right)

    def beside(d, src):
        return copy_to(src, slot(d, c), s_core.at[d], r_core.at[d], partner)

    own = w_ref.at[pl.ds(pl.multiple_of((back * 2 + c) * rows, 128), rows)]
    own[...] = kv_ref[...]
    for d in range(1, back + 1):
        @pl.when(z < d)
        def _():
            for core in (0, 1):
                slot(d, core)[...] = jnp.zeros(kv_ref.shape, kv_ref.dtype)

    pl.semaphore_wait(bar, 1 + (z < chips - 1).astype(jnp.int32))

    @pl.when(z < chips - 1)
    def _():
        along(1, kv_ref).start()

    beside(0, kv_ref).start()
    for d in range(1, back + 1):
        @pl.when(z >= d)
        def _():
            along(d, slot(d, c)).wait_recv()
            if d < back:
                @pl.when(z < chips - 1)
                def _():
                    along(d + 1, slot(d, c)).start()
            beside(d, slot(d, c)).start()

    def mine_to(d):
        return copy_to(slot(d, 1 - c), slot(d, 1 - c), s_core.at[d], r_core.at[d], partner)

    mine_to(0).wait_recv()
    beside(0, kv_ref).wait_send()

    @pl.when(z < chips - 1)
    def _():
        along(1, kv_ref).wait_send()

    for d in range(1, back + 1):
        @pl.when(z >= d)
        def _():
            mine_to(d).wait_recv()
            beside(d, slot(d, c)).wait_send()
            if d < back:
                @pl.when(z < chips - 1)
                def _():
                    along(d + 1, slot(d, c)).wait_send()


def exchange_keys(kv, n_tok, nback):
    back = nback // 2
    rows = kv.shape[0]
    dma = pltpu.SemaphoreType.DMA
    return pl.pallas_call(
        lambda *refs: keys_kernel(n_tok // 2, back, *refs),
        name="exchange_keys",
        out_shape=jax.ShapeDtypeStruct(((2 * back + 2) * rows, kv.shape[1]), kv.dtype),
        in_specs=[pl.BlockSpec(memory_space=pltpu.VMEM)],
        out_specs=pl.BlockSpec(memory_space=pltpu.VMEM),
        scratch_shapes=[dma((back,)), dma((back,)), dma((back + 1,)), dma((back + 1,))],
        compiler_params=pltpu.CompilerParams(collective_id=2, has_side_effects=True, vmem_limit_bytes=12 * 2**20),
    )(kv)


def home_kernel(chips, back, p_ref, h_ref, beside_in, sums, after_in, s_left, r_right, s_core, r_core):
    g, t = lax.axis_index("grp"), lax.axis_index("tok")
    z, c = t // 2, lax.rem(t, 2)
    rows = h_ref.shape[1]
    partner, left = (g, z * 2 + 1 - c), (g, t - 2)

    def block(d, core):
        return p_ref.at[pl.ds(pl.multiple_of(((back - d) * 2 + core) * rows, 128), rows)]

    bar = pltpu.get_barrier_semaphore()
    pl.semaphore_signal(bar, inc=1, device_id=partner, device_id_type=MESH)

    @pl.when(z < chips - 1)
    def _():
        pl.semaphore_signal(bar, inc=1, device_id=(g, t + 2), device_id_type=MESH)

    pl.semaphore_wait(bar, 1 + (z > 0).astype(jnp.int32))

    def beside(d):
        return copy_to(block(d, 1 - c), beside_in.at[d], s_core.at[d], r_core.at[d], partner)

    def along(d):
        return copy_to(sums.at[d - 1], after_in.at[d - 1], s_left.at[d - 1], r_right.at[d - 1], left)

    for d in range(back, 0, -1):
        @pl.when(z >= d)
        def _():
            beside(d).start()
    beside(0).start()
    for d in range(back, 0, -1):
        @pl.when(z >= d)
        def _():
            beside(d).wait_recv()
            sums[d - 1] = (block(d, c)[...].astype(F32) + beside_in[d].astype(F32)).astype(BF)
            if d < back:
                @pl.when(z < chips - 1)
                def _():
                    along(d + 1).wait_recv()
                    sums[d - 1] = (sums[d - 1].astype(F32) + after_in[d].astype(F32)).astype(BF)
            along(d).start()
    beside(0).wait_recv()
    h_ref[0] = block(0, c)[...].astype(F32) + beside_in[0].astype(F32)

    @pl.when(z < chips - 1)
    def _():
        along(1).wait_recv()
        h_ref[0] = h_ref[0] + after_in[0].astype(F32)

    beside(0).wait_send()
    for d in range(1, back + 1):
        @pl.when(z >= d)
        def _():
            beside(d).wait_send()
            along(d).wait_send()


def exchange_home(partial, n_tok, nback):
    back = nback // 2
    rows = partial.shape[0] // (2 * back + 2)
    width = partial.shape[1]
    dma = pltpu.SemaphoreType.DMA
    return pl.pallas_call(
        lambda *refs: home_kernel(n_tok // 2, back, *refs),
        name="exchange_home",
        out_shape=jax.ShapeDtypeStruct((1, rows, width), F32),
        in_specs=[pl.BlockSpec(memory_space=pltpu.VMEM)],
        out_specs=pl.BlockSpec(memory_space=pltpu.VMEM),
        scratch_shapes=[
            pltpu.VMEM((back + 1, rows, width), BF), pltpu.VMEM((back, rows, width), BF), pltpu.VMEM((back, rows, width), BF),
            dma((back,)), dma((back,)), dma((back + 1,)), dma((back + 1,)),
        ],
        compiler_params=pltpu.CompilerParams(collective_id=3, has_side_effects=True, vmem_limit_bytes=12 * 2**20),
    )(partial)


ROW_NAMES = ("normed_two", "d_mlp", "normed", "mixed", "d_gate", "d_up", "hidden", "d_packed")


def grads_kernel(count, *refs):
    r = {name: refs[i * count : (i + 1) * count] for i, name in enumerate(ROW_NAMES)}
    g_ref, left_t, slots, sems = refs[len(ROW_NAMES) * count :]
    for i, name in enumerate(ROW_NAMES[:4]):
        left_t[i] = jnp.concatenate([each[...].astype(F32).T.astype(BF) for each in r[name]], axis=1)

    def out_copy(p):
        return pltpu.make_async_copy(slots.at[p % 2], g_ref.at[p], sems.at[p % 2])

    split = 2 * COLS - left_t.shape[1]
    for p in range(PARTS):
        if p >= 2:
            out_copy(p - 2).wait()
        low = (p % 4) * COLS
        right = jnp.concatenate([each[:, low : low + COLS] for each in r[ROW_NAMES[4 + p // 4]]], axis=0)
        result = dot_nn(left_t[((0,) * 8 + (1,) * 4 + (2, 2, 3, 3))[p]], right)
        if p == PARTS - 1:
            result = jnp.concatenate([result[:, : COLS - split], dot_nn(left_t[2], right[:, COLS - split :])], axis=1)
        slots[p % 2] = result.astype(BF)
        out_copy(p).start()
    out_copy(PARTS - 2).wait()
    out_copy(PARTS - 1).wait()


def weight_gradients(rows):
    count = len(rows["d_mlp"])
    flat = [each for name in ROW_NAMES for each in rows[name]]
    tokens, width = rows["normed"][0].shape
    return pl.pallas_call(
        lambda *refs: grads_kernel(count, *refs),
        name="weight_gradients",
        out_shape=jax.ShapeDtypeStruct((PARTS, width, COLS), BF),
        in_specs=[pl.BlockSpec(memory_space=pltpu.VMEM)] * len(flat),
        out_specs=pl.BlockSpec(memory_space=pl.ANY),
        scratch_shapes=[pltpu.VMEM((4, width, count * tokens), BF), pltpu.VMEM((2, width, COLS), BF), pltpu.SemaphoreType.DMA((2,))],
        compiler_params=pltpu.CompilerParams(vmem_limit_bytes=60 * 2**20),
    )(*flat)


def spread_kernel(p_ref, gate, up, down, d_q, d_k, d_v, d_o, came, wide, q_full, k_full, o_full, v_full, sem_in, sem_out, sem_full):
    width = q_full.shape[0]
    order = [12, 13, 14, 15] + list(range(12))

    def fetch(i):
        return pltpu.make_async_copy(p_ref.at[order[i]], came.at[i % 3], sem_in.at[i % 3])

    def put(i):
        p = order[i]
        return pltpu.make_async_copy(wide.at[i % 2], (gate, up, down)[p // 4].at[:, pl.ds((p % 4) * COLS, COLS)], sem_out.at[i % 2])

    fulls = [(q_full, d_q), (k_full, d_k), (o_full, d_o), (v_full, d_v)]

    def put_full(j):
        return pltpu.make_async_copy(fulls[j][0], fulls[j][1], sem_full.at[j])

    fetch(0).start()
    fetch(1).start()
    for i, p in enumerate(order):
        if i + 2 < len(order):
            fetch(i + 2).start()
        fetch(i).wait()
        part = came.at[i % 3]
        if i >= 6:
            put(i - 2).wait()
        if p >= 12:
            full, other = (q_full, k_full) if p < 14 else (o_full, v_full)
            if p % 2 == 0:
                full[:, :COLS] = part[...].astype(F32)
            else:
                got = part[...].astype(F32)
                full[:, COLS:] = got[:, : width - COLS]
                other[...] = got[:, width - COLS :].T
                put_full(0 if p < 14 else 2).start()
                put_full(1 if p < 14 else 3).start()
        else:
            wide[i % 2] = part[...].astype(F32)
            put(i).start()
    put(len(order) - 2).wait()
    put(len(order) - 1).wait()
    for j in range(4):
        put_full(j).wait()


def spread_out(parts):
    n, width, cols = parts.shape
    kv = 2 * cols - width
    ff = 4 * cols
    shapes = [(width, ff), (width, ff), (width, ff), (width, width), (kv, width), (kv, width), (width, width)]
    vm = pltpu.VMEM
    return pl.pallas_call(
        spread_kernel,
        name="spread_out",
        out_shape=tuple(jax.ShapeDtypeStruct(s, F32) for s in shapes),
        in_specs=[pl.BlockSpec(memory_space=pl.ANY)],
        out_specs=tuple([pl.BlockSpec(memory_space=pl.ANY)] * 7),
        scratch_shapes=[
            vm((3, width, cols), BF), vm((2, width, cols), F32),
            vm((width, width), F32), vm((kv, width), F32), vm((width, width), F32), vm((kv, width), F32),
            pltpu.SemaphoreType.DMA((3,)), pltpu.SemaphoreType.DMA((2,)), pltpu.SemaphoreType.DMA((4,)),
        ],
        compiler_params=pltpu.CompilerParams(vmem_limit_bytes=60 * 2**20),
    )(parts)


def on_device(
    hidden_in,
    cotangent,
    lengths,
    active,
    norm_attn,
    w_query,
    w_key,
    w_value,
    w_out,
    norm_mlp,
    w_gate,
    w_up,
    w_down,
    w_router,
):
    n_tok = lax.axis_size("tok")
    n_grp = lax.axis_size("grp")
    me_index = lax.axis_index("tok")
    rows, width = hidden_in.shape
    nback = min(SPAN, n_tok // 2)

    share = norm_attn.shape[0]
    vectors = jnp.pad(jnp.stack([norm_attn, norm_mlp, w_router]), ((0, 0), (0, 128 - share)))
    small = jnp.concatenate([vectors, active.astype(BF), jnp.zeros((10, 128), BF)], axis=0)
    shards = (jnp.concatenate([w_query, w_key, w_out, w_value], axis=1), w_gate, w_up, w_down, small)
    whole = gather_rows(shards) if (n_grp, n_tok) == (4, 8) else [lax.all_gather(each, "tok", axis=0) for each in shards]
    weights = {name: each.reshape(-1, each.shape[-1]) for name, each in zip(WEIGHTS, whole)}
    gains = jnp.transpose(whole[4][:, :3, :share], (1, 0, 2)).reshape(3, width).astype(F32)
    gains = jnp.pad(gains, ((0, 5), (0, 0)))

    lengths_row = lengths[0]
    token = jnp.arange(rows, dtype=jnp.int32)
    global_rows = me_index * rows + token
    segment_rows = segment_of(lengths_row, global_rows)
    cosine, sine = rotary_tables(position_of(lengths_row, global_rows, segment_rows))
    tables = (jnp.concatenate([cosine] * 4, axis=1), jnp.concatenate([-sine, sine] * 2, axis=1))
    reach = (nback + 1) * rows
    global_keys = (me_index - nback) * rows + jnp.arange(reach, dtype=jnp.int32)
    live_all = jnp.transpose(whole[4][:, 3:6], (1, 0, 2)).reshape(3, -1)
    live_all = jnp.pad(live_all, ((0, 0), (nback * rows, 0)))
    live_keys = lax.dynamic_slice_in_dim(live_all, me_index * rows, reach, 1)
    reachable = (segment_rows[None, :] == segment_of(lengths_row, global_keys)[:, None]) & (
        global_keys[:, None] <= global_rows[None, :]
    )
    masks = jnp.where(reachable[None] & (live_keys[:, :, None] > 0), 1.0, 0.0).astype(F32)
    lives = [active[i].astype(F32)[:, None] for i in range(RECUR)]

    kept = []
    made = first_stage(hidden_in.T, tables, gains, weights)
    state = made["state"]
    for step in range(RECUR):
        kvw = exchange_keys(made["kv"], n_tok, nback)
        last = step == RECUR - 1
        done = forward_stage(state, made["q"], kvw, masks[step], lives[step], tables, gains, weights, last)
        kept.append({**done, "state": state, "q": made["q"], "kvw": kvw, "normed_r": made["normed"]})
        made, state = done, done.get("next")

    acc = jnp.zeros((8, 1024), F32)
    before = None
    rows_of = {name: [] for name in ROW_NAMES}
    for step in reversed(range(RECUR)):
        back = backward_stage(kept[step], before, masks[step], lives[step], tables, gains, acc, weights, cotangent.T)
        acc = back["acc_out"]
        if before is not None:
            rows_of["d_packed"].append(back["d_packed"])
        for name in ("d_mlp", "d_gate", "d_up"):
            rows_of[name].append(back[name])
        for name in ("normed_two", "mixed", "hidden"):
            rows_of[name].append(kept[step][name])
        rows_of["normed"].append(kept[step]["normed_r"])
        before = {"home": exchange_home(back["dkv"], n_tok, nback), "d_q": back["d_q"], "state": kept[step]["state"], "d_state": back["d_state"], "d_attn": back["d_attn"]}
    back = backward_stage(None, before, None, None, tables, gains, acc, weights, None)
    rows_of["d_packed"].append(back["d_packed"])
    acc = back["acc_out"]
    if (n_grp, n_tok) == (4, 8):
        lefts, rights = ([rows_of[name] for name in names] for names in (ROW_NAMES[:4], ROW_NAMES[4:]))
        parts, acc = summed_gradients(lefts, rights, acc)
    else:
        parts = weight_gradients(rows_of)
        parts = lax.psum(parts.astype(F32), ("grp", "tok")).astype(BF)
        acc = lax.psum(acc, ("grp", "tok"))
    d_gate, d_up, d_down, d_q, d_k, d_v, d_o = spread_out(parts)
    return (
        kept[-1]["output"].T,
        back["grad"].T,
        acc[0, :width],
        d_q,
        d_k.T,
        d_v.T,
        d_o,
        acc[1, :width],
        d_gate,
        d_up,
        d_down.T,
        acc[2, :width],
    )


def solution(mesh):
    placed = (
        P(("grp", "tok"), None),
        P(("grp", "tok"), None),
        P("grp", None),
        P(None, ("grp", "tok")),
        P("tok"),
        P("tok", None),
        P("tok", None),
        P("tok", None),
        P("tok", None),
        P("tok"),
        P("tok", None),
        P("tok", None),
        P("tok", None),
        P("tok"),
    )
    return jax.shard_map(
        on_device,
        mesh=mesh,
        in_specs=placed,
        out_specs=(
            P(("grp", "tok"), None),
            P(("grp", "tok"), None),
            P(),
            P(),
            P(),
            P(),
            P(),
            P(),
            P(),
            P(),
            P(),
            P(),
        ),
        check_vma=False,
    )
```

```python
import jax
import jax.numpy as jnp
from jax import lax
from jax.experimental import pallas as pl
from jax.experimental.pallas import tpu as pltpu
from jax.sharding import PartitionSpec as P

MESH = pl.DeviceIdType.MESH

H = 15
KVH = 5
HD = 64
RECUR = 3
SPAN = 16

epsilon = 1e-05
theta = 10000.0
masked = -1000000000.0

def ends_of(lengths_row):
    count = lengths_row.shape[0]
    until = jnp.arange(count)[:, None] >= jnp.arange(count)[None, :]
    return jnp.sum(jnp.where(until, lengths_row[None, :], 0), axis=1)


def segment_of(lengths_row, global_rows):
    ends_at = ends_of(lengths_row)
    return jnp.sum((global_rows[:, None] >= ends_at[None, :]).astype(jnp.int32), axis=1)


def position_of(lengths_row, global_rows, segments):
    ends_at = ends_of(lengths_row)
    starts_at = ends_at - lengths_row
    picked = segments[:, None] == jnp.arange(lengths_row.shape[0], dtype=jnp.int32)[None, :]
    return global_rows - jnp.sum(jnp.where(picked, starts_at[None, :], 0), axis=1)


def rotary_tables(positions):
    half_dim = HD // 2
    inverse = jnp.power(theta, -jnp.arange(half_dim, dtype=jnp.float32) * (2.0 / HD))
    angle = positions.astype(jnp.float32)[..., None] * inverse
    return (jnp.cos(angle), jnp.sin(angle))


F32 = jnp.float32
BF = jnp.bfloat16
CHUNK = 512
WEIGHTS = ("wa", "wg", "wu", "wd")
QK = (H + KVH) * HD
QKO = QK + H * HD


def dot_nn(left, right):
    return lax.dot_general(left, right, (((1,), (0,)), ((), ())), preferred_element_type=F32)


def dot_nt(left, right):
    return lax.dot_general(left, right, (((1,), (1,)), ((), ())), preferred_element_type=F32)


def rope_lanes(tensor, cosine, sine, sign):
    rows, width = tensor.shape
    lane = lax.broadcasted_iota(jnp.int32, (rows, 2 * HD), 1)
    first = lax.rem(lane, HD) < HD // 2
    out = []
    for i in range(0, width, 2 * HD):
        piece = tensor[:, i : i + 2 * HD]
        other = jnp.where(first, pltpu.roll(piece, 2 * HD - HD // 2, 1), pltpu.roll(piece, HD // 2, 1))
        out.append(piece * cosine + (other * sine) * sign)
    return jnp.concatenate(out, axis=1)


def inverse_of(rows):
    return lax.rsqrt(jnp.mean(rows * rows, axis=1, keepdims=True) + epsilon)


def front_part(r, wait, state, ready=None):
    gain = r["gains"][0:1, :]
    normed = (state * inverse_of(state) * gain).astype(BF)
    r["normed"][...] = normed
    wait("wa")
    values = dot_nn(normed, r["wa_v"][:, QKO:]).astype(BF)
    qw = H * HD
    even = qw // (2 * HD) * (2 * HD)
    tail = rope_lanes(dot_nn(normed, r["wa_v"][:, even:QK]), r["cos"][...], r["sin"][...], 1.0).astype(BF)
    r["kv"][...] = jnp.concatenate([tail[:, qw - even :], values], axis=1)
    if ready is not None:
        ready()
    queries = rope_lanes(dot_nn(normed, r["wa_v"][:, :even]), r["cos"][...], r["sin"][...], 1.0).astype(BF)
    r["q"][...] = jnp.concatenate([queries, tail[:, : qw - even]], axis=1)


def head_rows(tensor, g):
    per = H // KVH
    return jnp.concatenate([tensor[:, (g * per + i) * HD : (g * per + i + 1) * HD] for i in range(per)], axis=0)


def window(r):
    rows = r["mask"].shape[0]
    start = lax.rem(lax.axis_index("tok"), 2) * r["q_in"].shape[0]
    return r["kvw"][pl.ds(pl.multiple_of(start, 128), rows), :]


def attention_part(r):
    per = H // KVH
    kv = window(r)
    q = r["q_in"][...]
    rows = q.shape[0]
    allowed = jnp.concatenate([r["mask"][...]] * per, axis=1) > 0
    mixed_t, logs = [], []
    for g in range(KVH):
        k_g = kv[:, g * HD : (g + 1) * HD]
        v_g = kv[:, (KVH + g) * HD : (KVH + g + 1) * HD]
        scores = jnp.where(allowed, dot_nt(k_g, head_rows(q, g)) * HD**-0.5, masked)
        largest = jnp.max(scores, axis=0, keepdims=True)
        exponent = jnp.exp(scores - largest)
        total = jnp.sum(exponent, axis=0, keepdims=True)
        probs = (exponent * (1.0 / total)).astype(BF)
        mix = dot_nn(v_g.T, probs)
        mixed_t += [mix[:, i * rows : (i + 1) * rows] for i in range(per)]
        logs.append(largest + jnp.log(total))
    r["lse"][...] = jnp.concatenate(logs + [logs[0]] * (r["lse"].shape[0] - KVH), axis=0)
    return jnp.concatenate(mixed_t, axis=0).T.astype(BF)


def rest_part(r, wait):
    state = r["state"][...]
    mixed = attention_part(r)
    r["mixed"][...] = mixed
    wait("wa")
    attn_out = dot_nn(mixed, r["wa_v"][:, QK:QKO])
    middle = state + attn_out
    r["middle"][...] = middle
    normed_two = (middle * inverse_of(middle) * r["gains"][1:2, :]).astype(BF)
    r["normed_two"][...] = normed_two
    wait("wg")
    wait("wu")
    wait("wd")
    ff = r["wg_v"].shape[1]
    mlp = jnp.zeros(state.shape, F32)
    for i in range(0, ff, CHUNK):
        at = slice(i, i + CHUNK)
        gate = dot_nn(normed_two, r["wg_v"][:, at])
        up = dot_nn(normed_two, r["wu_v"][:, at])
        r["gate"][:, at] = gate
        r["up"][:, at] = up
        hidden = (gate * jax.nn.sigmoid(gate) * up).astype(BF)
        r["hidden"][:, at] = hidden
        mlp = mlp + dot_nn(hidden, r["wd_v"][at, :])
    branch = attn_out + mlp.astype(BF).astype(F32)
    r["branch"][...] = branch
    router = jax.nn.sigmoid(jnp.sum(state * r["gains"][2:3, :], axis=1, keepdims=True))
    return state + (r["live"][:, 0:1] * router) * branch


def norm_back(grad, rows, gain):
    inverse = inverse_of(rows)
    scaled = rows * inverse
    weighted = grad * gain
    inner = jnp.mean(weighted * scaled, axis=1, keepdims=True)
    return inverse * (weighted - scaled * inner), jnp.sum(grad * scaled, axis=0, keepdims=True)


def back_part(r, wait, grad_after):
    state, live = r["b_state"][...], r["b_live"][:, 0:1]
    width = state.shape[1]
    router_vec = r["gains"][2:3, :]
    router = jax.nn.sigmoid(jnp.sum(state * router_vec, axis=1, keepdims=True))
    d_branch = (live * router) * grad_after
    d_logit = live * (router * (1.0 - router)) * jnp.sum(r["b_branch"][...] * grad_after, axis=1, keepdims=True)
    d_router = jnp.sum(d_logit * state, axis=0, keepdims=True)
    d_mlp = d_branch.astype(BF)
    r["d_mlp"][...] = d_mlp
    wait("wd")
    wait("wg")
    wait("wu")
    ff = r["wg_v"].shape[1]
    d_two = jnp.zeros(state.shape, F32)
    for i in range(0, ff, CHUNK):
        at = slice(i, i + CHUNK)
        gate, up = r["b_gate"][:, at], r["b_up"][:, at]
        sig = jax.nn.sigmoid(gate)
        d_hidden = dot_nt(d_mlp, r["wd_v"][at, :])
        d_up = (d_hidden * (gate * sig)).astype(BF)
        d_gate = (d_hidden * up * (sig * (1.0 + gate * (1.0 - sig)))).astype(BF)
        r["d_up"][:, at] = d_up
        r["d_gate"][:, at] = d_gate
        d_two = d_two + dot_nt(d_gate, r["wg_v"][:, at]) + dot_nt(d_up, r["wu_v"][:, at])
    d_two = d_two.astype(BF).astype(F32)
    d_middle, d_gain_two = norm_back(d_two, r["b_middle"][...], r["gains"][1:2, :])
    r["acc_out"][1:2, :width] = r["acc"][1:2, :width] + d_gain_two
    r["acc_out"][2:3, :width] = r["acc"][2:3, :width] + d_router
    d_attn = (d_branch + d_middle).astype(BF)
    r["d_attn"][...] = d_attn
    r["d_state"][...] = grad_after + d_logit * router_vec + d_middle
    wait("wa")
    d_mixed = dot_nt(d_attn, r["wa_v"][:, QK:QKO]).astype(BF)

    per = H // KVH
    kv = window(r)
    q = r["q_in"][...]
    rows = q.shape[0]
    allowed = jnp.concatenate([r["mask"][...]] * per, axis=1) > 0
    d_keys, d_values, dq_t = [], [], []
    for g in range(KVH):
        k_g = kv[:, g * HD : (g + 1) * HD]
        v_g = kv[:, (KVH + g) * HD : (KVH + g + 1) * HD]
        q_g, do_g = head_rows(q, g), head_rows(d_mixed, g)
        scores = jnp.where(allowed, dot_nt(k_g, q_g) * HD**-0.5, masked)
        probs = jnp.exp(scores - r["b_lse"][g : g + 1, :])
        d_values.append(dot_nn(probs.astype(BF), do_g))
        d_probs = dot_nt(v_g, do_g)
        d_scores = (probs * (d_probs - jnp.sum(probs * d_probs, axis=0, keepdims=True))).astype(BF)
        d_keys.append(dot_nn(d_scores, q_g) * HD**-0.5)
        dq = dot_nn(k_g.T, d_scores) * HD**-0.5
        dq_t += [dq[:, i * rows : (i + 1) * rows] for i in range(per)]
    d_queries = jnp.concatenate(dq_t + [jnp.zeros((HD, rows), F32)], axis=0).T
    d_queries = rope_lanes(d_queries, r["cos"][...], r["sin"][...], -1.0)
    r["d_q"][...] = d_queries[:, : H * HD].astype(BF)
    start = lax.rem(lax.axis_index("tok"), 2) * rows
    partial = r["dkv"]
    keep = partial.shape[0] - kv.shape[0]
    partial[pl.ds(pl.multiple_of((1 - lax.rem(lax.axis_index("tok"), 2)) * kv.shape[0], 128), keep), :] = jnp.zeros((keep, kv.shape[1]), BF)
    partial[pl.ds(pl.multiple_of(start, 128), kv.shape[0]), :] = jnp.concatenate(d_keys + d_values, axis=1).astype(BF)


def home_part(r, wait):
    half = KVH * HD
    total = r["home"][0].astype(F32)
    for i in range(1, r["home"].shape[0]):
        total = total + r["home"][i].astype(F32)
    rows = total.shape[0]
    padded = jnp.concatenate([total[:, :half], jnp.zeros((rows, half % (2 * HD)), F32)], axis=1)
    d_keys = rope_lanes(padded, r["cos"][...], r["sin"][...], -1.0)[:, :half].astype(BF)
    d_values = total[:, half:].astype(BF)
    wait("wa")
    packed = jnp.concatenate([r["h_dq"][...], d_keys, r["h_d_attn"][...], d_values], axis=1)
    r["d_packed"][...] = packed
    d_normed = dot_nt(packed[:, :QK], r["wa_v"][:, :QK]) + dot_nt(d_values, r["wa_v"][:, QKO:])
    state = r["h_state"][...]
    width = state.shape[1]
    d_in, d_gain = norm_back(d_normed, state, r["gains"][0:1, :])
    r["acc_out"][0:1, :width] = r["acc"][0:1, :width] + d_gain
    return r["h_d_state"][...] + d_in


def stage(name, parts, needed, inputs, outputs, weights, rename=None):
    in_names, out_names = list(inputs), list(outputs)
    w_names = [w for w in needed]

    def body(*refs):
        it = iter(refs)
        r = {n: next(it) for n in in_names}
        for n in w_names:
            r[n + "_v"] = next(it)
        for n in out_names:
            r[n] = next(it)
        parts(r, lambda n: None)

    vm = pl.BlockSpec(memory_space=pltpu.VMEM)
    out = pl.pallas_call(
        body,
        name=name,
        out_shape=tuple(outputs.values()),
        in_specs=[vm] * (len(in_names) + len(w_names)),
        out_specs=tuple([vm] * len(out_names)),
        compiler_params=pltpu.CompilerParams(vmem_limit_bytes=20 * 2**20),
    )(*inputs.values(), *[weights[n] for n in w_names])
    return dict(zip(out_names, out))


def shaped(shape, kind):
    return jax.ShapeDtypeStruct(shape, kind)


def front_outs(rows, width):
    return {"normed": shaped((rows, width), BF), "q": shaped((rows, H * HD), BF), "kv": shaped((rows, 2 * KVH * HD), BF)}


def recursion_kernel(chips, back, in_names, out_names, scratch_names, *refs):
    names = in_names + list(WEIGHTS) + out_names + scratch_names
    r = dict(zip(names, refs, strict=True))
    g, t = lax.axis_index("grp"), lax.axis_index("tok")
    z, c = t // 2, lax.rem(t, 2)
    rows = r["hidden_in"].shape[1]
    partner, left, right = (g, z * 2 + 1 - c), (g, t - 2), (g, t + 2)

    copies = {n: pltpu.make_async_copy(r[n], r[n + "_v"], r["w_sem"].at[i]) for i, n in enumerate(WEIGHTS)}
    for n in WEIGHTS:
        copies[n].start()
    done = set()

    def wait(n):
        if n not in done:
            copies[n].wait()
            done.add(n)

    bar = pltpu.get_barrier_semaphore()
    pl.semaphore_signal(bar, inc=1, device_id=partner, device_id_type=MESH)

    @pl.when(z > 0)
    def _():
        pl.semaphore_signal(bar, inc=1, device_id=left, device_id_type=MESH)

    @pl.when(z < chips - 1)
    def _():
        pl.semaphore_signal(bar, inc=1, device_id=right, device_id_type=MESH)

    def at(d, core):
        return pl.ds(pl.multiple_of(((back - d) * 2 + core) * rows, 128), rows)

    r["acc_out"][...] = jnp.zeros(r["acc_out"].shape, F32)
    for step in range(RECUR):
        for d in range(1, back + 1):
            @pl.when(z < d)
            def _():
                for core in (0, 1):
                    r["kvw"][step, at(d, core), :] = jnp.zeros((rows, r["kvw"].shape[2]), BF)

    def of_step(step):
        every = {n: r[n] for n in ("gains", "cos", "sin", "acc_out", "d_state", "d_q", "d_attn", "dkv", "home")}
        every |= {n + "_v": r[n + "_v"] for n in WEIGHTS}
        for n in ("normed", "mixed", "normed_two", "hidden", "d_mlp", "d_gate", "d_up", "d_packed"):
            every[n] = r[n + str(step)]
        for n in ("q", "kvw", "mask", "live", "state", "lse", "middle", "branch", "gate", "up"):
            every[n] = r[n].at[step]
        every |= {"q_in": every["q"], "kv": r["kvw"].at[step, at(0, c)], "acc": r["acc_out"]}
        every |= {"b_" + n: every[n] for n in ("state", "live", "branch", "gate", "up", "middle", "lse")}
        every |= {"h_dq": r["d_q"], "h_state": every["state"], "h_d_state": r["d_state"], "h_d_attn": r["d_attn"]}
        return every

    def k_along(step, d):
        here = r["kvw"].at[step, at(d - 1, c)]
        return copy_to(here, r["kvw"].at[step, at(d, c)], r["k_s"].at[step, d - 1], r["k_r"].at[step, d - 1], right)

    def k_beside(step, d):
        here = r["kvw"].at[step, at(d, c)]
        return copy_to(here, here, r["kc_s"].at[step, d], r["kc_r"].at[step, d], partner)

    def keys_start(step):
        @pl.when(z < chips - 1)
        def _():
            k_along(step, 1).start()

        k_beside(step, 0).start()

    def keys_end(step):
        for d in range(1, back + 1):
            @pl.when(z >= d)
            def _():
                k_along(step, d).wait_recv()
                if d < back:
                    @pl.when(z < chips - 1)
                    def _():
                        k_along(step, d + 1).start()
                k_beside(step, d).start()

        k_beside(step, 0).wait_recv()
        for d in range(1, back + 1):
            @pl.when(z >= d)
            def _():
                k_beside(step, d).wait_recv()

    def keys_drain(step):
        k_beside(step, 0).wait_send()
        for d in range(1, back + 1):
            @pl.when(z >= d)
            def _():
                k_beside(step, d).wait_send()

            @pl.when((z >= d - 1) & (z < chips - 1))
            def _():
                k_along(step, d).wait_send()

    def h_beside(step, d):
        return copy_to(r["dkv"].at[at(d, 1 - c)], r["beside_in"].at[step, d], r["hc_s"].at[step, d], r["hc_r"].at[step, d], partner)

    def h_along(step, d):
        return copy_to(r["sums"].at[d - 1], r["after_in"].at[step, d - 1], r["h_s"].at[step, d - 1], r["h_r"].at[step, d - 1], left)

    def home_start(step):
        for d in range(back, 0, -1):
            @pl.when(z >= d)
            def _():
                h_beside(step, d).start()
        h_beside(step, 0).start()

    def home_end(step):
        for d in range(back, 0, -1):
            @pl.when(z >= d)
            def _():
                h_beside(step, d).wait_recv()
                r["sums"][d - 1] = (r["dkv"][at(d, c), :].astype(F32) + r["beside_in"][step, d].astype(F32)).astype(BF)
                if d < back:
                    @pl.when(z < chips - 1)
                    def _():
                        h_along(step, d + 1).wait_recv()
                        r["sums"][d - 1] = (r["sums"][d - 1].astype(F32) + r["after_in"][step, d].astype(F32)).astype(BF)
                h_along(step, d).start()
        h_beside(step, 0).wait_recv()
        r["home"][0] = r["dkv"][at(0, c), :].astype(F32) + r["beside_in"][step, 0].astype(F32)

        @pl.when(z < chips - 1)
        def _():
            h_along(step, 1).wait_recv()
            r["home"][0] = r["home"][0] + r["after_in"][step, 0].astype(F32)

        h_beside(step, 0).wait_send()
        for d in range(1, back + 1):
            @pl.when(z >= d)
            def _():
                h_beside(step, d).wait_send()
                h_along(step, d).wait_send()

    r["state"][0] = r["hidden_in"][...].astype(F32).T
    met = False
    for step in range(RECUR):
        here = of_step(step)

        def ready(step=step, first=step == 0):
            if first:
                pl.semaphore_wait(bar, 1 + (z < chips - 1).astype(jnp.int32) + (z > 0).astype(jnp.int32))
            keys_start(step)

        front_part(here, wait, here["state"][...], ready)
        keys_end(step)
        after = rest_part(here, wait)
        keys_drain(step)
        if step < RECUR - 1:
            r["state"][step + 1] = after
        else:
            r["output"][...] = after.T.astype(BF)
    grad = r["cot"][...].astype(F32).T
    for step in reversed(range(RECUR)):
        here = of_step(step)
        back_part(here, wait, grad)
        home_start(step)
        home_end(step)
        grad = home_part(here, wait)
    r["grad"][...] = grad.T


def all_recursions(hidden_in, cotangent, masks, lives, tables, gains, weights, n_tok, nback):
    back = nback // 2
    width, rows = hidden_in.shape
    ff = weights["wg"].shape[1]
    kvr = 2 * KVH * HD
    slots = (2 * back + 2) * rows
    ins = {"hidden_in": hidden_in, "cot": cotangent, "mask": masks, "live": lives, "cos": tables[0], "sin": tables[1], "gains": gains}
    outs = {"output": shaped((width, rows), BF), "grad": shaped((width, rows), F32), "acc_out": shaped((8, 1024), F32)}
    sizes = {"normed": width, "d_mlp": width, "mixed": H * HD, "normed_two": width, "hidden": ff, "d_gate": ff, "d_up": ff, "d_packed": QKO + kvr // 2}
    for name, size in sizes.items():
        for step in range(RECUR):
            outs[name + str(step)] = shaped((rows, size), BF)
    dma, vm = pltpu.SemaphoreType.DMA, pltpu.VMEM
    scratch = {n + "_v": vm(weights[n].shape, BF) for n in WEIGHTS}
    scratch |= {
        "state": vm((RECUR, rows, width), F32), "middle": vm((RECUR, rows, width), F32), "branch": vm((RECUR, rows, width), F32),
        "gate": vm((RECUR, rows, ff), F32), "up": vm((RECUR, rows, ff), F32), "lse": vm((RECUR, 8, (H // KVH) * rows), F32),
        "q": vm((RECUR, rows, H * HD), BF), "kvw": vm((RECUR, slots, kvr), BF), "d_state": vm((rows, width), F32),
        "d_q": vm((rows, H * HD), BF), "d_attn": vm((rows, width), BF), "dkv": vm((slots, kvr), BF), "home": vm((1, rows, kvr), F32),
        "beside_in": vm((RECUR, back + 1, rows, kvr), BF), "after_in": vm((RECUR, back, rows, kvr), BF), "sums": vm((back, rows, kvr), BF),
        "w_sem": dma((len(WEIGHTS),)), "k_s": dma((RECUR, back)), "k_r": dma((RECUR, back)), "kc_s": dma((RECUR, back + 1)),
        "kc_r": dma((RECUR, back + 1)), "h_s": dma((RECUR, back)), "h_r": dma((RECUR, back)), "hc_s": dma((RECUR, back + 1)), "hc_r": dma((RECUR, back + 1)),
    }
    spec = pl.BlockSpec(memory_space=pltpu.VMEM)
    got = pl.pallas_call(
        lambda *refs: recursion_kernel(n_tok // 2, back, list(ins), list(outs), list(scratch), *refs),
        name="all_recursions",
        out_shape=tuple(outs.values()),
        in_specs=[spec] * len(ins) + [pl.BlockSpec(memory_space=pl.ANY)] * len(WEIGHTS),
        out_specs=tuple([spec] * len(outs)),
        scratch_shapes=list(scratch.values()),
        compiler_params=pltpu.CompilerParams(collective_id=5, has_side_effects=True, vmem_limit_bytes=62 * 2**20),
    )(*ins.values(), *[weights[n] for n in WEIGHTS])
    return dict(zip(outs, got))


def forward_stage(state, q, kvw, mask, live, tables, gains, weights, last):
    rows, width = state.shape
    ff = weights["wg"].shape[1]
    outs = {
        "mixed": shaped((rows, H * HD), BF), "lse": shaped((8, (H // KVH) * rows), F32), "middle": shaped((rows, width), F32),
        "normed_two": shaped((rows, width), BF), "gate": shaped((rows, ff), F32), "up": shaped((rows, ff), F32),
        "hidden": shaped((rows, ff), BF), "branch": shaped((rows, width), F32),
    }
    if last:
        outs["output"] = shaped((width, rows), BF)
    else:
        outs |= front_outs(rows, width) | {"next": shaped((rows, width), F32)}

    def parts(r, wait):
        state_next = rest_part(r, wait)
        if last:
            r["output"][...] = state_next.T.astype(BF)
        else:
            r["next"][...] = state_next
            front_part(r, wait, state_next)

    needed = ("wa", "wg", "wu", "wd")
    ins = {"state": state, "q_in": q, "kvw": kvw, "mask": mask, "live": live, "cos": tables[0], "sin": tables[1], "gains": gains}
    return stage("forward", parts, needed, ins, outs, weights)


def first_stage(hidden_in, tables, gains, weights):
    width, rows = hidden_in.shape

    def parts(r, wait):
        state = r["hidden"][...].astype(F32).T
        r["state"][...] = state
        front_part(r, wait, state)

    outs = front_outs(rows, width) | {"state": shaped((rows, width), F32)}
    return stage("first", parts, ("wa",), {"hidden": hidden_in, "cos": tables[0], "sin": tables[1], "gains": gains}, outs, weights)


def backward_stage(kept, before, mask, live, tables, gains, acc, weights, cotangent):
    ins = {"cos": tables[0], "sin": tables[1], "gains": gains, "acc": acc}
    outs = {"acc_out": shaped(acc.shape, F32)}
    needed = ()
    rows, width = (kept or before)["state"].shape
    ff = weights["wg"].shape[1]
    kvr = 2 * KVH * HD
    if before is not None:
        ins |= {"home": before["home"], "h_dq": before["d_q"], "h_state": before["state"], "h_d_state": before["d_state"], "h_d_attn": before["d_attn"]}
        outs |= {"d_packed": shaped((rows, QKO + kvr // 2), BF)}
        needed += ("wa",)
    else:
        ins |= {"cot": cotangent}
    if kept is not None:
        ins |= {"b_state": kept["state"], "b_live": live, "b_branch": kept["branch"], "b_gate": kept["gate"], "b_up": kept["up"],
                "b_middle": kept["middle"], "b_lse": kept["lse"], "kvw": kept["kvw"], "q_in": kept["q"], "mask": mask}
        outs |= {"d_mlp": shaped((rows, width), BF), "d_up": shaped((rows, ff), BF), "d_gate": shaped((rows, ff), BF),
                 "d_attn": shaped((rows, width), BF), "d_state": shaped((rows, width), F32), "d_q": shaped((rows, H * HD), BF),
                 "dkv": shaped(kept["kvw"].shape, BF)}
        needed += ("wd", "wg", "wu") + (("wa",) if before is None else ())
    else:
        outs |= {"grad": shaped((width, rows), F32)}

    def parts(r, wait):
        r["acc_out"][...] = r["acc"][...]
        grad = home_part(r, wait) if before is not None else r["cot"][...].astype(F32).T
        if kept is not None:
            back_part(r, wait, grad)
        else:
            r["grad"][...] = grad.T

    return stage("backward", parts, needed, ins, outs, weights)


PARTS = 16
HALF = 480
COLS = 640
STREAMS = (
    ("x", True, 0, 80, 0), ("y", True, 80, 80, 0), ("x", False, 160, 48, 0), ("y", False, 208, 32, 0),
    ("x", True, 240, 80, 1), ("y", True, 320, 80, 1), ("x", False, 400, 32, 1), ("y", False, 432, 48, 1),
)
SLOTS = 4


def place():
    g, t = lax.axis_index("grp"), lax.axis_index("tok")
    return g // 2, lax.rem(g, 2), t // 2, lax.rem(t, 2)


def dev(y, x, z, c):
    return (y * 2 + x, z * 2 + c)


def pick(z, values):
    out = jnp.int32(values[3])
    for i in (2, 1, 0):
        out = jnp.where(z == i, jnp.int32(values[i]), out)
    return out


def copy_to(src, dst, send, recv, device):
    return pltpu.make_async_remote_copy(src_ref=src, dst_ref=dst, send_sem=send, recv_sem=recv, device_id=device, device_id_type=MESH)


def add_rows(dst, src, rows, step):
    def body(i, _):
        at = pl.ds(pl.multiple_of(i * step, step), step)
        dst[at, :] = dst[at, :] + src[at, :]
        return 0

    lax.fori_loop(0, rows // step, body, 0)


def tail_kernel(count, *refs):
    left_refs, refs = refs[: 4 * count], refs[4 * count :]
    right_refs, refs = refs[: 4 * count], refs[4 * count :]
    n_s = len(STREAMS)
    v_ref, o_ref, vo_ref, left_t, right, theirs, mine, other = refs[:8]
    ra, rz, rb = refs[8 : 8 + n_s], refs[8 + n_s : 8 + 2 * n_s], refs[8 + 2 * n_s : 8 + 3 * n_s]
    vrecv, load_sem, core_s, core_r, as_, ar, zs, zr, bs, br, ob, obr, oz, ozr, oa, oar, oc, ocr, vs, vr, own_sem = refs[8 + 3 * n_s :]
    y, x, z, c = place()
    partner = dev(y, x, z, 1 - c)
    across = {"x": dev(y, 1 - x, z, c), "y": dev(1 - y, x, z, c)}
    left_dev, right_dev = dev(y, x, z - 1, c), dev(y, x, z + 1, c)
    at_axis = {"x": x, "y": y}
    order = (pick(z, (3, 3, 0, 0)), pick(z, (2, 0, 3, 1)), pick(z, (1, 2, 1, 2)), z)
    far = dev(y, x, jnp.where(z < 2, z + 2, z - 2), c)
    tokens = left_refs[0].shape[0]

    loads = []
    for p in range(PARTS):
        for i in range(count):
            src = right_refs[(p // 4) * count + i].at[:, pl.ds((p % 4) * COLS, COLS)]
            loads.append(pltpu.make_async_copy(src, right.at[p, pl.ds(i * tokens, tokens)], load_sem.at[p * count + i]))
    for cp in loads:
        cp.start()

    bar = pltpu.get_barrier_semaphore()
    for d in (partner, across["x"], across["y"], far):
        pl.semaphore_signal(bar, inc=1, device_id=d, device_id_type=MESH)

    @pl.when(z > 0)
    def _():
        pl.semaphore_signal(bar, inc=1, device_id=left_dev, device_id_type=MESH)

    @pl.when(z < 3)
    def _():
        pl.semaphore_signal(bar, inc=1, device_id=right_dev, device_id_type=MESH)

    for j in range(4):
        left_t[j] = jnp.concatenate([each[...].astype(F32).T.astype(BF) for each in left_refs[j * count : (j + 1) * count]], axis=1)
    for cp in loads:
        cp.wait()
    pl.semaphore_wait(bar, 4 + (z > 0).astype(jnp.int32) + (z < 3).astype(jnp.int32))

    def part_xy(px, py, pz):
        return (px * 2 + py) * 4 + pz

    def part_of(s, pa, pb, pz):
        return part_xy(pa, pb, pz) if STREAMS[s][0] == "x" else part_xy(pb, pa, pz)

    def ab(s):
        a = STREAMS[s][0]
        b = "y" if a == "x" else "x"
        return at_axis[a], at_axis[b], across[a], across[b]

    waits = []
    seq = [(k, i, px, py) for k in range(4) for i, (px, py) in enumerate(((1 - x, 1 - y), (1 - x, y), (x, 1 - y), (x, y)))]

    def core_copy(j):
        k, _, px, py = seq[j]
        p = part_xy(px, py, order[k])
        return copy_to(theirs.at[j % SLOTS, pl.ds(pl.multiple_of((1 - c) * HALF, 16), HALF)], other.at[p], core_s.at[j], core_r.at[p], partner)

    def core_make(j):
        k, _, px, py = seq[j]
        p = part_xy(px, py, order[k])
        if j >= SLOTS:
            core_copy(j - SLOTS).wait_send()
        which = jnp.where(p < 8, 0, jnp.where(p < 12, 1, jnp.where(p < 14, 2, 3)))
        split = 2 * COLS - 2 * HALF
        theirs[j % SLOTS] = dot_nn(left_t[which], right[p]).astype(BF)

        @pl.when(p == PARTS - 1)
        def _():
            theirs[j % SLOTS, :, COLS - split :] = dot_nn(left_t[2], right[p, :, COLS - split :]).astype(BF)

        core_copy(j).start()

    def core_add(j):
        k, i, px, py = seq[j]
        p = part_xy(px, py, order[k])
        core_copy(j).wait_recv()
        mine[p] = theirs[j % SLOTS, pl.ds(pl.multiple_of(c * HALF, 16), HALF), :] + other[p]

    def a_copy(s, pb, pz):
        a, b, to_a, _ = ab(s)
        _, _, r0, n, _ = STREAMS[s]
        return copy_to(mine.at[part_of(s, 1 - a, pb, pz), pl.ds(r0, n)], ra[s].at[pb * 4 + pz], as_.at[s, pb * 4 + pz], ar.at[s, pb * 4 + pz], to_a)

    def a_send(j, batch):
        k, i, px, py = seq[j]
        for s in range(n_s):
            a_axis = STREAMS[s][0]
            if STREAMS[s][4] == batch and (i == 0 or (i == 1 and a_axis == "x") or (i == 2 and a_axis == "y")):
                cp = a_copy(s, py if a_axis == "x" else px, order[k])
                cp.start()
                waits.append(cp)

    def z_index(s, pb, slot):
        return pb * 5 + slot if STREAMS[s][1] else slot

    def z_copy(s, pb, pz, to_right):
        a, b, _, _ = ab(s)
        _, _, r0, n, _ = STREAMS[s]
        src = mine.at[part_of(s, a, pb, pz), pl.ds(r0, n)]
        i = z_index(s, pb, pz if to_right else jnp.where(pz == z - 1, 4, pz))
        return copy_to(src, rz[s].at[i], zs.at[s, i], zr.at[s, i], right_dev if to_right else left_dev)

    def z_take(s, pb, slot):
        a, _, _, _ = ab(s)
        _, _, r0, n, _ = STREAMS[s]
        i = z_index(s, pb, slot)
        copy_to(mine.at[0, pl.ds(r0, n)], rz[s].at[i], zs.at[s, i], zr.at[s, i], left_dev).wait_recv()
        pz = z if slot is z or isinstance(slot, int) else slot
        add_rows(mine.at[part_of(s, a, pb, pz), pl.ds(r0, n)], rz[s].at[i], n, 16)

    def z_step(s, pb, k):
        pz = order[k]
        if k < 3:
            up = jnp.where(pz > z, (z > 0).astype(jnp.int32), (z < 3).astype(jnp.int32))

            @pl.when(up == 1)
            def _():
                z_take(s, pb, pz)

            @pl.when(pz > z)
            def _():
                z_copy(s, pb, pz, True).start()

            @pl.when(pz < z)
            def _():
                z_copy(s, pb, pz, False).start()
        else:
            @pl.when(z > 0)
            def _():
                z_take(s, pb, z)

            @pl.when(z < 3)
            def _():
                z_take(s, pb, 4)

    def z_drain(s, pb, k):
        pz = order[k]

        @pl.when(pz > z)
        def _():
            z_copy(s, pb, pz, True).wait_send()

        @pl.when(pz < z)
        def _():
            z_copy(s, pb, pz, False).wait_send()

    def a_step(s, pb, k):
        a, b, to_a, _ = ab(s)
        _, _, r0, n, _ = STREAMS[s]
        pz = order[k]
        a_copy(s, pb, pz).wait_recv()
        add_rows(mine.at[part_of(s, a, pb, pz), pl.ds(r0, n)], ra[s].at[pb * 4 + pz], n, 16)

    def b_copy(s, pz):
        a, b, _, to_b = ab(s)
        _, second_z, r0, n, _ = STREAMS[s]
        i = 0 if second_z else pz
        return copy_to(mine.at[part_of(s, a, 1 - b, pz), pl.ds(r0, n)], rb[s].at[i], bs.at[s, i], br.at[s, i], to_b)

    def b_step(s, pz):
        a, b, _, _ = ab(s)
        _, second_z, r0, n, _ = STREAMS[s]
        i = 0 if second_z else pz
        b_copy(s, pz).wait_recv()
        add_rows(mine.at[part_of(s, a, b, pz), pl.ds(r0, n)], rb[s].at[i], n, 16)

    def of_batch(batch):
        return [s for s in range(n_s) if STREAMS[s][4] == batch]

    def first_step(batch, k):
        for s in of_batch(batch):
            _, b, _, _ = ab(s)
            a_step(s, 1 - b, k)
            if STREAMS[s][1]:
                z_step(s, 1 - b, k)
                a_step(s, b, k)
                z_step(s, b, k)
                if k == 3:
                    cp = b_copy(s, z)
                    cp.start()
                    waits.append(cp)
            else:
                cp = b_copy(s, order[k])
                cp.start()
                waits.append(cp)
                a_step(s, b, k)

    def second_step(batch, k):
        for s in of_batch(batch):
            _, b, _, _ = ab(s)
            if not STREAMS[s][1]:
                b_step(s, order[k])
                z_step(s, b, k)

    def vec_copy(i):
        to = (partner, across["x"], across["y"], dev(y, x, jnp.where(lax.rem(z, 2) == 0, z + 1, z - 1), c), far)[i]
        return copy_to(vo_ref, vrecv.at[i], vs.at[i], vr.at[i], to)

    def vec_end(i):
        vec_copy(i).wait()
        vo_ref[...] = vo_ref[...] + vrecv[i]

    half0 = c * HALF

    def out_at(s, p):
        _, _, r0, n, _ = STREAMS[s]
        return o_ref.at[p, pl.ds(pl.multiple_of(half0 + r0, 16), n)]

    def mine_at(s, p):
        _, _, r0, n, _ = STREAMS[s]
        return mine.at[p, pl.ds(r0, n)]

    def go(cp):
        cp.start()
        waits.append(cp)

    def to_core(s, p, src):
        return copy_to(src, out_at(s, p), oc.at[s, p], ocr.at[s, p], partner)

    def to_a(s, pb, pz, src):
        a, b, na, _ = ab(s)
        return copy_to(src, out_at(s, part_of(s, a, pb, pz)), oa.at[s, pb * 4 + pz], oar.at[s, pb * 4 + pz], na)

    def to_b(s, pz, src):
        a, b, _, nb = ab(s)
        return copy_to(src, out_at(s, part_of(s, a, b, pz)), ob.at[s, pz], obr.at[s, pz], nb)

    def to_z(s, pb, pz, src, to_right):
        a, b, _, _ = ab(s)
        i = pb * 8 + pz * 2 + (0 if to_right else 1)
        return copy_to(src, out_at(s, part_of(s, a, pb, pz)), oz.at[s, i], ozr.at[s, pb * 4 + pz], right_dev if to_right else left_dev)

    def spread_z(s, pb, pz, src, sides):
        if 0 in sides:
            @pl.when(z < 3)
            def _():
                to_z(s, pb, pz, src, True).start()
        if 1 in sides:
            @pl.when(z > 0)
            def _():
                to_z(s, pb, pz, src, False).start()

    def finish(batch):
        for s in of_batch(batch):
            a, b, _, _ = ab(s)
            p = part_of(s, a, b, z)
            b_step(s, z)
            if not STREAMS[s][1]:
                z_step(s, b, 3)
            src = mine_at(s, p)
            if STREAMS[s][1]:
                go(to_b(s, z, src))
                spread_z(s, b, z, src, (0, 1))
            else:
                spread_z(s, b, z, src, (0, 1))
                go(to_b(s, z, src))
            go(to_a(s, b, z, src))
            go(to_core(s, p, src))
            pltpu.make_async_copy(src, out_at(s, p), own_sem.at[s]).start()

    def got_b(s, pz):
        a, b, _, _ = ab(s)
        p = part_of(s, a, 1 - b, pz)
        src = out_at(s, p)
        copy_to(src, src, ob.at[s, pz], obr.at[s, pz], partner).wait_recv()
        if STREAMS[s][1]:
            spread_z(s, 1 - b, pz, src, (0, 1))
        to_a(s, 1 - b, pz, src).start()
        to_core(s, p, src).start()

    def got_z(s, pb, pz, from_left):
        a, b, _, _ = ab(s)
        p = part_of(s, a, pb, pz)
        src = out_at(s, p)
        copy_to(src, src, oz.at[s, 0], ozr.at[s, pb * 4 + pz], partner).wait_recv()
        spread_z(s, pb, pz, src, (0,) if from_left else (1,))
        to_a(s, pb, pz, src).start()
        if not STREAMS[s][1]:
            to_b(s, pz, src).start()
        to_core(s, p, src).start()

    def got_a(s, pb, pz):
        a, b, _, _ = ab(s)
        p = part_of(s, 1 - a, pb, pz)
        src = out_at(s, p)
        copy_to(src, src, oa.at[s, pb * 4 + pz], oar.at[s, pb * 4 + pz], partner).wait_recv()
        to_core(s, p, src).start()

    def gather_b(batch):
        for s in of_batch(batch):
            got_b(s, z)

    def gather_a(batch):
        for s in of_batch(batch):
            _, b, _, _ = ab(s)
            got_a(s, b, z)
            got_a(s, 1 - b, z)

    def from_side(t, side):
        return (z - t, z >= t) if side == 0 else (z + t, z + t <= 3)

    def gather_z(batch, t):
        for side in (0, 1):
            pz, there = from_side(t, side)

            @pl.when(there)
            def _():
                for s in of_batch(batch):
                    _, b, _, _ = ab(s)
                    got_z(s, b, pz, side == 0)
                    if STREAMS[s][1]:
                        got_z(s, 1 - b, pz, side == 0)

    def gather_rest(batch, t):
        for side in (0, 1):
            pz, there = from_side(t, side)

            @pl.when(there)
            def _():
                for s in of_batch(batch):
                    if not STREAMS[s][1]:
                        got_b(s, pz)
                for s in of_batch(batch):
                    _, b, _, _ = ab(s)
                    got_a(s, b, pz)
                    got_a(s, 1 - b, pz)

    vo_ref[...] = v_ref[...]
    vec_copy(0).start()

    def group(k, batches=(0,)):
        for i in range(4):
            j = k * 4 + i
            core_make(j)
            if j > 0:
                core_add(j - 1)
                a_send(j - 1, 0)
        if k == 3:
            core_add(15)
            a_send(15, 0)

    group(0)
    vec_end(0)
    vec_copy(1).start()
    group(1)
    vec_end(1)
    vec_copy(2).start()
    first_step(0, 0)
    group(2)
    vec_end(2)
    vec_copy(3).start()
    second_step(0, 0)
    first_step(0, 1)
    group(3)
    vec_end(3)
    vec_copy(4).start()
    second_step(0, 1)
    for j in range(0, 4):
        a_send(j, 1)
    first_step(0, 2)
    vec_end(4)
    second_step(0, 2)
    for j in range(4, 8):
        a_send(j, 1)
    first_step(0, 3)
    first_step(1, 0)
    finish(0)
    for j in range(8, 12):
        a_send(j, 1)
    second_step(1, 0)
    gather_b(0)
    first_step(1, 1)
    second_step(1, 1)
    gather_z(0, 1)
    for j in range(12, 16):
        a_send(j, 1)
    gather_a(0)
    first_step(1, 2)
    second_step(1, 2)
    gather_z(0, 2)
    gather_rest(0, 1)
    first_step(1, 3)
    finish(1)
    gather_z(0, 3)
    gather_rest(0, 2)
    gather_b(1)
    gather_z(1, 1)
    gather_rest(0, 3)
    gather_a(1)
    gather_z(1, 2)
    gather_rest(1, 1)
    gather_z(1, 3)
    gather_rest(1, 2)
    gather_rest(1, 3)

    for cp in waits:
        cp.wait_send()
    for j in range(PARTS - SLOTS, PARTS):
        core_copy(j).wait_send()
    for s in range(n_s):
        a, b, _, _ = ab(s)
        pltpu.make_async_copy(mine_at(s, part_of(s, a, b, z)), out_at(s, part_of(s, a, b, z)), own_sem.at[s]).wait()
        pbs = (b, 1 - b) if STREAMS[s][1] else (b,)
        for pb in pbs:
            for k in range(3):
                z_drain(s, pb, k)
        for pz in range(4):
            for pb in pbs:
                src = out_at(s, part_of(s, a, pb, pz))

                @pl.when((z >= pz) & (z < 3))
                def _():
                    to_z(s, pb, pz, src, True).wait_send()

                @pl.when((z <= pz) & (z > 0))
                def _():
                    to_z(s, pb, pz, src, False).wait_send()
            for pb in (0, 1):
                src = out_at(s, part_of(s, a, pb, pz))

                @pl.when(jnp.logical_not((pb == b) & (pz == z)))
                def _():
                    to_a(s, pb, pz, src).wait_send()
            if not STREAMS[s][1]:
                @pl.when(z != pz)
                def _():
                    to_b(s, pz, out_at(s, 0)).wait_send()
        for p in range(16):
            src = out_at(s, p)

            @pl.when(p != part_of(s, a, b, z))
            def _():
                to_core(s, p, src).wait_send()
            _, _, r0, n, _ = STREAMS[s]
            dst = o_ref.at[p, pl.ds(pl.multiple_of((1 - c) * HALF + r0, 16), n)]
            copy_to(dst, dst, oc.at[s, p], ocr.at[s, p], partner).wait_recv()


def summed_gradients(lefts, rights, vectors):
    dma = pltpu.SemaphoreType.DMA
    count = len(lefts[0])
    tokens, width = lefts[0][0].shape
    rows = count * tokens
    n_s = len(STREAMS)
    vm = pl.BlockSpec(memory_space=pltpu.VMEM)
    return pl.pallas_call(
        lambda *refs: tail_kernel(count, *refs),
        name="summed_gradients",
        out_shape=(jax.ShapeDtypeStruct((PARTS, width, COLS), BF), jax.ShapeDtypeStruct(vectors.shape, F32)),
        in_specs=[vm] * (4 * count) + [pl.BlockSpec(memory_space=pl.ANY)] * (4 * count) + [vm],
        out_specs=(pl.BlockSpec(memory_space=pl.ANY), vm),
        scratch_shapes=[
            pltpu.VMEM((4, width, rows), BF), pltpu.VMEM((PARTS, rows, COLS), BF), pltpu.VMEM((SLOTS, 2 * HALF, COLS), BF),
            pltpu.VMEM((PARTS, HALF, COLS), BF), pltpu.VMEM((PARTS, HALF, COLS), BF),
            *[pltpu.VMEM((8, s[3], COLS), BF) for s in STREAMS],
            *[pltpu.VMEM((10 if s[1] else 5, s[3], COLS), BF) for s in STREAMS],
            *[pltpu.VMEM((1 if s[1] else 4, s[3], COLS), BF) for s in STREAMS],
            pltpu.VMEM((5, *vectors.shape), F32),
            dma((PARTS * count,)), dma((16,)), dma((16,)),
            dma((n_s, 8)), dma((n_s, 8)), dma((n_s, 10)), dma((n_s, 10)), dma((n_s, 4)), dma((n_s, 4)),
            dma((n_s, 4)), dma((n_s, 4)), dma((n_s, 16)), dma((n_s, 8)), dma((n_s, 8)), dma((n_s, 8)), dma((n_s, 16)), dma((n_s, 16)),
            dma((5,)), dma((5,)), dma((n_s,)),
        ],
        compiler_params=pltpu.CompilerParams(collective_id=1, has_side_effects=True, vmem_limit_bytes=60 * 2**20),
    )(*[a for l in lefts for a in l], *[a for l in rights for a in l], vectors)


QUARTERS = 4


def gather_kernel(*refs):
    ins, outs = refs[:5], refs[5:10]
    zs, xs, ys, cs, got, cgot, own_s, own_c, own_r, ss, sr, sc, scr = refs[10:]
    y, x, z, c = place()
    partner, to_x, to_y = dev(y, x, z, 1 - c), dev(y, 1 - x, z, c), dev(1 - y, x, z, c)
    left, right = dev(y, x, z - 1, c), dev(y, x, z + 1, c)
    quarter = (x * 2 + y, (1 - x) * 2 + y, x * 2 + (1 - y), (1 - x) * 2 + (1 - y))
    lasting = []

    def go(cp, when=None):
        if when is None:
            cp.start()
        else:
            @pl.when(when)
            def _():
                cp.start()
        lasting.append((cp, when))

    def cut(ref, m, q):
        if m < 3:
            n = ref.shape[1] // QUARTERS
            return ref.at[:, pl.ds(pl.multiple_of(q * n, 128), n)]
        n = ref.shape[0] // QUARTERS
        return ref.at[pl.ds(pl.multiple_of(q * n, 16), n), :]

    def out_piece(m, kind, zz, core):
        return cut(outs[m].at[zz * 2 + core], m, quarter[kind])

    bar = pltpu.get_barrier_semaphore()
    for d in (partner, to_x, to_y):
        pl.semaphore_signal(bar, inc=1, device_id=d, device_id_type=MESH)

    @pl.when(z > 0)
    def _():
        pl.semaphore_signal(bar, inc=1, device_id=left, device_id_type=MESH)

    @pl.when(z < 3)
    def _():
        pl.semaphore_signal(bar, inc=1, device_id=right, device_id_type=MESH)

    pl.semaphore_wait(bar, 3 + (z > 0).astype(jnp.int32) + (z < 3).astype(jnp.int32))

    def small_copy(zz, core, src, device, sems):
        return copy_to(src, outs[4].at[zz * 2 + core], sems[0], sems[1], device)

    go(small_copy(z, c, ins[4], right, (ss.at[z, 0], sr.at[z])), z < 3)
    go(small_copy(z, c, ins[4], left, (ss.at[z, 1], sr.at[z])), z > 0)
    go(small_copy(z, c, ins[4], partner, (sc.at[z], scr.at[z])))
    for m in range(4):
        src, dst = cut(ins[m], m, quarter[0]), out_piece(m, 0, z, c)
        go(copy_to(src, dst, zs.at[m, z, 0], got.at[0, m, z], right), z < 3)
        go(copy_to(src, dst, zs.at[m, z, 1], got.at[0, m, z], left), z > 0)
    for m in range(4):
        go(copy_to(ins[m], outs[m].at[z * 2 + c], own_c.at[m], own_r.at[m], partner))
    local = [pltpu.make_async_copy(ins[m], outs[m].at[z * 2 + c], own_s.at[m]) for m in range(5)]
    for cp in local:
        cp.start()

    steps = [(t, side) for t in (1, 2, 3) for side in (0, 1)]

    def source(t, side):
        return (z - t, z >= t) if side == 0 else (z + t, z + t <= 3)

    def wait_for(kind, m, zz):
        piece = out_piece(m, kind, zz, c)
        copy_to(piece, piece, cs.at[kind, m, zz], got.at[kind, m, zz], partner).wait_recv()
        return piece

    def each(kind, m, t, side):
        zz, there = source(t, side)
        onward = (z < 3) if side == 0 else (z > 0)

        @pl.when(there)
        def _():
            piece = wait_for(kind, m, zz)
            first_x = m % 2 == 0
            sends = []
            if kind == 0:
                on = copy_to(piece, piece, zs.at[m, zz, side], got.at[0, m, zz], right if side == 0 else left)

                @pl.when(onward)
                def _():
                    on.start()

                sends.append(copy_to(piece, piece, xs.at[0, m, zz], got.at[1, m, zz], to_x))
                sends.append(copy_to(piece, piece, ys.at[0, m, zz], got.at[2, m, zz], to_y))
            elif kind == 1 and first_x:
                sends.append(copy_to(piece, piece, ys.at[1, m, zz], got.at[3, m, zz], to_y))
            elif kind == 2 and not first_x:
                sends.append(copy_to(piece, piece, xs.at[1, m, zz], got.at[3, m, zz], to_x))
            sends.append(copy_to(piece, piece, cs.at[kind, m, zz], cgot.at[kind, m, zz], partner))
            for cp in sends:
                cp.start()

        lasting.append((("s", kind, m, t, side), there))
        if kind == 0:
            lasting.append((("z", m, t, side), there & onward))

    def small_step(t, side):
        zz, there = source(t, side)

        @pl.when(there)
        def _():
            piece = outs[4].at[zz * 2 + c]
            copy_to(piece, piece, sc.at[zz], sr.at[zz], partner).wait_recv()

            @pl.when((z < 3) if side == 0 else (z > 0))
            def _():
                small_copy(zz, c, piece, right if side == 0 else left, (ss.at[zz, side], sr.at[zz])).start()

            small_copy(zz, c, piece, partner, (sc.at[zz], scr.at[zz])).start()

        lasting.append((("m", t, side), there))

    for t, side in steps:
        small_step(t, side)
    turns = [(t, m) for t in (1, 2, 3) for m in range(4)]
    for i in range(len(turns) + 3):
        if i < len(turns):
            t, m = turns[i]
            for side in (0, 1):
                each(0, m, t, side)
        if 0 <= i - 1 < len(turns):
            t, m = turns[i - 1]
            for side in (0, 1):
                each(1 if m % 2 == 0 else 2, m, t, side)
        if 0 <= i - 2 < len(turns):
            t, m = turns[i - 2]
            for side in (0, 1):
                each(2 if m % 2 == 0 else 1, m, t, side)
        if i - 3 >= 0:
            t, m = turns[i - 3]
            for side in (0, 1):
                each(3, m, t, side)

    for cp, when in lasting:
        if not isinstance(cp, tuple):
            if when is None:
                cp.wait_send()
            else:
                @pl.when(when)
                def _():
                    cp.wait_send()
        elif cp[0] == "z":
            _, m, t, side = cp
            zz, _ = source(t, side)
            piece = out_piece(m, 0, zz, c)

            @pl.when(when)
            def _():
                copy_to(piece, piece, zs.at[m, zz, side], got.at[0, m, zz], partner).wait_send()
        elif cp[0] == "m":
            _, t, side = cp
            zz, _ = source(t, side)
            piece = outs[4].at[zz * 2 + c]

            @pl.when(when)
            def _():
                @pl.when((z < 3) if side == 0 else (z > 0))
                def _():
                    small_copy(zz, c, piece, partner, (ss.at[zz, side], sr.at[zz])).wait_send()

                small_copy(zz, c, piece, partner, (sc.at[zz], scr.at[zz])).wait_send()
                other = outs[4].at[zz * 2 + 1 - c]
                copy_to(other, other, sc.at[zz], scr.at[zz], partner).wait_recv()
        else:
            _, kind, m, t, side = cp
            zz, _ = source(t, side)
            piece = out_piece(m, kind, zz, c)
            other = out_piece(m, kind, zz, 1 - c)
            first_x = m % 2 == 0

            @pl.when(when)
            def _():
                if kind == 0 or (kind == 2 and not first_x):
                    copy_to(piece, piece, xs.at[min(kind, 1), m, zz], got.at[1, m, zz], partner).wait_send()
                if kind == 0 or (kind == 1 and first_x):
                    copy_to(piece, piece, ys.at[min(kind, 1), m, zz], got.at[1, m, zz], partner).wait_send()
                copy_to(piece, piece, cs.at[kind, m, zz], cgot.at[kind, m, zz], partner).wait_send()
                copy_to(other, other, cs.at[kind, m, zz], cgot.at[kind, m, zz], partner).wait_recv()

    for m in range(4):
        other = outs[m].at[z * 2 + 1 - c]
        copy_to(other, other, own_c.at[m], own_r.at[m], partner).wait_recv()
    other = outs[4].at[z * 2 + 1 - c]
    copy_to(other, other, sc.at[z], scr.at[z], partner).wait_recv()
    for cp in local:
        cp.wait()


def gather_rows(shards):
    dma = pltpu.SemaphoreType.DMA
    return pl.pallas_call(
        gather_kernel,
        name="gather_rows",
        out_shape=tuple(jax.ShapeDtypeStruct((8, *s.shape), s.dtype) for s in shards),
        in_specs=[pl.BlockSpec(memory_space=pl.ANY)] * 5,
        out_specs=tuple([pl.BlockSpec(memory_space=pl.ANY)] * 5),
        scratch_shapes=[
            dma((4, 4, 2)), dma((2, 4, 4)), dma((2, 4, 4)), dma((4, 4, 4)), dma((4, 4, 4)), dma((4, 4, 4)),
            dma((5,)), dma((4,)), dma((4,)), dma((4, 2)), dma((4,)), dma((4,)), dma((4,)),
        ],
        compiler_params=pltpu.CompilerParams(collective_id=4, has_side_effects=True),
    )(*shards)


def keys_kernel(chips, back, kv_ref, w_ref, s_right, r_left, s_core, r_core):
    g, t = lax.axis_index("grp"), lax.axis_index("tok")
    z, c = t // 2, lax.rem(t, 2)
    rows = kv_ref.shape[0]
    partner, right = (g, z * 2 + 1 - c), (g, t + 2)

    def slot(d, core):
        return w_ref.at[pl.ds(pl.multiple_of(((back - d) * 2 + core) * rows, 128), rows)]

    bar = pltpu.get_barrier_semaphore()
    pl.semaphore_signal(bar, inc=1, device_id=partner, device_id_type=MESH)

    @pl.when(z > 0)
    def _():
        pl.semaphore_signal(bar, inc=1, device_id=(g, t - 2), device_id_type=MESH)

    def along(d, src):
        return copy_to(src, slot(d, c), s_right.at[d - 1], r_left.at[d - 1], right)

    def beside(d, src):
        return copy_to(src, slot(d, c), s_core.at[d], r_core.at[d], partner)

    own = w_ref.at[pl.ds(pl.multiple_of((back * 2 + c) * rows, 128), rows)]
    own[...] = kv_ref[...]
    for d in range(1, back + 1):
        @pl.when(z < d)
        def _():
            for core in (0, 1):
                slot(d, core)[...] = jnp.zeros(kv_ref.shape, kv_ref.dtype)

    pl.semaphore_wait(bar, 1 + (z < chips - 1).astype(jnp.int32))

    @pl.when(z < chips - 1)
    def _():
        along(1, kv_ref).start()

    beside(0, kv_ref).start()
    for d in range(1, back + 1):
        @pl.when(z >= d)
        def _():
            along(d, slot(d, c)).wait_recv()
            if d < back:
                @pl.when(z < chips - 1)
                def _():
                    along(d + 1, slot(d, c)).start()
            beside(d, slot(d, c)).start()

    def mine_to(d):
        return copy_to(slot(d, 1 - c), slot(d, 1 - c), s_core.at[d], r_core.at[d], partner)

    mine_to(0).wait_recv()
    beside(0, kv_ref).wait_send()

    @pl.when(z < chips - 1)
    def _():
        along(1, kv_ref).wait_send()

    for d in range(1, back + 1):
        @pl.when(z >= d)
        def _():
            mine_to(d).wait_recv()
            beside(d, slot(d, c)).wait_send()
            if d < back:
                @pl.when(z < chips - 1)
                def _():
                    along(d + 1, slot(d, c)).wait_send()


def exchange_keys(kv, n_tok, nback):
    back = nback // 2
    rows = kv.shape[0]
    dma = pltpu.SemaphoreType.DMA
    return pl.pallas_call(
        lambda *refs: keys_kernel(n_tok // 2, back, *refs),
        name="exchange_keys",
        out_shape=jax.ShapeDtypeStruct(((2 * back + 2) * rows, kv.shape[1]), kv.dtype),
        in_specs=[pl.BlockSpec(memory_space=pltpu.VMEM)],
        out_specs=pl.BlockSpec(memory_space=pltpu.VMEM),
        scratch_shapes=[dma((back,)), dma((back,)), dma((back + 1,)), dma((back + 1,))],
        compiler_params=pltpu.CompilerParams(collective_id=2, has_side_effects=True, vmem_limit_bytes=12 * 2**20),
    )(kv)


def home_kernel(chips, back, p_ref, h_ref, beside_in, sums, after_in, s_left, r_right, s_core, r_core):
    g, t = lax.axis_index("grp"), lax.axis_index("tok")
    z, c = t // 2, lax.rem(t, 2)
    rows = h_ref.shape[1]
    partner, left = (g, z * 2 + 1 - c), (g, t - 2)

    def block(d, core):
        return p_ref.at[pl.ds(pl.multiple_of(((back - d) * 2 + core) * rows, 128), rows)]

    bar = pltpu.get_barrier_semaphore()
    pl.semaphore_signal(bar, inc=1, device_id=partner, device_id_type=MESH)

    @pl.when(z < chips - 1)
    def _():
        pl.semaphore_signal(bar, inc=1, device_id=(g, t + 2), device_id_type=MESH)

    pl.semaphore_wait(bar, 1 + (z > 0).astype(jnp.int32))

    def beside(d):
        return copy_to(block(d, 1 - c), beside_in.at[d], s_core.at[d], r_core.at[d], partner)

    def along(d):
        return copy_to(sums.at[d - 1], after_in.at[d - 1], s_left.at[d - 1], r_right.at[d - 1], left)

    for d in range(back, 0, -1):
        @pl.when(z >= d)
        def _():
            beside(d).start()
    beside(0).start()
    for d in range(back, 0, -1):
        @pl.when(z >= d)
        def _():
            beside(d).wait_recv()
            sums[d - 1] = (block(d, c)[...].astype(F32) + beside_in[d].astype(F32)).astype(BF)
            if d < back:
                @pl.when(z < chips - 1)
                def _():
                    along(d + 1).wait_recv()
                    sums[d - 1] = (sums[d - 1].astype(F32) + after_in[d].astype(F32)).astype(BF)
            along(d).start()
    beside(0).wait_recv()
    h_ref[0] = block(0, c)[...].astype(F32) + beside_in[0].astype(F32)

    @pl.when(z < chips - 1)
    def _():
        along(1).wait_recv()
        h_ref[0] = h_ref[0] + after_in[0].astype(F32)

    beside(0).wait_send()
    for d in range(1, back + 1):
        @pl.when(z >= d)
        def _():
            beside(d).wait_send()
            along(d).wait_send()


def exchange_home(partial, n_tok, nback):
    back = nback // 2
    rows = partial.shape[0] // (2 * back + 2)
    width = partial.shape[1]
    dma = pltpu.SemaphoreType.DMA
    return pl.pallas_call(
        lambda *refs: home_kernel(n_tok // 2, back, *refs),
        name="exchange_home",
        out_shape=jax.ShapeDtypeStruct((1, rows, width), F32),
        in_specs=[pl.BlockSpec(memory_space=pltpu.VMEM)],
        out_specs=pl.BlockSpec(memory_space=pltpu.VMEM),
        scratch_shapes=[
            pltpu.VMEM((back + 1, rows, width), BF), pltpu.VMEM((back, rows, width), BF), pltpu.VMEM((back, rows, width), BF),
            dma((back,)), dma((back,)), dma((back + 1,)), dma((back + 1,)),
        ],
        compiler_params=pltpu.CompilerParams(collective_id=3, has_side_effects=True, vmem_limit_bytes=12 * 2**20),
    )(partial)


ROW_NAMES = ("normed_two", "d_mlp", "normed", "mixed", "d_gate", "d_up", "hidden", "d_packed")


def grads_kernel(count, *refs):
    r = {name: refs[i * count : (i + 1) * count] for i, name in enumerate(ROW_NAMES)}
    g_ref, left_t, slots, sems = refs[len(ROW_NAMES) * count :]
    for i, name in enumerate(ROW_NAMES[:4]):
        left_t[i] = jnp.concatenate([each[...].astype(F32).T.astype(BF) for each in r[name]], axis=1)

    def out_copy(p):
        return pltpu.make_async_copy(slots.at[p % 2], g_ref.at[p], sems.at[p % 2])

    split = 2 * COLS - left_t.shape[1]
    for p in range(PARTS):
        if p >= 2:
            out_copy(p - 2).wait()
        low = (p % 4) * COLS
        right = jnp.concatenate([each[:, low : low + COLS] for each in r[ROW_NAMES[4 + p // 4]]], axis=0)
        result = dot_nn(left_t[((0,) * 8 + (1,) * 4 + (2, 2, 3, 3))[p]], right)
        if p == PARTS - 1:
            result = jnp.concatenate([result[:, : COLS - split], dot_nn(left_t[2], right[:, COLS - split :])], axis=1)
        slots[p % 2] = result.astype(BF)
        out_copy(p).start()
    out_copy(PARTS - 2).wait()
    out_copy(PARTS - 1).wait()


def weight_gradients(rows):
    count = len(rows["d_mlp"])
    flat = [each for name in ROW_NAMES for each in rows[name]]
    tokens, width = rows["normed"][0].shape
    return pl.pallas_call(
        lambda *refs: grads_kernel(count, *refs),
        name="weight_gradients",
        out_shape=jax.ShapeDtypeStruct((PARTS, width, COLS), BF),
        in_specs=[pl.BlockSpec(memory_space=pltpu.VMEM)] * len(flat),
        out_specs=pl.BlockSpec(memory_space=pl.ANY),
        scratch_shapes=[pltpu.VMEM((4, width, count * tokens), BF), pltpu.VMEM((2, width, COLS), BF), pltpu.SemaphoreType.DMA((2,))],
        compiler_params=pltpu.CompilerParams(vmem_limit_bytes=60 * 2**20),
    )(*flat)


def spread_kernel(p_ref, gate, up, down, d_q, d_k, d_v, d_o, came, wide, q_full, k_full, o_full, v_full, sem_in, sem_out, sem_full):
    width = q_full.shape[0]
    order = [12, 13, 14, 15] + list(range(12))

    def fetch(i):
        return pltpu.make_async_copy(p_ref.at[order[i]], came.at[i % 3], sem_in.at[i % 3])

    def put(i):
        p = order[i]
        return pltpu.make_async_copy(wide.at[i % 2], (gate, up, down)[p // 4].at[:, pl.ds((p % 4) * COLS, COLS)], sem_out.at[i % 2])

    fulls = [(q_full, d_q), (k_full, d_k), (o_full, d_o), (v_full, d_v)]

    def put_full(j):
        return pltpu.make_async_copy(fulls[j][0], fulls[j][1], sem_full.at[j])

    fetch(0).start()
    fetch(1).start()
    for i, p in enumerate(order):
        if i + 2 < len(order):
            fetch(i + 2).start()
        fetch(i).wait()
        part = came.at[i % 3]
        if i >= 6:
            put(i - 2).wait()
        if p >= 12:
            full, other = (q_full, k_full) if p < 14 else (o_full, v_full)
            if p % 2 == 0:
                full[:, :COLS] = part[...].astype(F32)
            else:
                got = part[...].astype(F32)
                full[:, COLS:] = got[:, : width - COLS]
                other[...] = got[:, width - COLS :].T
                put_full(0 if p < 14 else 2).start()
                put_full(1 if p < 14 else 3).start()
        else:
            wide[i % 2] = part[...].astype(F32)
            put(i).start()
    put(len(order) - 2).wait()
    put(len(order) - 1).wait()
    for j in range(4):
        put_full(j).wait()


def spread_out(parts):
    n, width, cols = parts.shape
    kv = 2 * cols - width
    ff = 4 * cols
    shapes = [(width, ff), (width, ff), (width, ff), (width, width), (kv, width), (kv, width), (width, width)]
    vm = pltpu.VMEM
    return pl.pallas_call(
        spread_kernel,
        name="spread_out",
        out_shape=tuple(jax.ShapeDtypeStruct(s, F32) for s in shapes),
        in_specs=[pl.BlockSpec(memory_space=pl.ANY)],
        out_specs=tuple([pl.BlockSpec(memory_space=pl.ANY)] * 7),
        scratch_shapes=[
            vm((3, width, cols), BF), vm((2, width, cols), F32),
            vm((width, width), F32), vm((kv, width), F32), vm((width, width), F32), vm((kv, width), F32),
            pltpu.SemaphoreType.DMA((3,)), pltpu.SemaphoreType.DMA((2,)), pltpu.SemaphoreType.DMA((4,)),
        ],
        compiler_params=pltpu.CompilerParams(vmem_limit_bytes=60 * 2**20),
    )(parts)


def on_device(
    hidden_in,
    cotangent,
    lengths,
    active,
    norm_attn,
    w_query,
    w_key,
    w_value,
    w_out,
    norm_mlp,
    w_gate,
    w_up,
    w_down,
    w_router,
):
    n_tok = lax.axis_size("tok")
    n_grp = lax.axis_size("grp")
    me_index = lax.axis_index("tok")
    rows, width = hidden_in.shape
    nback = min(SPAN, n_tok // 2)

    share = norm_attn.shape[0]
    vectors = jnp.pad(jnp.stack([norm_attn, norm_mlp, w_router]), ((0, 0), (0, 128 - share)))
    small = jnp.concatenate([vectors, active.astype(BF), jnp.zeros((10, 128), BF)], axis=0)
    shards = (jnp.concatenate([w_query, w_key, w_out, w_value], axis=1), w_gate, w_up, w_down, small)
    whole = gather_rows(shards) if (n_grp, n_tok) == (4, 8) else [lax.all_gather(each, "tok", axis=0) for each in shards]
    weights = {name: each.reshape(-1, each.shape[-1]) for name, each in zip(WEIGHTS, whole)}
    gains = jnp.transpose(whole[4][:, :3, :share], (1, 0, 2)).reshape(3, width).astype(F32)
    gains = jnp.pad(gains, ((0, 5), (0, 0)))

    lengths_row = lengths[0]
    token = jnp.arange(rows, dtype=jnp.int32)
    global_rows = me_index * rows + token
    segment_rows = segment_of(lengths_row, global_rows)
    cosine, sine = rotary_tables(position_of(lengths_row, global_rows, segment_rows))
    tables = (jnp.concatenate([cosine] * 4, axis=1), jnp.concatenate([-sine, sine] * 2, axis=1))
    reach = (nback + 1) * rows
    global_keys = (me_index - nback) * rows + jnp.arange(reach, dtype=jnp.int32)
    live_all = jnp.transpose(whole[4][:, 3:6], (1, 0, 2)).reshape(3, -1)
    live_all = jnp.pad(live_all, ((0, 0), (nback * rows, 0)))
    live_keys = lax.dynamic_slice_in_dim(live_all, me_index * rows, reach, 1)
    reachable = (segment_rows[None, :] == segment_of(lengths_row, global_keys)[:, None]) & (
        global_keys[:, None] <= global_rows[None, :]
    )
    masks = jnp.where(reachable[None] & (live_keys[:, :, None] > 0), 1.0, 0.0).astype(F32)
    lives = [active[i].astype(F32)[:, None] for i in range(RECUR)]

    if (n_grp, n_tok) == (4, 8):
        done = all_recursions(hidden_in.T, cotangent.T, masks, jnp.stack(lives), tables, gains, weights, n_tok, nback)
        lefts, rights = ([[done[name + str(step)] for step in reversed(range(RECUR))] for name in names] for names in (ROW_NAMES[:4], ROW_NAMES[4:]))
        parts, acc = summed_gradients(lefts, rights, done["acc_out"])
        output, grad = done["output"], done["grad"]
    else:
        kept = []
        made = first_stage(hidden_in.T, tables, gains, weights)
        state = made["state"]
        for step in range(RECUR):
            kvw = exchange_keys(made["kv"], n_tok, nback)
            last = step == RECUR - 1
            done = forward_stage(state, made["q"], kvw, masks[step], lives[step], tables, gains, weights, last)
            kept.append({**done, "state": state, "q": made["q"], "kvw": kvw, "normed_r": made["normed"]})
            made, state = done, done.get("next")

        acc = jnp.zeros((8, 1024), F32)
        before = None
        rows_of = {name: [] for name in ROW_NAMES}
        for step in reversed(range(RECUR)):
            back = backward_stage(kept[step], before, masks[step], lives[step], tables, gains, acc, weights, cotangent.T)
            acc = back["acc_out"]
            if before is not None:
                rows_of["d_packed"].append(back["d_packed"])
            for name in ("d_mlp", "d_gate", "d_up"):
                rows_of[name].append(back[name])
            for name in ("normed_two", "mixed", "hidden"):
                rows_of[name].append(kept[step][name])
            rows_of["normed"].append(kept[step]["normed_r"])
            before = {"home": exchange_home(back["dkv"], n_tok, nback), "d_q": back["d_q"], "state": kept[step]["state"], "d_state": back["d_state"], "d_attn": back["d_attn"]}
        back = backward_stage(None, before, None, None, tables, gains, acc, weights, None)
        rows_of["d_packed"].append(back["d_packed"])
        acc = back["acc_out"]
        parts = weight_gradients(rows_of)
        parts = lax.psum(parts.astype(F32), ("grp", "tok")).astype(BF)
        acc = lax.psum(acc, ("grp", "tok"))
        output, grad = kept[-1]["output"], back["grad"]
    d_gate, d_up, d_down, d_q, d_k, d_v, d_o = spread_out(parts)
    return (
        output.T,
        grad.T,
        acc[0, :width],
        d_q,
        d_k.T,
        d_v.T,
        d_o,
        acc[1, :width],
        d_gate,
        d_up,
        d_down.T,
        acc[2, :width],
    )


def solution(mesh):
    placed = (
        P(("grp", "tok"), None),
        P(("grp", "tok"), None),
        P("grp", None),
        P(None, ("grp", "tok")),
        P("tok"),
        P("tok", None),
        P("tok", None),
        P("tok", None),
        P("tok", None),
        P("tok"),
        P("tok", None),
        P("tok", None),
        P("tok", None),
        P("tok"),
    )
    return jax.shard_map(
        on_device,
        mesh=mesh,
        in_specs=placed,
        out_specs=(
            P(("grp", "tok"), None),
            P(("grp", "tok"), None),
            P(),
            P(),
            P(),
            P(),
            P(),
            P(),
            P(),
            P(),
            P(),
            P(),
        ),
        check_vma=False,
    )
```

```python
import jax
import jax.numpy as jnp
from jax import lax
from jax.experimental import pallas as pl
from jax.experimental.pallas import tpu as pltpu
from jax.sharding import PartitionSpec as P

MESH = pl.DeviceIdType.MESH

H = 15
KVH = 5
HD = 64
RECUR = 3
SPAN = 16

epsilon = 1e-05
theta = 10000.0
masked = -1000000000.0

def ends_of(lengths_row):
    count = lengths_row.shape[0]
    until = jnp.arange(count)[:, None] >= jnp.arange(count)[None, :]
    return jnp.sum(jnp.where(until, lengths_row[None, :], 0), axis=1)


def segment_of(lengths_row, global_rows):
    ends_at = ends_of(lengths_row)
    return jnp.sum((global_rows[:, None] >= ends_at[None, :]).astype(jnp.int32), axis=1)


def position_of(lengths_row, global_rows, segments):
    ends_at = ends_of(lengths_row)
    starts_at = ends_at - lengths_row
    picked = segments[:, None] == jnp.arange(lengths_row.shape[0], dtype=jnp.int32)[None, :]
    return global_rows - jnp.sum(jnp.where(picked, starts_at[None, :], 0), axis=1)


def rotary_tables(positions):
    half_dim = HD // 2
    inverse = jnp.power(theta, -jnp.arange(half_dim, dtype=jnp.float32) * (2.0 / HD))
    angle = positions.astype(jnp.float32)[..., None] * inverse
    return (jnp.cos(angle), jnp.sin(angle))


F32 = jnp.float32
BF = jnp.bfloat16
CHUNK = 512
WEIGHTS = ("wa", "wg", "wu", "wd")
QK = (H + KVH) * HD
QKO = QK + H * HD


def dot_nn(left, right):
    return lax.dot_general(left, right, (((1,), (0,)), ((), ())), preferred_element_type=F32)


def dot_nt(left, right):
    return lax.dot_general(left, right, (((1,), (1,)), ((), ())), preferred_element_type=F32)


def rope_lanes(tensor, cosine, sine, sign):
    rows, width = tensor.shape
    lane = lax.broadcasted_iota(jnp.int32, (rows, 2 * HD), 1)
    first = lax.rem(lane, HD) < HD // 2
    out = []
    for i in range(0, width, 2 * HD):
        piece = tensor[:, i : i + 2 * HD]
        other = jnp.where(first, pltpu.roll(piece, 2 * HD - HD // 2, 1), pltpu.roll(piece, HD // 2, 1))
        out.append(piece * cosine + (other * sine) * sign)
    return jnp.concatenate(out, axis=1)


def inverse_of(rows):
    return lax.rsqrt(jnp.mean(rows * rows, axis=1, keepdims=True) + epsilon)


def front_part(r, wait, state, ready=None):
    gain = r["gains"][0:1, :]
    normed = (state * inverse_of(state) * gain).astype(BF)
    r["normed"][...] = normed
    wait("wa")
    values = dot_nn(normed, r["wa_v"][:, QKO:]).astype(BF)
    qw = H * HD
    even = qw // (2 * HD) * (2 * HD)
    tail = rope_lanes(dot_nn(normed, r["wa_v"][:, even:QK]), r["cos"][...], r["sin"][...], 1.0).astype(BF)
    r["kv"][...] = jnp.concatenate([tail[:, qw - even :], values], axis=1)
    if ready is not None:
        ready()
    queries = rope_lanes(dot_nn(normed, r["wa_v"][:, :even]), r["cos"][...], r["sin"][...], 1.0).astype(BF)
    r["q"][...] = jnp.concatenate([queries, tail[:, : qw - even]], axis=1)


def head_rows(tensor, g):
    per = H // KVH
    return jnp.concatenate([tensor[:, (g * per + i) * HD : (g * per + i + 1) * HD] for i in range(per)], axis=0)


def window(r):
    rows = r["mask"].shape[0]
    start = lax.rem(lax.axis_index("tok"), 2) * r["q_in"].shape[0]
    return r["kvw"][pl.ds(pl.multiple_of(start, 128), rows), :]


def attention_part(r):
    per = H // KVH
    kv = window(r)
    q = r["q_in"][...]
    rows = q.shape[0]
    allowed = jnp.concatenate([r["mask"][...]] * per, axis=1) > 0
    mixed_t, logs = [], []
    for g in range(KVH):
        k_g = kv[:, g * HD : (g + 1) * HD]
        v_g = kv[:, (KVH + g) * HD : (KVH + g + 1) * HD]
        scores = jnp.where(allowed, dot_nt(k_g, head_rows(q, g)) * HD**-0.5, masked)
        largest = jnp.max(scores, axis=0, keepdims=True)
        exponent = jnp.exp(scores - largest)
        total = jnp.sum(exponent, axis=0, keepdims=True)
        probs = (exponent * (1.0 / total)).astype(BF)
        mix = dot_nn(v_g.T, probs)
        mixed_t += [mix[:, i * rows : (i + 1) * rows] for i in range(per)]
        logs.append(largest + jnp.log(total))
    r["lse"][...] = jnp.concatenate(logs + [logs[0]] * (r["lse"].shape[0] - KVH), axis=0)
    return jnp.concatenate(mixed_t, axis=0).T.astype(BF)


def rest_part(r, wait):
    state = r["state"][...]
    mixed = attention_part(r)
    r["mixed"][...] = mixed
    wait("wa")
    attn_out = dot_nn(mixed, r["wa_v"][:, QK:QKO])
    middle = state + attn_out
    r["middle"][...] = middle
    normed_two = (middle * inverse_of(middle) * r["gains"][1:2, :]).astype(BF)
    r["normed_two"][...] = normed_two
    wait("wg")
    wait("wu")
    wait("wd")
    ff = r["wg_v"].shape[1]
    mlp = jnp.zeros(state.shape, F32)
    for i in range(0, ff, CHUNK):
        at = slice(i, i + CHUNK)
        gate = dot_nn(normed_two, r["wg_v"][:, at])
        up = dot_nn(normed_two, r["wu_v"][:, at])
        r["gate"][:, at] = gate
        r["up"][:, at] = up
        hidden = (gate * jax.nn.sigmoid(gate) * up).astype(BF)
        r["hidden"][:, at] = hidden
        mlp = mlp + dot_nn(hidden, r["wd_v"][at, :])
    branch = attn_out + mlp.astype(BF).astype(F32)
    r["branch"][...] = branch
    router = jax.nn.sigmoid(jnp.sum(state * r["gains"][2:3, :], axis=1, keepdims=True))
    return state + (r["live"][:, 0:1] * router) * branch


def norm_back(grad, rows, gain):
    inverse = inverse_of(rows)
    scaled = rows * inverse
    weighted = grad * gain
    inner = jnp.mean(weighted * scaled, axis=1, keepdims=True)
    return inverse * (weighted - scaled * inner), jnp.sum(grad * scaled, axis=0, keepdims=True)


def back_part(r, wait, grad_after):
    state, live = r["b_state"][...], r["b_live"][:, 0:1]
    width = state.shape[1]
    router_vec = r["gains"][2:3, :]
    router = jax.nn.sigmoid(jnp.sum(state * router_vec, axis=1, keepdims=True))
    d_branch = (live * router) * grad_after
    d_logit = live * (router * (1.0 - router)) * jnp.sum(r["b_branch"][...] * grad_after, axis=1, keepdims=True)
    d_router = jnp.sum(d_logit * state, axis=0, keepdims=True)
    d_mlp = d_branch.astype(BF)
    r["d_mlp"][...] = d_mlp
    wait("wd")
    wait("wg")
    wait("wu")
    ff = r["wg_v"].shape[1]
    d_two = jnp.zeros(state.shape, F32)
    for i in range(0, ff, CHUNK):
        at = slice(i, i + CHUNK)
        gate, up = r["b_gate"][:, at], r["b_up"][:, at]
        sig = jax.nn.sigmoid(gate)
        d_hidden = dot_nt(d_mlp, r["wd_v"][at, :])
        d_up = (d_hidden * (gate * sig)).astype(BF)
        d_gate = (d_hidden * up * (sig * (1.0 + gate * (1.0 - sig)))).astype(BF)
        r["d_up"][:, at] = d_up
        r["d_gate"][:, at] = d_gate
        d_two = d_two + dot_nt(d_gate, r["wg_v"][:, at]) + dot_nt(d_up, r["wu_v"][:, at])
    d_two = d_two.astype(BF).astype(F32)
    d_middle, d_gain_two = norm_back(d_two, r["b_middle"][...], r["gains"][1:2, :])
    r["acc_out"][1:2, :width] = r["acc"][1:2, :width] + d_gain_two
    r["acc_out"][2:3, :width] = r["acc"][2:3, :width] + d_router
    d_attn = (d_branch + d_middle).astype(BF)
    r["d_attn"][...] = d_attn
    r["d_state"][...] = grad_after + d_logit * router_vec + d_middle
    wait("wa")
    d_mixed = dot_nt(d_attn, r["wa_v"][:, QK:QKO]).astype(BF)

    per = H // KVH
    kv = window(r)
    q = r["q_in"][...]
    rows = q.shape[0]
    allowed = jnp.concatenate([r["mask"][...]] * per, axis=1) > 0
    d_keys, d_values, dq_t = [], [], []
    for g in range(KVH):
        k_g = kv[:, g * HD : (g + 1) * HD]
        v_g = kv[:, (KVH + g) * HD : (KVH + g + 1) * HD]
        q_g, do_g = head_rows(q, g), head_rows(d_mixed, g)
        scores = jnp.where(allowed, dot_nt(k_g, q_g) * HD**-0.5, masked)
        probs = jnp.exp(scores - r["b_lse"][g : g + 1, :])
        d_values.append(dot_nn(probs.astype(BF), do_g))
        d_probs = dot_nt(v_g, do_g)
        d_scores = (probs * (d_probs - jnp.sum(probs * d_probs, axis=0, keepdims=True))).astype(BF)
        d_keys.append(dot_nn(d_scores, q_g) * HD**-0.5)
        dq = dot_nn(k_g.T, d_scores) * HD**-0.5
        dq_t += [dq[:, i * rows : (i + 1) * rows] for i in range(per)]
    d_queries = jnp.concatenate(dq_t + [jnp.zeros((HD, rows), F32)], axis=0).T
    d_queries = rope_lanes(d_queries, r["cos"][...], r["sin"][...], -1.0)
    r["d_q"][...] = d_queries[:, : H * HD].astype(BF)
    start = lax.rem(lax.axis_index("tok"), 2) * rows
    partial = r["dkv"]
    keep = partial.shape[0] - kv.shape[0]
    partial[pl.ds(pl.multiple_of((1 - lax.rem(lax.axis_index("tok"), 2)) * kv.shape[0], 128), keep), :] = jnp.zeros((keep, kv.shape[1]), BF)
    partial[pl.ds(pl.multiple_of(start, 128), kv.shape[0]), :] = jnp.concatenate(d_keys + d_values, axis=1).astype(BF)


def home_part(r, wait):
    half = KVH * HD
    total = r["home"][0].astype(F32)
    for i in range(1, r["home"].shape[0]):
        total = total + r["home"][i].astype(F32)
    rows = total.shape[0]
    padded = jnp.concatenate([total[:, :half], jnp.zeros((rows, half % (2 * HD)), F32)], axis=1)
    d_keys = rope_lanes(padded, r["cos"][...], r["sin"][...], -1.0)[:, :half].astype(BF)
    d_values = total[:, half:].astype(BF)
    wait("wa")
    packed = jnp.concatenate([r["h_dq"][...], d_keys, r["h_d_attn"][...], d_values], axis=1)
    r["d_packed"][...] = packed
    d_normed = dot_nt(packed[:, :QK], r["wa_v"][:, :QK]) + dot_nt(d_values, r["wa_v"][:, QKO:])
    state = r["h_state"][...]
    width = state.shape[1]
    d_in, d_gain = norm_back(d_normed, state, r["gains"][0:1, :])
    r["acc_out"][0:1, :width] = r["acc"][0:1, :width] + d_gain
    return r["h_d_state"][...] + d_in


def stage(name, parts, needed, inputs, outputs, weights, rename=None):
    in_names, out_names = list(inputs), list(outputs)
    w_names = [w for w in needed]

    def body(*refs):
        it = iter(refs)
        r = {n: next(it) for n in in_names}
        for n in w_names:
            r[n + "_v"] = next(it)
        for n in out_names:
            r[n] = next(it)
        parts(r, lambda n: None)

    vm = pl.BlockSpec(memory_space=pltpu.VMEM)
    out = pl.pallas_call(
        body,
        name=name,
        out_shape=tuple(outputs.values()),
        in_specs=[vm] * (len(in_names) + len(w_names)),
        out_specs=tuple([vm] * len(out_names)),
        compiler_params=pltpu.CompilerParams(vmem_limit_bytes=20 * 2**20),
    )(*inputs.values(), *[weights[n] for n in w_names])
    return dict(zip(out_names, out))


def shaped(shape, kind):
    return jax.ShapeDtypeStruct(shape, kind)


def front_outs(rows, width):
    return {"normed": shaped((rows, width), BF), "q": shaped((rows, H * HD), BF), "kv": shaped((rows, 2 * KVH * HD), BF)}


def recursion_kernel(chips, back, in_names, out_names, scratch_names, *refs):
    names = in_names + list(WEIGHTS) + out_names + scratch_names
    r = dict(zip(names, refs, strict=True))
    g, t = lax.axis_index("grp"), lax.axis_index("tok")
    z, c = t // 2, lax.rem(t, 2)
    rows = r["hidden_in"].shape[1]
    partner, left, right = (g, z * 2 + 1 - c), (g, t - 2), (g, t + 2)

    copies = {n: pltpu.make_async_copy(r[n], r[n + "_v"], r["w_sem"].at[i]) for i, n in enumerate(WEIGHTS)}
    for n in WEIGHTS:
        copies[n].start()
    done = set()

    def wait(n):
        if n not in done:
            copies[n].wait()
            done.add(n)

    bar = pltpu.get_barrier_semaphore()
    pl.semaphore_signal(bar, inc=1, device_id=partner, device_id_type=MESH)

    @pl.when(z > 0)
    def _():
        pl.semaphore_signal(bar, inc=1, device_id=left, device_id_type=MESH)

    @pl.when(z < chips - 1)
    def _():
        pl.semaphore_signal(bar, inc=1, device_id=right, device_id_type=MESH)

    def at(d, core):
        return pl.ds(pl.multiple_of(((back - d) * 2 + core) * rows, 128), rows)

    r["acc_out"][...] = jnp.zeros(r["acc_out"].shape, F32)
    for step in range(RECUR):
        for d in range(1, back + 1):
            @pl.when(z < d)
            def _():
                for core in (0, 1):
                    r["kvw"][step, at(d, core), :] = jnp.zeros((rows, r["kvw"].shape[2]), BF)

    def of_step(step):
        every = {n: r[n] for n in ("gains", "cos", "sin", "acc_out", "d_state", "d_q", "d_attn", "dkv", "home")}
        every |= {n + "_v": r[n + "_v"] for n in WEIGHTS}
        for n in ("normed", "mixed", "normed_two", "hidden", "d_mlp", "d_gate", "d_up", "d_packed"):
            every[n] = r[n + str(step)]
        for n in ("q", "kvw", "mask", "live", "state", "lse", "middle", "branch", "gate", "up"):
            every[n] = r[n].at[step]
        every |= {"q_in": every["q"], "kv": r["kvw"].at[step, at(0, c)], "acc": r["acc_out"]}
        every |= {"b_" + n: every[n] for n in ("state", "live", "branch", "gate", "up", "middle", "lse")}
        every |= {"h_dq": r["d_q"], "h_state": every["state"], "h_d_state": r["d_state"], "h_d_attn": r["d_attn"]}
        return every

    def k_along(step, d):
        here = r["kvw"].at[step, at(d - 1, c)]
        return copy_to(here, r["kvw"].at[step, at(d, c)], r["k_s"].at[step, d - 1], r["k_r"].at[step, d - 1], right)

    def k_beside(step, d):
        here = r["kvw"].at[step, at(d, c)]
        return copy_to(here, here, r["kc_s"].at[step, d], r["kc_r"].at[step, d], partner)

    def keys_start(step):
        @pl.when(z < chips - 1)
        def _():
            k_along(step, 1).start()

        k_beside(step, 0).start()

    def keys_end(step):
        for d in range(1, back + 1):
            @pl.when(z >= d)
            def _():
                k_along(step, d).wait_recv()
                if d < back:
                    @pl.when(z < chips - 1)
                    def _():
                        k_along(step, d + 1).start()
                k_beside(step, d).start()

        k_beside(step, 0).wait_recv()
        for d in range(1, back + 1):
            @pl.when(z >= d)
            def _():
                k_beside(step, d).wait_recv()

    def keys_drain(step):
        k_beside(step, 0).wait_send()
        for d in range(1, back + 1):
            @pl.when(z >= d)
            def _():
                k_beside(step, d).wait_send()

            @pl.when((z >= d - 1) & (z < chips - 1))
            def _():
                k_along(step, d).wait_send()

    def h_beside(step, d):
        return copy_to(r["dkv"].at[at(d, 1 - c)], r["beside_in"].at[step, d], r["hc_s"].at[step, d], r["hc_r"].at[step, d], partner)

    def h_along(step, d):
        return copy_to(r["sums"].at[d - 1], r["after_in"].at[step, d - 1], r["h_s"].at[step, d - 1], r["h_r"].at[step, d - 1], left)

    def home_start(step):
        for d in range(back, 0, -1):
            @pl.when(z >= d)
            def _():
                h_beside(step, d).start()
        h_beside(step, 0).start()

    def home_end(step):
        for d in range(back, 0, -1):
            @pl.when(z >= d)
            def _():
                h_beside(step, d).wait_recv()
                r["sums"][d - 1] = (r["dkv"][at(d, c), :].astype(F32) + r["beside_in"][step, d].astype(F32)).astype(BF)
                if d < back:
                    @pl.when(z < chips - 1)
                    def _():
                        h_along(step, d + 1).wait_recv()
                        r["sums"][d - 1] = (r["sums"][d - 1].astype(F32) + r["after_in"][step, d].astype(F32)).astype(BF)
                h_along(step, d).start()
        h_beside(step, 0).wait_recv()
        r["home"][0] = r["dkv"][at(0, c), :].astype(F32) + r["beside_in"][step, 0].astype(F32)

        @pl.when(z < chips - 1)
        def _():
            h_along(step, 1).wait_recv()
            r["home"][0] = r["home"][0] + r["after_in"][step, 0].astype(F32)

        h_beside(step, 0).wait_send()
        for d in range(1, back + 1):
            @pl.when(z >= d)
            def _():
                h_beside(step, d).wait_send()
                h_along(step, d).wait_send()

    r["state"][0] = r["hidden_in"][...].astype(F32).T
    met = False
    for step in range(RECUR):
        here = of_step(step)

        def ready(step=step, first=step == 0):
            if first:
                pl.semaphore_wait(bar, 1 + (z < chips - 1).astype(jnp.int32) + (z > 0).astype(jnp.int32))
            keys_start(step)

        front_part(here, wait, here["state"][...], ready)
        keys_end(step)
        after = rest_part(here, wait)
        keys_drain(step)
        if step < RECUR - 1:
            r["state"][step + 1] = after
        else:
            r["output"][...] = after.T.astype(BF)
    grad = r["cot"][...].astype(F32).T
    for step in reversed(range(RECUR)):
        here = of_step(step)
        back_part(here, wait, grad)
        home_start(step)
        home_end(step)
        grad = home_part(here, wait)
    r["grad"][...] = grad.T


def all_recursions(hidden_in, cotangent, masks, lives, tables, gains, weights, n_tok, nback):
    back = nback // 2
    width, rows = hidden_in.shape
    ff = weights["wg"].shape[1]
    kvr = 2 * KVH * HD
    slots = (2 * back + 2) * rows
    ins = {"hidden_in": hidden_in, "cot": cotangent, "mask": masks, "live": lives, "cos": tables[0], "sin": tables[1], "gains": gains}
    outs = {"output": shaped((width, rows), BF), "grad": shaped((width, rows), F32), "acc_out": shaped((8, 1024), F32)}
    sizes = {"normed": width, "d_mlp": width, "mixed": H * HD, "normed_two": width, "hidden": ff, "d_gate": ff, "d_up": ff, "d_packed": QKO + kvr // 2}
    for name, size in sizes.items():
        for step in range(RECUR):
            outs[name + str(step)] = shaped((rows, size), BF)
    dma, vm = pltpu.SemaphoreType.DMA, pltpu.VMEM
    scratch = {n + "_v": vm(weights[n].shape, BF) for n in WEIGHTS}
    scratch |= {
        "state": vm((RECUR, rows, width), F32), "middle": vm((RECUR, rows, width), F32), "branch": vm((RECUR, rows, width), F32),
        "gate": vm((RECUR, rows, ff), F32), "up": vm((RECUR, rows, ff), F32), "lse": vm((RECUR, 8, (H // KVH) * rows), F32),
        "q": vm((RECUR, rows, H * HD), BF), "kvw": vm((RECUR, slots, kvr), BF), "d_state": vm((rows, width), F32),
        "d_q": vm((rows, H * HD), BF), "d_attn": vm((rows, width), BF), "dkv": vm((slots, kvr), BF), "home": vm((1, rows, kvr), F32),
        "beside_in": vm((RECUR, back + 1, rows, kvr), BF), "after_in": vm((RECUR, back, rows, kvr), BF), "sums": vm((back, rows, kvr), BF),
        "w_sem": dma((len(WEIGHTS),)), "k_s": dma((RECUR, back)), "k_r": dma((RECUR, back)), "kc_s": dma((RECUR, back + 1)),
        "kc_r": dma((RECUR, back + 1)), "h_s": dma((RECUR, back)), "h_r": dma((RECUR, back)), "hc_s": dma((RECUR, back + 1)), "hc_r": dma((RECUR, back + 1)),
    }
    spec = pl.BlockSpec(memory_space=pltpu.VMEM)
    got = pl.pallas_call(
        lambda *refs: recursion_kernel(n_tok // 2, back, list(ins), list(outs), list(scratch), *refs),
        name="all_recursions",
        out_shape=tuple(outs.values()),
        in_specs=[spec] * len(ins) + [pl.BlockSpec(memory_space=pl.ANY)] * len(WEIGHTS),
        out_specs=tuple([spec] * len(outs)),
        scratch_shapes=list(scratch.values()),
        compiler_params=pltpu.CompilerParams(collective_id=5, has_side_effects=True, vmem_limit_bytes=62 * 2**20),
    )(*ins.values(), *[weights[n] for n in WEIGHTS])
    return dict(zip(outs, got))


def forward_stage(state, q, kvw, mask, live, tables, gains, weights, last):
    rows, width = state.shape
    ff = weights["wg"].shape[1]
    outs = {
        "mixed": shaped((rows, H * HD), BF), "lse": shaped((8, (H // KVH) * rows), F32), "middle": shaped((rows, width), F32),
        "normed_two": shaped((rows, width), BF), "gate": shaped((rows, ff), F32), "up": shaped((rows, ff), F32),
        "hidden": shaped((rows, ff), BF), "branch": shaped((rows, width), F32),
    }
    if last:
        outs["output"] = shaped((width, rows), BF)
    else:
        outs |= front_outs(rows, width) | {"next": shaped((rows, width), F32)}

    def parts(r, wait):
        state_next = rest_part(r, wait)
        if last:
            r["output"][...] = state_next.T.astype(BF)
        else:
            r["next"][...] = state_next
            front_part(r, wait, state_next)

    needed = ("wa", "wg", "wu", "wd")
    ins = {"state": state, "q_in": q, "kvw": kvw, "mask": mask, "live": live, "cos": tables[0], "sin": tables[1], "gains": gains}
    return stage("forward", parts, needed, ins, outs, weights)


def first_stage(hidden_in, tables, gains, weights):
    width, rows = hidden_in.shape

    def parts(r, wait):
        state = r["hidden"][...].astype(F32).T
        r["state"][...] = state
        front_part(r, wait, state)

    outs = front_outs(rows, width) | {"state": shaped((rows, width), F32)}
    return stage("first", parts, ("wa",), {"hidden": hidden_in, "cos": tables[0], "sin": tables[1], "gains": gains}, outs, weights)


def backward_stage(kept, before, mask, live, tables, gains, acc, weights, cotangent):
    ins = {"cos": tables[0], "sin": tables[1], "gains": gains, "acc": acc}
    outs = {"acc_out": shaped(acc.shape, F32)}
    needed = ()
    rows, width = (kept or before)["state"].shape
    ff = weights["wg"].shape[1]
    kvr = 2 * KVH * HD
    if before is not None:
        ins |= {"home": before["home"], "h_dq": before["d_q"], "h_state": before["state"], "h_d_state": before["d_state"], "h_d_attn": before["d_attn"]}
        outs |= {"d_packed": shaped((rows, QKO + kvr // 2), BF)}
        needed += ("wa",)
    else:
        ins |= {"cot": cotangent}
    if kept is not None:
        ins |= {"b_state": kept["state"], "b_live": live, "b_branch": kept["branch"], "b_gate": kept["gate"], "b_up": kept["up"],
                "b_middle": kept["middle"], "b_lse": kept["lse"], "kvw": kept["kvw"], "q_in": kept["q"], "mask": mask}
        outs |= {"d_mlp": shaped((rows, width), BF), "d_up": shaped((rows, ff), BF), "d_gate": shaped((rows, ff), BF),
                 "d_attn": shaped((rows, width), BF), "d_state": shaped((rows, width), F32), "d_q": shaped((rows, H * HD), BF),
                 "dkv": shaped(kept["kvw"].shape, BF)}
        needed += ("wd", "wg", "wu") + (("wa",) if before is None else ())
    else:
        outs |= {"grad": shaped((width, rows), F32)}

    def parts(r, wait):
        r["acc_out"][...] = r["acc"][...]
        grad = home_part(r, wait) if before is not None else r["cot"][...].astype(F32).T
        if kept is not None:
            back_part(r, wait, grad)
        else:
            r["grad"][...] = grad.T

    return stage("backward", parts, needed, ins, outs, weights)


PARTS = 16
HALF = 480
COLS = 640
STREAMS = (
    ("x", True, 0, 80, 0),
    ("y", True, 80, 80, 0),
    ("x", True, 160, 80, 1),
    ("y", True, 240, 80, 1),
    ("x", True, 320, 80, 2),
    ("y", True, 400, 80, 2),
)
SCHEDULE = (
    (0, 0), (0, 1), (1, 0, 0), (0, 2), (1, 1, 0), (8, 0), (0, 3), (0, 4), (0, 5), (0, 6), (1, 5, 0), (1, 4, 0), (1, 2, 0), (0, 7),
    (1, 3, 0), (8, 1), (2, 0, 0), (0, 8), (0, 9), (1, 2, 1), (1, 8, 0), (1, 6, 0), (1, 7, 0), (2, 1, 0), (0, 10), (0, 11), (1, 10, 0),
    (8, 2), (2, 0, 1), (1, 1, 1), (0, 12), (0, 13), (1, 7, 1), (1, 9, 0), (1, 12, 0), (0, 14), (2, 1, 1), (1, 0, 1), (0, 15), (1, 11, 0),
    (0, 16), (8, 3), (1, 15, 0), (2, 0, 2), (1, 13, 0), (1, 14, 0), (2, 1, 2), (8, 4), (1, 11, 2), (1, 4, 1), (1, 3, 1), (1, 5, 1),
    (1, 6, 1), (2, 0, 3), (1, 8, 1), (2, 1, 3), (1, 10, 1), (2, 3, 0), (1, 9, 1), (2, 2, 0), (3, 0), (2, 3, 1), (3, 1), (1, 12, 1),
    (1, 14, 1), (4, 0), (1, 13, 1), (4, 1), (1, 15, 1), (1, 11, 1), (1, 4, 2), (2, 2, 1), (5, 1), (1, 1, 2), (2, 3, 2), (1, 6, 2),
    (6, 0, 1), (1, 0, 2), (2, 2, 2), (6, 1, 1), (1, 3, 2), (2, 3, 3), (1, 2, 2), (6, 0, 2), (1, 5, 2), (2, 2, 3), (6, 1, 2), (3, 2),
    (2, 5, 0), (3, 3), (1, 7, 2), (1, 9, 2), (7, 0, 1), (2, 4, 0), (6, 0, 3), (6, 1, 3), (2, 5, 1), (7, 1, 1), (1, 14, 2), (4, 2),
    (1, 13, 2), (1, 10, 2), (4, 3), (2, 4, 1), (7, 1, 3), (7, 1, 2), (6, 3, 1), (1, 8, 2), (5, 0), (1, 15, 2), (7, 0, 2), (6, 2, 1),
    (2, 4, 2), (1, 12, 2), (6, 2, 2), (2, 5, 2), (5, 3), (2, 4, 3), (6, 3, 2), (2, 5, 3), (3, 4), (6, 3, 3), (3, 5), (7, 3, 3), (7, 3, 1),
    (7, 0, 3), (4, 4), (4, 5), (6, 2, 3), (6, 4, 1), (6, 5, 1), (7, 5, 1), (6, 4, 2), (7, 4, 1), (7, 2, 3), (7, 2, 1), (5, 2), (7, 4, 2),
    (6, 5, 2), (6, 4, 3), (5, 5), (7, 5, 2), (7, 2, 2), (5, 4), (7, 3, 2), (6, 5, 3), (7, 4, 3), (7, 5, 3),
)
SLOTS = 4


def place():
    g, t = lax.axis_index("grp"), lax.axis_index("tok")
    return g // 2, lax.rem(g, 2), t // 2, lax.rem(t, 2)


def dev(y, x, z, c):
    return (y * 2 + x, z * 2 + c)


def pick(z, values):
    out = jnp.int32(values[3])
    for i in (2, 1, 0):
        out = jnp.where(z == i, jnp.int32(values[i]), out)
    return out


def copy_to(src, dst, send, recv, device):
    return pltpu.make_async_remote_copy(src_ref=src, dst_ref=dst, send_sem=send, recv_sem=recv, device_id=device, device_id_type=MESH)


def add_rows(dst, src, rows, step):
    def body(i, _):
        at = pl.ds(pl.multiple_of(i * step, step), step)
        dst[at, :] = dst[at, :] + src[at, :]
        return 0

    lax.fori_loop(0, rows // step, body, 0)


def tail_kernel(count, *refs):
    left_refs, refs = refs[: 4 * count], refs[4 * count :]
    right_refs, refs = refs[: 4 * count], refs[4 * count :]
    n_s = len(STREAMS)
    v_ref, o_ref, vo_ref, left_t, right, theirs, mine, other = refs[:8]
    ra, rz, rb = refs[8 : 8 + n_s], refs[8 + n_s : 8 + 2 * n_s], refs[8 + 2 * n_s : 8 + 3 * n_s]
    vrecv, load_sem, core_s, core_r, as_, ar, zs, zr, bs, br, ob, obr, oz, ozr, oa, oar, oc, ocr, vs, vr, own_sem = refs[8 + 3 * n_s :]
    y, x, z, c = place()
    partner = dev(y, x, z, 1 - c)
    across = {"x": dev(y, 1 - x, z, c), "y": dev(1 - y, x, z, c)}
    left_dev, right_dev = dev(y, x, z - 1, c), dev(y, x, z + 1, c)
    at_axis = {"x": x, "y": y}
    order = (pick(z, (3, 3, 0, 0)), pick(z, (2, 0, 3, 1)), pick(z, (1, 2, 1, 2)), z)
    far = dev(y, x, jnp.where(z < 2, z + 2, z - 2), c)
    tokens = left_refs[0].shape[0]

    loads = []
    for p in range(PARTS):
        for i in range(count):
            src = right_refs[(p // 4) * count + i].at[:, pl.ds((p % 4) * COLS, COLS)]
            loads.append(pltpu.make_async_copy(src, right.at[p, pl.ds(i * tokens, tokens)], load_sem.at[p * count + i]))
    for cp in loads:
        cp.start()

    bar = pltpu.get_barrier_semaphore()
    for d in (partner, across["x"], across["y"], far):
        pl.semaphore_signal(bar, inc=1, device_id=d, device_id_type=MESH)

    @pl.when(z > 0)
    def _():
        pl.semaphore_signal(bar, inc=1, device_id=left_dev, device_id_type=MESH)

    @pl.when(z < 3)
    def _():
        pl.semaphore_signal(bar, inc=1, device_id=right_dev, device_id_type=MESH)

    for j in range(4):
        left_t[j] = jnp.concatenate([each[...].astype(F32).T.astype(BF) for each in left_refs[j * count : (j + 1) * count]], axis=1)
    for cp in loads:
        cp.wait()
    pl.semaphore_wait(bar, 4 + (z > 0).astype(jnp.int32) + (z < 3).astype(jnp.int32))

    def part_xy(px, py, pz):
        return (px * 2 + py) * 4 + pz

    def part_of(s, pa, pb, pz):
        return part_xy(pa, pb, pz) if STREAMS[s][0] == "x" else part_xy(pb, pa, pz)

    def ab(s):
        a = STREAMS[s][0]
        b = "y" if a == "x" else "x"
        return at_axis[a], at_axis[b], across[a], across[b]

    waits = []
    seq = [(k, i, px, py) for k in range(4) for i, (px, py) in enumerate(((1 - x, 1 - y), (1 - x, y), (x, 1 - y), (x, y)))]

    def core_copy(j):
        k, _, px, py = seq[j]
        p = part_xy(px, py, order[k])
        return copy_to(theirs.at[j % SLOTS, pl.ds(pl.multiple_of((1 - c) * HALF, 16), HALF)], other.at[p], core_s.at[j], core_r.at[p], partner)

    def core_make(j):
        k, _, px, py = seq[j]
        p = part_xy(px, py, order[k])
        if j >= SLOTS:
            core_copy(j - SLOTS).wait_send()
        which = jnp.where(p < 8, 0, jnp.where(p < 12, 1, jnp.where(p < 14, 2, 3)))
        split = 2 * COLS - 2 * HALF
        theirs[j % SLOTS] = dot_nn(left_t[which], right[p]).astype(BF)

        @pl.when(p == PARTS - 1)
        def _():
            theirs[j % SLOTS, :, COLS - split :] = dot_nn(left_t[2], right[p, :, COLS - split :]).astype(BF)

        core_copy(j).start()

    def core_add(j):
        k, i, px, py = seq[j]
        p = part_xy(px, py, order[k])
        core_copy(j).wait_recv()
        mine[p] = theirs[j % SLOTS, pl.ds(pl.multiple_of(c * HALF, 16), HALF), :] + other[p]

    def a_copy(s, pb, pz):
        a, b, to_a, _ = ab(s)
        _, _, r0, n, _ = STREAMS[s]
        return copy_to(mine.at[part_of(s, 1 - a, pb, pz), pl.ds(r0, n)], ra[s].at[pb * 4 + pz], as_.at[s, pb * 4 + pz], ar.at[s, pb * 4 + pz], to_a)

    def a_send(j, batch):
        k, i, px, py = seq[j]
        for s in range(n_s):
            a_axis = STREAMS[s][0]
            if STREAMS[s][4] == batch and (i == 0 or (i == 1 and a_axis == "x") or (i == 2 and a_axis == "y")):
                cp = a_copy(s, py if a_axis == "x" else px, order[k])
                cp.start()
                waits.append(cp)

    def z_index(s, pb, slot):
        return pb * 5 + slot if STREAMS[s][1] else slot

    def z_copy(s, pb, pz, to_right):
        a, b, _, _ = ab(s)
        _, _, r0, n, _ = STREAMS[s]
        src = mine.at[part_of(s, a, pb, pz), pl.ds(r0, n)]
        i = z_index(s, pb, pz if to_right else jnp.where(pz == z - 1, 4, pz))
        return copy_to(src, rz[s].at[i], zs.at[s, i], zr.at[s, i], right_dev if to_right else left_dev)

    def z_take(s, pb, slot):
        a, _, _, _ = ab(s)
        _, _, r0, n, _ = STREAMS[s]
        i = z_index(s, pb, slot)
        copy_to(mine.at[0, pl.ds(r0, n)], rz[s].at[i], zs.at[s, i], zr.at[s, i], left_dev).wait_recv()
        pz = z if slot is z or isinstance(slot, int) else slot
        add_rows(mine.at[part_of(s, a, pb, pz), pl.ds(r0, n)], rz[s].at[i], n, 16)

    def z_step(s, pb, k):
        pz = order[k]
        if k < 3:
            up = jnp.where(pz > z, (z > 0).astype(jnp.int32), (z < 3).astype(jnp.int32))

            @pl.when(up == 1)
            def _():
                z_take(s, pb, pz)

            @pl.when(pz > z)
            def _():
                z_copy(s, pb, pz, True).start()

            @pl.when(pz < z)
            def _():
                z_copy(s, pb, pz, False).start()
        else:
            @pl.when(z > 0)
            def _():
                z_take(s, pb, z)

            @pl.when(z < 3)
            def _():
                z_take(s, pb, 4)

    def z_drain(s, pb, k):
        pz = order[k]

        @pl.when(pz > z)
        def _():
            z_copy(s, pb, pz, True).wait_send()

        @pl.when(pz < z)
        def _():
            z_copy(s, pb, pz, False).wait_send()

    def a_step(s, pb, k):
        a, b, to_a, _ = ab(s)
        _, _, r0, n, _ = STREAMS[s]
        pz = order[k]
        a_copy(s, pb, pz).wait_recv()
        add_rows(mine.at[part_of(s, a, pb, pz), pl.ds(r0, n)], ra[s].at[pb * 4 + pz], n, 16)

    def b_copy(s, pz):
        a, b, _, to_b = ab(s)
        _, second_z, r0, n, _ = STREAMS[s]
        i = 0 if second_z else pz
        return copy_to(mine.at[part_of(s, a, 1 - b, pz), pl.ds(r0, n)], rb[s].at[i], bs.at[s, i], br.at[s, i], to_b)

    def b_step(s, pz):
        a, b, _, _ = ab(s)
        _, second_z, r0, n, _ = STREAMS[s]
        i = 0 if second_z else pz
        b_copy(s, pz).wait_recv()
        add_rows(mine.at[part_of(s, a, b, pz), pl.ds(r0, n)], rb[s].at[i], n, 16)

    def of_batch(batch):
        return [s for s in range(n_s) if STREAMS[s][4] == batch]

    def first_step(only, k):
        for s in (only,):
            _, b, _, _ = ab(s)
            a_step(s, 1 - b, k)
            if STREAMS[s][1]:
                z_step(s, 1 - b, k)
                a_step(s, b, k)
                z_step(s, b, k)
                if k == 3:
                    cp = b_copy(s, z)
                    cp.start()
                    waits.append(cp)
            else:
                cp = b_copy(s, order[k])
                cp.start()
                waits.append(cp)
                a_step(s, b, k)

    def second_step(batch, k):
        for s in of_batch(batch):
            _, b, _, _ = ab(s)
            if not STREAMS[s][1]:
                b_step(s, order[k])
                z_step(s, b, k)

    def vec_copy(i):
        to = (partner, across["x"], across["y"], dev(y, x, jnp.where(lax.rem(z, 2) == 0, z + 1, z - 1), c), far)[i]
        return copy_to(vo_ref, vrecv.at[i], vs.at[i], vr.at[i], to)

    def vec_end(i):
        vec_copy(i).wait()
        vo_ref[...] = vo_ref[...] + vrecv[i]

    half0 = c * HALF

    def out_at(s, p):
        _, _, r0, n, _ = STREAMS[s]
        return o_ref.at[p, pl.ds(pl.multiple_of(half0 + r0, 16), n)]

    def mine_at(s, p):
        _, _, r0, n, _ = STREAMS[s]
        return mine.at[p, pl.ds(r0, n)]

    def go(cp):
        cp.start()
        waits.append(cp)

    def to_core(s, p, src):
        return copy_to(src, out_at(s, p), oc.at[s, p], ocr.at[s, p], partner)

    def to_a(s, pb, pz, src):
        a, b, na, _ = ab(s)
        return copy_to(src, out_at(s, part_of(s, a, pb, pz)), oa.at[s, pb * 4 + pz], oar.at[s, pb * 4 + pz], na)

    def to_b(s, pz, src):
        a, b, _, nb = ab(s)
        return copy_to(src, out_at(s, part_of(s, a, b, pz)), ob.at[s, pz], obr.at[s, pz], nb)

    def to_z(s, pb, pz, src, to_right):
        a, b, _, _ = ab(s)
        i = pb * 8 + pz * 2 + (0 if to_right else 1)
        return copy_to(src, out_at(s, part_of(s, a, pb, pz)), oz.at[s, i], ozr.at[s, pb * 4 + pz], right_dev if to_right else left_dev)

    def spread_z(s, pb, pz, src, sides):
        if 0 in sides:
            @pl.when(z < 3)
            def _():
                to_z(s, pb, pz, src, True).start()
        if 1 in sides:
            @pl.when(z > 0)
            def _():
                to_z(s, pb, pz, src, False).start()

    def finish(only):
        for s in (only,):
            a, b, _, _ = ab(s)
            p = part_of(s, a, b, z)
            b_step(s, z)
            if not STREAMS[s][1]:
                z_step(s, b, 3)
            src = mine_at(s, p)
            if STREAMS[s][1]:
                go(to_b(s, z, src))
                spread_z(s, b, z, src, (0, 1))
            else:
                spread_z(s, b, z, src, (0, 1))
                go(to_b(s, z, src))
            go(to_a(s, b, z, src))
            go(to_core(s, p, src))
            pltpu.make_async_copy(src, out_at(s, p), own_sem.at[s]).start()

    def got_b(s, pz):
        a, b, _, _ = ab(s)
        p = part_of(s, a, 1 - b, pz)
        src = out_at(s, p)
        copy_to(src, src, ob.at[s, pz], obr.at[s, pz], partner).wait_recv()
        if STREAMS[s][1]:
            spread_z(s, 1 - b, pz, src, (0, 1))
        to_a(s, 1 - b, pz, src).start()
        to_core(s, p, src).start()

    def got_z(s, pb, pz, from_left):
        a, b, _, _ = ab(s)
        p = part_of(s, a, pb, pz)
        src = out_at(s, p)
        copy_to(src, src, oz.at[s, 0], ozr.at[s, pb * 4 + pz], partner).wait_recv()
        spread_z(s, pb, pz, src, (0,) if from_left else (1,))
        to_a(s, pb, pz, src).start()
        if not STREAMS[s][1]:
            to_b(s, pz, src).start()
        to_core(s, p, src).start()

    def got_a(s, pb, pz):
        a, b, _, _ = ab(s)
        p = part_of(s, 1 - a, pb, pz)
        src = out_at(s, p)
        copy_to(src, src, oa.at[s, pb * 4 + pz], oar.at[s, pb * 4 + pz], partner).wait_recv()
        to_core(s, p, src).start()

    def gather_b(only):
        for s in (only,):
            got_b(s, z)

    def gather_a(only):
        for s in (only,):
            _, b, _, _ = ab(s)
            got_a(s, b, z)
            got_a(s, 1 - b, z)

    def from_side(t, side):
        return (z - t, z >= t) if side == 0 else (z + t, z + t <= 3)

    def gather_z(only, t):
        for side in (0, 1):
            pz, there = from_side(t, side)

            @pl.when(there)
            def _():
                _, b, _, _ = ab(only)
                got_z(only, b, pz, side == 0)
                got_z(only, 1 - b, pz, side == 0)

    def gather_rest(only, t):
        for side in (0, 1):
            pz, there = from_side(t, side)

            @pl.when(there)
            def _():
                _, b, _, _ = ab(only)
                got_a(only, b, pz)
                got_a(only, 1 - b, pz)

    def make(j):
        if j < PARTS:
            core_make(j)
        if j > 0:
            core_add(j - 1)

    def vec_end_start(i):
        vec_end(i)
        if i < 4:
            vec_copy(i + 1).start()

    vo_ref[...] = v_ref[...]
    vec_copy(0).start()

    actions = (make, a_send, first_step, finish, gather_b, gather_a, gather_z, gather_rest, vec_end_start)
    for kind, *which in SCHEDULE:
        actions[kind](*which)

    for cp in waits:
        cp.wait_send()
    for j in range(PARTS - SLOTS, PARTS):
        core_copy(j).wait_send()
    for s in range(n_s):
        a, b, _, _ = ab(s)
        pltpu.make_async_copy(mine_at(s, part_of(s, a, b, z)), out_at(s, part_of(s, a, b, z)), own_sem.at[s]).wait()
        pbs = (b, 1 - b) if STREAMS[s][1] else (b,)
        for pb in pbs:
            for k in range(3):
                z_drain(s, pb, k)
        for pz in range(4):
            for pb in pbs:
                src = out_at(s, part_of(s, a, pb, pz))

                @pl.when((z >= pz) & (z < 3))
                def _():
                    to_z(s, pb, pz, src, True).wait_send()

                @pl.when((z <= pz) & (z > 0))
                def _():
                    to_z(s, pb, pz, src, False).wait_send()
            for pb in (0, 1):
                src = out_at(s, part_of(s, a, pb, pz))

                @pl.when(jnp.logical_not((pb == b) & (pz == z)))
                def _():
                    to_a(s, pb, pz, src).wait_send()
            if not STREAMS[s][1]:
                @pl.when(z != pz)
                def _():
                    to_b(s, pz, out_at(s, 0)).wait_send()
        for p in range(16):
            src = out_at(s, p)

            @pl.when(p != part_of(s, a, b, z))
            def _():
                to_core(s, p, src).wait_send()
            _, _, r0, n, _ = STREAMS[s]
            dst = o_ref.at[p, pl.ds(pl.multiple_of((1 - c) * HALF + r0, 16), n)]
            copy_to(dst, dst, oc.at[s, p], ocr.at[s, p], partner).wait_recv()


def summed_gradients(lefts, rights, vectors):
    dma = pltpu.SemaphoreType.DMA
    count = len(lefts[0])
    tokens, width = lefts[0][0].shape
    rows = count * tokens
    n_s = len(STREAMS)
    vm = pl.BlockSpec(memory_space=pltpu.VMEM)
    return pl.pallas_call(
        lambda *refs: tail_kernel(count, *refs),
        name="summed_gradients",
        out_shape=(jax.ShapeDtypeStruct((PARTS, width, COLS), BF), jax.ShapeDtypeStruct(vectors.shape, F32)),
        in_specs=[vm] * (4 * count) + [pl.BlockSpec(memory_space=pl.ANY)] * (4 * count) + [vm],
        out_specs=(pl.BlockSpec(memory_space=pl.ANY), vm),
        scratch_shapes=[
            pltpu.VMEM((4, width, rows), BF), pltpu.VMEM((PARTS, rows, COLS), BF), pltpu.VMEM((SLOTS, 2 * HALF, COLS), BF),
            pltpu.VMEM((PARTS, HALF, COLS), BF), pltpu.VMEM((PARTS, HALF, COLS), BF),
            *[pltpu.VMEM((8, s[3], COLS), BF) for s in STREAMS],
            *[pltpu.VMEM((10 if s[1] else 5, s[3], COLS), BF) for s in STREAMS],
            *[pltpu.VMEM((1 if s[1] else 4, s[3], COLS), BF) for s in STREAMS],
            pltpu.VMEM((5, *vectors.shape), F32),
            dma((PARTS * count,)), dma((16,)), dma((16,)),
            dma((n_s, 8)), dma((n_s, 8)), dma((n_s, 10)), dma((n_s, 10)), dma((n_s, 4)), dma((n_s, 4)),
            dma((n_s, 4)), dma((n_s, 4)), dma((n_s, 16)), dma((n_s, 8)), dma((n_s, 8)), dma((n_s, 8)), dma((n_s, 16)), dma((n_s, 16)),
            dma((5,)), dma((5,)), dma((n_s,)),
        ],
        compiler_params=pltpu.CompilerParams(collective_id=1, has_side_effects=True, vmem_limit_bytes=60 * 2**20),
    )(*[a for l in lefts for a in l], *[a for l in rights for a in l], vectors)


QUARTERS = 4
UNITS = ((0, 0, 1536, True, True), (0, 1536, 1024, False, True), (1, 0, 2560, True, False), (2, 0, 2560, True, True), (3, 0, 320, True, False))
FIRST = (0, 2, 3, 4, 1)
SMALL_AT = (5, 10, 15)


def gather_kernel(*refs):
    q_ref, k_ref, o_ref, v_ref = refs[:4]
    ins, outs, packed = (refs[17], *refs[4:8]), refs[8:13], refs[17]
    turned = [each[...].astype(F32).T.astype(BF) for each in (k_ref, v_ref)]
    packed[...] = jnp.concatenate([q_ref[...], turned[0], o_ref[...], turned[1]], axis=1)
    zs, xs, ys, cs, got, cgot, own_s, own_c, own_r, ss, sr, sc, scr = (*refs[13:17], *refs[18:])
    y, x, z, c = place()
    partner, to_x, to_y = dev(y, x, z, 1 - c), dev(y, 1 - x, z, c), dev(1 - y, x, z, c)
    left, right = dev(y, x, z - 1, c), dev(y, x, z + 1, c)
    quarter = (x * 2 + y, (1 - x) * 2 + y, x * 2 + (1 - y), (1 - x) * 2 + (1 - y))
    lasting = []

    def go(cp, when=None):
        if when is None:
            cp.start()
        else:
            @pl.when(when)
            def _():
                cp.start()
        lasting.append((cp, when))

    def cut(ref, u, q):
        m, first, size, shared, _ = UNITS[u]
        n = size // QUARTERS if shared else size
        begin = first + q * n if shared else first
        if m < 3:
            return ref.at[:, pl.ds(pl.multiple_of(begin, 128), n)]
        return ref.at[pl.ds(pl.multiple_of(begin, 16), n), :]

    def out_piece(u, kind, zz, core):
        return cut(outs[UNITS[u][0]].at[zz * 2 + core], u, quarter[kind])

    bar = pltpu.get_barrier_semaphore()
    for d in (partner, to_x, to_y):
        pl.semaphore_signal(bar, inc=1, device_id=d, device_id_type=MESH)

    @pl.when(z > 0)
    def _():
        pl.semaphore_signal(bar, inc=1, device_id=left, device_id_type=MESH)

    @pl.when(z < 3)
    def _():
        pl.semaphore_signal(bar, inc=1, device_id=right, device_id_type=MESH)

    pl.semaphore_wait(bar, 3 + (z > 0).astype(jnp.int32) + (z < 3).astype(jnp.int32))

    def small_copy(zz, core, src, device, sems):
        return copy_to(src, outs[4].at[zz * 2 + core], sems[0], sems[1], device)

    go(small_copy(z, c, ins[4], right, (ss.at[z, 0], sr.at[z])), z < 3)
    go(small_copy(z, c, ins[4], left, (ss.at[z, 1], sr.at[z])), z > 0)
    go(small_copy(z, c, ins[4], partner, (sc.at[z], scr.at[z])))
    for u in FIRST:
        src, dst = cut(ins[UNITS[u][0]], u, quarter[0]), out_piece(u, 0, z, c)
        go(copy_to(src, dst, zs.at[u, z, 0], got.at[0, u, z], right), z < 3)
        go(copy_to(src, dst, zs.at[u, z, 1], got.at[0, u, z], left), z > 0)
    for m in range(4):
        go(copy_to(ins[m], outs[m].at[z * 2 + c], own_c.at[m], own_r.at[m], partner))
    local = [pltpu.make_async_copy(ins[m], outs[m].at[z * 2 + c], own_s.at[m]) for m in range(5)]
    for cp in local:
        cp.start()

    steps = [(t, side) for t in (1, 2, 3) for side in (0, 1)]

    def source(t, side):
        return (z - t, z >= t) if side == 0 else (z + t, z + t <= 3)

    def wait_for(kind, u, zz):
        piece = out_piece(u, kind, zz, c)
        copy_to(piece, piece, cs.at[kind, u, zz], got.at[kind, u, zz], partner).wait_recv()
        return piece

    def sends(kind, u, zz, piece):
        shared, first_x = UNITS[u][3], UNITS[u][4]
        out = []
        if shared and (kind == 0 or (kind == 2 and not first_x)):
            out.append(copy_to(piece, piece, xs.at[min(kind, 1), u, zz], got.at[1 if kind == 0 else 3, u, zz], to_x))
        if shared and (kind == 0 or (kind == 1 and first_x)):
            out.append(copy_to(piece, piece, ys.at[min(kind, 1), u, zz], got.at[2 if kind == 0 else 3, u, zz], to_y))
        out.append(copy_to(piece, piece, cs.at[kind, u, zz], cgot.at[kind, u, zz], partner))
        return out

    def each(kind, u, t, side):
        if kind and not UNITS[u][3]:
            return
        zz, there = source(t, side)
        onward = (z < 3) if side == 0 else (z > 0)

        @pl.when(there)
        def _():
            piece = wait_for(kind, u, zz)
            if kind == 0:
                on = copy_to(piece, piece, zs.at[u, zz, side], got.at[0, u, zz], right if side == 0 else left)

                @pl.when(onward)
                def _():
                    on.start()

            for cp in sends(kind, u, zz, piece):
                cp.start()

        lasting.append((("s", kind, u, t, side), there))
        if kind == 0:
            lasting.append((("z", u, t, side), there & onward))

    def small_step(t, side):
        zz, there = source(t, side)

        @pl.when(there)
        def _():
            piece = outs[4].at[zz * 2 + c]
            copy_to(piece, piece, sc.at[zz], sr.at[zz], partner).wait_recv()

            @pl.when((z < 3) if side == 0 else (z > 0))
            def _():
                small_copy(zz, c, piece, right if side == 0 else left, (ss.at[zz, side], sr.at[zz])).start()

            small_copy(zz, c, piece, partner, (sc.at[zz], scr.at[zz])).start()

        lasting.append((("m", t, side), there))

    turns = [(t, u) for t in (1, 2, 3) for u in FIRST]
    for i in range(len(turns) + 3):
        if i < len(turns):
            t, u = turns[i]
            for side in (0, 1):
                each(0, u, t, side)
        if 0 <= i - 1 < len(turns):
            t, u = turns[i - 1]
            for side in (0, 1):
                each(1 if UNITS[u][4] else 2, u, t, side)
        if 0 <= i - 2 < len(turns):
            t, u = turns[i - 2]
            for side in (0, 1):
                each(2 if UNITS[u][4] else 1, u, t, side)
        if i - 3 >= 0:
            t, u = turns[i - 3]
            for side in (0, 1):
                each(3, u, t, side)
        if i in SMALL_AT:
            for side in (0, 1):
                small_step(SMALL_AT.index(i) + 1, side)

    for cp, when in lasting:
        if not isinstance(cp, tuple):
            if when is None:
                cp.wait_send()
            else:
                @pl.when(when)
                def _():
                    cp.wait_send()
        elif cp[0] == "z":
            _, u, t, side = cp
            zz, _ = source(t, side)
            piece = out_piece(u, 0, zz, c)

            @pl.when(when)
            def _():
                copy_to(piece, piece, zs.at[u, zz, side], got.at[0, u, zz], partner).wait_send()
        elif cp[0] == "m":
            _, t, side = cp
            zz, _ = source(t, side)
            piece = outs[4].at[zz * 2 + c]

            @pl.when(when)
            def _():
                @pl.when((z < 3) if side == 0 else (z > 0))
                def _():
                    small_copy(zz, c, piece, partner, (ss.at[zz, side], sr.at[zz])).wait_send()

                small_copy(zz, c, piece, partner, (sc.at[zz], scr.at[zz])).wait_send()
                other = outs[4].at[zz * 2 + 1 - c]
                copy_to(other, other, sc.at[zz], scr.at[zz], partner).wait_recv()
        else:
            _, kind, u, t, side = cp
            zz, _ = source(t, side)
            piece = out_piece(u, kind, zz, c)
            other = out_piece(u, kind, zz, 1 - c)

            @pl.when(when)
            def _():
                for cp in sends(kind, u, zz, piece):
                    cp.wait_send()
                copy_to(other, other, cs.at[kind, u, zz], cgot.at[kind, u, zz], partner).wait_recv()

    for m in range(4):
        other = outs[m].at[z * 2 + 1 - c]
        copy_to(other, other, own_c.at[m], own_r.at[m], partner).wait_recv()
    other = outs[4].at[z * 2 + 1 - c]
    copy_to(other, other, sc.at[z], scr.at[z], partner).wait_recv()
    for cp in local:
        cp.wait()


def gather_rows(w_query, w_key_t, w_out, w_value_t, others):
    dma = pltpu.SemaphoreType.DMA
    rows, width = w_query.shape
    packed = (rows, 2 * (width + w_key_t.shape[0]))
    shapes = [packed] + [each.shape for each in others]
    n = len(UNITS)
    return pl.pallas_call(
        gather_kernel,
        name="gather_rows",
        out_shape=tuple(jax.ShapeDtypeStruct((8, *each), BF) for each in shapes),
        in_specs=[pl.BlockSpec(memory_space=pltpu.VMEM)] * 4 + [pl.BlockSpec(memory_space=pl.ANY)] * 4,
        out_specs=tuple([pl.BlockSpec(memory_space=pl.ANY)] * 5),
        scratch_shapes=[
            dma((n, 4, 2)), dma((2, n, 4)), dma((2, n, 4)), dma((4, n, 4)), pltpu.VMEM(packed, BF), dma((4, n, 4)), dma((4, n, 4)),
            dma((5,)), dma((4,)), dma((4,)), dma((4, 2)), dma((4,)), dma((4,)), dma((4,)),
        ],
        compiler_params=pltpu.CompilerParams(collective_id=4, has_side_effects=True),
    )(w_query, w_key_t, w_out, w_value_t, *others)


def keys_kernel(chips, back, kv_ref, w_ref, s_right, r_left, s_core, r_core):
    g, t = lax.axis_index("grp"), lax.axis_index("tok")
    z, c = t // 2, lax.rem(t, 2)
    rows = kv_ref.shape[0]
    partner, right = (g, z * 2 + 1 - c), (g, t + 2)

    def slot(d, core):
        return w_ref.at[pl.ds(pl.multiple_of(((back - d) * 2 + core) * rows, 128), rows)]

    bar = pltpu.get_barrier_semaphore()
    pl.semaphore_signal(bar, inc=1, device_id=partner, device_id_type=MESH)

    @pl.when(z > 0)
    def _():
        pl.semaphore_signal(bar, inc=1, device_id=(g, t - 2), device_id_type=MESH)

    def along(d, src):
        return copy_to(src, slot(d, c), s_right.at[d - 1], r_left.at[d - 1], right)

    def beside(d, src):
        return copy_to(src, slot(d, c), s_core.at[d], r_core.at[d], partner)

    own = w_ref.at[pl.ds(pl.multiple_of((back * 2 + c) * rows, 128), rows)]
    own[...] = kv_ref[...]
    for d in range(1, back + 1):
        @pl.when(z < d)
        def _():
            for core in (0, 1):
                slot(d, core)[...] = jnp.zeros(kv_ref.shape, kv_ref.dtype)

    pl.semaphore_wait(bar, 1 + (z < chips - 1).astype(jnp.int32))

    @pl.when(z < chips - 1)
    def _():
        along(1, kv_ref).start()

    beside(0, kv_ref).start()
    for d in range(1, back + 1):
        @pl.when(z >= d)
        def _():
            along(d, slot(d, c)).wait_recv()
            if d < back:
                @pl.when(z < chips - 1)
                def _():
                    along(d + 1, slot(d, c)).start()
            beside(d, slot(d, c)).start()

    def mine_to(d):
        return copy_to(slot(d, 1 - c), slot(d, 1 - c), s_core.at[d], r_core.at[d], partner)

    mine_to(0).wait_recv()
    beside(0, kv_ref).wait_send()

    @pl.when(z < chips - 1)
    def _():
        along(1, kv_ref).wait_send()

    for d in range(1, back + 1):
        @pl.when(z >= d)
        def _():
            mine_to(d).wait_recv()
            beside(d, slot(d, c)).wait_send()
            if d < back:
                @pl.when(z < chips - 1)
                def _():
                    along(d + 1, slot(d, c)).wait_send()


def exchange_keys(kv, n_tok, nback):
    back = nback // 2
    rows = kv.shape[0]
    dma = pltpu.SemaphoreType.DMA
    return pl.pallas_call(
        lambda *refs: keys_kernel(n_tok // 2, back, *refs),
        name="exchange_keys",
        out_shape=jax.ShapeDtypeStruct(((2 * back + 2) * rows, kv.shape[1]), kv.dtype),
        in_specs=[pl.BlockSpec(memory_space=pltpu.VMEM)],
        out_specs=pl.BlockSpec(memory_space=pltpu.VMEM),
        scratch_shapes=[dma((back,)), dma((back,)), dma((back + 1,)), dma((back + 1,))],
        compiler_params=pltpu.CompilerParams(collective_id=2, has_side_effects=True, vmem_limit_bytes=12 * 2**20),
    )(kv)


def home_kernel(chips, back, p_ref, h_ref, beside_in, sums, after_in, s_left, r_right, s_core, r_core):
    g, t = lax.axis_index("grp"), lax.axis_index("tok")
    z, c = t // 2, lax.rem(t, 2)
    rows = h_ref.shape[1]
    partner, left = (g, z * 2 + 1 - c), (g, t - 2)

    def block(d, core):
        return p_ref.at[pl.ds(pl.multiple_of(((back - d) * 2 + core) * rows, 128), rows)]

    bar = pltpu.get_barrier_semaphore()
    pl.semaphore_signal(bar, inc=1, device_id=partner, device_id_type=MESH)

    @pl.when(z < chips - 1)
    def _():
        pl.semaphore_signal(bar, inc=1, device_id=(g, t + 2), device_id_type=MESH)

    pl.semaphore_wait(bar, 1 + (z > 0).astype(jnp.int32))

    def beside(d):
        return copy_to(block(d, 1 - c), beside_in.at[d], s_core.at[d], r_core.at[d], partner)

    def along(d):
        return copy_to(sums.at[d - 1], after_in.at[d - 1], s_left.at[d - 1], r_right.at[d - 1], left)

    for d in range(back, 0, -1):
        @pl.when(z >= d)
        def _():
            beside(d).start()
    beside(0).start()
    for d in range(back, 0, -1):
        @pl.when(z >= d)
        def _():
            beside(d).wait_recv()
            sums[d - 1] = (block(d, c)[...].astype(F32) + beside_in[d].astype(F32)).astype(BF)
            if d < back:
                @pl.when(z < chips - 1)
                def _():
                    along(d + 1).wait_recv()
                    sums[d - 1] = (sums[d - 1].astype(F32) + after_in[d].astype(F32)).astype(BF)
            along(d).start()
    beside(0).wait_recv()
    h_ref[0] = block(0, c)[...].astype(F32) + beside_in[0].astype(F32)

    @pl.when(z < chips - 1)
    def _():
        along(1).wait_recv()
        h_ref[0] = h_ref[0] + after_in[0].astype(F32)

    beside(0).wait_send()
    for d in range(1, back + 1):
        @pl.when(z >= d)
        def _():
            beside(d).wait_send()
            along(d).wait_send()


def exchange_home(partial, n_tok, nback):
    back = nback // 2
    rows = partial.shape[0] // (2 * back + 2)
    width = partial.shape[1]
    dma = pltpu.SemaphoreType.DMA
    return pl.pallas_call(
        lambda *refs: home_kernel(n_tok // 2, back, *refs),
        name="exchange_home",
        out_shape=jax.ShapeDtypeStruct((1, rows, width), F32),
        in_specs=[pl.BlockSpec(memory_space=pltpu.VMEM)],
        out_specs=pl.BlockSpec(memory_space=pltpu.VMEM),
        scratch_shapes=[
            pltpu.VMEM((back + 1, rows, width), BF), pltpu.VMEM((back, rows, width), BF), pltpu.VMEM((back, rows, width), BF),
            dma((back,)), dma((back,)), dma((back + 1,)), dma((back + 1,)),
        ],
        compiler_params=pltpu.CompilerParams(collective_id=3, has_side_effects=True, vmem_limit_bytes=12 * 2**20),
    )(partial)


ROW_NAMES = ("normed_two", "d_mlp", "normed", "mixed", "d_gate", "d_up", "hidden", "d_packed")


def grads_kernel(count, *refs):
    r = {name: refs[i * count : (i + 1) * count] for i, name in enumerate(ROW_NAMES)}
    g_ref, left_t, slots, sems = refs[len(ROW_NAMES) * count :]
    for i, name in enumerate(ROW_NAMES[:4]):
        left_t[i] = jnp.concatenate([each[...].astype(F32).T.astype(BF) for each in r[name]], axis=1)

    def out_copy(p):
        return pltpu.make_async_copy(slots.at[p % 2], g_ref.at[p], sems.at[p % 2])

    split = 2 * COLS - left_t.shape[1]
    for p in range(PARTS):
        if p >= 2:
            out_copy(p - 2).wait()
        low = (p % 4) * COLS
        right = jnp.concatenate([each[:, low : low + COLS] for each in r[ROW_NAMES[4 + p // 4]]], axis=0)
        result = dot_nn(left_t[((0,) * 8 + (1,) * 4 + (2, 2, 3, 3))[p]], right)
        if p == PARTS - 1:
            result = jnp.concatenate([result[:, : COLS - split], dot_nn(left_t[2], right[:, COLS - split :])], axis=1)
        slots[p % 2] = result.astype(BF)
        out_copy(p).start()
    out_copy(PARTS - 2).wait()
    out_copy(PARTS - 1).wait()


def weight_gradients(rows):
    count = len(rows["d_mlp"])
    flat = [each for name in ROW_NAMES for each in rows[name]]
    tokens, width = rows["normed"][0].shape
    return pl.pallas_call(
        lambda *refs: grads_kernel(count, *refs),
        name="weight_gradients",
        out_shape=jax.ShapeDtypeStruct((PARTS, width, COLS), BF),
        in_specs=[pl.BlockSpec(memory_space=pltpu.VMEM)] * len(flat),
        out_specs=pl.BlockSpec(memory_space=pl.ANY),
        scratch_shapes=[pltpu.VMEM((4, width, count * tokens), BF), pltpu.VMEM((2, width, COLS), BF), pltpu.SemaphoreType.DMA((2,))],
        compiler_params=pltpu.CompilerParams(vmem_limit_bytes=60 * 2**20),
    )(*flat)


def spread_kernel(p_ref, gate, up, down, d_q, d_k, d_v, d_o, came, wide, q_full, k_full, o_full, v_full, sem_in, sem_out, sem_full):
    width = q_full.shape[0]
    order = [12, 13, 14, 15] + list(range(12))

    def fetch(i):
        return pltpu.make_async_copy(p_ref.at[order[i]], came.at[i % 3], sem_in.at[i % 3])

    def put(i):
        p = order[i]
        return pltpu.make_async_copy(wide.at[i % 2], (gate, up, down)[p // 4].at[:, pl.ds((p % 4) * COLS, COLS)], sem_out.at[i % 2])

    fulls = [(q_full, d_q), (k_full, d_k), (o_full, d_o), (v_full, d_v)]

    def put_full(j):
        return pltpu.make_async_copy(fulls[j][0], fulls[j][1], sem_full.at[j])

    fetch(0).start()
    fetch(1).start()
    for i, p in enumerate(order):
        if i + 2 < len(order):
            fetch(i + 2).start()
        fetch(i).wait()
        part = came.at[i % 3]
        if i >= 6:
            put(i - 2).wait()
        if p >= 12:
            full, other = (q_full, k_full) if p < 14 else (o_full, v_full)
            if p % 2 == 0:
                full[:, :COLS] = part[...].astype(F32)
            else:
                got = part[...].astype(F32)
                full[:, COLS:] = got[:, : width - COLS]
                other[...] = got[:, width - COLS :].T
                put_full(0 if p < 14 else 2).start()
                put_full(1 if p < 14 else 3).start()
        else:
            wide[i % 2] = part[...].astype(F32)
            put(i).start()
    put(len(order) - 2).wait()
    put(len(order) - 1).wait()
    for j in range(4):
        put_full(j).wait()


def spread_out(parts):
    n, width, cols = parts.shape
    kv = 2 * cols - width
    ff = 4 * cols
    shapes = [(width, ff), (width, ff), (width, ff), (width, width), (kv, width), (kv, width), (width, width)]
    vm = pltpu.VMEM
    return pl.pallas_call(
        spread_kernel,
        name="spread_out",
        out_shape=tuple(jax.ShapeDtypeStruct(s, F32) for s in shapes),
        in_specs=[pl.BlockSpec(memory_space=pl.ANY)],
        out_specs=tuple([pl.BlockSpec(memory_space=pl.ANY)] * 7),
        scratch_shapes=[
            vm((3, width, cols), BF), vm((2, width, cols), F32),
            vm((width, width), F32), vm((kv, width), F32), vm((width, width), F32), vm((kv, width), F32),
            pltpu.SemaphoreType.DMA((3,)), pltpu.SemaphoreType.DMA((2,)), pltpu.SemaphoreType.DMA((4,)),
        ],
        compiler_params=pltpu.CompilerParams(vmem_limit_bytes=60 * 2**20),
    )(parts)


def on_device(
    hidden_in,
    cotangent,
    lengths,
    active,
    norm_attn,
    w_query,
    w_key,
    w_value,
    w_out,
    norm_mlp,
    w_gate,
    w_up,
    w_down,
    w_router,
):
    n_tok = lax.axis_size("tok")
    n_grp = lax.axis_size("grp")
    me_index = lax.axis_index("tok")
    rows, width = hidden_in.shape
    nback = min(SPAN, n_tok // 2)

    share = norm_attn.shape[0]
    vectors = jnp.pad(jnp.stack([norm_attn, norm_mlp, w_router]), ((0, 0), (0, 128 - share)))
    small = jnp.concatenate([vectors, active.astype(BF), jnp.zeros((10, 128), BF)], axis=0)
    others = (w_gate, w_up, w_down, small)
    if (n_grp, n_tok) == (4, 8):
        whole = gather_rows(w_query, w_key.T, w_out, w_value.T, others)
    else:
        packed = jnp.concatenate([w_query, w_key, w_out, w_value], axis=1)
        whole = [lax.all_gather(each, "tok", axis=0) for each in (packed, *others)]
    weights = {name: each.reshape(-1, each.shape[-1]) for name, each in zip(WEIGHTS, whole)}
    gains = jnp.transpose(whole[4][:, :3, :share], (1, 0, 2)).reshape(3, width).astype(F32)
    gains = jnp.pad(gains, ((0, 5), (0, 0)))

    lengths_row = lengths[0]
    token = jnp.arange(rows, dtype=jnp.int32)
    global_rows = me_index * rows + token
    segment_rows = segment_of(lengths_row, global_rows)
    cosine, sine = rotary_tables(position_of(lengths_row, global_rows, segment_rows))
    tables = (jnp.concatenate([cosine] * 4, axis=1), jnp.concatenate([-sine, sine] * 2, axis=1))
    reach = (nback + 1) * rows
    global_keys = (me_index - nback) * rows + jnp.arange(reach, dtype=jnp.int32)
    live_all = jnp.transpose(whole[4][:, 3:6], (1, 0, 2)).reshape(3, -1)
    live_all = jnp.pad(live_all, ((0, 0), (nback * rows, 0)))
    live_keys = lax.dynamic_slice_in_dim(live_all, me_index * rows, reach, 1)
    reachable = (segment_rows[None, :] == segment_of(lengths_row, global_keys)[:, None]) & (
        global_keys[:, None] <= global_rows[None, :]
    )
    masks = jnp.where(reachable[None] & (live_keys[:, :, None] > 0), 1.0, 0.0).astype(F32)
    lives = [active[i].astype(F32)[:, None] for i in range(RECUR)]

    if (n_grp, n_tok) == (4, 8):
        done = all_recursions(hidden_in.T, cotangent.T, masks, jnp.stack(lives), tables, gains, weights, n_tok, nback)
        lefts, rights = ([[done[name + str(step)] for step in reversed(range(RECUR))] for name in names] for names in (ROW_NAMES[:4], ROW_NAMES[4:]))
        parts, acc = summed_gradients(lefts, rights, done["acc_out"])
        output, grad = done["output"], done["grad"]
    else:
        kept = []
        made = first_stage(hidden_in.T, tables, gains, weights)
        state = made["state"]
        for step in range(RECUR):
            kvw = exchange_keys(made["kv"], n_tok, nback)
            last = step == RECUR - 1
            done = forward_stage(state, made["q"], kvw, masks[step], lives[step], tables, gains, weights, last)
            kept.append({**done, "state": state, "q": made["q"], "kvw": kvw, "normed_r": made["normed"]})
            made, state = done, done.get("next")

        acc = jnp.zeros((8, 1024), F32)
        before = None
        rows_of = {name: [] for name in ROW_NAMES}
        for step in reversed(range(RECUR)):
            back = backward_stage(kept[step], before, masks[step], lives[step], tables, gains, acc, weights, cotangent.T)
            acc = back["acc_out"]
            if before is not None:
                rows_of["d_packed"].append(back["d_packed"])
            for name in ("d_mlp", "d_gate", "d_up"):
                rows_of[name].append(back[name])
            for name in ("normed_two", "mixed", "hidden"):
                rows_of[name].append(kept[step][name])
            rows_of["normed"].append(kept[step]["normed_r"])
            before = {"home": exchange_home(back["dkv"], n_tok, nback), "d_q": back["d_q"], "state": kept[step]["state"], "d_state": back["d_state"], "d_attn": back["d_attn"]}
        back = backward_stage(None, before, None, None, tables, gains, acc, weights, None)
        rows_of["d_packed"].append(back["d_packed"])
        acc = back["acc_out"]
        parts = weight_gradients(rows_of)
        parts = lax.psum(parts.astype(F32), ("grp", "tok")).astype(BF)
        acc = lax.psum(acc, ("grp", "tok"))
        output, grad = kept[-1]["output"], back["grad"]
    d_gate, d_up, d_down, d_q, d_k, d_v, d_o = spread_out(parts)
    return (
        output.T,
        grad.T,
        acc[0, :width],
        d_q,
        d_k.T,
        d_v.T,
        d_o,
        acc[1, :width],
        d_gate,
        d_up,
        d_down.T,
        acc[2, :width],
    )


def solution(mesh):
    placed = (
        P(("grp", "tok"), None),
        P(("grp", "tok"), None),
        P("grp", None),
        P(None, ("grp", "tok")),
        P("tok"),
        P("tok", None),
        P("tok", None),
        P("tok", None),
        P("tok", None),
        P("tok"),
        P("tok", None),
        P("tok", None),
        P("tok", None),
        P("tok"),
    )
    return jax.shard_map(
        on_device,
        mesh=mesh,
        in_specs=placed,
        out_specs=(
            P(("grp", "tok"), None),
            P(("grp", "tok"), None),
            P(),
            P(),
            P(),
            P(),
            P(),
            P(),
            P(),
            P(),
            P(),
            P(),
        ),
        check_vma=False,
    )
```

```python
import jax
import jax.numpy as jnp
from jax import lax
from jax.experimental import pallas as pl
from jax.experimental.pallas import tpu as pltpu
from jax.sharding import PartitionSpec as P

MESH = pl.DeviceIdType.MESH

H = 15
KVH = 5
HD = 64
RECUR = 3
SPAN = 16

epsilon = 1e-05
theta = 10000.0
masked = -1000000000.0

def ends_of(lengths_row):
    count = lengths_row.shape[0]
    until = jnp.arange(count)[:, None] >= jnp.arange(count)[None, :]
    return jnp.sum(jnp.where(until, lengths_row[None, :], 0), axis=1)


def segment_of(lengths_row, global_rows):
    ends_at = ends_of(lengths_row)
    return jnp.sum((global_rows[:, None] >= ends_at[None, :]).astype(jnp.int32), axis=1)


def position_of(lengths_row, global_rows, segments):
    ends_at = ends_of(lengths_row)
    starts_at = ends_at - lengths_row
    picked = segments[:, None] == jnp.arange(lengths_row.shape[0], dtype=jnp.int32)[None, :]
    return global_rows - jnp.sum(jnp.where(picked, starts_at[None, :], 0), axis=1)


def rotary_tables(positions):
    half_dim = HD // 2
    inverse = jnp.power(theta, -jnp.arange(half_dim, dtype=jnp.float32) * (2.0 / HD))
    angle = positions.astype(jnp.float32)[..., None] * inverse
    return (jnp.cos(angle), jnp.sin(angle))


F32 = jnp.float32
BF = jnp.bfloat16
CHUNK = 512
ROW_NAMES = ("normed_two", "d_mlp", "normed", "mixed", "d_gate", "d_up", "hidden", "d_packed")
WEIGHTS = ("wa", "wg", "wu", "wd")
QK = (H + KVH) * HD
QKO = QK + H * HD


def dot_nn(left, right):
    return lax.dot_general(left, right, (((1,), (0,)), ((), ())), preferred_element_type=F32)


def dot_nt(left, right):
    return lax.dot_general(left, right, (((1,), (1,)), ((), ())), preferred_element_type=F32)


def rope_lanes(tensor, cosine, sine, sign):
    rows, width = tensor.shape
    lane = lax.broadcasted_iota(jnp.int32, (rows, 2 * HD), 1)
    first = lax.rem(lane, HD) < HD // 2
    out = []
    for i in range(0, width, 2 * HD):
        piece = tensor[:, i : i + 2 * HD]
        other = jnp.where(first, pltpu.roll(piece, 2 * HD - HD // 2, 1), pltpu.roll(piece, HD // 2, 1))
        out.append(piece * cosine + (other * sine) * sign)
    return jnp.concatenate(out, axis=1)


def inverse_of(rows):
    return lax.rsqrt(jnp.mean(rows * rows, axis=1, keepdims=True) + epsilon)


def front_part(r, wait, state, ready=None):
    gain = r["gains"][0:1, :]
    normed = (state * inverse_of(state) * gain).astype(BF)
    r["normed"][...] = normed
    wait("wa")
    values = dot_nn(normed, r["wa_v"][:, QKO:]).astype(BF)
    qw = H * HD
    even = qw // (2 * HD) * (2 * HD)
    tail = rope_lanes(dot_nn(normed, r["wa_v"][:, even:QK]), r["cos"][...], r["sin"][...], 1.0).astype(BF)
    keys = tail[:, qw - even :]
    r["kv"][...] = jnp.concatenate([each[:, g * HD : (g + 1) * HD] for g in range(KVH) for each in (keys, values)], axis=1)
    if ready is not None:
        ready()
    queries = rope_lanes(dot_nn(normed, r["wa_v"][:, :even]), r["cos"][...], r["sin"][...], 1.0).astype(BF)
    r["q"][...] = jnp.concatenate([queries, tail[:, : qw - even]], axis=1)


def head_rows(tensor, g):
    per = H // KVH
    return jnp.concatenate([tensor[:, (g * per + i) * HD : (g * per + i + 1) * HD] for i in range(per)], axis=0)


def key_rows(r):
    start = lax.rem(lax.axis_index("tok"), 2) * r["q_in"].shape[0]
    return pl.ds(pl.multiple_of(start, 128), r["mask"].shape[0])


def attention_part(r, arrived=None):
    per = H // KVH
    q = r["q_in"][...]
    rows = q.shape[0]
    allowed = jnp.concatenate([r["mask"][...]] * per, axis=1) > 0
    mixed_t, logs = [], []
    for g in range(KVH):
        if arrived is not None:
            arrived(g)
        kv = r["kvw"][key_rows(r), 2 * g * HD : 2 * (g + 1) * HD]
        scores = jnp.where(allowed, dot_nt(kv[:, :HD], head_rows(q, g)) * HD**-0.5, masked)
        largest = jnp.max(scores, axis=0, keepdims=True)
        exponent = jnp.exp(scores - largest)
        total = jnp.sum(exponent, axis=0, keepdims=True)
        probs = (exponent * (1.0 / total)).astype(BF)
        mix = dot_nn(kv[:, HD:].T, probs)
        mixed_t += [mix[:, i * rows : (i + 1) * rows] for i in range(per)]
        logs.append(largest + jnp.log(total))
    r["lse"][...] = jnp.concatenate(logs + [logs[0]] * (r["lse"].shape[0] - KVH), axis=0)
    return jnp.concatenate(mixed_t, axis=0).T.astype(BF)


def rest_part(r, wait, arrived=None):
    state = r["state"][...]
    mixed = attention_part(r, arrived)
    r["mixed"][...] = mixed
    wait("wa")
    attn_out = dot_nn(mixed, r["wa_v"][:, QK:QKO])
    middle = state + attn_out
    r["middle"][...] = middle
    normed_two = (middle * inverse_of(middle) * r["gains"][1:2, :]).astype(BF)
    r["normed_two"][...] = normed_two
    wait("wg")
    wait("wu")
    wait("wd")
    ff = r["wg_v"].shape[1]
    mlp = jnp.zeros(state.shape, F32)
    for i in range(0, ff, CHUNK):
        at = slice(i, i + CHUNK)
        gate = dot_nn(normed_two, r["wg_v"][:, at])
        up = dot_nn(normed_two, r["wu_v"][:, at])
        r["gate"][:, at] = gate
        r["up"][:, at] = up
        hidden = (gate * jax.nn.sigmoid(gate) * up).astype(BF)
        r["hidden"][:, at] = hidden
        mlp = mlp + dot_nn(hidden, r["wd_v"][at, :])
    branch = attn_out + mlp.astype(BF).astype(F32)
    r["branch"][...] = branch
    router = jax.nn.sigmoid(jnp.sum(state * r["gains"][2:3, :], axis=1, keepdims=True))
    return state + (r["live"][:, 0:1] * router) * branch


def norm_back(grad, rows, gain):
    inverse = inverse_of(rows)
    scaled = rows * inverse
    weighted = grad * gain
    inner = jnp.mean(weighted * scaled, axis=1, keepdims=True)
    return inverse * (weighted - scaled * inner), jnp.sum(grad * scaled, axis=0, keepdims=True)


def back_part(r, wait, grad_after, made=None):
    state, live = r["b_state"][...], r["b_live"][:, 0:1]
    width = state.shape[1]
    router_vec = r["gains"][2:3, :]
    router = jax.nn.sigmoid(jnp.sum(state * router_vec, axis=1, keepdims=True))
    d_branch = (live * router) * grad_after
    d_logit = live * (router * (1.0 - router)) * jnp.sum(r["b_branch"][...] * grad_after, axis=1, keepdims=True)
    d_router = jnp.sum(d_logit * state, axis=0, keepdims=True)
    d_mlp = d_branch.astype(BF)
    r["d_mlp"][...] = d_mlp
    wait("wd")
    wait("wg")
    wait("wu")
    ff = r["wg_v"].shape[1]
    d_two = jnp.zeros(state.shape, F32)
    for i in range(0, ff, CHUNK):
        at = slice(i, i + CHUNK)
        gate, up = r["b_gate"][:, at], r["b_up"][:, at]
        sig = jax.nn.sigmoid(gate)
        d_hidden = dot_nt(d_mlp, r["wd_v"][at, :])
        d_up = (d_hidden * (gate * sig)).astype(BF)
        d_gate = (d_hidden * up * (sig * (1.0 + gate * (1.0 - sig)))).astype(BF)
        r["d_up"][:, at] = d_up
        r["d_gate"][:, at] = d_gate
        d_two = d_two + dot_nt(d_gate, r["wg_v"][:, at]) + dot_nt(d_up, r["wu_v"][:, at])
    d_two = d_two.astype(BF).astype(F32)
    d_middle, d_gain_two = norm_back(d_two, r["b_middle"][...], r["gains"][1:2, :])
    r["acc_out"][1:2, :width] = r["acc"][1:2, :width] + d_gain_two
    r["acc_out"][2:3, :width] = r["acc"][2:3, :width] + d_router
    d_attn = (d_branch + d_middle).astype(BF)
    r["d_attn"][...] = d_attn
    r["d_state"][...] = grad_after + d_logit * router_vec + d_middle
    wait("wa")
    d_mixed = dot_nt(d_attn, r["wa_v"][:, QK:QKO]).astype(BF)

    per = H // KVH
    q = r["q_in"][...]
    rows = q.shape[0]
    allowed = jnp.concatenate([r["mask"][...]] * per, axis=1) > 0
    partial, reach = r["dkv"], r["mask"].shape[0]
    keep = partial.shape[0] - reach
    unused = (1 - lax.rem(lax.axis_index("tok"), 2)) * reach
    partial[pl.ds(pl.multiple_of(unused, 128), keep), :] = jnp.zeros((keep, partial.shape[1]), BF)
    dq_t = []
    for g in range(KVH):
        lanes = slice(2 * g * HD, 2 * (g + 1) * HD)
        kv = r["kvw"][key_rows(r), lanes]
        k_g, v_g = kv[:, :HD], kv[:, HD:]
        q_g, do_g = head_rows(q, g), head_rows(d_mixed, g)
        scores = jnp.where(allowed, dot_nt(k_g, q_g) * HD**-0.5, masked)
        probs = jnp.exp(scores - r["b_lse"][g : g + 1, :])
        d_values = dot_nn(probs.astype(BF), do_g)
        d_probs = dot_nt(v_g, do_g)
        d_scores = (probs * (d_probs - jnp.sum(probs * d_probs, axis=0, keepdims=True))).astype(BF)
        d_keys = dot_nn(d_scores, q_g) * HD**-0.5
        partial[key_rows(r), lanes] = jnp.concatenate([d_keys, d_values], axis=1).astype(BF)
        dq = dot_nn(k_g.T, d_scores) * HD**-0.5
        dq_t += [dq[:, i * rows : (i + 1) * rows] for i in range(per)]
        if made is not None:
            made(g)
    d_queries = jnp.concatenate(dq_t + [jnp.zeros((HD, rows), F32)], axis=0).T
    d_queries = rope_lanes(d_queries, r["cos"][...], r["sin"][...], -1.0)
    r["d_q"][...] = d_queries[:, : H * HD].astype(BF)


def home_part(r, wait):
    total = r["home"][0]
    turned = rope_lanes(total, r["cos"][...], r["sin"][...], -1.0).astype(BF)
    low = total.astype(BF)
    d_keys = jnp.concatenate([turned[:, 2 * g * HD : (2 * g + 1) * HD] for g in range(KVH)], axis=1)
    d_values = jnp.concatenate([low[:, (2 * g + 1) * HD : 2 * (g + 1) * HD] for g in range(KVH)], axis=1)
    wait("wa")
    packed = jnp.concatenate([r["h_dq"][...], d_keys, r["h_d_attn"][...], d_values], axis=1)
    r["d_packed"][...] = packed
    d_normed = dot_nt(packed[:, :QK], r["wa_v"][:, :QK]) + dot_nt(d_values, r["wa_v"][:, QKO:])
    state = r["h_state"][...]
    width = state.shape[1]
    d_in, d_gain = norm_back(d_normed, state, r["gains"][0:1, :])
    r["acc_out"][0:1, :width] = r["acc"][0:1, :width] + d_gain
    return r["h_d_state"][...] + d_in


def stage(name, parts, needed, inputs, outputs, weights, rename=None):
    in_names, out_names = list(inputs), list(outputs)
    w_names = [w for w in needed]

    def body(*refs):
        it = iter(refs)
        r = {n: next(it) for n in in_names}
        for n in w_names:
            r[n + "_v"] = next(it)
        for n in out_names:
            r[n] = next(it)
        parts(r, lambda n: None)

    vm = pl.BlockSpec(memory_space=pltpu.VMEM)
    out = pl.pallas_call(
        body,
        name=name,
        out_shape=tuple(outputs.values()),
        in_specs=[vm] * (len(in_names) + len(w_names)),
        out_specs=tuple([vm] * len(out_names)),
        compiler_params=pltpu.CompilerParams(vmem_limit_bytes=20 * 2**20),
    )(*inputs.values(), *[weights[n] for n in w_names])
    return dict(zip(out_names, out))


def shaped(shape, kind):
    return jax.ShapeDtypeStruct(shape, kind)


def front_outs(rows, width):
    return {"normed": shaped((rows, width), BF), "q": shaped((rows, H * HD), BF), "kv": shaped((rows, 2 * KVH * HD), BF)}


FIRST_HEADS = (KVH + 1) // 2
PIECES = ((0, 2 * HD * FIRST_HEADS), (2 * HD * FIRST_HEADS, 2 * HD * (KVH - FIRST_HEADS)))


def recursion_kernel(chips, back, in_names, out_names, scratch_names, *refs):
    names = in_names + list(WEIGHTS) + out_names + scratch_names
    r = dict(zip(names, refs, strict=True))
    g, t = lax.axis_index("grp"), lax.axis_index("tok")
    z, c = t // 2, lax.rem(t, 2)
    rows = r["hidden_in"].shape[1]
    partner, left, right = (g, z * 2 + 1 - c), (g, t - 2), (g, t + 2)

    copies = {n: pltpu.make_async_copy(r[n], r[n + "_v"], r["w_sem"].at[i]) for i, n in enumerate(WEIGHTS)}
    for n in WEIGHTS:
        copies[n].start()
    done = set()

    def wait(n):
        if n not in done:
            copies[n].wait()
            done.add(n)

    bar = pltpu.get_barrier_semaphore()
    pl.semaphore_signal(bar, inc=1, device_id=partner, device_id_type=MESH)

    @pl.when(z > 0)
    def _():
        pl.semaphore_signal(bar, inc=1, device_id=left, device_id_type=MESH)

    @pl.when(z < chips - 1)
    def _():
        pl.semaphore_signal(bar, inc=1, device_id=right, device_id_type=MESH)

    def at(d, core):
        return pl.ds(pl.multiple_of(((back - d) * 2 + core) * rows, 128), rows)

    r["acc_out"][...] = jnp.zeros(r["acc_out"].shape, F32)
    for step in range(RECUR):
        for d in range(1, back + 1):
            @pl.when(z < d)
            def _():
                for core in (0, 1):
                    r["kvw"][step, at(d, core), :] = jnp.zeros((rows, r["kvw"].shape[2]), BF)

    def of_step(step):
        every = {n: r[n] for n in ("gains", "cos", "sin", "acc_out", "d_state", "d_q", "d_attn", "dkv", "home")}
        every |= {n + "_v": r[n + "_v"] for n in WEIGHTS}
        every |= {n: r[n] for n in ROW_NAMES[:4]}
        every |= {n: r[n + str(step)] for n in ROW_NAMES[4:]}
        for n in ("q", "kvw", "mask", "live", "state", "lse", "middle", "branch", "gate", "up"):
            every[n] = r[n].at[step]
        every |= {"q_in": every["q"], "kv": r["kvw"].at[step, at(0, c)], "acc": r["acc_out"]}
        every |= {"b_" + n: every[n] for n in ("state", "live", "branch", "gate", "up", "middle", "lse")}
        every |= {"h_dq": r["d_q"], "h_state": every["state"], "h_d_state": r["d_state"], "h_d_attn": r["d_attn"]}
        return every

    def k_along(step, d, j):
        src, dst = (r["kvw"].at[step, at(e, c), pl.ds(*PIECES[j])] for e in (d - 1, d))
        return copy_to(src, dst, r["k_s"].at[step, j, d - 1], r["k_r"].at[step, j, d - 1], right)

    def k_beside(step, d, j):
        here = r["kvw"].at[step, at(d, c), pl.ds(*PIECES[j])]
        return copy_to(here, here, r["kc_s"].at[step, j, d], r["kc_r"].at[step, j, d], partner)

    def keys_start(step):
        for j in (0, 1):
            @pl.when(z < chips - 1)
            def _():
                k_along(step, 1, j).start()

            k_beside(step, 0, j).start()

    def keys_pass(step, d, j):
        @pl.when(z >= d)
        def _():
            k_along(step, d, j).wait_recv()
            if d < back:
                @pl.when(z < chips - 1)
                def _():
                    k_along(step, d + 1, j).start()
            k_beside(step, d, j).start()

    def keys_end(step, j):
        k_beside(step, 0, j).wait_recv()
        for d in range(1, back + 1):
            @pl.when(z >= d)
            def _():
                k_beside(step, d, j).wait_recv()

    def keys_arrived(step, g):
        if g == 0:
            for d in range(1, back):
                keys_pass(step, d, 0)
                keys_pass(step, d, 1)
            keys_pass(step, back, 0)
            keys_end(step, 0)
        if g == FIRST_HEADS:
            keys_pass(step, back, 1)
            keys_end(step, 1)

    def keys_drain(step):
        for j in (0, 1):
            k_beside(step, 0, j).wait_send()
            for d in range(1, back + 1):
                @pl.when(z >= d)
                def _():
                    k_beside(step, d, j).wait_send()

                @pl.when((z >= d - 1) & (z < chips - 1))
                def _():
                    k_along(step, d, j).wait_send()

    def h_beside(step, d, j):
        piece = pl.ds(*PIECES[j])
        return copy_to(r["dkv"].at[at(d, 1 - c), piece], r["beside_in"].at[step, d, :, piece], r["hc_s"].at[step, j, d], r["hc_r"].at[step, j, d], partner)

    def h_along(step, d, j):
        piece = pl.ds(*PIECES[j])
        return copy_to(r["sums"].at[d - 1, :, piece], r["after_in"].at[step, d - 1, :, piece], r["h_s"].at[step, j, d - 1], r["h_r"].at[step, j, d - 1], left)

    def home_start(step, j):
        for d in range(back, 0, -1):
            @pl.when(z >= d)
            def _():
                h_beside(step, d, j).start()
        h_beside(step, 0, j).start()

    def home_pass(step, d, j):
        lanes = slice(PIECES[j][0], sum(PIECES[j]))

        @pl.when(z >= d)
        def _():
            h_beside(step, d, j).wait_recv()
            total = r["dkv"][at(d, c), lanes].astype(F32) + r["beside_in"][step, d, :, lanes].astype(F32)
            r["sums"][d - 1, :, lanes] = total.astype(BF)
            if d < back:
                @pl.when(z < chips - 1)
                def _():
                    h_along(step, d + 1, j).wait_recv()
                    more = r["sums"][d - 1, :, lanes].astype(F32) + r["after_in"][step, d, :, lanes].astype(F32)
                    r["sums"][d - 1, :, lanes] = more.astype(BF)
            h_along(step, d, j).start()

    def home_made(step, g):
        if g == FIRST_HEADS - 1:
            home_start(step, 0)
        if g == FIRST_HEADS:
            home_pass(step, back, 0)
        if g == KVH - 1:
            home_start(step, 1)

    def home_end(step):
        home_pass(step, back, 1)
        for d in range(back - 1, 0, -1):
            for j in (0, 1):
                home_pass(step, d, j)
        for j in (0, 1):
            h_beside(step, 0, j).wait_recv()
        r["home"][0] = r["dkv"][at(0, c), :].astype(F32) + r["beside_in"][step, 0].astype(F32)

        @pl.when(z < chips - 1)
        def _():
            for j in (0, 1):
                h_along(step, 1, j).wait_recv()
            r["home"][0] = r["home"][0] + r["after_in"][step, 0].astype(F32)

        for j in (0, 1):
            h_beside(step, 0, j).wait_send()
            for d in range(1, back + 1):
                @pl.when(z >= d)
                def _():
                    h_beside(step, d, j).wait_send()
                    h_along(step, d, j).wait_send()

    def turn(name, step):
        r[name + "_t" + str(step)][...] = r[name][...].astype(F32).T.astype(BF)

    r["state"][0] = r["hidden_in"][...].astype(F32).T
    met = False
    for step in range(RECUR):
        here = of_step(step)

        def ready(step=step, first=step == 0):
            if first:
                pl.semaphore_wait(bar, 1 + (z < chips - 1).astype(jnp.int32) + (z > 0).astype(jnp.int32))
            keys_start(step)

        front_part(here, wait, here["state"][...], ready)
        turn("normed", step)
        if step > 0:
            turn("mixed", step - 1)
            turn("normed_two", step - 1)
        after = rest_part(here, wait, lambda g, step=step: keys_arrived(step, g))
        keys_drain(step)
        if step < RECUR - 1:
            r["state"][step + 1] = after
        else:
            r["output"][...] = after.T.astype(BF)
    grad = r["cot"][...].astype(F32).T
    for step in reversed(range(RECUR)):
        here = of_step(step)
        back_part(here, wait, grad, lambda g, step=step: home_made(step, g))
        turn("d_mlp", step)
        if step == RECUR - 1:
            turn("mixed", step)
            turn("normed_two", step)
        home_end(step)
        grad = home_part(here, wait)
    r["grad"][...] = grad.T


def all_recursions(hidden_in, cotangent, masks, lives, tables, gains, weights, n_tok, nback):
    back = nback // 2
    width, rows = hidden_in.shape
    ff = weights["wg"].shape[1]
    kvr = 2 * KVH * HD
    slots = (2 * back + 2) * rows
    ins = {"hidden_in": hidden_in, "cot": cotangent, "mask": masks, "live": lives, "cos": tables[0], "sin": tables[1], "gains": gains}
    outs = {"output": shaped((width, rows), BF), "grad": shaped((width, rows), F32), "acc_out": shaped((8, 1024), F32)}
    for step in range(RECUR):
        outs |= {name + "_t" + str(step): shaped((width, rows), BF) for name in ROW_NAMES[:4]}
        outs |= {name + str(step): shaped((rows, ff), BF) for name in ROW_NAMES[4:]}
    dma, vm = pltpu.SemaphoreType.DMA, pltpu.VMEM
    scratch = {n + "_v": vm(weights[n].shape, BF) for n in WEIGHTS}
    scratch |= {
        "state": vm((RECUR, rows, width), F32), "middle": vm((RECUR, rows, width), F32), "branch": vm((RECUR, rows, width), F32),
        "gate": vm((RECUR, rows, ff), F32), "up": vm((RECUR, rows, ff), F32), "lse": vm((RECUR, 8, (H // KVH) * rows), F32),
        "q": vm((RECUR, rows, H * HD), BF), "kvw": vm((RECUR, slots, kvr), BF), "d_state": vm((rows, width), F32),
        "d_q": vm((rows, H * HD), BF), "d_attn": vm((rows, width), BF), "dkv": vm((slots, kvr), BF), "home": vm((1, rows, kvr), F32),
        "beside_in": vm((RECUR, back + 1, rows, kvr), BF), "after_in": vm((RECUR, back, rows, kvr), BF), "sums": vm((back, rows, kvr), BF),
        "w_sem": dma((len(WEIGHTS),)),
    }
    scratch |= {name: vm((rows, width), BF) for name in ROW_NAMES[:4]}
    scratch |= {name: dma((RECUR, 2, back)) for name in ("k_s", "k_r", "h_s", "h_r")}
    scratch |= {name: dma((RECUR, 2, back + 1)) for name in ("kc_s", "kc_r", "hc_s", "hc_r")}
    spec = pl.BlockSpec(memory_space=pltpu.VMEM)
    got = pl.pallas_call(
        lambda *refs: recursion_kernel(n_tok // 2, back, list(ins), list(outs), list(scratch), *refs),
        name="all_recursions",
        out_shape=tuple(outs.values()),
        in_specs=[spec] * len(ins) + [pl.BlockSpec(memory_space=pl.ANY)] * len(WEIGHTS),
        out_specs=tuple([spec] * len(outs)),
        scratch_shapes=list(scratch.values()),
        compiler_params=pltpu.CompilerParams(collective_id=5, has_side_effects=True, vmem_limit_bytes=62 * 2**20),
    )(*ins.values(), *[weights[n] for n in WEIGHTS])
    return dict(zip(outs, got))


def forward_stage(state, q, kvw, mask, live, tables, gains, weights, last):
    rows, width = state.shape
    ff = weights["wg"].shape[1]
    outs = {
        "mixed": shaped((rows, H * HD), BF), "lse": shaped((8, (H // KVH) * rows), F32), "middle": shaped((rows, width), F32),
        "normed_two": shaped((rows, width), BF), "gate": shaped((rows, ff), F32), "up": shaped((rows, ff), F32),
        "hidden": shaped((rows, ff), BF), "branch": shaped((rows, width), F32),
    }
    if last:
        outs["output"] = shaped((width, rows), BF)
    else:
        outs |= front_outs(rows, width) | {"next": shaped((rows, width), F32)}

    def parts(r, wait):
        state_next = rest_part(r, wait)
        if last:
            r["output"][...] = state_next.T.astype(BF)
        else:
            r["next"][...] = state_next
            front_part(r, wait, state_next)

    needed = ("wa", "wg", "wu", "wd")
    ins = {"state": state, "q_in": q, "kvw": kvw, "mask": mask, "live": live, "cos": tables[0], "sin": tables[1], "gains": gains}
    return stage("forward", parts, needed, ins, outs, weights)


def first_stage(hidden_in, tables, gains, weights):
    width, rows = hidden_in.shape

    def parts(r, wait):
        state = r["hidden"][...].astype(F32).T
        r["state"][...] = state
        front_part(r, wait, state)

    outs = front_outs(rows, width) | {"state": shaped((rows, width), F32)}
    return stage("first", parts, ("wa",), {"hidden": hidden_in, "cos": tables[0], "sin": tables[1], "gains": gains}, outs, weights)


def backward_stage(kept, before, mask, live, tables, gains, acc, weights, cotangent):
    ins = {"cos": tables[0], "sin": tables[1], "gains": gains, "acc": acc}
    outs = {"acc_out": shaped(acc.shape, F32)}
    needed = ()
    rows, width = (kept or before)["state"].shape
    ff = weights["wg"].shape[1]
    kvr = 2 * KVH * HD
    if before is not None:
        ins |= {"home": before["home"], "h_dq": before["d_q"], "h_state": before["state"], "h_d_state": before["d_state"], "h_d_attn": before["d_attn"]}
        outs |= {"d_packed": shaped((rows, QKO + kvr // 2), BF)}
        needed += ("wa",)
    else:
        ins |= {"cot": cotangent}
    if kept is not None:
        ins |= {"b_state": kept["state"], "b_live": live, "b_branch": kept["branch"], "b_gate": kept["gate"], "b_up": kept["up"],
                "b_middle": kept["middle"], "b_lse": kept["lse"], "kvw": kept["kvw"], "q_in": kept["q"], "mask": mask}
        outs |= {"d_mlp": shaped((rows, width), BF), "d_up": shaped((rows, ff), BF), "d_gate": shaped((rows, ff), BF),
                 "d_attn": shaped((rows, width), BF), "d_state": shaped((rows, width), F32), "d_q": shaped((rows, H * HD), BF),
                 "dkv": shaped(kept["kvw"].shape, BF)}
        needed += ("wd", "wg", "wu") + (("wa",) if before is None else ())
    else:
        outs |= {"grad": shaped((width, rows), F32)}

    def parts(r, wait):
        r["acc_out"][...] = r["acc"][...]
        grad = home_part(r, wait) if before is not None else r["cot"][...].astype(F32).T
        if kept is not None:
            back_part(r, wait, grad)
        else:
            r["grad"][...] = grad.T

    return stage("backward", parts, needed, ins, outs, weights)


PARTS = 16
HALF = 480
COLS = 640
STREAMS = (
    ("x", True, 0, 80, 0),
    ("y", True, 80, 80, 0),
    ("x", True, 160, 80, 1),
    ("y", True, 240, 80, 1),
    ("x", True, 320, 80, 2),
    ("y", True, 400, 80, 2),
)
SCHEDULE = (
    (0, 0), (0, 1), (1, 0, 0), (0, 2), (1, 1, 0), (8, 0), (0, 3), (0, 4), (0, 5), (0, 6), (1, 5, 0), (1, 4, 0), (1, 2, 0), (0, 7),
    (1, 3, 0), (8, 1), (2, 0, 0), (0, 8), (0, 9), (1, 2, 1), (1, 8, 0), (1, 6, 0), (1, 7, 0), (2, 1, 0), (0, 10), (0, 11), (1, 10, 0),
    (8, 2), (2, 0, 1), (1, 1, 1), (0, 12), (0, 13), (1, 7, 1), (1, 9, 0), (1, 12, 0), (0, 14), (2, 1, 1), (1, 0, 1), (0, 15), (1, 11, 0),
    (0, 16), (8, 3), (1, 15, 0), (2, 0, 2), (1, 13, 0), (1, 14, 0), (2, 1, 2), (8, 4), (1, 11, 2), (1, 4, 1), (1, 3, 1), (1, 5, 1),
    (1, 6, 1), (2, 0, 3), (1, 8, 1), (2, 1, 3), (1, 10, 1), (2, 3, 0), (1, 9, 1), (2, 2, 0), (3, 0), (2, 3, 1), (3, 1), (1, 12, 1),
    (1, 14, 1), (4, 0), (1, 13, 1), (4, 1), (1, 15, 1), (1, 11, 1), (1, 4, 2), (2, 2, 1), (5, 1), (1, 1, 2), (2, 3, 2), (1, 6, 2),
    (6, 0, 1), (1, 0, 2), (2, 2, 2), (6, 1, 1), (1, 3, 2), (2, 3, 3), (1, 2, 2), (6, 0, 2), (1, 5, 2), (2, 2, 3), (6, 1, 2), (3, 2),
    (2, 5, 0), (3, 3), (1, 7, 2), (1, 9, 2), (7, 0, 1), (2, 4, 0), (6, 0, 3), (6, 1, 3), (2, 5, 1), (7, 1, 1), (1, 14, 2), (4, 2),
    (1, 13, 2), (1, 10, 2), (4, 3), (2, 4, 1), (7, 1, 3), (7, 1, 2), (6, 3, 1), (1, 8, 2), (5, 0), (1, 15, 2), (7, 0, 2), (6, 2, 1),
    (2, 4, 2), (1, 12, 2), (6, 2, 2), (2, 5, 2), (5, 3), (2, 4, 3), (6, 3, 2), (2, 5, 3), (3, 4), (6, 3, 3), (3, 5), (7, 3, 3), (7, 3, 1),
    (7, 0, 3), (4, 4), (4, 5), (6, 2, 3), (6, 4, 1), (6, 5, 1), (7, 5, 1), (6, 4, 2), (7, 4, 1), (7, 2, 3), (7, 2, 1), (5, 2), (7, 4, 2),
    (6, 5, 2), (6, 4, 3), (5, 5), (7, 5, 2), (7, 2, 2), (5, 4), (7, 3, 2), (6, 5, 3), (7, 4, 3), (7, 5, 3),
)
SLOTS = 4


def place():
    g, t = lax.axis_index("grp"), lax.axis_index("tok")
    return g // 2, lax.rem(g, 2), t // 2, lax.rem(t, 2)


def dev(y, x, z, c):
    return (y * 2 + x, z * 2 + c)


def pick(z, values):
    out = jnp.int32(values[3])
    for i in (2, 1, 0):
        out = jnp.where(z == i, jnp.int32(values[i]), out)
    return out


def copy_to(src, dst, send, recv, device):
    return pltpu.make_async_remote_copy(src_ref=src, dst_ref=dst, send_sem=send, recv_sem=recv, device_id=device, device_id_type=MESH)


def add_rows(dst, src, rows, step):
    def body(i, _):
        at = pl.ds(pl.multiple_of(i * step, step), step)
        dst[at, :] = dst[at, :] + src[at, :]
        return 0

    lax.fori_loop(0, rows // step, body, 0)


def tail_kernel(count, *refs):
    left_refs, refs = refs[: 4 * count], refs[4 * count :]
    right_refs, refs = refs[: 4 * count], refs[4 * count :]
    n_s = len(STREAMS)
    v_ref, o_ref, vo_ref, left_t, right, theirs, mine, other = refs[:8]
    ra, rz, rb = refs[8 : 8 + n_s], refs[8 + n_s : 8 + 2 * n_s], refs[8 + 2 * n_s : 8 + 3 * n_s]
    vrecv, left_sem, load_sem, core_s, core_r, as_, ar, zs, zr, bs, br, ob, obr, oz, ozr, oa, oar, oc, ocr, vs, vr, own_sem = refs[8 + 3 * n_s :]
    y, x, z, c = place()
    partner = dev(y, x, z, 1 - c)
    across = {"x": dev(y, 1 - x, z, c), "y": dev(1 - y, x, z, c)}
    left_dev, right_dev = dev(y, x, z - 1, c), dev(y, x, z + 1, c)
    at_axis = {"x": x, "y": y}
    order = (pick(z, (3, 3, 0, 0)), pick(z, (2, 0, 3, 1)), pick(z, (1, 2, 1, 2)), z)
    far = dev(y, x, jnp.where(z < 2, z + 2, z - 2), c)
    tokens = left_refs[0].shape[1]
    lefts = [pltpu.make_async_copy(each, left_t.at[i // count, :, pl.ds(i % count * tokens, tokens)], left_sem.at[i]) for i, each in enumerate(left_refs)]

    def load(p, src, i):
        return pltpu.make_async_copy(src, right.at[p, pl.ds(i * tokens, tokens)], load_sem.at[p * count + i])

    for k in range(4):
        for j in range(4):
            for i in range(count):
                if k == 0:
                    lefts[j * count + i].start()
                columns = pl.ds(pl.multiple_of(order[k] * COLS, COLS), COLS)
                load(j * 4 + order[k], right_refs[j * count + i].at[:, columns], i).start()

    bar = pltpu.get_barrier_semaphore()
    for d in (partner, across["x"], across["y"], far):
        pl.semaphore_signal(bar, inc=1, device_id=d, device_id_type=MESH)

    @pl.when(z > 0)
    def _():
        pl.semaphore_signal(bar, inc=1, device_id=left_dev, device_id_type=MESH)

    @pl.when(z < 3)
    def _():
        pl.semaphore_signal(bar, inc=1, device_id=right_dev, device_id_type=MESH)

    for cp in lefts:
        cp.wait()
    pl.semaphore_wait(bar, 4 + (z > 0).astype(jnp.int32) + (z < 3).astype(jnp.int32))

    def part_xy(px, py, pz):
        return (px * 2 + py) * 4 + pz

    def part_of(s, pa, pb, pz):
        return part_xy(pa, pb, pz) if STREAMS[s][0] == "x" else part_xy(pb, pa, pz)

    def ab(s):
        a = STREAMS[s][0]
        b = "y" if a == "x" else "x"
        return at_axis[a], at_axis[b], across[a], across[b]

    waits = []
    seq = [(k, i, px, py) for k in range(4) for i, (px, py) in enumerate(((1 - x, 1 - y), (1 - x, y), (x, 1 - y), (x, y)))]

    def core_copy(j):
        k, _, px, py = seq[j]
        p = part_xy(px, py, order[k])
        return copy_to(theirs.at[j % SLOTS, pl.ds(pl.multiple_of((1 - c) * HALF, 16), HALF)], other.at[p], core_s.at[j], core_r.at[p], partner)

    def core_make(j):
        k, _, px, py = seq[j]
        p = part_xy(px, py, order[k])
        for i in range(count):
            load(p, right_refs[0].at[:, pl.ds(0, COLS)], i).wait()
        if j >= SLOTS:
            core_copy(j - SLOTS).wait_send()
        which = jnp.where(p < 8, 0, jnp.where(p < 12, 1, jnp.where(p < 14, 2, 3)))
        split = 2 * COLS - 2 * HALF
        theirs[j % SLOTS] = dot_nn(left_t[which], right[p]).astype(BF)

        @pl.when(p == PARTS - 1)
        def _():
            theirs[j % SLOTS, :, COLS - split :] = dot_nn(left_t[2], right[p, :, COLS - split :]).astype(BF)

        core_copy(j).start()

    def core_add(j):
        k, i, px, py = seq[j]
        p = part_xy(px, py, order[k])
        core_copy(j).wait_recv()
        mine[p] = theirs[j % SLOTS, pl.ds(pl.multiple_of(c * HALF, 16), HALF), :] + other[p]

    def a_copy(s, pb, pz):
        a, b, to_a, _ = ab(s)
        _, _, r0, n, _ = STREAMS[s]
        return copy_to(mine.at[part_of(s, 1 - a, pb, pz), pl.ds(r0, n)], ra[s].at[pb * 4 + pz], as_.at[s, pb * 4 + pz], ar.at[s, pb * 4 + pz], to_a)

    def a_send(j, batch):
        k, i, px, py = seq[j]
        for s in range(n_s):
            a_axis = STREAMS[s][0]
            if STREAMS[s][4] == batch and (i == 0 or (i == 1 and a_axis == "x") or (i == 2 and a_axis == "y")):
                cp = a_copy(s, py if a_axis == "x" else px, order[k])
                cp.start()
                waits.append(cp)

    def z_index(s, pb, slot):
        return pb * 5 + slot if STREAMS[s][1] else slot

    def z_copy(s, pb, pz, to_right):
        a, b, _, _ = ab(s)
        _, _, r0, n, _ = STREAMS[s]
        src = mine.at[part_of(s, a, pb, pz), pl.ds(r0, n)]
        i = z_index(s, pb, pz if to_right else jnp.where(pz == z - 1, 4, pz))
        return copy_to(src, rz[s].at[i], zs.at[s, i], zr.at[s, i], right_dev if to_right else left_dev)

    def z_take(s, pb, slot):
        a, _, _, _ = ab(s)
        _, _, r0, n, _ = STREAMS[s]
        i = z_index(s, pb, slot)
        copy_to(mine.at[0, pl.ds(r0, n)], rz[s].at[i], zs.at[s, i], zr.at[s, i], left_dev).wait_recv()
        pz = z if slot is z or isinstance(slot, int) else slot
        add_rows(mine.at[part_of(s, a, pb, pz), pl.ds(r0, n)], rz[s].at[i], n, 16)

    def z_step(s, pb, k):
        pz = order[k]
        if k < 3:
            up = jnp.where(pz > z, (z > 0).astype(jnp.int32), (z < 3).astype(jnp.int32))

            @pl.when(up == 1)
            def _():
                z_take(s, pb, pz)

            @pl.when(pz > z)
            def _():
                z_copy(s, pb, pz, True).start()

            @pl.when(pz < z)
            def _():
                z_copy(s, pb, pz, False).start()
        else:
            @pl.when(z > 0)
            def _():
                z_take(s, pb, z)

            @pl.when(z < 3)
            def _():
                z_take(s, pb, 4)

    def z_drain(s, pb, k):
        pz = order[k]

        @pl.when(pz > z)
        def _():
            z_copy(s, pb, pz, True).wait_send()

        @pl.when(pz < z)
        def _():
            z_copy(s, pb, pz, False).wait_send()

    def a_step(s, pb, k):
        a, b, to_a, _ = ab(s)
        _, _, r0, n, _ = STREAMS[s]
        pz = order[k]
        a_copy(s, pb, pz).wait_recv()
        add_rows(mine.at[part_of(s, a, pb, pz), pl.ds(r0, n)], ra[s].at[pb * 4 + pz], n, 16)

    def b_copy(s, pz):
        a, b, _, to_b = ab(s)
        _, second_z, r0, n, _ = STREAMS[s]
        i = 0 if second_z else pz
        return copy_to(mine.at[part_of(s, a, 1 - b, pz), pl.ds(r0, n)], rb[s].at[i], bs.at[s, i], br.at[s, i], to_b)

    def b_step(s, pz):
        a, b, _, _ = ab(s)
        _, second_z, r0, n, _ = STREAMS[s]
        i = 0 if second_z else pz
        b_copy(s, pz).wait_recv()
        add_rows(mine.at[part_of(s, a, b, pz), pl.ds(r0, n)], rb[s].at[i], n, 16)

    def of_batch(batch):
        return [s for s in range(n_s) if STREAMS[s][4] == batch]

    def first_step(only, k):
        for s in (only,):
            _, b, _, _ = ab(s)
            a_step(s, 1 - b, k)
            if STREAMS[s][1]:
                z_step(s, 1 - b, k)
                a_step(s, b, k)
                z_step(s, b, k)
                if k == 3:
                    cp = b_copy(s, z)
                    cp.start()
                    waits.append(cp)
            else:
                cp = b_copy(s, order[k])
                cp.start()
                waits.append(cp)
                a_step(s, b, k)

    def second_step(batch, k):
        for s in of_batch(batch):
            _, b, _, _ = ab(s)
            if not STREAMS[s][1]:
                b_step(s, order[k])
                z_step(s, b, k)

    def vec_copy(i):
        to = (partner, across["x"], across["y"], dev(y, x, jnp.where(lax.rem(z, 2) == 0, z + 1, z - 1), c), far)[i]
        return copy_to(vo_ref, vrecv.at[i], vs.at[i], vr.at[i], to)

    def vec_end(i):
        vec_copy(i).wait()
        vo_ref[...] = vo_ref[...] + vrecv[i]

    half0 = c * HALF

    def out_at(s, p):
        _, _, r0, n, _ = STREAMS[s]
        return o_ref.at[p, pl.ds(pl.multiple_of(half0 + r0, 16), n)]

    def mine_at(s, p):
        _, _, r0, n, _ = STREAMS[s]
        return mine.at[p, pl.ds(r0, n)]

    def go(cp):
        cp.start()
        waits.append(cp)

    def to_core(s, p, src):
        return copy_to(src, out_at(s, p), oc.at[s, p], ocr.at[s, p], partner)

    def to_a(s, pb, pz, src):
        a, b, na, _ = ab(s)
        return copy_to(src, out_at(s, part_of(s, a, pb, pz)), oa.at[s, pb * 4 + pz], oar.at[s, pb * 4 + pz], na)

    def to_b(s, pz, src):
        a, b, _, nb = ab(s)
        return copy_to(src, out_at(s, part_of(s, a, b, pz)), ob.at[s, pz], obr.at[s, pz], nb)

    def to_z(s, pb, pz, src, to_right):
        a, b, _, _ = ab(s)
        i = pb * 8 + pz * 2 + (0 if to_right else 1)
        return copy_to(src, out_at(s, part_of(s, a, pb, pz)), oz.at[s, i], ozr.at[s, pb * 4 + pz], right_dev if to_right else left_dev)

    def spread_z(s, pb, pz, src, sides):
        if 0 in sides:
            @pl.when(z < 3)
            def _():
                to_z(s, pb, pz, src, True).start()
        if 1 in sides:
            @pl.when(z > 0)
            def _():
                to_z(s, pb, pz, src, False).start()

    def finish(only):
        for s in (only,):
            a, b, _, _ = ab(s)
            p = part_of(s, a, b, z)
            b_step(s, z)
            if not STREAMS[s][1]:
                z_step(s, b, 3)
            src = mine_at(s, p)
            if STREAMS[s][1]:
                go(to_b(s, z, src))
                spread_z(s, b, z, src, (0, 1))
            else:
                spread_z(s, b, z, src, (0, 1))
                go(to_b(s, z, src))
            go(to_a(s, b, z, src))
            go(to_core(s, p, src))
            pltpu.make_async_copy(src, out_at(s, p), own_sem.at[s]).start()

    def got_b(s, pz):
        a, b, _, _ = ab(s)
        p = part_of(s, a, 1 - b, pz)
        src = out_at(s, p)
        copy_to(src, src, ob.at[s, pz], obr.at[s, pz], partner).wait_recv()
        if STREAMS[s][1]:
            spread_z(s, 1 - b, pz, src, (0, 1))
        to_a(s, 1 - b, pz, src).start()
        to_core(s, p, src).start()

    def got_z(s, pb, pz, from_left):
        a, b, _, _ = ab(s)
        p = part_of(s, a, pb, pz)
        src = out_at(s, p)
        copy_to(src, src, oz.at[s, 0], ozr.at[s, pb * 4 + pz], partner).wait_recv()
        spread_z(s, pb, pz, src, (0,) if from_left else (1,))
        to_a(s, pb, pz, src).start()
        if not STREAMS[s][1]:
            to_b(s, pz, src).start()
        to_core(s, p, src).start()

    def got_a(s, pb, pz):
        a, b, _, _ = ab(s)
        p = part_of(s, 1 - a, pb, pz)
        src = out_at(s, p)
        copy_to(src, src, oa.at[s, pb * 4 + pz], oar.at[s, pb * 4 + pz], partner).wait_recv()
        to_core(s, p, src).start()

    def gather_b(only):
        for s in (only,):
            got_b(s, z)

    def gather_a(only):
        for s in (only,):
            _, b, _, _ = ab(s)
            got_a(s, b, z)
            got_a(s, 1 - b, z)

    def from_side(t, side):
        return (z - t, z >= t) if side == 0 else (z + t, z + t <= 3)

    def gather_z(only, t):
        for side in (0, 1):
            pz, there = from_side(t, side)

            @pl.when(there)
            def _():
                _, b, _, _ = ab(only)
                got_z(only, b, pz, side == 0)
                got_z(only, 1 - b, pz, side == 0)

    def gather_rest(only, t):
        for side in (0, 1):
            pz, there = from_side(t, side)

            @pl.when(there)
            def _():
                _, b, _, _ = ab(only)
                got_a(only, b, pz)
                got_a(only, 1 - b, pz)

    def make(j):
        if j < PARTS:
            core_make(j)
        if j > 0:
            core_add(j - 1)

    def vec_end_start(i):
        vec_end(i)
        if i < 4:
            vec_copy(i + 1).start()

    vo_ref[...] = v_ref[...]
    vec_copy(0).start()

    actions = (make, a_send, first_step, finish, gather_b, gather_a, gather_z, gather_rest, vec_end_start)
    for kind, *which in SCHEDULE:
        actions[kind](*which)

    for cp in waits:
        cp.wait_send()
    for j in range(PARTS - SLOTS, PARTS):
        core_copy(j).wait_send()
    for s in range(n_s):
        a, b, _, _ = ab(s)
        pltpu.make_async_copy(mine_at(s, part_of(s, a, b, z)), out_at(s, part_of(s, a, b, z)), own_sem.at[s]).wait()
        pbs = (b, 1 - b) if STREAMS[s][1] else (b,)
        for pb in pbs:
            for k in range(3):
                z_drain(s, pb, k)
        for pz in range(4):
            for pb in pbs:
                src = out_at(s, part_of(s, a, pb, pz))

                @pl.when((z >= pz) & (z < 3))
                def _():
                    to_z(s, pb, pz, src, True).wait_send()

                @pl.when((z <= pz) & (z > 0))
                def _():
                    to_z(s, pb, pz, src, False).wait_send()
            for pb in (0, 1):
                src = out_at(s, part_of(s, a, pb, pz))

                @pl.when(jnp.logical_not((pb == b) & (pz == z)))
                def _():
                    to_a(s, pb, pz, src).wait_send()
            if not STREAMS[s][1]:
                @pl.when(z != pz)
                def _():
                    to_b(s, pz, out_at(s, 0)).wait_send()
        for p in range(16):
            src = out_at(s, p)

            @pl.when(p != part_of(s, a, b, z))
            def _():
                to_core(s, p, src).wait_send()
            _, _, r0, n, _ = STREAMS[s]
            dst = o_ref.at[p, pl.ds(pl.multiple_of((1 - c) * HALF + r0, 16), n)]
            copy_to(dst, dst, oc.at[s, p], ocr.at[s, p], partner).wait_recv()


def summed_gradients(lefts, rights, vectors):
    dma = pltpu.SemaphoreType.DMA
    count = len(lefts[0])
    width, tokens = lefts[0][0].shape
    rows = count * tokens
    n_s = len(STREAMS)
    vm = pl.BlockSpec(memory_space=pltpu.VMEM)
    return pl.pallas_call(
        lambda *refs: tail_kernel(count, *refs),
        name="summed_gradients",
        out_shape=(jax.ShapeDtypeStruct((PARTS, width, COLS), BF), jax.ShapeDtypeStruct(vectors.shape, F32)),
        in_specs=[pl.BlockSpec(memory_space=pl.ANY)] * (8 * count) + [vm],
        out_specs=(pl.BlockSpec(memory_space=pl.ANY), vm),
        scratch_shapes=[
            pltpu.VMEM((4, width, rows), BF), pltpu.VMEM((PARTS, rows, COLS), BF), pltpu.VMEM((SLOTS, 2 * HALF, COLS), BF),
            pltpu.VMEM((PARTS, HALF, COLS), BF), pltpu.VMEM((PARTS, HALF, COLS), BF),
            *[pltpu.VMEM((8, s[3], COLS), BF) for s in STREAMS],
            *[pltpu.VMEM((10 if s[1] else 5, s[3], COLS), BF) for s in STREAMS],
            *[pltpu.VMEM((1 if s[1] else 4, s[3], COLS), BF) for s in STREAMS],
            pltpu.VMEM((5, *vectors.shape), F32),
            dma((4 * count,)), dma((PARTS * count,)), dma((16,)), dma((16,)),
            dma((n_s, 8)), dma((n_s, 8)), dma((n_s, 10)), dma((n_s, 10)), dma((n_s, 4)), dma((n_s, 4)),
            dma((n_s, 4)), dma((n_s, 4)), dma((n_s, 16)), dma((n_s, 8)), dma((n_s, 8)), dma((n_s, 8)), dma((n_s, 16)), dma((n_s, 16)),
            dma((5,)), dma((5,)), dma((n_s,)),
        ],
        compiler_params=pltpu.CompilerParams(collective_id=1, has_side_effects=True, vmem_limit_bytes=60 * 2**20),
    )(*[a for l in lefts for a in l], *[a for l in rights for a in l], vectors)


QUARTERS = 4
UNITS = ((0, 0, 1536, True, True), (0, 1536, 1024, False, True), (1, 0, 2560, True, False), (2, 0, 2560, True, True), (3, 0, 320, True, False))
FIRST = (0, 2, 3, 4, 1)
SMALL_AT = (5, 10, 15)


def gather_kernel(*refs):
    q_ref, k_ref, o_ref, v_ref = refs[:4]
    ins, outs, packed = (refs[17], *refs[4:8]), refs[8:13], refs[17]
    turned = [each[...].astype(F32).T.astype(BF) for each in (k_ref, v_ref)]
    packed[...] = jnp.concatenate([q_ref[...], turned[0], o_ref[...], turned[1]], axis=1)
    zs, xs, ys, cs, got, cgot, own_s, own_c, own_r, ss, sr, sc, scr = (*refs[13:17], *refs[18:])
    y, x, z, c = place()
    partner, to_x, to_y = dev(y, x, z, 1 - c), dev(y, 1 - x, z, c), dev(1 - y, x, z, c)
    left, right = dev(y, x, z - 1, c), dev(y, x, z + 1, c)
    quarter = (x * 2 + y, (1 - x) * 2 + y, x * 2 + (1 - y), (1 - x) * 2 + (1 - y))
    lasting = []

    def go(cp, when=None):
        if when is None:
            cp.start()
        else:
            @pl.when(when)
            def _():
                cp.start()
        lasting.append((cp, when))

    def cut(ref, u, q):
        m, first, size, shared, _ = UNITS[u]
        n = size // QUARTERS if shared else size
        begin = first + q * n if shared else first
        if m < 3:
            return ref.at[:, pl.ds(pl.multiple_of(begin, 128), n)]
        return ref.at[pl.ds(pl.multiple_of(begin, 16), n), :]

    def out_piece(u, kind, zz, core):
        return cut(outs[UNITS[u][0]].at[zz * 2 + core], u, quarter[kind])

    bar = pltpu.get_barrier_semaphore()
    for d in (partner, to_x, to_y):
        pl.semaphore_signal(bar, inc=1, device_id=d, device_id_type=MESH)

    @pl.when(z > 0)
    def _():
        pl.semaphore_signal(bar, inc=1, device_id=left, device_id_type=MESH)

    @pl.when(z < 3)
    def _():
        pl.semaphore_signal(bar, inc=1, device_id=right, device_id_type=MESH)

    pl.semaphore_wait(bar, 3 + (z > 0).astype(jnp.int32) + (z < 3).astype(jnp.int32))

    def small_copy(zz, core, src, device, sems):
        return copy_to(src, outs[4].at[zz * 2 + core], sems[0], sems[1], device)

    go(small_copy(z, c, ins[4], right, (ss.at[z, 0], sr.at[z])), z < 3)
    go(small_copy(z, c, ins[4], left, (ss.at[z, 1], sr.at[z])), z > 0)
    go(small_copy(z, c, ins[4], partner, (sc.at[z], scr.at[z])))
    for u in FIRST:
        src, dst = cut(ins[UNITS[u][0]], u, quarter[0]), out_piece(u, 0, z, c)
        go(copy_to(src, dst, zs.at[u, z, 0], got.at[0, u, z], right), z < 3)
        go(copy_to(src, dst, zs.at[u, z, 1], got.at[0, u, z], left), z > 0)
    for m in range(4):
        go(copy_to(ins[m], outs[m].at[z * 2 + c], own_c.at[m], own_r.at[m], partner))
    local = [pltpu.make_async_copy(ins[m], outs[m].at[z * 2 + c], own_s.at[m]) for m in range(5)]
    for cp in local:
        cp.start()

    steps = [(t, side) for t in (1, 2, 3) for side in (0, 1)]

    def source(t, side):
        return (z - t, z >= t) if side == 0 else (z + t, z + t <= 3)

    def wait_for(kind, u, zz):
        piece = out_piece(u, kind, zz, c)
        copy_to(piece, piece, cs.at[kind, u, zz], got.at[kind, u, zz], partner).wait_recv()
        return piece

    def sends(kind, u, zz, piece):
        shared, first_x = UNITS[u][3], UNITS[u][4]
        out = []
        if shared and (kind == 0 or (kind == 2 and not first_x)):
            out.append(copy_to(piece, piece, xs.at[min(kind, 1), u, zz], got.at[1 if kind == 0 else 3, u, zz], to_x))
        if shared and (kind == 0 or (kind == 1 and first_x)):
            out.append(copy_to(piece, piece, ys.at[min(kind, 1), u, zz], got.at[2 if kind == 0 else 3, u, zz], to_y))
        out.append(copy_to(piece, piece, cs.at[kind, u, zz], cgot.at[kind, u, zz], partner))
        return out

    def each(kind, u, t, side):
        if kind and not UNITS[u][3]:
            return
        zz, there = source(t, side)
        onward = (z < 3) if side == 0 else (z > 0)

        @pl.when(there)
        def _():
            piece = wait_for(kind, u, zz)
            if kind == 0:
                on = copy_to(piece, piece, zs.at[u, zz, side], got.at[0, u, zz], right if side == 0 else left)

                @pl.when(onward)
                def _():
                    on.start()

            for cp in sends(kind, u, zz, piece):
                cp.start()

        lasting.append((("s", kind, u, t, side), there))
        if kind == 0:
            lasting.append((("z", u, t, side), there & onward))

    def small_step(t, side):
        zz, there = source(t, side)

        @pl.when(there)
        def _():
            piece = outs[4].at[zz * 2 + c]
            copy_to(piece, piece, sc.at[zz], sr.at[zz], partner).wait_recv()

            @pl.when((z < 3) if side == 0 else (z > 0))
            def _():
                small_copy(zz, c, piece, right if side == 0 else left, (ss.at[zz, side], sr.at[zz])).start()

            small_copy(zz, c, piece, partner, (sc.at[zz], scr.at[zz])).start()

        lasting.append((("m", t, side), there))

    turns = [(t, u) for t in (1, 2, 3) for u in FIRST]
    for i in range(len(turns) + 3):
        if i < len(turns):
            t, u = turns[i]
            for side in (0, 1):
                each(0, u, t, side)
        if 0 <= i - 1 < len(turns):
            t, u = turns[i - 1]
            for side in (0, 1):
                each(1 if UNITS[u][4] else 2, u, t, side)
        if 0 <= i - 2 < len(turns):
            t, u = turns[i - 2]
            for side in (0, 1):
                each(2 if UNITS[u][4] else 1, u, t, side)
        if i - 3 >= 0:
            t, u = turns[i - 3]
            for side in (0, 1):
                each(3, u, t, side)
        if i in SMALL_AT:
            for side in (0, 1):
                small_step(SMALL_AT.index(i) + 1, side)

    for cp, when in lasting:
        if not isinstance(cp, tuple):
            if when is None:
                cp.wait_send()
            else:
                @pl.when(when)
                def _():
                    cp.wait_send()
        elif cp[0] == "z":
            _, u, t, side = cp
            zz, _ = source(t, side)
            piece = out_piece(u, 0, zz, c)

            @pl.when(when)
            def _():
                copy_to(piece, piece, zs.at[u, zz, side], got.at[0, u, zz], partner).wait_send()
        elif cp[0] == "m":
            _, t, side = cp
            zz, _ = source(t, side)
            piece = outs[4].at[zz * 2 + c]

            @pl.when(when)
            def _():
                @pl.when((z < 3) if side == 0 else (z > 0))
                def _():
                    small_copy(zz, c, piece, partner, (ss.at[zz, side], sr.at[zz])).wait_send()

                small_copy(zz, c, piece, partner, (sc.at[zz], scr.at[zz])).wait_send()
                other = outs[4].at[zz * 2 + 1 - c]
                copy_to(other, other, sc.at[zz], scr.at[zz], partner).wait_recv()
        else:
            _, kind, u, t, side = cp
            zz, _ = source(t, side)
            piece = out_piece(u, kind, zz, c)
            other = out_piece(u, kind, zz, 1 - c)

            @pl.when(when)
            def _():
                for cp in sends(kind, u, zz, piece):
                    cp.wait_send()
                copy_to(other, other, cs.at[kind, u, zz], cgot.at[kind, u, zz], partner).wait_recv()

    for m in range(4):
        other = outs[m].at[z * 2 + 1 - c]
        copy_to(other, other, own_c.at[m], own_r.at[m], partner).wait_recv()
    other = outs[4].at[z * 2 + 1 - c]
    copy_to(other, other, sc.at[z], scr.at[z], partner).wait_recv()
    for cp in local:
        cp.wait()


def gather_rows(w_query, w_key_t, w_out, w_value_t, others):
    dma = pltpu.SemaphoreType.DMA
    rows, width = w_query.shape
    packed = (rows, 2 * (width + w_key_t.shape[0]))
    shapes = [packed] + [each.shape for each in others]
    n = len(UNITS)
    return pl.pallas_call(
        gather_kernel,
        name="gather_rows",
        out_shape=tuple(jax.ShapeDtypeStruct((8, *each), BF) for each in shapes),
        in_specs=[pl.BlockSpec(memory_space=pltpu.VMEM)] * 4 + [pl.BlockSpec(memory_space=pl.ANY)] * 4,
        out_specs=tuple([pl.BlockSpec(memory_space=pl.ANY)] * 5),
        scratch_shapes=[
            dma((n, 4, 2)), dma((2, n, 4)), dma((2, n, 4)), dma((4, n, 4)), pltpu.VMEM(packed, BF), dma((4, n, 4)), dma((4, n, 4)),
            dma((5,)), dma((4,)), dma((4,)), dma((4, 2)), dma((4,)), dma((4,)), dma((4,)),
        ],
        compiler_params=pltpu.CompilerParams(collective_id=4, has_side_effects=True),
    )(w_query, w_key_t, w_out, w_value_t, *others)


def keys_kernel(chips, back, kv_ref, w_ref, s_right, r_left, s_core, r_core):
    g, t = lax.axis_index("grp"), lax.axis_index("tok")
    z, c = t // 2, lax.rem(t, 2)
    rows = kv_ref.shape[0]
    partner, right = (g, z * 2 + 1 - c), (g, t + 2)

    def slot(d, core):
        return w_ref.at[pl.ds(pl.multiple_of(((back - d) * 2 + core) * rows, 128), rows)]

    bar = pltpu.get_barrier_semaphore()
    pl.semaphore_signal(bar, inc=1, device_id=partner, device_id_type=MESH)

    @pl.when(z > 0)
    def _():
        pl.semaphore_signal(bar, inc=1, device_id=(g, t - 2), device_id_type=MESH)

    def along(d, src):
        return copy_to(src, slot(d, c), s_right.at[d - 1], r_left.at[d - 1], right)

    def beside(d, src):
        return copy_to(src, slot(d, c), s_core.at[d], r_core.at[d], partner)

    own = w_ref.at[pl.ds(pl.multiple_of((back * 2 + c) * rows, 128), rows)]
    own[...] = kv_ref[...]
    for d in range(1, back + 1):
        @pl.when(z < d)
        def _():
            for core in (0, 1):
                slot(d, core)[...] = jnp.zeros(kv_ref.shape, kv_ref.dtype)

    pl.semaphore_wait(bar, 1 + (z < chips - 1).astype(jnp.int32))

    @pl.when(z < chips - 1)
    def _():
        along(1, kv_ref).start()

    beside(0, kv_ref).start()
    for d in range(1, back + 1):
        @pl.when(z >= d)
        def _():
            along(d, slot(d, c)).wait_recv()
            if d < back:
                @pl.when(z < chips - 1)
                def _():
                    along(d + 1, slot(d, c)).start()
            beside(d, slot(d, c)).start()

    def mine_to(d):
        return copy_to(slot(d, 1 - c), slot(d, 1 - c), s_core.at[d], r_core.at[d], partner)

    mine_to(0).wait_recv()
    beside(0, kv_ref).wait_send()

    @pl.when(z < chips - 1)
    def _():
        along(1, kv_ref).wait_send()

    for d in range(1, back + 1):
        @pl.when(z >= d)
        def _():
            mine_to(d).wait_recv()
            beside(d, slot(d, c)).wait_send()
            if d < back:
                @pl.when(z < chips - 1)
                def _():
                    along(d + 1, slot(d, c)).wait_send()


def exchange_keys(kv, n_tok, nback):
    back = nback // 2
    rows = kv.shape[0]
    dma = pltpu.SemaphoreType.DMA
    return pl.pallas_call(
        lambda *refs: keys_kernel(n_tok // 2, back, *refs),
        name="exchange_keys",
        out_shape=jax.ShapeDtypeStruct(((2 * back + 2) * rows, kv.shape[1]), kv.dtype),
        in_specs=[pl.BlockSpec(memory_space=pltpu.VMEM)],
        out_specs=pl.BlockSpec(memory_space=pltpu.VMEM),
        scratch_shapes=[dma((back,)), dma((back,)), dma((back + 1,)), dma((back + 1,))],
        compiler_params=pltpu.CompilerParams(collective_id=2, has_side_effects=True, vmem_limit_bytes=12 * 2**20),
    )(kv)


def home_kernel(chips, back, p_ref, h_ref, beside_in, sums, after_in, s_left, r_right, s_core, r_core):
    g, t = lax.axis_index("grp"), lax.axis_index("tok")
    z, c = t // 2, lax.rem(t, 2)
    rows = h_ref.shape[1]
    partner, left = (g, z * 2 + 1 - c), (g, t - 2)

    def block(d, core):
        return p_ref.at[pl.ds(pl.multiple_of(((back - d) * 2 + core) * rows, 128), rows)]

    bar = pltpu.get_barrier_semaphore()
    pl.semaphore_signal(bar, inc=1, device_id=partner, device_id_type=MESH)

    @pl.when(z < chips - 1)
    def _():
        pl.semaphore_signal(bar, inc=1, device_id=(g, t + 2), device_id_type=MESH)

    pl.semaphore_wait(bar, 1 + (z > 0).astype(jnp.int32))

    def beside(d):
        return copy_to(block(d, 1 - c), beside_in.at[d], s_core.at[d], r_core.at[d], partner)

    def along(d):
        return copy_to(sums.at[d - 1], after_in.at[d - 1], s_left.at[d - 1], r_right.at[d - 1], left)

    for d in range(back, 0, -1):
        @pl.when(z >= d)
        def _():
            beside(d).start()
    beside(0).start()
    for d in range(back, 0, -1):
        @pl.when(z >= d)
        def _():
            beside(d).wait_recv()
            sums[d - 1] = (block(d, c)[...].astype(F32) + beside_in[d].astype(F32)).astype(BF)
            if d < back:
                @pl.when(z < chips - 1)
                def _():
                    along(d + 1).wait_recv()
                    sums[d - 1] = (sums[d - 1].astype(F32) + after_in[d].astype(F32)).astype(BF)
            along(d).start()
    beside(0).wait_recv()
    h_ref[0] = block(0, c)[...].astype(F32) + beside_in[0].astype(F32)

    @pl.when(z < chips - 1)
    def _():
        along(1).wait_recv()
        h_ref[0] = h_ref[0] + after_in[0].astype(F32)

    beside(0).wait_send()
    for d in range(1, back + 1):
        @pl.when(z >= d)
        def _():
            beside(d).wait_send()
            along(d).wait_send()


def exchange_home(partial, n_tok, nback):
    back = nback // 2
    rows = partial.shape[0] // (2 * back + 2)
    width = partial.shape[1]
    dma = pltpu.SemaphoreType.DMA
    return pl.pallas_call(
        lambda *refs: home_kernel(n_tok // 2, back, *refs),
        name="exchange_home",
        out_shape=jax.ShapeDtypeStruct((1, rows, width), F32),
        in_specs=[pl.BlockSpec(memory_space=pltpu.VMEM)],
        out_specs=pl.BlockSpec(memory_space=pltpu.VMEM),
        scratch_shapes=[
            pltpu.VMEM((back + 1, rows, width), BF), pltpu.VMEM((back, rows, width), BF), pltpu.VMEM((back, rows, width), BF),
            dma((back,)), dma((back,)), dma((back + 1,)), dma((back + 1,)),
        ],
        compiler_params=pltpu.CompilerParams(collective_id=3, has_side_effects=True, vmem_limit_bytes=12 * 2**20),
    )(partial)


def grads_kernel(count, *refs):
    r = {name: refs[i * count : (i + 1) * count] for i, name in enumerate(ROW_NAMES)}
    g_ref, left_t, slots, sems = refs[len(ROW_NAMES) * count :]
    for i, name in enumerate(ROW_NAMES[:4]):
        left_t[i] = jnp.concatenate([each[...].astype(F32).T.astype(BF) for each in r[name]], axis=1)

    def out_copy(p):
        return pltpu.make_async_copy(slots.at[p % 2], g_ref.at[p], sems.at[p % 2])

    split = 2 * COLS - left_t.shape[1]
    for p in range(PARTS):
        if p >= 2:
            out_copy(p - 2).wait()
        low = (p % 4) * COLS
        right = jnp.concatenate([each[:, low : low + COLS] for each in r[ROW_NAMES[4 + p // 4]]], axis=0)
        result = dot_nn(left_t[((0,) * 8 + (1,) * 4 + (2, 2, 3, 3))[p]], right)
        if p == PARTS - 1:
            result = jnp.concatenate([result[:, : COLS - split], dot_nn(left_t[2], right[:, COLS - split :])], axis=1)
        slots[p % 2] = result.astype(BF)
        out_copy(p).start()
    out_copy(PARTS - 2).wait()
    out_copy(PARTS - 1).wait()


def weight_gradients(rows):
    count = len(rows["d_mlp"])
    flat = [each for name in ROW_NAMES for each in rows[name]]
    tokens, width = rows["normed"][0].shape
    return pl.pallas_call(
        lambda *refs: grads_kernel(count, *refs),
        name="weight_gradients",
        out_shape=jax.ShapeDtypeStruct((PARTS, width, COLS), BF),
        in_specs=[pl.BlockSpec(memory_space=pltpu.VMEM)] * len(flat),
        out_specs=pl.BlockSpec(memory_space=pl.ANY),
        scratch_shapes=[pltpu.VMEM((4, width, count * tokens), BF), pltpu.VMEM((2, width, COLS), BF), pltpu.SemaphoreType.DMA((2,))],
        compiler_params=pltpu.CompilerParams(vmem_limit_bytes=60 * 2**20),
    )(*flat)


def spread_kernel(p_ref, gate, up, down, d_q, d_k, d_v, d_o, came, wide, q_full, k_full, o_full, v_full, sem_in, sem_out, sem_full):
    width = q_full.shape[0]
    order = [12, 13, 14, 15] + list(range(12))

    def fetch(i):
        return pltpu.make_async_copy(p_ref.at[order[i]], came.at[i % 3], sem_in.at[i % 3])

    def put(i):
        p = order[i]
        return pltpu.make_async_copy(wide.at[i % 2], (gate, up, down)[p // 4].at[:, pl.ds((p % 4) * COLS, COLS)], sem_out.at[i % 2])

    fulls = [(q_full, d_q), (k_full, d_k), (o_full, d_o), (v_full, d_v)]

    def put_full(j):
        return pltpu.make_async_copy(fulls[j][0], fulls[j][1], sem_full.at[j])

    fetch(0).start()
    fetch(1).start()
    for i, p in enumerate(order):
        if i + 2 < len(order):
            fetch(i + 2).start()
        fetch(i).wait()
        part = came.at[i % 3]
        if i >= 6:
            put(i - 2).wait()
        if p >= 12:
            full, other = (q_full, k_full) if p < 14 else (o_full, v_full)
            if p % 2 == 0:
                full[:, :COLS] = part[...].astype(F32)
            else:
                got = part[...].astype(F32)
                full[:, COLS:] = got[:, : width - COLS]
                other[...] = got[:, width - COLS :].T
                put_full(0 if p < 14 else 2).start()
                put_full(1 if p < 14 else 3).start()
        else:
            wide[i % 2] = part[...].astype(F32)
            put(i).start()
    put(len(order) - 2).wait()
    put(len(order) - 1).wait()
    for j in range(4):
        put_full(j).wait()


def spread_out(parts):
    n, width, cols = parts.shape
    kv = 2 * cols - width
    ff = 4 * cols
    shapes = [(width, ff), (width, ff), (width, ff), (width, width), (kv, width), (kv, width), (width, width)]
    vm = pltpu.VMEM
    return pl.pallas_call(
        spread_kernel,
        name="spread_out",
        out_shape=tuple(jax.ShapeDtypeStruct(s, F32) for s in shapes),
        in_specs=[pl.BlockSpec(memory_space=pl.ANY)],
        out_specs=tuple([pl.BlockSpec(memory_space=pl.ANY)] * 7),
        scratch_shapes=[
            vm((3, width, cols), BF), vm((2, width, cols), F32),
            vm((width, width), F32), vm((kv, width), F32), vm((width, width), F32), vm((kv, width), F32),
            pltpu.SemaphoreType.DMA((3,)), pltpu.SemaphoreType.DMA((2,)), pltpu.SemaphoreType.DMA((4,)),
        ],
        compiler_params=pltpu.CompilerParams(vmem_limit_bytes=60 * 2**20),
    )(parts)


def on_device(
    hidden_in,
    cotangent,
    lengths,
    active,
    norm_attn,
    w_query,
    w_key,
    w_value,
    w_out,
    norm_mlp,
    w_gate,
    w_up,
    w_down,
    w_router,
):
    n_tok = lax.axis_size("tok")
    n_grp = lax.axis_size("grp")
    me_index = lax.axis_index("tok")
    rows, width = hidden_in.shape
    nback = min(SPAN, n_tok // 2)

    share = norm_attn.shape[0]
    vectors = jnp.pad(jnp.stack([norm_attn, norm_mlp, w_router]), ((0, 0), (0, 128 - share)))
    small = jnp.concatenate([vectors, active.astype(BF), jnp.zeros((10, 128), BF)], axis=0)
    others = (w_gate, w_up, w_down, small)
    if (n_grp, n_tok) == (4, 8):
        whole = gather_rows(w_query, w_key.T, w_out, w_value.T, others)
    else:
        packed = jnp.concatenate([w_query, w_key, w_out, w_value], axis=1)
        whole = [lax.all_gather(each, "tok", axis=0) for each in (packed, *others)]
    weights = {name: each.reshape(-1, each.shape[-1]) for name, each in zip(WEIGHTS, whole)}
    gains = jnp.transpose(whole[4][:, :3, :share], (1, 0, 2)).reshape(3, width).astype(F32)
    gains = jnp.pad(gains, ((0, 5), (0, 0)))

    lengths_row = lengths[0]
    token = jnp.arange(rows, dtype=jnp.int32)
    global_rows = me_index * rows + token
    segment_rows = segment_of(lengths_row, global_rows)
    cosine, sine = rotary_tables(position_of(lengths_row, global_rows, segment_rows))
    tables = (jnp.concatenate([cosine] * 4, axis=1), jnp.concatenate([-sine, sine] * 2, axis=1))
    reach = (nback + 1) * rows
    global_keys = (me_index - nback) * rows + jnp.arange(reach, dtype=jnp.int32)
    live_all = jnp.transpose(whole[4][:, 3:6], (1, 0, 2)).reshape(3, -1)
    live_all = jnp.pad(live_all, ((0, 0), (nback * rows, 0)))
    live_keys = lax.dynamic_slice_in_dim(live_all, me_index * rows, reach, 1)
    reachable = (segment_rows[None, :] == segment_of(lengths_row, global_keys)[:, None]) & (
        global_keys[:, None] <= global_rows[None, :]
    )
    masks = jnp.where(reachable[None] & (live_keys[:, :, None] > 0), 1.0, 0.0).astype(F32)
    lives = [active[i].astype(F32)[:, None] for i in range(RECUR)]

    if (n_grp, n_tok) == (4, 8):
        done = all_recursions(hidden_in.T, cotangent.T, masks, jnp.stack(lives), tables, gains, weights, n_tok, nback)
        names = [name + "_t" for name in ROW_NAMES[:4]] + list(ROW_NAMES[4:])
        rows_of = [[done[name + str(step)] for step in reversed(range(RECUR))] for name in names]
        lefts, rights = rows_of[:4], rows_of[4:]
        parts, acc = summed_gradients(lefts, rights, done["acc_out"])
        output, grad = done["output"], done["grad"]
    else:
        kept = []
        made = first_stage(hidden_in.T, tables, gains, weights)
        state = made["state"]
        for step in range(RECUR):
            kvw = exchange_keys(made["kv"], n_tok, nback)
            last = step == RECUR - 1
            done = forward_stage(state, made["q"], kvw, masks[step], lives[step], tables, gains, weights, last)
            kept.append({**done, "state": state, "q": made["q"], "kvw": kvw, "normed_r": made["normed"]})
            made, state = done, done.get("next")

        acc = jnp.zeros((8, 1024), F32)
        before = None
        rows_of = {name: [] for name in ROW_NAMES}
        for step in reversed(range(RECUR)):
            back = backward_stage(kept[step], before, masks[step], lives[step], tables, gains, acc, weights, cotangent.T)
            acc = back["acc_out"]
            if before is not None:
                rows_of["d_packed"].append(back["d_packed"])
            for name in ("d_mlp", "d_gate", "d_up"):
                rows_of[name].append(back[name])
            for name in ("normed_two", "mixed", "hidden"):
                rows_of[name].append(kept[step][name])
            rows_of["normed"].append(kept[step]["normed_r"])
            before = {"home": exchange_home(back["dkv"], n_tok, nback), "d_q": back["d_q"], "state": kept[step]["state"], "d_state": back["d_state"], "d_attn": back["d_attn"]}
        back = backward_stage(None, before, None, None, tables, gains, acc, weights, None)
        rows_of["d_packed"].append(back["d_packed"])
        acc = back["acc_out"]
        parts = weight_gradients(rows_of)
        parts = lax.psum(parts.astype(F32), ("grp", "tok")).astype(BF)
        acc = lax.psum(acc, ("grp", "tok"))
        output, grad = kept[-1]["output"], back["grad"]
    d_gate, d_up, d_down, d_q, d_k, d_v, d_o = spread_out(parts)
    return (
        output.T,
        grad.T,
        acc[0, :width],
        d_q,
        d_k.T,
        d_v.T,
        d_o,
        acc[1, :width],
        d_gate,
        d_up,
        d_down.T,
        acc[2, :width],
    )


def solution(mesh):
    placed = (
        P(("grp", "tok"), None),
        P(("grp", "tok"), None),
        P("grp", None),
        P(None, ("grp", "tok")),
        P("tok"),
        P("tok", None),
        P("tok", None),
        P("tok", None),
        P("tok", None),
        P("tok"),
        P("tok", None),
        P("tok", None),
        P("tok", None),
        P("tok"),
    )
    return jax.shard_map(
        on_device,
        mesh=mesh,
        in_specs=placed,
        out_specs=(
            P(("grp", "tok"), None),
            P(("grp", "tok"), None),
            P(),
            P(),
            P(),
            P(),
            P(),
            P(),
            P(),
            P(),
            P(),
            P(),
        ),
        check_vma=False,
    )
```

```python
import jax
import jax.numpy as jnp
from jax import lax
from jax.experimental import pallas as pl
from jax.experimental.pallas import tpu as pltpu
from jax.sharding import PartitionSpec as P

MESH = pl.DeviceIdType.MESH

H = 15
KVH = 5
HD = 64
RECUR = 3
SPAN = 16

epsilon = 1e-05
theta = 10000.0
masked = -1000000000.0

def ends_of(lengths_row):
    count = lengths_row.shape[0]
    until = jnp.arange(count)[:, None] >= jnp.arange(count)[None, :]
    return jnp.sum(jnp.where(until, lengths_row[None, :], 0), axis=1)


def segment_of(lengths_row, global_rows):
    ends_at = ends_of(lengths_row)
    return jnp.sum((global_rows[:, None] >= ends_at[None, :]).astype(jnp.int32), axis=1)


def position_of(lengths_row, global_rows, segments):
    ends_at = ends_of(lengths_row)
    starts_at = ends_at - lengths_row
    picked = segments[:, None] == jnp.arange(lengths_row.shape[0], dtype=jnp.int32)[None, :]
    return global_rows - jnp.sum(jnp.where(picked, starts_at[None, :], 0), axis=1)


def rotary_tables(positions):
    half_dim = HD // 2
    inverse = jnp.power(theta, -jnp.arange(half_dim, dtype=jnp.float32) * (2.0 / HD))
    angle = positions.astype(jnp.float32)[..., None] * inverse
    return (jnp.cos(angle), jnp.sin(angle))


F32 = jnp.float32
BF = jnp.bfloat16
CHUNK = 512
ROW_NAMES = ("normed_two", "d_mlp", "normed", "mixed", "d_gate", "d_up", "hidden", "d_packed")
WEIGHTS = ("wa", "wg", "wu", "wd")
QK = (H + KVH) * HD
QKO = QK + H * HD


def dot_nn(left, right):
    return lax.dot_general(left, right, (((1,), (0,)), ((), ())), preferred_element_type=F32)


def dot_nt(left, right):
    return lax.dot_general(left, right, (((1,), (1,)), ((), ())), preferred_element_type=F32)


def rope_lanes(tensor, cosine, sine, sign):
    rows, width = tensor.shape
    lane = lax.broadcasted_iota(jnp.int32, (rows, 2 * HD), 1)
    first = lax.rem(lane, HD) < HD // 2
    out = []
    for i in range(0, width, 2 * HD):
        piece = tensor[:, i : i + 2 * HD]
        other = jnp.where(first, pltpu.roll(piece, 2 * HD - HD // 2, 1), pltpu.roll(piece, HD // 2, 1))
        out.append(piece * cosine + (other * sine) * sign)
    return jnp.concatenate(out, axis=1)


def inverse_of(rows):
    return lax.rsqrt(jnp.mean(rows * rows, axis=1, keepdims=True) + epsilon)


def front_part(r, wait, state, ready=None):
    gain = r["gains"][0:1, :]
    normed = (state * inverse_of(state) * gain).astype(BF)
    r["normed"][...] = normed
    wait("wa")
    values = dot_nn(normed, r["wa_v"][:, QKO:]).astype(BF)
    qw = H * HD
    even = qw // (2 * HD) * (2 * HD)
    tail = rope_lanes(dot_nn(normed, r["wa_v"][:, even:QK]), r["cos"][...], r["sin"][...], 1.0).astype(BF)
    keys = tail[:, qw - even :]
    r["kv"][...] = jnp.concatenate([each[:, g * HD : (g + 1) * HD] for g in range(KVH) for each in (keys, values)], axis=1)
    if ready is not None:
        ready()
    queries = rope_lanes(dot_nn(normed, r["wa_v"][:, :even]), r["cos"][...], r["sin"][...], 1.0).astype(BF)
    r["q"][...] = jnp.concatenate([queries, tail[:, : qw - even]], axis=1)


def head_rows(tensor, g):
    per = H // KVH
    return jnp.concatenate([tensor[:, (g * per + i) * HD : (g * per + i + 1) * HD] for i in range(per)], axis=0)


def key_rows(r):
    start = lax.rem(lax.axis_index("tok"), 2) * r["q_in"].shape[0]
    return pl.ds(pl.multiple_of(start, 128), r["mask"].shape[0])


def attention_part(r, arrived=None):
    per = H // KVH
    q = r["q_in"][...]
    rows = q.shape[0]
    allowed = jnp.concatenate([r["mask"][...]] * per, axis=1) > 0
    mixed_t, logs = [], []
    for g in range(KVH):
        if arrived is not None:
            arrived(g)
        kv = r["kvw"][key_rows(r), 2 * g * HD : 2 * (g + 1) * HD]
        scores = jnp.where(allowed, dot_nt(kv[:, :HD], head_rows(q, g)) * HD**-0.5, masked)
        largest = jnp.max(scores, axis=0, keepdims=True)
        exponent = jnp.exp(scores - largest)
        total = jnp.sum(exponent, axis=0, keepdims=True)
        probs = (exponent * (1.0 / total)).astype(BF)
        mix = dot_nn(kv[:, HD:].T, probs)
        mixed_t += [mix[:, i * rows : (i + 1) * rows] for i in range(per)]
        logs.append(largest + jnp.log(total))
    r["lse"][...] = jnp.concatenate(logs + [logs[0]] * (r["lse"].shape[0] - KVH), axis=0)
    return jnp.concatenate(mixed_t, axis=0).T.astype(BF)


def rest_part(r, wait, arrived=None):
    state = r["state"][...]
    mixed = attention_part(r, arrived)
    r["mixed"][...] = mixed
    wait("wa")
    attn_out = dot_nn(mixed, r["wa_v"][:, QK:QKO])
    middle = state + attn_out
    r["middle"][...] = middle
    normed_two = (middle * inverse_of(middle) * r["gains"][1:2, :]).astype(BF)
    r["normed_two"][...] = normed_two
    wait("wg")
    wait("wu")
    wait("wd")
    ff = r["wg_v"].shape[1]
    mlp = jnp.zeros(state.shape, F32)
    for i in range(0, ff, CHUNK):
        at = slice(i, i + CHUNK)
        gate = dot_nn(normed_two, r["wg_v"][:, at])
        up = dot_nn(normed_two, r["wu_v"][:, at])
        r["gate"][:, at] = gate
        r["up"][:, at] = up
        hidden = (gate * jax.nn.sigmoid(gate) * up).astype(BF)
        r["hidden"][:, at] = hidden
        mlp = mlp + dot_nn(hidden, r["wd_v"][at, :])
    branch = attn_out + mlp.astype(BF).astype(F32)
    r["branch"][...] = branch
    router = jax.nn.sigmoid(jnp.sum(state * r["gains"][2:3, :], axis=1, keepdims=True))
    return state + (r["live"][:, 0:1] * router) * branch


def norm_back(grad, rows, gain):
    inverse = inverse_of(rows)
    scaled = rows * inverse
    weighted = grad * gain
    inner = jnp.mean(weighted * scaled, axis=1, keepdims=True)
    return inverse * (weighted - scaled * inner), jnp.sum(grad * scaled, axis=0, keepdims=True)


def back_part(r, wait, grad_after, made=None):
    state, live = r["b_state"][...], r["b_live"][:, 0:1]
    width = state.shape[1]
    router_vec = r["gains"][2:3, :]
    router = jax.nn.sigmoid(jnp.sum(state * router_vec, axis=1, keepdims=True))
    d_branch = (live * router) * grad_after
    d_logit = live * (router * (1.0 - router)) * jnp.sum(r["b_branch"][...] * grad_after, axis=1, keepdims=True)
    d_router = jnp.sum(d_logit * state, axis=0, keepdims=True)
    d_mlp = d_branch.astype(BF)
    r["d_mlp"][...] = d_mlp
    wait("wd")
    wait("wg")
    wait("wu")
    ff = r["wg_v"].shape[1]
    d_two = jnp.zeros(state.shape, F32)
    for i in range(0, ff, CHUNK):
        at = slice(i, i + CHUNK)
        gate, up = r["b_gate"][:, at], r["b_up"][:, at]
        sig = jax.nn.sigmoid(gate)
        d_hidden = dot_nt(d_mlp, r["wd_v"][at, :])
        d_up = (d_hidden * (gate * sig)).astype(BF)
        d_gate = (d_hidden * up * (sig * (1.0 + gate * (1.0 - sig)))).astype(BF)
        r["d_up"][:, at] = d_up
        r["d_gate"][:, at] = d_gate
        d_two = d_two + dot_nt(d_gate, r["wg_v"][:, at]) + dot_nt(d_up, r["wu_v"][:, at])
    d_two = d_two.astype(BF).astype(F32)
    d_middle, d_gain_two = norm_back(d_two, r["b_middle"][...], r["gains"][1:2, :])
    r["acc_out"][1:2, :width] = r["acc"][1:2, :width] + d_gain_two
    r["acc_out"][2:3, :width] = r["acc"][2:3, :width] + d_router
    d_attn = (d_branch + d_middle).astype(BF)
    r["d_attn"][...] = d_attn
    r["d_state"][...] = grad_after + d_logit * router_vec + d_middle
    wait("wa")
    d_mixed = dot_nt(d_attn, r["wa_v"][:, QK:QKO]).astype(BF)

    per = H // KVH
    q = r["q_in"][...]
    rows = q.shape[0]
    allowed = jnp.concatenate([r["mask"][...]] * per, axis=1) > 0
    partial, reach = r["dkv"], r["mask"].shape[0]
    keep = partial.shape[0] - reach
    unused = (1 - lax.rem(lax.axis_index("tok"), 2)) * reach
    partial[pl.ds(pl.multiple_of(unused, 128), keep), :] = jnp.zeros((keep, partial.shape[1]), BF)
    dq_t = []
    for g in range(KVH):
        lanes = slice(2 * g * HD, 2 * (g + 1) * HD)
        kv = r["kvw"][key_rows(r), lanes]
        k_g, v_g = kv[:, :HD], kv[:, HD:]
        q_g, do_g = head_rows(q, g), head_rows(d_mixed, g)
        scores = jnp.where(allowed, dot_nt(k_g, q_g) * HD**-0.5, masked)
        probs = jnp.exp(scores - r["b_lse"][g : g + 1, :])
        d_values = dot_nn(probs.astype(BF), do_g)
        d_probs = dot_nt(v_g, do_g)
        d_scores = (probs * (d_probs - jnp.sum(probs * d_probs, axis=0, keepdims=True))).astype(BF)
        d_keys = dot_nn(d_scores, q_g) * HD**-0.5
        partial[key_rows(r), lanes] = jnp.concatenate([d_keys, d_values], axis=1).astype(BF)
        dq = dot_nn(k_g.T, d_scores) * HD**-0.5
        dq_t += [dq[:, i * rows : (i + 1) * rows] for i in range(per)]
        if made is not None:
            made(g)
    d_queries = jnp.concatenate(dq_t + [jnp.zeros((HD, rows), F32)], axis=0).T
    d_queries = rope_lanes(d_queries, r["cos"][...], r["sin"][...], -1.0)
    r["d_q"][...] = d_queries[:, : H * HD].astype(BF)


def home_part(r, wait):
    total = r["home"][0]
    turned = rope_lanes(total, r["cos"][...], r["sin"][...], -1.0).astype(BF)
    low = total.astype(BF)
    d_keys = jnp.concatenate([turned[:, 2 * g * HD : (2 * g + 1) * HD] for g in range(KVH)], axis=1)
    d_values = jnp.concatenate([low[:, (2 * g + 1) * HD : 2 * (g + 1) * HD] for g in range(KVH)], axis=1)
    wait("wa")
    packed = jnp.concatenate([r["h_dq"][...], d_keys, r["h_d_attn"][...], d_values], axis=1)
    r["d_packed"][...] = packed
    d_normed = dot_nt(packed[:, :QK], r["wa_v"][:, :QK]) + dot_nt(d_values, r["wa_v"][:, QKO:])
    state = r["h_state"][...]
    width = state.shape[1]
    d_in, d_gain = norm_back(d_normed, state, r["gains"][0:1, :])
    r["acc_out"][0:1, :width] = r["acc"][0:1, :width] + d_gain
    return r["h_d_state"][...] + d_in


def stage(name, parts, needed, inputs, outputs, weights, rename=None):
    in_names, out_names = list(inputs), list(outputs)
    w_names = [w for w in needed]

    def body(*refs):
        it = iter(refs)
        r = {n: next(it) for n in in_names}
        for n in w_names:
            r[n + "_v"] = next(it)
        for n in out_names:
            r[n] = next(it)
        parts(r, lambda n: None)

    vm = pl.BlockSpec(memory_space=pltpu.VMEM)
    out = pl.pallas_call(
        body,
        name=name,
        out_shape=tuple(outputs.values()),
        in_specs=[vm] * (len(in_names) + len(w_names)),
        out_specs=tuple([vm] * len(out_names)),
        compiler_params=pltpu.CompilerParams(vmem_limit_bytes=20 * 2**20),
    )(*inputs.values(), *[weights[n] for n in w_names])
    return dict(zip(out_names, out))


def shaped(shape, kind):
    return jax.ShapeDtypeStruct(shape, kind)


def front_outs(rows, width):
    return {"normed": shaped((rows, width), BF), "q": shaped((rows, H * HD), BF), "kv": shaped((rows, 2 * KVH * HD), BF)}


FIRST_HEADS = (KVH + 1) // 2
PIECES = ((0, 2 * HD * FIRST_HEADS), (2 * HD * FIRST_HEADS, 2 * HD * (KVH - FIRST_HEADS)))


def recursion_kernel(chips, back, in_names, out_names, scratch_names, *refs):
    names = in_names + list(WEIGHTS) + out_names + scratch_names
    r = dict(zip(names, refs, strict=True))
    g, t = lax.axis_index("grp"), lax.axis_index("tok")
    z, c = t // 2, lax.rem(t, 2)
    rows = r["hidden_in"].shape[1]
    partner, left, right = (g, z * 2 + 1 - c), (g, t - 2), (g, t + 2)

    copies = {n: pltpu.make_async_copy(r[n], r[n + "_v"], r["w_sem"].at[i]) for i, n in enumerate(WEIGHTS)}
    for n in WEIGHTS:
        copies[n].start()
    done = set()

    def wait(n):
        if n not in done:
            copies[n].wait()
            done.add(n)

    bar = pltpu.get_barrier_semaphore()
    pl.semaphore_signal(bar, inc=1, device_id=partner, device_id_type=MESH)

    @pl.when(z > 0)
    def _():
        pl.semaphore_signal(bar, inc=1, device_id=left, device_id_type=MESH)

    @pl.when(z < chips - 1)
    def _():
        pl.semaphore_signal(bar, inc=1, device_id=right, device_id_type=MESH)

    def at(d, core):
        return pl.ds(pl.multiple_of(((back - d) * 2 + core) * rows, 128), rows)

    r["acc_out"][...] = jnp.zeros(r["acc_out"].shape, F32)
    for step in range(RECUR):
        for d in range(1, back + 1):
            @pl.when(z < d)
            def _():
                for core in (0, 1):
                    r["kvw"][step, at(d, core), :] = jnp.zeros((rows, r["kvw"].shape[2]), BF)

    def of_step(step):
        every = {n: r[n] for n in ("gains", "cos", "sin", "acc_out", "d_state", "d_q", "d_attn", "dkv", "home")}
        every |= {n + "_v": r[n + "_v"] for n in WEIGHTS}
        every |= {n: r[n] for n in ROW_NAMES[:4]}
        every |= {n: r[n + str(step)] for n in ROW_NAMES[4:]}
        for n in ("q", "kvw", "mask", "live", "state", "lse", "middle", "branch", "gate", "up"):
            every[n] = r[n].at[step]
        every |= {"q_in": every["q"], "kv": r["kvw"].at[step, at(0, c)], "acc": r["acc_out"]}
        every |= {"b_" + n: every[n] for n in ("state", "live", "branch", "gate", "up", "middle", "lse")}
        every |= {"h_dq": r["d_q"], "h_state": every["state"], "h_d_state": r["d_state"], "h_d_attn": r["d_attn"]}
        return every

    def k_along(step, d, j):
        src, dst = (r["kvw"].at[step, at(e, c), pl.ds(*PIECES[j])] for e in (d - 1, d))
        return copy_to(src, dst, r["k_s"].at[step, j, d - 1], r["k_r"].at[step, j, d - 1], right)

    def k_beside(step, d, j):
        here = r["kvw"].at[step, at(d, c), pl.ds(*PIECES[j])]
        return copy_to(here, here, r["kc_s"].at[step, j, d], r["kc_r"].at[step, j, d], partner)

    def keys_start(step):
        for j in (0, 1):
            @pl.when(z < chips - 1)
            def _():
                k_along(step, 1, j).start()

            k_beside(step, 0, j).start()

    def keys_pass(step, d, j):
        @pl.when(z >= d)
        def _():
            k_along(step, d, j).wait_recv()
            if d < back:
                @pl.when(z < chips - 1)
                def _():
                    k_along(step, d + 1, j).start()
            k_beside(step, d, j).start()

    def keys_end(step, j):
        k_beside(step, 0, j).wait_recv()
        for d in range(1, back + 1):
            @pl.when(z >= d)
            def _():
                k_beside(step, d, j).wait_recv()

    def keys_arrived(step, g):
        if g == 0:
            for d in range(1, back):
                keys_pass(step, d, 0)
                keys_pass(step, d, 1)
            keys_pass(step, back, 0)
            keys_end(step, 0)
        if g == FIRST_HEADS:
            keys_pass(step, back, 1)
            keys_end(step, 1)

    def keys_drain(step):
        for j in (0, 1):
            k_beside(step, 0, j).wait_send()
            for d in range(1, back + 1):
                @pl.when(z >= d)
                def _():
                    k_beside(step, d, j).wait_send()

                @pl.when((z >= d - 1) & (z < chips - 1))
                def _():
                    k_along(step, d, j).wait_send()

    def h_beside(step, d, j):
        piece = pl.ds(*PIECES[j])
        return copy_to(r["dkv"].at[at(d, 1 - c), piece], r["beside_in"].at[step, d, :, piece], r["hc_s"].at[step, j, d], r["hc_r"].at[step, j, d], partner)

    def h_along(step, d, j):
        piece = pl.ds(*PIECES[j])
        return copy_to(r["sums"].at[d - 1, :, piece], r["after_in"].at[step, d - 1, :, piece], r["h_s"].at[step, j, d - 1], r["h_r"].at[step, j, d - 1], left)

    def home_start(step, j):
        for d in range(back, 0, -1):
            @pl.when(z >= d)
            def _():
                h_beside(step, d, j).start()
        h_beside(step, 0, j).start()

    def home_pass(step, d, j):
        lanes = slice(PIECES[j][0], sum(PIECES[j]))

        @pl.when(z >= d)
        def _():
            h_beside(step, d, j).wait_recv()
            total = r["dkv"][at(d, c), lanes].astype(F32) + r["beside_in"][step, d, :, lanes].astype(F32)
            r["sums"][d - 1, :, lanes] = total.astype(BF)
            if d < back:
                @pl.when(z < chips - 1)
                def _():
                    h_along(step, d + 1, j).wait_recv()
                    more = r["sums"][d - 1, :, lanes].astype(F32) + r["after_in"][step, d, :, lanes].astype(F32)
                    r["sums"][d - 1, :, lanes] = more.astype(BF)
            h_along(step, d, j).start()

    def home_made(step, g):
        if g == FIRST_HEADS - 1:
            home_start(step, 0)
        if g == FIRST_HEADS:
            home_pass(step, back, 0)
        if g == KVH - 1:
            home_start(step, 1)

    def home_end(step):
        home_pass(step, back, 1)
        for d in range(back - 1, 0, -1):
            for j in (0, 1):
                home_pass(step, d, j)
        for j in (0, 1):
            h_beside(step, 0, j).wait_recv()
        r["home"][0] = r["dkv"][at(0, c), :].astype(F32) + r["beside_in"][step, 0].astype(F32)

        @pl.when(z < chips - 1)
        def _():
            for j in (0, 1):
                h_along(step, 1, j).wait_recv()
            r["home"][0] = r["home"][0] + r["after_in"][step, 0].astype(F32)

        for j in (0, 1):
            h_beside(step, 0, j).wait_send()
            for d in range(1, back + 1):
                @pl.when(z >= d)
                def _():
                    h_beside(step, d, j).wait_send()
                    h_along(step, d, j).wait_send()

    def turn(name, step):
        r[name + "_t" + str(step)][...] = r[name][...].astype(F32).T.astype(BF)

    r["state"][0] = r["hidden_in"][...].astype(F32).T
    met = False
    for step in range(RECUR):
        here = of_step(step)

        def ready(step=step, first=step == 0):
            if first:
                pl.semaphore_wait(bar, 1 + (z < chips - 1).astype(jnp.int32) + (z > 0).astype(jnp.int32))
            keys_start(step)

        front_part(here, wait, here["state"][...], ready)
        turn("normed", step)
        if step > 0:
            turn("mixed", step - 1)
            turn("normed_two", step - 1)
        after = rest_part(here, wait, lambda g, step=step: keys_arrived(step, g))
        keys_drain(step)
        if step < RECUR - 1:
            r["state"][step + 1] = after
        else:
            r["output"][...] = after.T.astype(BF)
    grad = r["cot"][...].astype(F32).T
    for step in reversed(range(RECUR)):
        here = of_step(step)
        back_part(here, wait, grad, lambda g, step=step: home_made(step, g))
        turn("d_mlp", step)
        if step == RECUR - 1:
            turn("mixed", step)
            turn("normed_two", step)
        home_end(step)
        grad = home_part(here, wait)
    r["grad"][...] = grad.T


def all_recursions(hidden_in, cotangent, masks, lives, tables, gains, weights, n_tok, nback):
    back = nback // 2
    width, rows = hidden_in.shape
    ff = weights["wg"].shape[1]
    kvr = 2 * KVH * HD
    slots = (2 * back + 2) * rows
    ins = {"hidden_in": hidden_in, "cot": cotangent, "mask": masks, "live": lives, "cos": tables[0], "sin": tables[1], "gains": gains}
    outs = {"output": shaped((width, rows), BF), "grad": shaped((width, rows), F32), "acc_out": shaped((8, 1024), F32)}
    for step in range(RECUR):
        outs |= {name + "_t" + str(step): shaped((width, rows), BF) for name in ROW_NAMES[:4]}
        outs |= {name + str(step): shaped((rows, ff), BF) for name in ROW_NAMES[4:]}
    dma, vm = pltpu.SemaphoreType.DMA, pltpu.VMEM
    scratch = {n + "_v": vm(weights[n].shape, BF) for n in WEIGHTS}
    scratch |= {
        "state": vm((RECUR, rows, width), F32), "middle": vm((RECUR, rows, width), F32), "branch": vm((RECUR, rows, width), F32),
        "gate": vm((RECUR, rows, ff), F32), "up": vm((RECUR, rows, ff), F32), "lse": vm((RECUR, 8, (H // KVH) * rows), F32),
        "q": vm((RECUR, rows, H * HD), BF), "kvw": vm((RECUR, slots, kvr), BF), "d_state": vm((rows, width), F32),
        "d_q": vm((rows, H * HD), BF), "d_attn": vm((rows, width), BF), "dkv": vm((slots, kvr), BF), "home": vm((1, rows, kvr), F32),
        "beside_in": vm((RECUR, back + 1, rows, kvr), BF), "after_in": vm((RECUR, back, rows, kvr), BF), "sums": vm((back, rows, kvr), BF),
        "w_sem": dma((len(WEIGHTS),)),
    }
    scratch |= {name: vm((rows, width), BF) for name in ROW_NAMES[:4]}
    scratch |= {name: dma((RECUR, 2, back)) for name in ("k_s", "k_r", "h_s", "h_r")}
    scratch |= {name: dma((RECUR, 2, back + 1)) for name in ("kc_s", "kc_r", "hc_s", "hc_r")}
    spec = pl.BlockSpec(memory_space=pltpu.VMEM)
    got = pl.pallas_call(
        lambda *refs: recursion_kernel(n_tok // 2, back, list(ins), list(outs), list(scratch), *refs),
        name="all_recursions",
        out_shape=tuple(outs.values()),
        in_specs=[spec] * len(ins) + [pl.BlockSpec(memory_space=pl.ANY)] * len(WEIGHTS),
        out_specs=tuple([spec] * len(outs)),
        scratch_shapes=list(scratch.values()),
        compiler_params=pltpu.CompilerParams(collective_id=5, has_side_effects=True, vmem_limit_bytes=62 * 2**20),
    )(*ins.values(), *[weights[n] for n in WEIGHTS])
    return dict(zip(outs, got))


def forward_stage(state, q, kvw, mask, live, tables, gains, weights, last):
    rows, width = state.shape
    ff = weights["wg"].shape[1]
    outs = {
        "mixed": shaped((rows, H * HD), BF), "lse": shaped((8, (H // KVH) * rows), F32), "middle": shaped((rows, width), F32),
        "normed_two": shaped((rows, width), BF), "gate": shaped((rows, ff), F32), "up": shaped((rows, ff), F32),
        "hidden": shaped((rows, ff), BF), "branch": shaped((rows, width), F32),
    }
    if last:
        outs["output"] = shaped((width, rows), BF)
    else:
        outs |= front_outs(rows, width) | {"next": shaped((rows, width), F32)}

    def parts(r, wait):
        state_next = rest_part(r, wait)
        if last:
            r["output"][...] = state_next.T.astype(BF)
        else:
            r["next"][...] = state_next
            front_part(r, wait, state_next)

    needed = ("wa", "wg", "wu", "wd")
    ins = {"state": state, "q_in": q, "kvw": kvw, "mask": mask, "live": live, "cos": tables[0], "sin": tables[1], "gains": gains}
    return stage("forward", parts, needed, ins, outs, weights)


def first_stage(hidden_in, tables, gains, weights):
    width, rows = hidden_in.shape

    def parts(r, wait):
        state = r["hidden"][...].astype(F32).T
        r["state"][...] = state
        front_part(r, wait, state)

    outs = front_outs(rows, width) | {"state": shaped((rows, width), F32)}
    return stage("first", parts, ("wa",), {"hidden": hidden_in, "cos": tables[0], "sin": tables[1], "gains": gains}, outs, weights)


def backward_stage(kept, before, mask, live, tables, gains, acc, weights, cotangent):
    ins = {"cos": tables[0], "sin": tables[1], "gains": gains, "acc": acc}
    outs = {"acc_out": shaped(acc.shape, F32)}
    needed = ()
    rows, width = (kept or before)["state"].shape
    ff = weights["wg"].shape[1]
    kvr = 2 * KVH * HD
    if before is not None:
        ins |= {"home": before["home"], "h_dq": before["d_q"], "h_state": before["state"], "h_d_state": before["d_state"], "h_d_attn": before["d_attn"]}
        outs |= {"d_packed": shaped((rows, QKO + kvr // 2), BF)}
        needed += ("wa",)
    else:
        ins |= {"cot": cotangent}
    if kept is not None:
        ins |= {"b_state": kept["state"], "b_live": live, "b_branch": kept["branch"], "b_gate": kept["gate"], "b_up": kept["up"],
                "b_middle": kept["middle"], "b_lse": kept["lse"], "kvw": kept["kvw"], "q_in": kept["q"], "mask": mask}
        outs |= {"d_mlp": shaped((rows, width), BF), "d_up": shaped((rows, ff), BF), "d_gate": shaped((rows, ff), BF),
                 "d_attn": shaped((rows, width), BF), "d_state": shaped((rows, width), F32), "d_q": shaped((rows, H * HD), BF),
                 "dkv": shaped(kept["kvw"].shape, BF)}
        needed += ("wd", "wg", "wu") + (("wa",) if before is None else ())
    else:
        outs |= {"grad": shaped((width, rows), F32)}

    def parts(r, wait):
        r["acc_out"][...] = r["acc"][...]
        grad = home_part(r, wait) if before is not None else r["cot"][...].astype(F32).T
        if kept is not None:
            back_part(r, wait, grad)
        else:
            r["grad"][...] = grad.T

    return stage("backward", parts, needed, ins, outs, weights)


PARTS = 16
HALF = 480
COLS = 640
STREAMS = (
    ("x", True, 0, 80, 0),
    ("y", True, 80, 80, 0),
    ("x", True, 160, 80, 1),
    ("y", True, 240, 80, 1),
    ("x", True, 320, 80, 2),
    ("y", True, 400, 80, 2),
)
SCHEDULE = (
    (0, 0), (0, 1), (1, 0, 0), (0, 2), (1, 1, 0), (8, 0), (0, 3), (0, 4), (0, 5), (0, 6), (1, 5, 0), (1, 4, 0), (1, 2, 0), (0, 7),
    (1, 3, 0), (8, 1), (2, 0, 0), (0, 8), (0, 9), (1, 2, 1), (1, 8, 0), (1, 6, 0), (1, 7, 0), (2, 1, 0), (0, 10), (0, 11), (1, 10, 0),
    (8, 2), (2, 0, 1), (1, 1, 1), (0, 12), (0, 13), (1, 7, 1), (1, 9, 0), (1, 12, 0), (0, 14), (2, 1, 1), (1, 0, 1), (0, 15), (1, 11, 0),
    (0, 16), (8, 3), (1, 15, 0), (2, 0, 2), (1, 13, 0), (1, 14, 0), (2, 1, 2), (8, 4), (1, 11, 2), (1, 4, 1), (1, 3, 1), (1, 5, 1),
    (1, 6, 1), (2, 0, 3), (1, 8, 1), (2, 1, 3), (1, 10, 1), (2, 3, 0), (1, 9, 1), (2, 2, 0), (3, 0), (2, 3, 1), (3, 1), (1, 12, 1),
    (1, 14, 1), (4, 0), (1, 13, 1), (4, 1), (1, 15, 1), (1, 11, 1), (1, 4, 2), (2, 2, 1), (5, 1), (1, 1, 2), (2, 3, 2), (1, 6, 2),
    (6, 0, 1), (1, 0, 2), (2, 2, 2), (6, 1, 1), (1, 3, 2), (2, 3, 3), (1, 2, 2), (6, 0, 2), (1, 5, 2), (2, 2, 3), (6, 1, 2), (3, 2),
    (2, 5, 0), (3, 3), (1, 7, 2), (1, 9, 2), (7, 0, 1), (2, 4, 0), (6, 0, 3), (6, 1, 3), (2, 5, 1), (7, 1, 1), (1, 14, 2), (4, 2),
    (1, 13, 2), (1, 10, 2), (4, 3), (2, 4, 1), (7, 1, 3), (7, 1, 2), (6, 3, 1), (1, 8, 2), (5, 0), (1, 15, 2), (7, 0, 2), (6, 2, 1),
    (2, 4, 2), (1, 12, 2), (6, 2, 2), (2, 5, 2), (5, 3), (2, 4, 3), (6, 3, 2), (2, 5, 3), (3, 4), (6, 3, 3), (3, 5), (7, 3, 3), (7, 3, 1),
    (7, 0, 3), (4, 4), (4, 5), (6, 2, 3), (6, 4, 1), (6, 5, 1), (7, 5, 1), (6, 4, 2), (7, 4, 1), (7, 2, 3), (7, 2, 1), (5, 2), (7, 4, 2),
    (6, 5, 2), (6, 4, 3), (5, 5), (7, 5, 2), (7, 2, 2), (5, 4), (7, 3, 2), (6, 5, 3), (7, 4, 3), (7, 5, 3),
)
SLOTS = 4


def place():
    g, t = lax.axis_index("grp"), lax.axis_index("tok")
    return g // 2, lax.rem(g, 2), t // 2, lax.rem(t, 2)


def dev(y, x, z, c):
    return (y * 2 + x, z * 2 + c)


def pick(z, values):
    out = jnp.int32(values[3])
    for i in (2, 1, 0):
        out = jnp.where(z == i, jnp.int32(values[i]), out)
    return out


def copy_to(src, dst, send, recv, device):
    return pltpu.make_async_remote_copy(src_ref=src, dst_ref=dst, send_sem=send, recv_sem=recv, device_id=device, device_id_type=MESH)


def add_rows(dst, src, rows, step):
    def body(i, _):
        at = pl.ds(pl.multiple_of(i * step, step), step)
        dst[at, :] = dst[at, :] + src[at, :]
        return 0

    lax.fori_loop(0, rows // step, body, 0)


def tail_kernel(count, *refs):
    left_refs, refs = refs[: 4 * count], refs[4 * count :]
    right_refs, refs = refs[: 4 * count], refs[4 * count :]
    n_s = len(STREAMS)
    v_ref, o_ref, vo_ref, left_t, right, theirs, mine, other = refs[:8]
    ra, rz, rb = refs[8 : 8 + n_s], refs[8 + n_s : 8 + 2 * n_s], refs[8 + 2 * n_s : 8 + 3 * n_s]
    vrecv, left_sem, load_sem, core_s, core_r, as_, ar, zs, zr, bs, br, ob, obr, oz, ozr, oa, oar, oc, ocr, vs, vr, own_sem = refs[8 + 3 * n_s :]
    y, x, z, c = place()
    partner = dev(y, x, z, 1 - c)
    across = {"x": dev(y, 1 - x, z, c), "y": dev(1 - y, x, z, c)}
    left_dev, right_dev = dev(y, x, z - 1, c), dev(y, x, z + 1, c)
    at_axis = {"x": x, "y": y}
    order = (pick(z, (3, 3, 0, 0)), pick(z, (2, 0, 3, 1)), pick(z, (1, 2, 1, 2)), z)
    far = dev(y, x, jnp.where(z < 2, z + 2, z - 2), c)
    tokens = left_refs[0].shape[1]
    lefts = [pltpu.make_async_copy(each, left_t.at[i // count, :, pl.ds(i % count * tokens, tokens)], left_sem.at[i]) for i, each in enumerate(left_refs)]

    def load(p, src, i):
        return pltpu.make_async_copy(src, right.at[p, pl.ds(i * tokens, tokens)], load_sem.at[p * count + i])

    for k in range(4):
        for j in range(4):
            for i in range(count):
                if k == 0:
                    lefts[j * count + i].start()
                columns = pl.ds(pl.multiple_of(order[k] * COLS, COLS), COLS)
                load(j * 4 + order[k], right_refs[j * count + i].at[:, columns], i).start()

    bar = pltpu.get_barrier_semaphore()
    for d in (partner, across["x"], across["y"], far):
        pl.semaphore_signal(bar, inc=1, device_id=d, device_id_type=MESH)

    @pl.when(z > 0)
    def _():
        pl.semaphore_signal(bar, inc=1, device_id=left_dev, device_id_type=MESH)

    @pl.when(z < 3)
    def _():
        pl.semaphore_signal(bar, inc=1, device_id=right_dev, device_id_type=MESH)

    for cp in lefts:
        cp.wait()
    pl.semaphore_wait(bar, 4 + (z > 0).astype(jnp.int32) + (z < 3).astype(jnp.int32))

    def part_xy(px, py, pz):
        return (px * 2 + py) * 4 + pz

    def part_of(s, pa, pb, pz):
        return part_xy(pa, pb, pz) if STREAMS[s][0] == "x" else part_xy(pb, pa, pz)

    def ab(s):
        a = STREAMS[s][0]
        b = "y" if a == "x" else "x"
        return at_axis[a], at_axis[b], across[a], across[b]

    waits = []
    seq = [(k, i, px, py) for k in range(4) for i, (px, py) in enumerate(((1 - x, 1 - y), (1 - x, y), (x, 1 - y), (x, y)))]

    def core_copy(j):
        k, _, px, py = seq[j]
        p = part_xy(px, py, order[k])
        return copy_to(theirs.at[j % SLOTS, pl.ds(pl.multiple_of((1 - c) * HALF, 16), HALF)], other.at[p], core_s.at[j], core_r.at[p], partner)

    def core_make(j):
        k, _, px, py = seq[j]
        p = part_xy(px, py, order[k])
        for i in range(count):
            load(p, right_refs[0].at[:, pl.ds(0, COLS)], i).wait()
        if j >= SLOTS:
            core_copy(j - SLOTS).wait_send()
        which = jnp.where(p < 8, 0, jnp.where(p < 12, 1, jnp.where(p < 14, 2, 3)))
        split = 2 * COLS - 2 * HALF
        theirs[j % SLOTS] = dot_nn(left_t[which], right[p]).astype(BF)

        @pl.when(p == PARTS - 1)
        def _():
            theirs[j % SLOTS, :, COLS - split :] = dot_nn(left_t[2], right[p, :, COLS - split :]).astype(BF)

        core_copy(j).start()

    def core_add(j):
        k, i, px, py = seq[j]
        p = part_xy(px, py, order[k])
        core_copy(j).wait_recv()
        mine[p] = theirs[j % SLOTS, pl.ds(pl.multiple_of(c * HALF, 16), HALF), :] + other[p]

    def a_copy(s, pb, pz):
        a, b, to_a, _ = ab(s)
        _, _, r0, n, _ = STREAMS[s]
        return copy_to(mine.at[part_of(s, 1 - a, pb, pz), pl.ds(r0, n)], ra[s].at[pb * 4 + pz], as_.at[s, pb * 4 + pz], ar.at[s, pb * 4 + pz], to_a)

    def a_send(j, batch):
        k, i, px, py = seq[j]
        for s in range(n_s):
            a_axis = STREAMS[s][0]
            if STREAMS[s][4] == batch and (i == 0 or (i == 1 and a_axis == "x") or (i == 2 and a_axis == "y")):
                cp = a_copy(s, py if a_axis == "x" else px, order[k])
                cp.start()
                waits.append(cp)

    def z_index(s, pb, slot):
        return pb * 5 + slot if STREAMS[s][1] else slot

    def z_copy(s, pb, pz, to_right):
        a, b, _, _ = ab(s)
        _, _, r0, n, _ = STREAMS[s]
        src = mine.at[part_of(s, a, pb, pz), pl.ds(r0, n)]
        i = z_index(s, pb, pz if to_right else jnp.where(pz == z - 1, 4, pz))
        return copy_to(src, rz[s].at[i], zs.at[s, i], zr.at[s, i], right_dev if to_right else left_dev)

    def z_take(s, pb, slot):
        a, _, _, _ = ab(s)
        _, _, r0, n, _ = STREAMS[s]
        i = z_index(s, pb, slot)
        copy_to(mine.at[0, pl.ds(r0, n)], rz[s].at[i], zs.at[s, i], zr.at[s, i], left_dev).wait_recv()
        pz = z if slot is z or isinstance(slot, int) else slot
        add_rows(mine.at[part_of(s, a, pb, pz), pl.ds(r0, n)], rz[s].at[i], n, 16)

    def z_step(s, pb, k):
        pz = order[k]
        if k < 3:
            up = jnp.where(pz > z, (z > 0).astype(jnp.int32), (z < 3).astype(jnp.int32))

            @pl.when(up == 1)
            def _():
                z_take(s, pb, pz)

            @pl.when(pz > z)
            def _():
                z_copy(s, pb, pz, True).start()

            @pl.when(pz < z)
            def _():
                z_copy(s, pb, pz, False).start()
        else:
            @pl.when(z > 0)
            def _():
                z_take(s, pb, z)

            @pl.when(z < 3)
            def _():
                z_take(s, pb, 4)

    def z_drain(s, pb, k):
        pz = order[k]

        @pl.when(pz > z)
        def _():
            z_copy(s, pb, pz, True).wait_send()

        @pl.when(pz < z)
        def _():
            z_copy(s, pb, pz, False).wait_send()

    def a_step(s, pb, k):
        a, b, to_a, _ = ab(s)
        _, _, r0, n, _ = STREAMS[s]
        pz = order[k]
        a_copy(s, pb, pz).wait_recv()
        add_rows(mine.at[part_of(s, a, pb, pz), pl.ds(r0, n)], ra[s].at[pb * 4 + pz], n, 16)

    def b_copy(s, pz):
        a, b, _, to_b = ab(s)
        _, second_z, r0, n, _ = STREAMS[s]
        i = 0 if second_z else pz
        return copy_to(mine.at[part_of(s, a, 1 - b, pz), pl.ds(r0, n)], rb[s].at[i], bs.at[s, i], br.at[s, i], to_b)

    def b_step(s, pz):
        a, b, _, _ = ab(s)
        _, second_z, r0, n, _ = STREAMS[s]
        i = 0 if second_z else pz
        b_copy(s, pz).wait_recv()
        add_rows(mine.at[part_of(s, a, b, pz), pl.ds(r0, n)], rb[s].at[i], n, 16)

    def of_batch(batch):
        return [s for s in range(n_s) if STREAMS[s][4] == batch]

    def first_step(only, k):
        for s in (only,):
            _, b, _, _ = ab(s)
            a_step(s, 1 - b, k)
            if STREAMS[s][1]:
                z_step(s, 1 - b, k)
                a_step(s, b, k)
                z_step(s, b, k)
                if k == 3:
                    cp = b_copy(s, z)
                    cp.start()
                    waits.append(cp)
            else:
                cp = b_copy(s, order[k])
                cp.start()
                waits.append(cp)
                a_step(s, b, k)

    def second_step(batch, k):
        for s in of_batch(batch):
            _, b, _, _ = ab(s)
            if not STREAMS[s][1]:
                b_step(s, order[k])
                z_step(s, b, k)

    def vec_copy(i):
        to = (partner, across["x"], across["y"], dev(y, x, jnp.where(lax.rem(z, 2) == 0, z + 1, z - 1), c), far)[i]
        return copy_to(vo_ref, vrecv.at[i], vs.at[i], vr.at[i], to)

    def vec_end(i):
        vec_copy(i).wait()
        vo_ref[...] = vo_ref[...] + vrecv[i]

    half0 = c * HALF

    def out_at(s, p):
        _, _, r0, n, _ = STREAMS[s]
        return o_ref.at[p, pl.ds(pl.multiple_of(half0 + r0, 16), n)]

    def mine_at(s, p):
        _, _, r0, n, _ = STREAMS[s]
        return mine.at[p, pl.ds(r0, n)]

    def go(cp):
        cp.start()
        waits.append(cp)

    def to_core(s, p, src):
        return copy_to(src, out_at(s, p), oc.at[s, p], ocr.at[s, p], partner)

    def to_a(s, pb, pz, src):
        a, b, na, _ = ab(s)
        return copy_to(src, out_at(s, part_of(s, a, pb, pz)), oa.at[s, pb * 4 + pz], oar.at[s, pb * 4 + pz], na)

    def to_b(s, pz, src):
        a, b, _, nb = ab(s)
        return copy_to(src, out_at(s, part_of(s, a, b, pz)), ob.at[s, pz], obr.at[s, pz], nb)

    def to_z(s, pb, pz, src, to_right):
        a, b, _, _ = ab(s)
        i = pb * 8 + pz * 2 + (0 if to_right else 1)
        return copy_to(src, out_at(s, part_of(s, a, pb, pz)), oz.at[s, i], ozr.at[s, pb * 4 + pz], right_dev if to_right else left_dev)

    def spread_z(s, pb, pz, src, sides):
        if 0 in sides:
            @pl.when(z < 3)
            def _():
                to_z(s, pb, pz, src, True).start()
        if 1 in sides:
            @pl.when(z > 0)
            def _():
                to_z(s, pb, pz, src, False).start()

    def finish(only):
        for s in (only,):
            a, b, _, _ = ab(s)
            p = part_of(s, a, b, z)
            b_step(s, z)
            if not STREAMS[s][1]:
                z_step(s, b, 3)
            src = mine_at(s, p)
            if STREAMS[s][1]:
                go(to_b(s, z, src))
                spread_z(s, b, z, src, (0, 1))
            else:
                spread_z(s, b, z, src, (0, 1))
                go(to_b(s, z, src))
            go(to_a(s, b, z, src))
            go(to_core(s, p, src))
            pltpu.make_async_copy(src, out_at(s, p), own_sem.at[s]).start()

    def got_b(s, pz):
        a, b, _, _ = ab(s)
        p = part_of(s, a, 1 - b, pz)
        src = out_at(s, p)
        copy_to(src, src, ob.at[s, pz], obr.at[s, pz], partner).wait_recv()
        if STREAMS[s][1]:
            spread_z(s, 1 - b, pz, src, (0, 1))
        to_a(s, 1 - b, pz, src).start()
        to_core(s, p, src).start()

    def got_z(s, pb, pz, from_left):
        a, b, _, _ = ab(s)
        p = part_of(s, a, pb, pz)
        src = out_at(s, p)
        copy_to(src, src, oz.at[s, 0], ozr.at[s, pb * 4 + pz], partner).wait_recv()
        spread_z(s, pb, pz, src, (0,) if from_left else (1,))
        to_a(s, pb, pz, src).start()
        if not STREAMS[s][1]:
            to_b(s, pz, src).start()
        to_core(s, p, src).start()

    def got_a(s, pb, pz):
        a, b, _, _ = ab(s)
        p = part_of(s, 1 - a, pb, pz)
        src = out_at(s, p)
        copy_to(src, src, oa.at[s, pb * 4 + pz], oar.at[s, pb * 4 + pz], partner).wait_recv()
        to_core(s, p, src).start()

    def gather_b(only):
        for s in (only,):
            got_b(s, z)

    def gather_a(only):
        for s in (only,):
            _, b, _, _ = ab(s)
            got_a(s, b, z)
            got_a(s, 1 - b, z)

    def from_side(t, side):
        return (z - t, z >= t) if side == 0 else (z + t, z + t <= 3)

    def gather_z(only, t):
        for side in (0, 1):
            pz, there = from_side(t, side)

            @pl.when(there)
            def _():
                _, b, _, _ = ab(only)
                got_z(only, b, pz, side == 0)
                got_z(only, 1 - b, pz, side == 0)

    def gather_rest(only, t):
        for side in (0, 1):
            pz, there = from_side(t, side)

            @pl.when(there)
            def _():
                _, b, _, _ = ab(only)
                got_a(only, b, pz)
                got_a(only, 1 - b, pz)

    def make(j):
        if j < PARTS:
            core_make(j)
        if j > 0:
            core_add(j - 1)

    def vec_end_start(i):
        vec_end(i)
        if i < 4:
            vec_copy(i + 1).start()

    vo_ref[...] = v_ref[...]
    vec_copy(0).start()

    actions = (make, a_send, first_step, finish, gather_b, gather_a, gather_z, gather_rest, vec_end_start)
    for kind, *which in SCHEDULE:
        actions[kind](*which)

    for cp in waits:
        cp.wait_send()
    for j in range(PARTS - SLOTS, PARTS):
        core_copy(j).wait_send()
    for s in range(n_s):
        a, b, _, _ = ab(s)
        pltpu.make_async_copy(mine_at(s, part_of(s, a, b, z)), out_at(s, part_of(s, a, b, z)), own_sem.at[s]).wait()
        pbs = (b, 1 - b) if STREAMS[s][1] else (b,)
        for pb in pbs:
            for k in range(3):
                z_drain(s, pb, k)
        for pz in range(4):
            for pb in pbs:
                src = out_at(s, part_of(s, a, pb, pz))

                @pl.when((z >= pz) & (z < 3))
                def _():
                    to_z(s, pb, pz, src, True).wait_send()

                @pl.when((z <= pz) & (z > 0))
                def _():
                    to_z(s, pb, pz, src, False).wait_send()
            for pb in (0, 1):
                src = out_at(s, part_of(s, a, pb, pz))

                @pl.when(jnp.logical_not((pb == b) & (pz == z)))
                def _():
                    to_a(s, pb, pz, src).wait_send()
            if not STREAMS[s][1]:
                @pl.when(z != pz)
                def _():
                    to_b(s, pz, out_at(s, 0)).wait_send()
        for p in range(16):
            src = out_at(s, p)

            @pl.when(p != part_of(s, a, b, z))
            def _():
                to_core(s, p, src).wait_send()
            _, _, r0, n, _ = STREAMS[s]
            dst = o_ref.at[p, pl.ds(pl.multiple_of((1 - c) * HALF + r0, 16), n)]
            copy_to(dst, dst, oc.at[s, p], ocr.at[s, p], partner).wait_recv()


def summed_gradients(lefts, rights, vectors):
    dma = pltpu.SemaphoreType.DMA
    count = len(lefts[0])
    width, tokens = lefts[0][0].shape
    rows = count * tokens
    n_s = len(STREAMS)
    vm = pl.BlockSpec(memory_space=pltpu.VMEM)
    return pl.pallas_call(
        lambda *refs: tail_kernel(count, *refs),
        name="summed_gradients",
        out_shape=(jax.ShapeDtypeStruct((PARTS, width, COLS), BF), jax.ShapeDtypeStruct(vectors.shape, F32)),
        in_specs=[pl.BlockSpec(memory_space=pl.ANY)] * (8 * count) + [vm],
        out_specs=(pl.BlockSpec(memory_space=pl.ANY), vm),
        scratch_shapes=[
            pltpu.VMEM((4, width, rows), BF), pltpu.VMEM((PARTS, rows, COLS), BF), pltpu.VMEM((SLOTS, 2 * HALF, COLS), BF),
            pltpu.VMEM((PARTS, HALF, COLS), BF), pltpu.VMEM((PARTS, HALF, COLS), BF),
            *[pltpu.VMEM((8, s[3], COLS), BF) for s in STREAMS],
            *[pltpu.VMEM((10 if s[1] else 5, s[3], COLS), BF) for s in STREAMS],
            *[pltpu.VMEM((1 if s[1] else 4, s[3], COLS), BF) for s in STREAMS],
            pltpu.VMEM((5, *vectors.shape), F32),
            dma((4 * count,)), dma((PARTS * count,)), dma((16,)), dma((16,)),
            dma((n_s, 8)), dma((n_s, 8)), dma((n_s, 10)), dma((n_s, 10)), dma((n_s, 4)), dma((n_s, 4)),
            dma((n_s, 4)), dma((n_s, 4)), dma((n_s, 16)), dma((n_s, 8)), dma((n_s, 8)), dma((n_s, 8)), dma((n_s, 16)), dma((n_s, 16)),
            dma((5,)), dma((5,)), dma((n_s,)),
        ],
        compiler_params=pltpu.CompilerParams(collective_id=1, has_side_effects=True, vmem_limit_bytes=60 * 2**20),
    )(*[a for l in lefts for a in l], *[a for l in rights for a in l], vectors)


QUARTERS = 4
UNITS = ((0, 0, 1536, True, True), (0, 1536, 1024, False, True), (1, 0, 2560, True, False), (2, 0, 2560, True, True), (3, 0, 320, True, False))
FIRST = (0, 2, 3, 4, 1)
SMALL_AT = (5, 10, 15)


def gather_kernel(*refs):
    q_ref, k_ref, o_ref, v_ref = refs[:4]
    ins, outs, packed = (refs[17], *refs[4:8]), refs[8:13], refs[17]
    turned = [each[...].astype(F32).T.astype(BF) for each in (k_ref, v_ref)]
    packed[...] = jnp.concatenate([q_ref[...], turned[0], o_ref[...], turned[1]], axis=1)
    zs, xs, ys, cs, got, cgot, own_s, own_c, own_r, ss, sr, sc, scr = (*refs[13:17], *refs[18:])
    y, x, z, c = place()
    partner, to_x, to_y = dev(y, x, z, 1 - c), dev(y, 1 - x, z, c), dev(1 - y, x, z, c)
    left, right = dev(y, x, z - 1, c), dev(y, x, z + 1, c)
    quarter = (x * 2 + y, (1 - x) * 2 + y, x * 2 + (1 - y), (1 - x) * 2 + (1 - y))
    lasting = []

    def go(cp, when=None):
        if when is None:
            cp.start()
        else:
            @pl.when(when)
            def _():
                cp.start()
        lasting.append((cp, when))

    def cut(ref, u, q):
        m, first, size, shared, _ = UNITS[u]
        n = size // QUARTERS if shared else size
        begin = first + q * n if shared else first
        if m < 3:
            return ref.at[:, pl.ds(pl.multiple_of(begin, 128), n)]
        return ref.at[pl.ds(pl.multiple_of(begin, 16), n), :]

    def out_piece(u, kind, zz, core):
        return cut(outs[UNITS[u][0]].at[zz * 2 + core], u, quarter[kind])

    bar = pltpu.get_barrier_semaphore()
    for d in (partner, to_x, to_y):
        pl.semaphore_signal(bar, inc=1, device_id=d, device_id_type=MESH)

    @pl.when(z > 0)
    def _():
        pl.semaphore_signal(bar, inc=1, device_id=left, device_id_type=MESH)

    @pl.when(z < 3)
    def _():
        pl.semaphore_signal(bar, inc=1, device_id=right, device_id_type=MESH)

    pl.semaphore_wait(bar, 3 + (z > 0).astype(jnp.int32) + (z < 3).astype(jnp.int32))

    def small_copy(zz, core, src, device, sems):
        return copy_to(src, outs[4].at[zz * 2 + core], sems[0], sems[1], device)

    go(small_copy(z, c, ins[4], right, (ss.at[z, 0], sr.at[z])), z < 3)
    go(small_copy(z, c, ins[4], left, (ss.at[z, 1], sr.at[z])), z > 0)
    go(small_copy(z, c, ins[4], partner, (sc.at[z], scr.at[z])))
    for u in FIRST:
        src, dst = cut(ins[UNITS[u][0]], u, quarter[0]), out_piece(u, 0, z, c)
        go(copy_to(src, dst, zs.at[u, z, 0], got.at[0, u, z], right), z < 3)
        go(copy_to(src, dst, zs.at[u, z, 1], got.at[0, u, z], left), z > 0)
    for m in range(4):
        go(copy_to(ins[m], outs[m].at[z * 2 + c], own_c.at[m], own_r.at[m], partner))
    local = [pltpu.make_async_copy(ins[m], outs[m].at[z * 2 + c], own_s.at[m]) for m in range(5)]
    for cp in local:
        cp.start()

    steps = [(t, side) for t in (1, 2, 3) for side in (0, 1)]

    def source(t, side):
        return (z - t, z >= t) if side == 0 else (z + t, z + t <= 3)

    def wait_for(kind, u, zz):
        piece = out_piece(u, kind, zz, c)
        copy_to(piece, piece, cs.at[kind, u, zz], got.at[kind, u, zz], partner).wait_recv()
        return piece

    def sends(kind, u, zz, piece):
        shared, first_x = UNITS[u][3], UNITS[u][4]
        out = []
        if shared and (kind == 0 or (kind == 2 and not first_x)):
            out.append(copy_to(piece, piece, xs.at[min(kind, 1), u, zz], got.at[1 if kind == 0 else 3, u, zz], to_x))
        if shared and (kind == 0 or (kind == 1 and first_x)):
            out.append(copy_to(piece, piece, ys.at[min(kind, 1), u, zz], got.at[2 if kind == 0 else 3, u, zz], to_y))
        out.append(copy_to(piece, piece, cs.at[kind, u, zz], cgot.at[kind, u, zz], partner))
        return out

    def each(kind, u, t, side):
        if kind and not UNITS[u][3]:
            return
        zz, there = source(t, side)
        onward = (z < 3) if side == 0 else (z > 0)

        @pl.when(there)
        def _():
            piece = wait_for(kind, u, zz)
            if kind == 0:
                on = copy_to(piece, piece, zs.at[u, zz, side], got.at[0, u, zz], right if side == 0 else left)

                @pl.when(onward)
                def _():
                    on.start()

            for cp in sends(kind, u, zz, piece):
                cp.start()

        lasting.append((("s", kind, u, t, side), there))
        if kind == 0:
            lasting.append((("z", u, t, side), there & onward))

    def small_step(t, side):
        zz, there = source(t, side)

        @pl.when(there)
        def _():
            piece = outs[4].at[zz * 2 + c]
            copy_to(piece, piece, sc.at[zz], sr.at[zz], partner).wait_recv()

            @pl.when((z < 3) if side == 0 else (z > 0))
            def _():
                small_copy(zz, c, piece, right if side == 0 else left, (ss.at[zz, side], sr.at[zz])).start()

            small_copy(zz, c, piece, partner, (sc.at[zz], scr.at[zz])).start()

        lasting.append((("m", t, side), there))

    turns = [(t, u) for t in (1, 2, 3) for u in FIRST]
    for i in range(len(turns) + 3):
        if i < len(turns):
            t, u = turns[i]
            for side in (0, 1):
                each(0, u, t, side)
        if 0 <= i - 1 < len(turns):
            t, u = turns[i - 1]
            for side in (0, 1):
                each(1 if UNITS[u][4] else 2, u, t, side)
        if 0 <= i - 2 < len(turns):
            t, u = turns[i - 2]
            for side in (0, 1):
                each(2 if UNITS[u][4] else 1, u, t, side)
        if i - 3 >= 0:
            t, u = turns[i - 3]
            for side in (0, 1):
                each(3, u, t, side)
        if i in SMALL_AT:
            for side in (0, 1):
                small_step(SMALL_AT.index(i) + 1, side)

    for cp, when in lasting:
        if not isinstance(cp, tuple):
            if when is None:
                cp.wait_send()
            else:
                @pl.when(when)
                def _():
                    cp.wait_send()
        elif cp[0] == "z":
            _, u, t, side = cp
            zz, _ = source(t, side)
            piece = out_piece(u, 0, zz, c)

            @pl.when(when)
            def _():
                copy_to(piece, piece, zs.at[u, zz, side], got.at[0, u, zz], partner).wait_send()
        elif cp[0] == "m":
            _, t, side = cp
            zz, _ = source(t, side)
            piece = outs[4].at[zz * 2 + c]

            @pl.when(when)
            def _():
                @pl.when((z < 3) if side == 0 else (z > 0))
                def _():
                    small_copy(zz, c, piece, partner, (ss.at[zz, side], sr.at[zz])).wait_send()

                small_copy(zz, c, piece, partner, (sc.at[zz], scr.at[zz])).wait_send()
                other = outs[4].at[zz * 2 + 1 - c]
                copy_to(other, other, sc.at[zz], scr.at[zz], partner).wait_recv()
        else:
            _, kind, u, t, side = cp
            zz, _ = source(t, side)
            piece = out_piece(u, kind, zz, c)
            other = out_piece(u, kind, zz, 1 - c)

            @pl.when(when)
            def _():
                for cp in sends(kind, u, zz, piece):
                    cp.wait_send()
                copy_to(other, other, cs.at[kind, u, zz], cgot.at[kind, u, zz], partner).wait_recv()

    for m in range(4):
        other = outs[m].at[z * 2 + 1 - c]
        copy_to(other, other, own_c.at[m], own_r.at[m], partner).wait_recv()
    other = outs[4].at[z * 2 + 1 - c]
    copy_to(other, other, sc.at[z], scr.at[z], partner).wait_recv()
    for cp in local:
        cp.wait()


def gather_rows(w_query, w_key_t, w_out, w_value_t, others):
    dma = pltpu.SemaphoreType.DMA
    rows, width = w_query.shape
    packed = (rows, 2 * (width + w_key_t.shape[0]))
    shapes = [packed] + [each.shape for each in others]
    n = len(UNITS)
    return pl.pallas_call(
        gather_kernel,
        name="gather_rows",
        out_shape=tuple(jax.ShapeDtypeStruct((8, *each), BF) for each in shapes),
        in_specs=[pl.BlockSpec(memory_space=pltpu.VMEM)] * 4 + [pl.BlockSpec(memory_space=pl.ANY)] * 4,
        out_specs=tuple([pl.BlockSpec(memory_space=pl.ANY)] * 5),
        scratch_shapes=[
            dma((n, 4, 2)), dma((2, n, 4)), dma((2, n, 4)), dma((4, n, 4)), pltpu.VMEM(packed, BF), dma((4, n, 4)), dma((4, n, 4)),
            dma((5,)), dma((4,)), dma((4,)), dma((4, 2)), dma((4,)), dma((4,)), dma((4,)),
        ],
        compiler_params=pltpu.CompilerParams(collective_id=4, has_side_effects=True),
    )(w_query, w_key_t, w_out, w_value_t, *others)


def keys_kernel(chips, back, kv_ref, w_ref, s_right, r_left, s_core, r_core):
    g, t = lax.axis_index("grp"), lax.axis_index("tok")
    z, c = t // 2, lax.rem(t, 2)
    rows = kv_ref.shape[0]
    partner, right = (g, z * 2 + 1 - c), (g, t + 2)

    def slot(d, core):
        return w_ref.at[pl.ds(pl.multiple_of(((back - d) * 2 + core) * rows, 128), rows)]

    bar = pltpu.get_barrier_semaphore()
    pl.semaphore_signal(bar, inc=1, device_id=partner, device_id_type=MESH)

    @pl.when(z > 0)
    def _():
        pl.semaphore_signal(bar, inc=1, device_id=(g, t - 2), device_id_type=MESH)

    def along(d, src):
        return copy_to(src, slot(d, c), s_right.at[d - 1], r_left.at[d - 1], right)

    def beside(d, src):
        return copy_to(src, slot(d, c), s_core.at[d], r_core.at[d], partner)

    own = w_ref.at[pl.ds(pl.multiple_of((back * 2 + c) * rows, 128), rows)]
    own[...] = kv_ref[...]
    for d in range(1, back + 1):
        @pl.when(z < d)
        def _():
            for core in (0, 1):
                slot(d, core)[...] = jnp.zeros(kv_ref.shape, kv_ref.dtype)

    pl.semaphore_wait(bar, 1 + (z < chips - 1).astype(jnp.int32))

    @pl.when(z < chips - 1)
    def _():
        along(1, kv_ref).start()

    beside(0, kv_ref).start()
    for d in range(1, back + 1):
        @pl.when(z >= d)
        def _():
            along(d, slot(d, c)).wait_recv()
            if d < back:
                @pl.when(z < chips - 1)
                def _():
                    along(d + 1, slot(d, c)).start()
            beside(d, slot(d, c)).start()

    def mine_to(d):
        return copy_to(slot(d, 1 - c), slot(d, 1 - c), s_core.at[d], r_core.at[d], partner)

    mine_to(0).wait_recv()
    beside(0, kv_ref).wait_send()

    @pl.when(z < chips - 1)
    def _():
        along(1, kv_ref).wait_send()

    for d in range(1, back + 1):
        @pl.when(z >= d)
        def _():
            mine_to(d).wait_recv()
            beside(d, slot(d, c)).wait_send()
            if d < back:
                @pl.when(z < chips - 1)
                def _():
                    along(d + 1, slot(d, c)).wait_send()


def exchange_keys(kv, n_tok, nback):
    back = nback // 2
    rows = kv.shape[0]
    dma = pltpu.SemaphoreType.DMA
    return pl.pallas_call(
        lambda *refs: keys_kernel(n_tok // 2, back, *refs),
        name="exchange_keys",
        out_shape=jax.ShapeDtypeStruct(((2 * back + 2) * rows, kv.shape[1]), kv.dtype),
        in_specs=[pl.BlockSpec(memory_space=pltpu.VMEM)],
        out_specs=pl.BlockSpec(memory_space=pltpu.VMEM),
        scratch_shapes=[dma((back,)), dma((back,)), dma((back + 1,)), dma((back + 1,))],
        compiler_params=pltpu.CompilerParams(collective_id=2, has_side_effects=True, vmem_limit_bytes=12 * 2**20),
    )(kv)


def home_kernel(chips, back, p_ref, h_ref, beside_in, sums, after_in, s_left, r_right, s_core, r_core):
    g, t = lax.axis_index("grp"), lax.axis_index("tok")
    z, c = t // 2, lax.rem(t, 2)
    rows = h_ref.shape[1]
    partner, left = (g, z * 2 + 1 - c), (g, t - 2)

    def block(d, core):
        return p_ref.at[pl.ds(pl.multiple_of(((back - d) * 2 + core) * rows, 128), rows)]

    bar = pltpu.get_barrier_semaphore()
    pl.semaphore_signal(bar, inc=1, device_id=partner, device_id_type=MESH)

    @pl.when(z < chips - 1)
    def _():
        pl.semaphore_signal(bar, inc=1, device_id=(g, t + 2), device_id_type=MESH)

    pl.semaphore_wait(bar, 1 + (z > 0).astype(jnp.int32))

    def beside(d):
        return copy_to(block(d, 1 - c), beside_in.at[d], s_core.at[d], r_core.at[d], partner)

    def along(d):
        return copy_to(sums.at[d - 1], after_in.at[d - 1], s_left.at[d - 1], r_right.at[d - 1], left)

    for d in range(back, 0, -1):
        @pl.when(z >= d)
        def _():
            beside(d).start()
    beside(0).start()
    for d in range(back, 0, -1):
        @pl.when(z >= d)
        def _():
            beside(d).wait_recv()
            sums[d - 1] = (block(d, c)[...].astype(F32) + beside_in[d].astype(F32)).astype(BF)
            if d < back:
                @pl.when(z < chips - 1)
                def _():
                    along(d + 1).wait_recv()
                    sums[d - 1] = (sums[d - 1].astype(F32) + after_in[d].astype(F32)).astype(BF)
            along(d).start()
    beside(0).wait_recv()
    h_ref[0] = block(0, c)[...].astype(F32) + beside_in[0].astype(F32)

    @pl.when(z < chips - 1)
    def _():
        along(1).wait_recv()
        h_ref[0] = h_ref[0] + after_in[0].astype(F32)

    beside(0).wait_send()
    for d in range(1, back + 1):
        @pl.when(z >= d)
        def _():
            beside(d).wait_send()
            along(d).wait_send()


def exchange_home(partial, n_tok, nback):
    back = nback // 2
    rows = partial.shape[0] // (2 * back + 2)
    width = partial.shape[1]
    dma = pltpu.SemaphoreType.DMA
    return pl.pallas_call(
        lambda *refs: home_kernel(n_tok // 2, back, *refs),
        name="exchange_home",
        out_shape=jax.ShapeDtypeStruct((1, rows, width), F32),
        in_specs=[pl.BlockSpec(memory_space=pltpu.VMEM)],
        out_specs=pl.BlockSpec(memory_space=pltpu.VMEM),
        scratch_shapes=[
            pltpu.VMEM((back + 1, rows, width), BF), pltpu.VMEM((back, rows, width), BF), pltpu.VMEM((back, rows, width), BF),
            dma((back,)), dma((back,)), dma((back + 1,)), dma((back + 1,)),
        ],
        compiler_params=pltpu.CompilerParams(collective_id=3, has_side_effects=True, vmem_limit_bytes=12 * 2**20),
    )(partial)


def grads_kernel(count, *refs):
    r = {name: refs[i * count : (i + 1) * count] for i, name in enumerate(ROW_NAMES)}
    g_ref, left_t, slots, sems = refs[len(ROW_NAMES) * count :]
    for i, name in enumerate(ROW_NAMES[:4]):
        left_t[i] = jnp.concatenate([each[...].astype(F32).T.astype(BF) for each in r[name]], axis=1)

    def out_copy(p):
        return pltpu.make_async_copy(slots.at[p % 2], g_ref.at[p], sems.at[p % 2])

    split = 2 * COLS - left_t.shape[1]
    for p in range(PARTS):
        if p >= 2:
            out_copy(p - 2).wait()
        low = (p % 4) * COLS
        right = jnp.concatenate([each[:, low : low + COLS] for each in r[ROW_NAMES[4 + p // 4]]], axis=0)
        result = dot_nn(left_t[((0,) * 8 + (1,) * 4 + (2, 2, 3, 3))[p]], right)
        if p == PARTS - 1:
            result = jnp.concatenate([result[:, : COLS - split], dot_nn(left_t[2], right[:, COLS - split :])], axis=1)
        slots[p % 2] = result.astype(BF)
        out_copy(p).start()
    out_copy(PARTS - 2).wait()
    out_copy(PARTS - 1).wait()


def weight_gradients(rows):
    count = len(rows["d_mlp"])
    flat = [each for name in ROW_NAMES for each in rows[name]]
    tokens, width = rows["normed"][0].shape
    return pl.pallas_call(
        lambda *refs: grads_kernel(count, *refs),
        name="weight_gradients",
        out_shape=jax.ShapeDtypeStruct((PARTS, width, COLS), BF),
        in_specs=[pl.BlockSpec(memory_space=pltpu.VMEM)] * len(flat),
        out_specs=pl.BlockSpec(memory_space=pl.ANY),
        scratch_shapes=[pltpu.VMEM((4, width, count * tokens), BF), pltpu.VMEM((2, width, COLS), BF), pltpu.SemaphoreType.DMA((2,))],
        compiler_params=pltpu.CompilerParams(vmem_limit_bytes=60 * 2**20),
    )(*flat)


def spread_kernel(p_ref, out_in, grad_in, acc_in, gate, up, down, d_q, d_k, d_v, d_o, out_ref, grad_ref, one, two, three, came, wide, q_full, k_full, o_full, v_full, sem_in, sem_out, sem_full):
    width = q_full.shape[0]
    order = [12, 13, 14, 15] + list(range(12))

    def fetch(i):
        return pltpu.make_async_copy(p_ref.at[order[i]], came.at[i % 3], sem_in.at[i % 3])

    def put(i):
        p = order[i]
        return pltpu.make_async_copy(wide.at[i % 2], (gate, up, down)[p // 4].at[:, pl.ds((p % 4) * COLS, COLS)], sem_out.at[i % 2])

    fulls = [(q_full, d_q), (k_full, d_k), (o_full, d_o), (v_full, d_v)]

    def put_full(j):
        return pltpu.make_async_copy(fulls[j][0], fulls[j][1], sem_full.at[j])

    fetch(0).start()
    fetch(1).start()
    out_ref[...] = out_in[...]
    grad_ref[...] = grad_in[...]
    for i, each in enumerate((one, two, three)):
        each[...] = acc_in[i, :width]
    for i, p in enumerate(order):
        if i + 2 < len(order):
            fetch(i + 2).start()
        fetch(i).wait()
        part = came.at[i % 3]
        if i >= 6:
            put(i - 2).wait()
        if p >= 12:
            full, other = (q_full, k_full) if p < 14 else (o_full, v_full)
            if p % 2 == 0:
                full[:, :COLS] = part[...].astype(F32)
            else:
                got = part[...].astype(F32)
                full[:, COLS:] = got[:, : width - COLS]
                other[...] = got[:, width - COLS :].T
                put_full(0 if p < 14 else 2).start()
                put_full(1 if p < 14 else 3).start()
        else:
            wide[i % 2] = part[...].astype(F32)
            put(i).start()
    put(len(order) - 2).wait()
    put(len(order) - 1).wait()
    for j in range(4):
        put_full(j).wait()


def spread_out(parts, output, grad, acc):
    n, width, cols = parts.shape
    kv = 2 * cols - width
    ff = 4 * cols
    shapes = [(width, ff), (width, ff), (width, ff), (width, width), (kv, width), (kv, width), (width, width)]
    vm = pltpu.VMEM
    return pl.pallas_call(
        spread_kernel,
        name="spread_out",
        out_shape=tuple(shaped(s, F32) for s in shapes) + (shaped(output.shape, BF), shaped(grad.shape, F32)) + (shaped((width,), F32),) * 3,
        in_specs=[pl.BlockSpec(memory_space=pl.ANY)] + [pl.BlockSpec(memory_space=vm)] * 3,
        out_specs=tuple([pl.BlockSpec(memory_space=pl.ANY)] * 7 + [pl.BlockSpec(memory_space=vm)] * 5),
        scratch_shapes=[
            vm((3, width, cols), BF), vm((2, width, cols), F32),
            vm((width, width), F32), vm((kv, width), F32), vm((width, width), F32), vm((kv, width), F32),
            pltpu.SemaphoreType.DMA((3,)), pltpu.SemaphoreType.DMA((2,)), pltpu.SemaphoreType.DMA((4,)),
        ],
        compiler_params=pltpu.CompilerParams(vmem_limit_bytes=60 * 2**20),
    )(parts, output, grad, acc)


def on_device(
    hidden_in,
    cotangent,
    lengths,
    active,
    norm_attn,
    w_query,
    w_key,
    w_value,
    w_out,
    norm_mlp,
    w_gate,
    w_up,
    w_down,
    w_router,
):
    n_tok = lax.axis_size("tok")
    n_grp = lax.axis_size("grp")
    me_index = lax.axis_index("tok")
    rows, width = hidden_in.shape
    nback = min(SPAN, n_tok // 2)

    share = norm_attn.shape[0]
    vectors = jnp.pad(jnp.stack([norm_attn, norm_mlp, w_router]), ((0, 0), (0, 128 - share)))
    small = jnp.concatenate([vectors, active.astype(BF), jnp.zeros((10, 128), BF)], axis=0)
    others = (w_gate, w_up, w_down, small)
    if (n_grp, n_tok) == (4, 8):
        whole = gather_rows(w_query, w_key.T, w_out, w_value.T, others)
    else:
        packed = jnp.concatenate([w_query, w_key, w_out, w_value], axis=1)
        whole = [lax.all_gather(each, "tok", axis=0) for each in (packed, *others)]
    weights = {name: each.reshape(-1, each.shape[-1]) for name, each in zip(WEIGHTS, whole)}
    gains = jnp.transpose(whole[4][:, :3, :share], (1, 0, 2)).reshape(3, width).astype(F32)
    gains = jnp.pad(gains, ((0, 5), (0, 0)))

    lengths_row = lengths[0]
    token = jnp.arange(rows, dtype=jnp.int32)
    global_rows = me_index * rows + token
    segment_rows = segment_of(lengths_row, global_rows)
    cosine, sine = rotary_tables(position_of(lengths_row, global_rows, segment_rows))
    tables = (jnp.concatenate([cosine] * 4, axis=1), jnp.concatenate([-sine, sine] * 2, axis=1))
    reach = (nback + 1) * rows
    global_keys = (me_index - nback) * rows + jnp.arange(reach, dtype=jnp.int32)
    live_all = jnp.transpose(whole[4][:, 3:6], (1, 0, 2)).reshape(3, -1)
    live_all = jnp.pad(live_all, ((0, 0), (nback * rows, 0)))
    live_keys = lax.dynamic_slice_in_dim(live_all, me_index * rows, reach, 1)
    reachable = (segment_rows[None, :] == segment_of(lengths_row, global_keys)[:, None]) & (
        global_keys[:, None] <= global_rows[None, :]
    )
    masks = jnp.where(reachable[None] & (live_keys[:, :, None] > 0), 1.0, 0.0).astype(F32)
    lives = [active[i].astype(F32)[:, None] for i in range(RECUR)]

    if (n_grp, n_tok) == (4, 8):
        done = all_recursions(hidden_in.T, cotangent.T, masks, jnp.stack(lives), tables, gains, weights, n_tok, nback)
        names = [name + "_t" for name in ROW_NAMES[:4]] + list(ROW_NAMES[4:])
        rows_of = [[done[name + str(step)] for step in reversed(range(RECUR))] for name in names]
        lefts, rights = rows_of[:4], rows_of[4:]
        parts, acc = summed_gradients(lefts, rights, done["acc_out"])
        output, grad = done["output"], done["grad"]
    else:
        kept = []
        made = first_stage(hidden_in.T, tables, gains, weights)
        state = made["state"]
        for step in range(RECUR):
            kvw = exchange_keys(made["kv"], n_tok, nback)
            last = step == RECUR - 1
            done = forward_stage(state, made["q"], kvw, masks[step], lives[step], tables, gains, weights, last)
            kept.append({**done, "state": state, "q": made["q"], "kvw": kvw, "normed_r": made["normed"]})
            made, state = done, done.get("next")

        acc = jnp.zeros((8, 1024), F32)
        before = None
        rows_of = {name: [] for name in ROW_NAMES}
        for step in reversed(range(RECUR)):
            back = backward_stage(kept[step], before, masks[step], lives[step], tables, gains, acc, weights, cotangent.T)
            acc = back["acc_out"]
            if before is not None:
                rows_of["d_packed"].append(back["d_packed"])
            for name in ("d_mlp", "d_gate", "d_up"):
                rows_of[name].append(back[name])
            for name in ("normed_two", "mixed", "hidden"):
                rows_of[name].append(kept[step][name])
            rows_of["normed"].append(kept[step]["normed_r"])
            before = {"home": exchange_home(back["dkv"], n_tok, nback), "d_q": back["d_q"], "state": kept[step]["state"], "d_state": back["d_state"], "d_attn": back["d_attn"]}
        back = backward_stage(None, before, None, None, tables, gains, acc, weights, None)
        rows_of["d_packed"].append(back["d_packed"])
        acc = back["acc_out"]
        parts = weight_gradients(rows_of)
        parts = lax.psum(parts.astype(F32), ("grp", "tok")).astype(BF)
        acc = lax.psum(acc, ("grp", "tok"))
        output, grad = kept[-1]["output"], back["grad"]
    d_gate, d_up, d_down, d_q, d_k, d_v, d_o, output, grad, *small_grads = spread_out(parts, output, grad, acc)
    return (
        output.T,
        grad.T,
        small_grads[0],
        d_q,
        d_k.T,
        d_v.T,
        d_o,
        small_grads[1],
        d_gate,
        d_up,
        d_down.T,
        small_grads[2],
    )


def solution(mesh):
    placed = (
        P(("grp", "tok"), None),
        P(("grp", "tok"), None),
        P("grp", None),
        P(None, ("grp", "tok")),
        P("tok"),
        P("tok", None),
        P("tok", None),
        P("tok", None),
        P("tok", None),
        P("tok"),
        P("tok", None),
        P("tok", None),
        P("tok", None),
        P("tok"),
    )
    return jax.shard_map(
        on_device,
        mesh=mesh,
        in_specs=placed,
        out_specs=(
            P(("grp", "tok"), None),
            P(("grp", "tok"), None),
            P(),
            P(),
            P(),
            P(),
            P(),
            P(),
            P(),
            P(),
            P(),
            P(),
        ),
        check_vma=False,
    )
```
